128 devices in a mesh: pts: 32 (over x, y, core), rep: 4 (over z).
Axes of the slice: x: 4, y: 4, z: 4, core: 2. Of those that a mesh axis runs over, the one named last changes fastest.
Arguments:
- points: bfloat16 [65536, 512], P(('pts', 'rep')), may hold values from -6 to 6
- perm: int32 [65536], P(('pts', 'rep')), may hold values from 0 to 65535, as said below
- inverse: int32 [65536], P(('pts', 'rep')), may hold values from 0 to 65535, as said below
- lengths: int32 [128], P(('pts', 'rep')), may hold values from 128 to 512, as said below
- neighbours: int32 [27, 65536], P(None, ('pts', 'rep')), may hold values from -1 to 65535, as said below
- conv_weight: bfloat16 [13824, 512], P('pts', 'rep'), may hold values from -0.0546875 to 0.0546875
- conv_bias: bfloat16 [512], P(('pts', 'rep')), may hold values from -1 to 1
- encode_weight: bfloat16 [512, 512], P(('pts', 'rep')), may hold values from -0.25 to 0.25
- encode_bias: bfloat16 [512], P(('pts', 'rep')), may hold values from -1 to 1
- encode_gain: bfloat16 [512], P(('pts', 'rep')), may hold values from 2 to 8
- encode_shift: bfloat16 [512], P(('pts', 'rep')), may hold values from -1 to 1
- before_gain: bfloat16 [512], P(('pts', 'rep')), may hold values from 0.5 to 1.5
- before_shift: bfloat16 [512], P(('pts', 'rep')), may hold values from -1 to 1
- triple_weight: bfloat16 [512, 1536], P(('pts', 'rep')), may hold values from -0.25 to 0.25
- query_bias: bfloat16 [512], P(('pts', 'rep')), may hold values from -1 to 1
- value_bias: bfloat16 [512], P(('pts', 'rep')), may hold values from -1 to 1
- output_weight: bfloat16 [512, 512], P(('pts', 'rep')), may hold values from -0.75 to 0.75
- output_bias: bfloat16 [512], P(('pts', 'rep')), may hold values from -1 to 1
- second_gain: bfloat16 [512], P(('pts', 'rep')), may hold values from 0.5 to 1.5
- second_shift: bfloat16 [512], P(('pts', 'rep')), may hold values from -1 to 1
- expand_weight: bfloat16 [512, 2048], P(('pts', 'rep')), may hold values from -0.25 to 0.25
- expand_bias: bfloat16 [2048], P(('pts', 'rep')), may hold values from -1 to 1
- reduce_weight: bfloat16 [2048, 512], P(('pts', 'rep')), may hold values from -0.125 to 0.125
- reduce_bias: bfloat16 [512], P(('pts', 'rep')), may hold values from -1 to 1
- grad_out: bfloat16 [65536, 512], P(('pts', 'rep')), may hold values from -6 to 6
Outputs:
- result: bfloat16 [65536, 512], P(('pts', 'rep'))
- points_grad: bfloat16 [65536, 512], P(('pts', 'rep'))
- conv_weight_grad: float32 [13824, 512], P('pts', 'rep')
- conv_bias_grad: float32 [512], P(('pts', 'rep'))
- encode_weight_grad: float32 [512, 512], P(('pts', 'rep'))
- encode_bias_grad: float32 [512], P(('pts', 'rep'))
- encode_gain_grad: float32 [512], P(('pts', 'rep'))
- encode_shift_grad: float32 [512], P(('pts', 'rep'))
- before_gain_grad: float32 [512], P(('pts', 'rep'))
- before_shift_grad: float32 [512], P(('pts', 'rep'))
- triple_weight_grad: float32 [512, 1536], P(('pts', 'rep'))
- query_bias_grad: float32 [512], P(('pts', 'rep'))
- value_bias_grad: float32 [512], P(('pts', 'rep'))
- output_weight_grad: float32 [512, 512], P(('pts', 'rep'))
- output_bias_grad: float32 [512], P(('pts', 'rep'))
- second_gain_grad: float32 [512], P(('pts', 'rep'))
- second_shift_grad: float32 [512], P(('pts', 'rep'))
- expand_weight_grad: float32 [512, 2048], P(('pts', 'rep'))
- expand_bias_grad: float32 [2048], P(('pts', 'rep'))
- reduce_weight_grad: float32 [2048, 512], P(('pts', 'rep'))
- reduce_bias_grad: float32 [512], P(('pts', 'rep'))
The draws below stay inside these ranges and needn't reach their ends.
Inputs may be any that keep to these rules, and one draw needn't show every extreme that they name: perm is a permutation of the 65536 rows. The number of rows that device i (rows i * 512 onward of the previous order) sends to device j (rows j * 512 onward of the new order) depends only on (j - i) mod 128; it is at most 8, and 8 is reached. inverse is the inverse permutation of perm. `lengths`: some patch is full and some has exactly 128 valid points. -1 marks a missing neighbour; otherwise |neighbours[o, p] - p| <= 128, and both -128 and 128 occur; neighbours[13, p] = p.
All inputs are finite; a program needn't handle non-finite values.
Results may differ from the reference program's by a relative error of at most 0.017.
Values may be sent and summed in bfloat16 or wider, within the bound.
A program may use at most 320 MiB of HBM per device.

```python
import math
import jax
import jax.numpy as jnp
from jax import lax

D = 512
HEAD_DIM = 16
FF = 2048
OFFSETS = 27
TOK_DEV = 512
HEADS = 32
PATCHES = 128
TOKENS = 65536
CAP = 8
HALO = 128


def local_order(order_key):
    return jax.random.permutation(order_key, TOK_DEV).astype(jnp.int32)


def curve_maps(key):
    slot_count = PATCHES * CAP
    score = jax.random.permutation(jax.random.fold_in(key, 11), slot_count).astype(jnp.int32)
    favoured = jax.random.randint(jax.random.fold_in(key, 12), (), 0, PATCHES)
    slot_shift = jnp.arange(slot_count, dtype=jnp.int32) // CAP
    score = jnp.where(slot_shift == favoured, score - slot_count, score)
    order = jnp.argsort(score, stable=True).astype(jnp.int32)
    shifts = jnp.sort(order[:TOK_DEV] // CAP)
    old_local = jax.vmap(local_order)(jax.random.split(jax.random.fold_in(key, 13), PATCHES))
    new_local = jax.vmap(local_order)(jax.random.split(jax.random.fold_in(key, 14), PATCHES))
    target = jnp.arange(PATCHES, dtype=jnp.int32)[:, None]
    source = (target - shifts[None, :]) % PATCHES
    column = jnp.arange(TOK_DEV, dtype=jnp.int32)[None, :]
    old_rows = source * TOK_DEV + old_local[source, column]
    new_rows = target * TOK_DEV + new_local
    perm = jnp.zeros((TOKENS,), jnp.int32).at[new_rows.reshape(-1)].set(old_rows.reshape(-1))
    inverse = jnp.zeros((TOKENS,), jnp.int32).at[old_rows.reshape(-1)].set(new_rows.reshape(-1))
    return (perm, inverse)


def draw_perm(key, part):
    return curve_maps(key)[0]


def draw_inverse(key, part):
    return curve_maps(key)[1]


def draw_lengths(key, part):
    key = jax.random.fold_in(key, 3)
    full = jax.random.randint(jax.random.fold_in(key, 1), (PATCHES,), 0, 2)
    partial_value = jax.random.randint(jax.random.fold_in(key, 2), (PATCHES,), TOK_DEV // 4, TOK_DEV)
    lengths = jnp.where(full == 1, TOK_DEV, partial_value).astype(jnp.int32)
    chosen = jax.random.randint(jax.random.fold_in(key, 4), (), 0, PATCHES)
    other = (chosen + 1 + jax.random.randint(jax.random.fold_in(key, 5), (), 0, PATCHES - 1)) % PATCHES
    lengths = lengths.at[chosen].set(TOK_DEV)
    return lengths.at[other].set(TOK_DEV // 4)


def draw_neighbours(key, part):
    key = jax.random.fold_in(key, 5)
    row_ids = jnp.arange(TOKENS, dtype=jnp.int32)[None, :]
    reach = jax.random.randint(jax.random.fold_in(key, 1), (OFFSETS, TOKENS), HALO // 2, HALO + 1)
    direction = jax.random.randint(jax.random.fold_in(key, 6), (OFFSETS, TOKENS), 0, 2) * 2 - 1
    delta = reach * direction
    present = jax.random.randint(jax.random.fold_in(key, 2), (OFFSETS, TOKENS), 0, 4) < 3
    target = row_ids + delta
    valid = present & (target >= 0) & (target < TOKENS)
    result = jnp.where(valid, target, -1).astype(jnp.int32)
    result = result.at[OFFSETS // 2].set(jnp.arange(TOKENS, dtype=jnp.int32))
    lower_row = jax.random.randint(jax.random.fold_in(key, 3), (), HALO, TOKENS)
    upper_row = jax.random.randint(jax.random.fold_in(key, 4), (), 0, TOKENS - HALO)
    result = result.at[0, lower_row].set(lower_row - HALO)
    return result.at[OFFSETS - 1, upper_row].set(upper_row + HALO)


def block_scale(key, extent, cuts, least, high):
    loudness, own = 1.0, jax.random.fold_in(key, 6)
    for position, shards_of in cuts:
        draws = jnp.exp(jax.random.uniform(jax.random.fold_in(own, position), (shards_of,), jnp.float32, least / len(cuts), high / len(cuts)))
        loudness = loudness * jnp.repeat(draws, extent[position] // shards_of).reshape([-1 if axis == position else 1 for axis in range(len(extent))])
    return loudness


def normal_values(stream_key, extent, scale, most, cuts=(), held_as=jnp.bfloat16):
    gain = block_scale(stream_key, extent, cuts, -0.22, 0.18) if cuts else 1.0
    drawn = jax.random.normal(stream_key, extent, jnp.float32) * scale * gain
    return jnp.minimum(jnp.maximum(drawn, -most), most).astype(held_as)


def setup_inputs(seed: int = 0) -> dict:
    keys = jax.random.split(jax.random.key(seed), 26)
    return {
        "points": normal_values(keys[0], (TOKENS, D), 1.0, 6.0, ((0, 128),)),
        "perm": draw_perm(jax.random.fold_in(keys[25], 71), 0),
        "inverse": draw_inverse(jax.random.fold_in(keys[25], 71), 0),
        "lengths": draw_lengths(jax.random.fold_in(keys[25], 71), 0),
        "neighbours": draw_neighbours(jax.random.fold_in(keys[25], 71), 0),
        "conv_weight": normal_values(keys[5], (OFFSETS * D, D), (OFFSETS * D) ** -0.5, 0.0546875, ((0, 32), (1, 4))),
        "conv_bias": normal_values(keys[6], (D,), 0.2, 1.0, ((0, 128),)),
        "encode_weight": normal_values(keys[7], (D, D), D ** -0.5, 0.25, ((0, 128),)),
        "encode_bias": normal_values(keys[8], (D,), 0.2, 1.0, ((0, 128),)),
        "encode_gain": jnp.clip(jnp.exp(math.log(8.0) - 1.3862944 * jax.random.uniform(keys[9], (D,), jnp.float32) ** block_scale(keys[9], (D,), ((0, 128),), -0.2, 0.2)), 2.0, 8.0).astype(jnp.bfloat16),
        "encode_shift": normal_values(keys[10], (D,), 0.2, 1.0, ((0, 128),)),
        "before_gain": jnp.clip(1.0 + 0.1 * jax.random.normal(keys[11], (D,), jnp.float32), 0.5, 1.5).astype(jnp.bfloat16),
        "before_shift": normal_values(keys[12], (D,), 0.2, 1.0, ((0, 128),)),
        "triple_weight": normal_values(keys[13], (D, 3 * D), D ** -0.5, 0.25, ((0, 128),)),
        "query_bias": normal_values(keys[14], (D,), 0.2, 1.0, ((0, 128),)),
        "value_bias": normal_values(keys[15], (D,), 0.2, 1.0, ((0, 128),)),
        "output_weight": normal_values(keys[16], (D, D), (D // 8) ** -0.5, 0.75, ((0, 128),)),
        "output_bias": normal_values(keys[17], (D,), 0.2, 1.0, ((0, 128),)),
        "second_gain": jnp.clip(1.0 + 0.1 * jax.random.normal(keys[18], (D,), jnp.float32), 0.5, 1.5).astype(jnp.bfloat16),
        "second_shift": normal_values(keys[19], (D,), 0.2, 1.0, ((0, 128),)),
        "expand_weight": normal_values(keys[20], (D, FF), D ** -0.5, 0.25, ((0, 128),)),
        "expand_bias": normal_values(keys[21], (FF,), 0.2, 1.0, ((0, 128),)),
        "reduce_weight": normal_values(keys[22], (FF, D), FF ** -0.5, 0.125, ((0, 128),)),
        "reduce_bias": normal_values(keys[23], (D,), 0.2, 1.0, ((0, 128),)),
        "grad_out": normal_values(keys[24], (TOKENS, D), 1.0, 6.0, ((0, 128),)),
    }


epsilon = 1e-05
precise = lax.Precision.HIGHEST

@jax.custom_vjp
def low(v):
    return lax.optimization_barrier(v.astype(jnp.bfloat16)).astype(jnp.float32)

@jax.custom_vjp
def low_back(v):
    return v

def low_keep(v):
    return (low(v), None)

def low_pass(kept, grad):
    return (grad,)

def back_keep(v):
    return (v, None)

def back_low(kept, grad):
    return (low(grad),)
low.defvjp(low_keep, low_pass)
low_back.defvjp(back_keep, back_low)

def norm_rows(row_values, norm_gain, norm_shift):
    centred = row_values - lax.optimization_barrier(jnp.mean(row_values, axis=-1, keepdims=True))
    spread = lax.optimization_barrier(jnp.mean(centred * centred, axis=-1, keepdims=True))
    return centred * lax.rsqrt(spread + epsilon) * norm_gain + norm_shift

def product(left, right):
    return jnp.dot(left, right, precision=precise)

def patch_block(params, ordered, patch_index, valid_count, offsets):
    conv_weight, conv_bias, encode_weight, encode_bias, encode_gain, encode_shift, before_gain, before_shift, triple_weight, query_bias, value_bias, output_weight, output_bias, second_gain, second_shift, expand_weight, expand_bias, reduce_weight, reduce_bias = params
    own = lax.dynamic_slice_in_dim(ordered, patch_index * TOK_DEV, TOK_DEV, 0)
    present = offsets >= 0
    picked = jnp.take(ordered, jnp.where(present, offsets, 0), axis=0)
    picked = jnp.where(present[:, :, None], picked, 0.0)
    kernel = conv_weight.reshape(OFFSETS, D, D)
    conv = jnp.einsum('otd,ode->te', picked, kernel, precision=precise) + conv_bias
    conv = low(low_back(conv))
    linear = low_back(product(conv, encode_weight) + encode_bias)
    first = own + norm_rows(linear, encode_gain, encode_shift)
    normed = low(norm_rows(first, before_gain, before_shift))
    triple = product(normed, triple_weight)
    queries = low(low_back(triple[:, :D] + query_bias)).reshape(TOK_DEV, HEADS, HEAD_DIM)
    keys_all = low(low_back(triple[:, D:2 * D])).reshape(TOK_DEV, HEADS, HEAD_DIM)
    values_all = low(low_back(triple[:, 2 * D:] + value_bias)).reshape(TOK_DEV, HEADS, HEAD_DIM)
    scores = jnp.einsum('thd,shd->hts', queries, keys_all, precision=precise) * HEAD_DIM ** (-0.5)
    visible = jnp.arange(TOK_DEV) < valid_count
    scores = low_back(jnp.where(visible[None, None, :], scores, -1e+30))
    peak = lax.optimization_barrier(jnp.max(scores, axis=-1, keepdims=True))
    weights = jnp.exp(scores - peak)
    weights = low(weights / lax.optimization_barrier(jnp.sum(weights, axis=-1, keepdims=True)))
    mixed = jnp.einsum('hts,shd->thd', weights, values_all, precision=precise).reshape(TOK_DEV, D)
    mixed = low(low_back(mixed))
    attended = low_back(product(mixed, output_weight) + output_bias)
    second = first + attended
    normed_two = low(norm_rows(second, second_gain, second_shift))
    hidden = low_back(product(normed_two, expand_weight) + expand_bias)
    active = low(jax.nn.gelu(hidden, approximate=False))
    branch = low_back(product(active, reduce_weight) + reduce_bias)
    return second + branch

def reference(points, perm, inverse, lengths, neighbours, conv_weight, conv_bias, encode_weight, encode_bias, encode_gain, encode_shift, before_gain, before_shift, triple_weight, query_bias, value_bias, output_weight, output_bias, second_gain, second_shift, expand_weight, expand_bias, reduce_weight, reduce_bias, grad_out):
    params = tuple((weight_item.astype(jnp.float32) for weight_item in (conv_weight, conv_bias, encode_weight, encode_bias, encode_gain, encode_shift, before_gain, before_shift, triple_weight, query_bias, value_bias, output_weight, output_bias, second_gain, second_shift, expand_weight, expand_bias, reduce_weight, reduce_bias)))
    ordered = points.astype(jnp.float32)[perm]
    patch_offsets = neighbours.reshape(OFFSETS, PATCHES, TOK_DEV).transpose(1, 0, 2)

    def forward(weight_set, rows_in):
        rows_in = low_back(rows_in)

        def one_patch(packed):
            return jax.checkpoint(patch_block)(weight_set, rows_in, packed[0], packed[1], packed[2])
        blocks = lax.map(one_patch, (jnp.arange(PATCHES, dtype=jnp.int32), lengths, patch_offsets))
        return blocks.reshape(TOKENS, D)
    result, pullback = jax.vjp(forward, params, ordered)
    weight_grads, ordered_grad = pullback(grad_out.astype(jnp.float32))
    points_grad = ordered_grad[inverse]
    grad_conv, grad_conv_bias, grad_encode, grad_encode_bias, grad_encode_gain, grad_encode_shift, grad_before_gain, grad_before_shift, grad_triple, grad_query_bias, grad_value_bias, grad_output, grad_output_bias, grad_second_gain, grad_second_shift, grad_expand, grad_expand_bias, grad_reduce, grad_reduce_bias = weight_grads
    return (result.astype(jnp.bfloat16), points_grad.astype(jnp.bfloat16), grad_conv, grad_conv_bias, grad_encode, grad_encode_bias, grad_encode_gain, grad_encode_shift, grad_before_gain, grad_before_shift, grad_triple, grad_query_bias, grad_value_bias, grad_output, grad_output_bias, grad_second_gain, grad_second_shift, grad_expand, grad_expand_bias, grad_reduce, grad_reduce_bias)
```

```python
import jax
import jax.numpy as jnp
from jax import lax
from jax.experimental import pallas as pl
from jax.experimental.pallas import tpu as pltpu
from jax.sharding import PartitionSpec as P

HEAD_DIM = 16

MESH = pl.DeviceIdType.MESH
BF = jnp.bfloat16
F32 = jnp.float32


def place():
    p = lax.axis_index("pts")
    return {
        "x": lax.div(p, 8),
        "y": lax.rem(lax.div(p, 2), 4),
        "c": lax.rem(p, 2),
        "z": lax.axis_index("rep"),
    }


def device_at(at):
    return ((at["x"] * 4 + at["y"]) * 2 + at["c"], at["z"])


def moved(at, axis, step):
    size = 2 if axis == "c" else 4
    return {**at, axis: lax.rem(at[axis] + step, size)}


def greet(at):
    barrier = pltpu.get_barrier_semaphore()
    friends = [("x", 1), ("x", 3), ("y", 1), ("y", 3), ("z", 1), ("z", 2), ("z", 3), ("c", 1)]
    for axis, step in friends:
        pl.semaphore_signal(
            barrier, inc=1, device_id=device_at(moved(at, axis, step)), device_id_type=MESH
        )
    pl.semaphore_wait(barrier, len(friends))


def whole(value):
    return slice(None) if value is None else value


def conv_view(ref, sel, h):
    r0, r1 = h
    return ref.at[
        whole(sel.get("z")), whole(sel.get("x")), whole(sel.get("y")), sel["c"], pl.ds(r0, r1 - r0), :
    ]


def wide_view(ref, sel, h):
    k0, k1 = h
    return ref.at[
        whole(sel.get("z")), pl.ds(k0, k1 - k0), whole(sel.get("x")), whole(sel.get("y")), sel["c"]
    ]


def tall_view(ref, sel, h):
    l0, l1 = h
    return ref.at[
        whole(sel.get("x")), whole(sel.get("y")), sel["c"], whole(sel.get("z")), :, pl.ds(l0, l1 - l0)
    ]


def flat_view(ref, sel, h):
    return ref.at[whole(sel.get("x")), whole(sel.get("y")), sel["c"]]


STREAMS = (
    ("cz", 0, conv_view, "xyz", ((0, 64), (64, 112))),
    ("cx", 0, conv_view, "yzx", ((112, 192), (192, 272))),
    ("cy", 0, conv_view, "zxy", ((272, 352), (352, 432))),
    ("m2", 2, tall_view, "zyx", ((0, 256), (256, 512))),
    ("m1", 1, wide_view, "xyz", ((0, 5), (5, 9))),
    ("vt", 3, flat_view, "xy", ((0, 16),)),
)
SLOTS = 40


def gather_kernel(conv, m1p, m2, vt, gc, g1, g2, gv, pre, m1b, prev, vb, sends, recvs, locs, presend, prerecv):
    at = place()
    greet(at)
    outs = (gc, g1, g2, gv)
    pending = []
    crossing = []

    def push(src, dst, k, to, keep=True):
        copy = pltpu.make_async_remote_copy(
            src_ref=src,
            dst_ref=dst,
            send_sem=sends.at[k[0], k[1]],
            recv_sem=recvs.at[k[0], k[1]],
            device_id=device_at(to),
            device_id_type=MESH,
        )
        copy.start()
        pending.append(copy)
        return copy

    def own_view(s, h):
        name, op, view, order, halves = s
        if op == 0:
            return conv.at[pl.ds(h[0], h[1] - h[0]), :]
        if op == 1:
            return m1b.at[pl.ds(h[0], h[1] - h[0])]
        if op == 2:
            return m2.at[:, pl.ds(h[0], h[1] - h[0])]
        return vb

    pre_copies = []
    for step in (1, 2, 3):
        to = moved(at, "z", step)
        for j, (src, dst) in enumerate(((m1p.at[to["z"]], pre.at[step]), (vt, prev.at[step]))):
            copy = pltpu.make_async_remote_copy(
                src_ref=src,
                dst_ref=dst,
                send_sem=presend.at[j, step],
                recv_sem=prerecv.at[j, step],
                device_id=device_at(to),
                device_id_type=MESH,
            )
            copy.start()
            pre_copies.append(copy)

    local_copies = {}

    def keep_own(i):
        name, op, view, order, halves = STREAMS[i]
        for j, h in enumerate(halves):
            copy = pltpu.make_async_copy(
                own_view(STREAMS[i], h), view(outs[op], at, h), locs.at[i, j]
            )
            copy.start()
            local_copies[(i, j)] = copy

    state = {}

    def block_sel(order, phase, index=None, axis=None):
        sel = {"c": at["c"]}
        for a in "xyz":
            if a in order and order.index(a) < phase:
                continue
            sel[a] = at[a]
        if axis is not None:
            sel[axis] = index
        return sel

    def begin(i, phase):
        name, op, view, order, halves = STREAMS[i]
        axis = order[phase]
        n = len(halves)
        sel = block_sel(order, phase)
        copies = {}
        for d, hs in ((1, range(n)), (3, reversed(range(n)))):
            for h in hs:
                dst = view(outs[op], sel, halves[h])
                src = own_view(STREAMS[i], halves[h]) if phase == 0 else dst
                k = (i, phase * 6 + (0 if d == 1 else 2) + h)
                copies[(d, h)] = push(src, dst, k, moved(at, axis, d))
        state[(i, phase)] = copies
        if phase == len(order) - 1:
            for h in range(n):
                dst = view(outs[op], sel, halves[h])
                crossing.append(push(dst, dst, (i, 20 + h), moved(at, "c", 1)))

    def relay(i, phase):
        name, op, view, order, halves = STREAMS[i]
        axis = order[phase]
        last = phase == len(order) - 1
        n = len(halves)
        copies = state[(i, phase)]
        base = phase * 6
        other = moved(at, "c", 1)
        for d in (1, 3):
            h = 0 if d == 1 else n - 1
            if n == 1 and d == 3:
                continue
            copies[(d, h)].wait_recv()
            sel = block_sel(order, phase, lax.rem(at[axis] + 4 - d, 4), axis)
            ref = view(outs[op], sel, halves[h])
            copies[(d, "f")] = push(ref, ref, (i, base + (4 if d == 1 else 5)), moved(at, axis, d))
            if last:
                crossing.append(push(ref, ref, (i, 22 + d), other))
        for d in (1, 3):
            for h in range(n):
                if h == (0 if d == 1 else n - 1) and not (n == 1 and d == 3):
                    continue
                copies[(d, h)].wait_recv()
                if last:
                    sel = block_sel(order, phase, lax.rem(at[axis] + 4 - d, 4), axis)
                    ref = view(outs[op], sel, halves[h])
                    crossing.append(push(ref, ref, (i, 26 + d), other))

    def finish(i, phase):
        name, op, view, order, halves = STREAMS[i]
        axis = order[phase]
        last = phase == len(order) - 1
        n = len(halves)
        copies = state[(i, phase)]
        other = moved(at, "c", 1)
        for d in (1, 3):
            if (d, "f") not in copies:
                continue
            copies[(d, "f")].wait_recv()
            if last:
                h = 0 if d == 1 else n - 1
                sel = block_sel(order, phase, lax.rem(at[axis] + 2, 4), axis)
                ref = view(outs[op], sel, halves[h])
                crossing.append(push(ref, ref, (i, 30 + d), other))

    early = (0, 1, 2, 3)
    for i in early:
        begin(i, 0)
        keep_own(i)
    for copy in pre_copies:
        copy.wait()
    mine = m1p.at[at["z"]]
    pre[0] = mine[...]

    def tile(k, _):
        pieces = [
            pre[lax.rem(at["z"] - s + 4, 4), k].astype(F32) for s in range(4)
        ]
        m1b[k] = jnp.concatenate(pieces, axis=0).astype(BF)
        return 0

    lax.fori_loop(0, 9, tile, 0)
    vb[...] = (
        vt[...].astype(F32) + prev[1].astype(F32) + prev[2].astype(F32) + prev[3].astype(F32)
    ).astype(BF)
    for i in (4, 5):
        begin(i, 0)
        keep_own(i)
    for phase in (0, 1, 2):
        live = [i for i in range(len(STREAMS)) if phase < len(STREAMS[i][3])]
        for i in live:
            relay(i, phase)
        for i in live:
            finish(i, phase)
            if phase == 0:
                for h in range(len(STREAMS[i][4])):
                    local_copies[(i, h)].wait()
            if phase + 1 < len(STREAMS[i][3]):
                begin(i, phase + 1)
    for copy in crossing:
        copy.wait_recv()
    for copy in pending:
        copy.wait_send()


ANY = pl.BlockSpec(memory_space=pl.ANY)
VM = pl.BlockSpec(memory_space=pltpu.VMEM)


def gather_weights(conv, m1p, m2, vt):
    shape = jax.ShapeDtypeStruct
    n = len(STREAMS)
    return pl.pallas_call(
        gather_kernel,
        out_shape=(
            shape((4, 4, 4, 2, 432, 128), BF),
            shape((4, 9, 4, 4, 2, 16, 128), BF),
            shape((4, 4, 2, 4, 16, 512), BF),
            shape((4, 4, 2, 16, 128), BF),
        ),
        in_specs=[ANY, VM, ANY, VM],
        out_specs=[ANY] * 4,
        scratch_shapes=[
            pltpu.VMEM((4, 9, 4, 128), BF),
            pltpu.VMEM((9, 16, 128), BF),
            pltpu.VMEM((4, 16, 128), BF),
            pltpu.VMEM((16, 128), BF),
            pltpu.SemaphoreType.DMA((n, SLOTS)),
            pltpu.SemaphoreType.DMA((n, SLOTS)),
            pltpu.SemaphoreType.DMA((n, 2)),
            pltpu.SemaphoreType.DMA((2, 4)),
            pltpu.SemaphoreType.DMA((2, 4)),
        ],
        compiler_params=pltpu.CompilerParams(collective_id=0, has_side_effects=True),
        name="gather_weights",
    )(conv, m1p, m2, vt)


RS_FRIENDS = [("x", 1), ("x", 2), ("x", 3), ("y", 1), ("y", 2), ("y", 3), ("z", 1), ("z", 2), ("z", 3), ("c", 1)]


def greet_all(at):
    barrier = pltpu.get_barrier_semaphore()
    for axis, step in RS_FRIENDS:
        pl.semaphore_signal(
            barrier, inc=1, device_id=device_at(moved(at, axis, step)), device_id_type=MESH
        )
    pl.semaphore_wait(barrier, len(RS_FRIENDS))


RS_STREAMS = (
    ("cz", 0, "zxycRL", {"R": 112, "L": 128}, "R", 0, "zyx", ((0, 64), (64, 112))),
    ("cx", 0, "zxycRL", {"R": 160, "L": 128}, "R", 112, "xzy", ((0, 80), (80, 160))),
    ("cy", 0, "zxycRL", {"R": 160, "L": 128}, "R", 272, "yxz", ((0, 80), (80, 160))),
    ("m2", 2, "xyczSL", {"S": 16, "L": 512}, "L", 0, "xyz", ((0, 256), (256, 512))),
    ("m1", 1, "zKxycSL", {"K": 9, "S": 16, "L": 128}, "K", 0, "zyx", ((0, 5), (5, 9))),
)
RS_ORDER = (4, 3, 0, 1, 2)


def cut_view(ref, layout, sel, cut=None, span=None, base=0):
    index = []
    for dim in layout:
        if dim in sel:
            index.append(sel[dim])
        elif dim == cut and span is not None:
            index.append(pl.ds(base + span[0], span[1] - span[0]))
        else:
            index.append(slice(None))
    return ref.at[tuple(index)]


def sizes_of(layout, plain):
    return tuple(plain[d] if d in plain else 4 for d in layout)


def rs_buffers():
    shapes = []
    for name, op, layout, plain, cut, base, order, halves in RS_STREAMS:
        inner = layout.replace("c", "")
        shapes += [sizes_of(inner, plain)] * 2
        left = inner
        for axis in order:
            left = left.replace(axis, "")
            for span in (halves[0], halves[1]):
                shapes.append(sizes_of(left, {**plain, cut: span[1] - span[0]}))
            shapes += [sizes_of(left, plain)] * 2
    return [pltpu.VMEM(s, BF) for s in shapes]


PER_STREAM = 14


def scatter_kernel(gc, g1, g2, gv, oc, o1, o2, ov, *scratch):
    bufs = scratch[: PER_STREAM * len(RS_STREAMS)]
    post, postr, vx, vr, sends, recvs, locs, vsend, vrecv, psend, precv = scratch[PER_STREAM * len(RS_STREAMS) :]
    at = place()
    greet_all(at)
    ops = (gc, g1, g2)
    pending = []
    other = moved(at, "c", 1)

    def push(src, dst, send, recv, to):
        copy = pltpu.make_async_remote_copy(
            src_ref=src, dst_ref=dst, send_sem=send, recv_sem=recv,
            device_id=device_at(to), device_id_type=MESH,
        )
        copy.start()
        pending.append(copy)
        return copy

    def stream(i):
        name, op, layout, plain, cut, base, order, halves = RS_STREAMS[i]
        mine = bufs[i * PER_STREAM : (i + 1) * PER_STREAM]
        return layout, layout.replace("c", ""), cut, base, order, halves, mine, ops[op], plain

    def add(dst, dst_layout, dst_sel, srcs, cut, span, plain):
        free = [d for d in dst_layout if d in "xyz" and d not in dst_sel]
        count = 4 ** len(free)

        def one(n, _):
            sel = dict(dst_sel)
            for k, d in enumerate(reversed(free)):
                sel[d] = lax.rem(lax.div(n, 4**k), 4)
            where = cut_view(dst, dst_layout, sel, cut, span)
            total = where[...].astype(F32)
            for src, src_layout, src_sel, src_span in srcs:
                full = {**{d: sel[d] for d in free}, **src_sel}
                total = total + cut_view(src, src_layout, full, cut, src_span)[...].astype(F32)
            where[...] = total.astype(BF)
            return 0

        if count == 1:
            one(0, 0)
        else:
            lax.fori_loop(0, count, one, 0)

    STEPS = (2, 1, 3, 0)

    def load(i):
        layout, inner, cut, base, order, halves, mine, src, plain = stream(i)
        axis = order[0]
        span = (0, plain[cut])
        copies = []
        for k, step in enumerate(STEPS):
            a = lax.rem(at[axis] + step, 4)
            theirs = cut_view(src, layout, {"c": other["c"], axis: a}, cut, span, base)
            here = cut_view(src, layout, {"c": at["c"], axis: a}, cut, span, base)
            sib = push(theirs, cut_view(mine[1], inner, {axis: a}), sends.at[i, k], recvs.at[i, k], other)
            loc = pltpu.make_async_copy(here, cut_view(mine[0], inner, {axis: a}), locs.at[i, k])
            loc.start()
            copies.append((sib, loc))
        return copies

    def start_phase(i, phase, loaded):
        layout, inner, cut, base, order, halves, mine, src, plain = stream(i)
        axis = order[phase]
        done = {a: at[a] for a in order[:phase]}
        left = "".join(d for d in inner if d not in order[: phase + 1])
        r0, r1, rp, rm = mine[2 + 4 * phase : 6 + 4 * phase]
        A = mine[0]
        slot = lambda k: (sends.at[i, 4 + phase * 6 + k], recvs.at[i, 4 + phase * 6 + k])
        span = (0, plain[cut])
        n = at[axis]
        up, down = moved(at, axis, 1), moved(at, axis, 3)
        view = lambda a, h: cut_view(A, inner, {**done, axis: a}, cut, h)
        got = {}
        for k, step in enumerate(STEPS):
            a = lax.rem(n + step, 4)
            if loaded is not None:
                sib, loc = loaded[k]
                sib.wait_recv()
                loc.wait()
                add(A, inner, {axis: a}, [(mine[1], inner, {axis: a}, span)], cut, span, plain)
            if step == 2:
                got["r0"] = push(view(a, halves[0]), r0, *slot(0), up)
                got["r1"] = push(view(a, halves[1]), r1, *slot(1), down)
            elif step == 1:
                got["p1"] = push(view(a, halves[1]), cut_view(rp, left, {}, cut, halves[1]), *slot(2), up)
            elif step == 3:
                got["m0"] = push(view(a, halves[0]), cut_view(rm, left, {}, cut, halves[0]), *slot(3), down)
        return got

    def middle(i, phase, got):
        layout, inner, cut, base, order, halves, mine, src, plain = stream(i)
        axis = order[phase]
        done = {a: at[a] for a in order[:phase]}
        left = "".join(d for d in inner if d not in order[: phase + 1])
        r0, r1, rp, rm = mine[2 + 4 * phase : 6 + 4 * phase]
        A = mine[0]
        slot = lambda k: (sends.at[i, 4 + phase * 6 + k], recvs.at[i, 4 + phase * 6 + k])
        up, down = moved(at, axis, 1), moved(at, axis, 3)
        view = lambda a, h: cut_view(A, inner, {**done, axis: a}, cut, h)
        local = lambda h: (0, h[1] - h[0])
        got["r0"].wait_recv()
        add(A, inner, {**done, axis: up[axis]}, [(r0, left, {}, local(halves[0]))], cut, halves[0], plain)
        got["p0"] = push(view(up[axis], halves[0]), cut_view(rp, left, {}, cut, halves[0]), *slot(4), up)
        got["r1"].wait_recv()
        add(A, inner, {**done, axis: down[axis]}, [(r1, left, {}, local(halves[1]))], cut, halves[1], plain)
        got["m1"] = push(view(down[axis], halves[1]), cut_view(rm, left, {}, cut, halves[1]), *slot(5), down)

    def close(i, phase, got):
        layout, inner, cut, base, order, halves, mine, src, plain = stream(i)
        axis = order[phase]
        done = {a: at[a] for a in order[: phase + 1]}
        left = "".join(d for d in inner if d not in order[: phase + 1])
        r0, r1, rp, rm = mine[2 + 4 * phase : 6 + 4 * phase]
        for k in ("p1", "m0", "p0", "m1"):
            got[k].wait_recv()
        span = (0, plain[cut])
        add(mine[0], inner, done, [(rp, left, {}, span), (rm, left, {}, span)], cut, span, plain)

    vstate = []

    def vector_step(k):
        axis, steps = (("c", (1,)), ("z", (1, 2, 3)), ("y", (1, 2, 3)), ("x", (1, 2, 3)))[k]
        copies = []
        for s in steps:
            to = moved(at, axis, s)
            if axis == "x":
                src, dst = vx.at[3, to["x"]], vr.at[3, s, 0]
            else:
                src, dst = (gv if k == 0 else vx.at[k]), vr.at[k, s]
            copies.append(push(src, dst, vsend.at[k, s], vrecv.at[k, s], to))
        return copies

    def vector_add(k, copies):
        for copy in copies:
            copy.wait_recv()
        if k == 3:
            total = vx[3, at["x"]]
            for s in (1, 2, 3):
                total = total + vr[3, s, 0]
            ov[...] = total
            return
        total = gv[...] if k == 0 else vx[k]
        for s in (1,) if k == 0 else (1, 2, 3):
            total = total + vr[k, s]
        vx[k + 1] = total

    vcopies = vector_step(0)
    loaded = {i: load(i) for i in RS_ORDER}
    state = {}
    for i in RS_ORDER:
        state[i] = start_phase(i, 0, loaded[i])
    for phase in range(3):
        vector_add(phase, vcopies)
        vcopies = vector_step(phase + 1)
        for i in RS_ORDER:
            middle(i, phase, state[i])
        for i in RS_ORDER:
            close(i, phase, state[i])
            if phase < 2:
                state[i] = start_phase(i, phase + 1, None)
    vector_add(3, vcopies)
    for i in (0, 1, 2):
        layout, inner, cut, base, order, halves, mine, src, plain = stream(i)
        oc[pl.ds(base, plain["R"]), :] = mine[0][at["z"], at["x"], at["y"]].astype(F32)
    o2[...] = bufs[3 * PER_STREAM][at["x"], at["y"], at["z"]].astype(F32)
    m1 = bufs[4 * PER_STREAM]
    wide = m1[at["z"], :, at["x"], at["y"]].astype(F32)
    for q in range(4):
        post[q] = wide[:, 4 * q : 4 * q + 4, :].astype(BF)
    copies = []
    for s in (1, 2, 3):
        to = moved(at, "z", s)
        copies.append(push(post.at[to["z"]], postr.at[s], psend.at[s], precv.at[s], to))
    o1[at["z"]] = post[at["z"]].astype(F32)
    for s in (1, 2, 3):
        copies[s - 1].wait_recv()
        o1[lax.rem(at["z"] + 4 - s, 4)] = postr[s].astype(F32)
    for copy in pending:
        copy.wait_send()


def scatter_grads(gc, g1, g2, gv):
    shape = jax.ShapeDtypeStruct
    n = len(RS_STREAMS)
    return pl.pallas_call(
        scatter_kernel,
        out_shape=(
            shape((432, 128), F32),
            shape((4, 9, 4, 128), F32),
            shape((16, 512), F32),
            shape((16, 128), F32),
        ),
        in_specs=[ANY, ANY, ANY, VM],
        out_specs=[VM] * 4,
        scratch_shapes=rs_buffers()
        + [
            pltpu.VMEM((4, 9, 4, 128), BF),
            pltpu.VMEM((4, 9, 4, 128), BF),
            pltpu.VMEM((4, 4, 16, 128), F32),
            pltpu.VMEM((4, 4, 4, 16, 128), F32),
            pltpu.SemaphoreType.DMA((n, 22)),
            pltpu.SemaphoreType.DMA((n, 22)),
            pltpu.SemaphoreType.DMA((n, 4)),
            pltpu.SemaphoreType.DMA((4, 4)),
            pltpu.SemaphoreType.DMA((4, 4)),
            pltpu.SemaphoreType.DMA((4,)),
            pltpu.SemaphoreType.DMA((4,)),
        ],
        compiler_params=pltpu.CompilerParams(
            collective_id=1, has_side_effects=True, vmem_limit_bytes=58 * 2**20
        ),
        name="scatter_grads",
    )(gc, g1, g2, gv)


epsilon = 1e-05


def with_halo(cells, sides, width):
    for axis, dim in sides:
        count = lax.axis_size(axis)
        ends = count - 1
        head = lax.slice_in_dim(cells, 0, width, axis=dim)
        tail = lax.slice_in_dim(cells, cells.shape[dim] - width, cells.shape[dim], axis=dim)
        cells = jnp.concatenate(
            [
                lax.ppermute(tail, axis, [(i, (i + 1) % count) for i in range(ends)]),
                cells,
                lax.ppermute(head, axis, [((i + 1) % count, i) for i in range(ends)]),
            ],
            axis=dim,
        )
    return cells


def norm_rows(row_values, norm_gain, norm_shift):
    centred = row_values - jnp.mean(row_values, axis=-1, keepdims=True)
    spread = jnp.mean(centred * centred, axis=-1, keepdims=True)
    return centred * lax.rsqrt(spread + epsilon) * norm_gain + norm_shift


def norm_back(row_values, norm_gain, norm_shift, incoming):
    unused_out, pullback = jax.vjp(norm_rows, row_values, norm_gain, norm_shift)
    return pullback(incoming)


def gelu_exact(values_in):
    return jax.nn.gelu(values_in, approximate=False)


def widen(array_in):
    return array_in.astype(jnp.float32)


def column_sum(array_in):
    return jnp.sum(array_in.astype(jnp.float32), axis=0)


def forward_product(left, weight):
    return jnp.dot(left, weight, preferred_element_type=jnp.float32)


def inner_grad(left, right):
    return jnp.einsum("td,te->de", left, right, preferred_element_type=jnp.float32)


def back_product(grad_rows, weight):
    return jnp.einsum("te,de->td", grad_rows, weight, preferred_element_type=jnp.float32)


def rank_within(labels, count):
    onehot = (labels[:, None] == jnp.arange(count, dtype=jnp.int32)[None, :]).astype(jnp.int32)
    before = jnp.cumsum(onehot, axis=0) - onehot
    return jnp.sum(before * onehot, axis=1)


def pick_rows(extended_rows, index_rows):
    padded = jnp.concatenate(
        [extended_rows, jnp.zeros((1, extended_rows.shape[1]), extended_rows.dtype)], axis=0
    )
    return jnp.take(padded, index_rows, axis=0)


def per_device(
    points,
    perm,
    inverse,
    lengths,
    neighbours,
    conv_weight,
    conv_bias,
    encode_weight,
    encode_bias,
    encode_gain,
    encode_shift,
    before_gain,
    before_shift,
    triple_weight,
    query_bias,
    value_bias,
    output_weight,
    output_bias,
    second_gain,
    second_shift,
    expand_weight,
    expand_bias,
    reduce_weight,
    reduce_bias,
    grad_out,
):
    rows, width = points.shape
    devices = lax.axis_size(("pts", "rep"))
    offset_count = neighbours.shape[0]
    capacity = 2 * rows // devices
    halo_rows = rows // 4
    extent = rows + 2 * halo_rows + 1
    heads = width // HEAD_DIM
    scale = HEAD_DIM ** (-0.5)
    device = lax.axis_index(("pts", "rep"))
    pts, rep = lax.axis_index("pts"), lax.axis_index("rep")
    lane = lax.rem(pts, 8) * 16 + rep * 4
    wide_piece = jnp.concatenate([encode_weight, triple_weight, output_weight, expand_weight], axis=1)
    wide_piece = wide_piece.reshape(4, 36, 128).transpose(1, 0, 2).reshape(4, 9, 4, 128)
    vector_piece = jnp.concatenate(
        [
            jnp.stack(
                [
                    conv_bias,
                    encode_bias,
                    encode_gain,
                    encode_shift,
                    before_gain,
                    before_shift,
                    query_bias,
                    value_bias,
                    output_bias,
                    second_gain,
                    second_shift,
                    reduce_bias,
                ]
            ),
            expand_bias.reshape(4, 4),
        ],
        axis=0,
    )
    vector_tile = lax.dynamic_update_slice(jnp.zeros((16, 128), BF), vector_piece, (0, lane))
    got_conv, got_wide, got_tall, got_vectors = gather_weights(
        conv_weight, wide_piece, reduce_weight, vector_tile
    )
    kernel = got_conv.reshape(4, 27, 512, 128).transpose(1, 2, 0, 3).reshape(27, 512, 512)
    wide_full = got_wide.reshape(36, 512, 128).transpose(1, 0, 2).reshape(512, 4608)
    full_encode = wide_full[:, :512]
    full_triple = wide_full[:, 512:2048]
    full_output = wide_full[:, 2048:2560]
    full_expand = wide_full[:, 2560:]
    full_reduce = got_tall.reshape(2048, 512)
    vectors = got_vectors.reshape(4, 8, 16, 128).astype(F32).sum(axis=1)
    vectors = vectors.transpose(1, 0, 2).reshape(16, 512)
    (
        full_conv_bias,
        full_encode_bias,
        full_encode_gain,
        full_encode_shift,
        full_before_gain,
        full_before_shift,
        full_query_bias,
        full_value_bias,
        full_output_bias,
        full_second_gain,
        full_second_shift,
        full_reduce_bias,
    ) = [vectors[k] for k in range(12)]
    full_expand_bias = vectors[12:].reshape(4, 128, 4).transpose(1, 0, 2).reshape(2048)
    gain_zero = widen(full_encode_gain)
    shift_zero = widen(full_encode_shift)
    gain_one = widen(full_before_gain)
    shift_one = widen(full_before_shift)
    gain_two = widen(full_second_gain)
    shift_two = widen(full_second_shift)
    destination = inverse // rows
    send_index = destination * capacity + rank_within(destination, devices)
    outgoing = jnp.zeros((devices * capacity, width), jnp.bfloat16).at[send_index].set(points)
    incoming = lax.all_to_all(
        outgoing.reshape(devices, capacity, width),
        ("pts", "rep"),
        split_axis=0,
        concat_axis=0,
        tiled=True,
    )
    incoming = incoming.reshape(devices * capacity, width)
    source = perm // rows
    same_source = source[:, None] == source[None, :]
    earlier = perm[None, :] < perm[:, None]
    take_index = source * capacity + jnp.sum(same_source & earlier, axis=1)
    ordered = incoming[take_index]
    extended = with_halo(ordered, ((("pts", "rep"), 0),), halo_rows)
    present = neighbours >= 0
    local_index = jnp.where(present, neighbours - (device * rows - halo_rows), rows + 2 * halo_rows)
    picked = pick_rows(extended, local_index)
    conv = jnp.einsum("otd,ode->te", picked, kernel, preferred_element_type=jnp.float32)
    conv_low = (conv + widen(full_conv_bias)).astype(jnp.bfloat16)
    linear = forward_product(conv_low, full_encode) + widen(full_encode_bias)
    first = widen(ordered) + norm_rows(linear, gain_zero, shift_zero)
    normed = norm_rows(first, gain_one, shift_one).astype(jnp.bfloat16)
    triple = forward_product(normed, full_triple)
    queries = (
        (triple[:, :width] + widen(full_query_bias))
        .astype(jnp.bfloat16)
        .reshape(rows, heads, HEAD_DIM)
    )
    keys_all = triple[:, width : 2 * width].astype(jnp.bfloat16).reshape(rows, heads, HEAD_DIM)
    values_all = (
        (triple[:, 2 * width :] + widen(full_value_bias))
        .astype(jnp.bfloat16)
        .reshape(rows, heads, HEAD_DIM)
    )
    visible = jnp.arange(rows) < lengths[0]

    def score_block():
        scores = (
            jnp.einsum("thd,shd->hts", queries, keys_all, preferred_element_type=jnp.float32)
            * scale
        )
        return jnp.where(visible[None, None, :], scores, -1e30)

    scores = score_block()
    peak = jnp.max(scores, axis=-1, keepdims=True)
    log_total = peak + jnp.log(jnp.sum(jnp.exp(scores - peak), axis=-1, keepdims=True))
    probs_low = jnp.exp(scores - log_total).astype(jnp.bfloat16)
    mixed = jnp.einsum("hts,shd->thd", probs_low, values_all, preferred_element_type=jnp.float32)
    mixed = mixed.reshape(rows, width).astype(jnp.bfloat16)
    second = first + forward_product(mixed, full_output) + widen(full_output_bias)
    normed_two = norm_rows(second, gain_two, shift_two).astype(jnp.bfloat16)
    hidden = forward_product(normed_two, full_expand) + widen(full_expand_bias)
    active = gelu_exact(hidden).astype(jnp.bfloat16)
    result = (second + forward_product(active, full_reduce) + widen(full_reduce_bias)).astype(
        jnp.bfloat16
    )
    grad_reduce = inner_grad(active, grad_out)
    grad_reduce_bias = column_sum(grad_out)
    grad_active = back_product(grad_out, full_reduce)
    grad_hidden = jax.vjp(gelu_exact, hidden)[1](grad_active)[0].astype(jnp.bfloat16)
    grad_expand = inner_grad(normed_two, grad_hidden)
    grad_expand_bias = column_sum(grad_hidden)
    grad_normed_two = back_product(grad_hidden, full_expand)
    two_back, grad_gain_two, grad_shift_two = norm_back(
        second, gain_two, shift_two, grad_normed_two
    )
    grad_second = widen(grad_out) + two_back
    grad_attended = grad_second.astype(jnp.bfloat16)
    grad_output = inner_grad(mixed, grad_attended)
    grad_output_bias = column_sum(grad_attended)
    grad_mixed = (
        back_product(grad_attended, full_output).astype(jnp.bfloat16).reshape(rows, heads, HEAD_DIM)
    )
    probs = jnp.exp(score_block() - log_total)
    probs_again = probs.astype(jnp.bfloat16)
    grad_values = jnp.einsum(
        "hts,thd->shd", probs_again, grad_mixed, preferred_element_type=jnp.float32
    ).astype(jnp.bfloat16)
    grad_probs = jnp.einsum(
        "thd,shd->hts", grad_mixed, values_all, preferred_element_type=jnp.float32
    )
    grad_scores = probs * (grad_probs - jnp.sum(probs * grad_probs, axis=-1, keepdims=True))
    grad_scores = grad_scores.astype(jnp.bfloat16)
    grad_queries = (
        jnp.einsum("hts,shd->thd", grad_scores, keys_all, preferred_element_type=jnp.float32)
        * scale
    ).astype(jnp.bfloat16)
    grad_keys = (
        jnp.einsum("hts,thd->shd", grad_scores, queries, preferred_element_type=jnp.float32) * scale
    ).astype(jnp.bfloat16)
    grad_triple_rows = jnp.concatenate(
        [
            grad_queries.reshape(rows, width),
            grad_keys.reshape(rows, width),
            grad_values.reshape(rows, width),
        ],
        axis=1,
    )
    grad_triple = inner_grad(normed, grad_triple_rows)
    grad_query_bias = column_sum(grad_queries.reshape(rows, width))
    grad_value_bias = column_sum(grad_values.reshape(rows, width))
    grad_normed = back_product(grad_triple_rows, full_triple)
    one_back, grad_gain_one, grad_shift_one = norm_back(first, gain_one, shift_one, grad_normed)
    grad_first = grad_second + one_back
    grad_linear, grad_gain_zero, grad_shift_zero = norm_back(
        linear, gain_zero, shift_zero, grad_first
    )
    grad_linear = grad_linear.astype(jnp.bfloat16)
    grad_encode = inner_grad(conv_low, grad_linear)
    grad_encode_bias = column_sum(grad_linear)
    grad_conv = back_product(grad_linear, full_encode).astype(jnp.bfloat16)
    grad_conv_bias = column_sum(grad_conv)
    grad_kernel = jnp.einsum(
        "otd,te->ode", picked, grad_conv, preferred_element_type=jnp.float32
    ).astype(BF)
    grad_picked = jnp.einsum("te,ode->otd", grad_conv, kernel, preferred_element_type=jnp.float32)
    grad_extended = jnp.zeros((extent, width), jnp.float32)
    grad_extended = grad_extended.at[local_index.reshape(-1)].add(grad_picked.reshape(-1, width))
    rim_terms = jnp.concatenate(
        [grad_extended[:halo_rows], grad_extended[rows + halo_rows : rows + 2 * halo_rows]], axis=0
    )
    rim_arrived = with_halo(rim_terms, ((("pts", "rep"), 0),), halo_rows)
    grad_ordered = grad_first + grad_extended[halo_rows : halo_rows + rows]
    grad_ordered = grad_ordered.at[:halo_rows].add(rim_arrived[:halo_rows])
    grad_ordered = grad_ordered.at[rows - halo_rows :].add(rim_arrived[3 * halo_rows :])
    returning = (
        jnp.zeros((devices * capacity, width), jnp.bfloat16)
        .at[take_index]
        .set(grad_ordered.astype(jnp.bfloat16))
    )
    arrived = lax.all_to_all(
        returning.reshape(devices, capacity, width),
        ("pts", "rep"),
        split_axis=0,
        concat_axis=0,
        tiled=True,
    )
    points_grad = arrived.reshape(devices * capacity, width)[send_index]
    vector_grads = jnp.concatenate(
        [
            jnp.stack(
                [
                    grad_conv_bias,
                    grad_encode_bias,
                    grad_gain_zero,
                    grad_shift_zero,
                    grad_gain_one,
                    grad_shift_one,
                    grad_query_bias,
                    grad_value_bias,
                    grad_output_bias,
                    grad_gain_two,
                    grad_shift_two,
                    grad_reduce_bias,
                ]
            ),
            grad_expand_bias.reshape(128, 4, 4).transpose(1, 0, 2).reshape(4, 512),
        ],
        axis=0,
    )
    grad_wide = jnp.concatenate([grad_encode, grad_triple, grad_output, grad_expand], axis=1)
    grad_wide = grad_wide.astype(BF).reshape(512, 36, 128).transpose(1, 0, 2)
    kernel_grad, wide_out, tall_out, vector_out = scatter_grads(
        grad_kernel.reshape(13824, 4, 128).transpose(1, 0, 2).reshape(4, 4, 4, 2, 432, 128),
        grad_wide.reshape(4, 9, 4, 4, 2, 16, 128),
        grad_reduce.astype(BF).reshape(4, 4, 2, 4, 16, 512),
        vector_grads.reshape(16, 4, 128).transpose(1, 0, 2),
    )
    wide_out = wide_out.reshape(36, 4, 128).transpose(1, 0, 2).reshape(4, 4608)
    vector_out = lax.dynamic_slice(vector_out, (0, lane), (16, 4))
    reduced = (
        vector_out[0],
        wide_out[:, :512],
        vector_out[1],
        vector_out[2],
        vector_out[3],
        vector_out[4],
        vector_out[5],
        wide_out[:, 512:2048],
        vector_out[6],
        vector_out[7],
        wide_out[:, 2048:2560],
        vector_out[8],
        vector_out[9],
        vector_out[10],
        wide_out[:, 2560:],
        vector_out[12:].reshape(16),
        tall_out,
        vector_out[11],
    )
    return (result, points_grad, kernel_grad) + tuple(reduced)


def solution(mesh):
    in_specs = (
        P(("pts", "rep"), None),
        P(("pts", "rep")),
        P(("pts", "rep")),
        P(("pts", "rep")),
        P(None, ("pts", "rep")),
        P("pts", "rep"),
        P(("pts", "rep")),
        P(("pts", "rep"), None),
        P(("pts", "rep")),
        P(("pts", "rep")),
        P(("pts", "rep")),
        P(("pts", "rep")),
        P(("pts", "rep")),
        P(("pts", "rep"), None),
        P(("pts", "rep")),
        P(("pts", "rep")),
        P(("pts", "rep"), None),
        P(("pts", "rep")),
        P(("pts", "rep")),
        P(("pts", "rep")),
        P(("pts", "rep"), None),
        P(("pts", "rep")),
        P(("pts", "rep"), None),
        P(("pts", "rep")),
        P(("pts", "rep"), None),
    )
    out_specs = (
        P(("pts", "rep"), None),
        P(("pts", "rep"), None),
        P("pts", "rep"),
        P(("pts", "rep")),
        P(("pts", "rep"), None),
        P(("pts", "rep")),
        P(("pts", "rep")),
        P(("pts", "rep")),
        P(("pts", "rep")),
        P(("pts", "rep")),
        P(("pts", "rep"), None),
        P(("pts", "rep")),
        P(("pts", "rep")),
        P(("pts", "rep"), None),
        P(("pts", "rep")),
        P(("pts", "rep")),
        P(("pts", "rep")),
        P(("pts", "rep"), None),
        P(("pts", "rep")),
        P(("pts", "rep"), None),
        P(("pts", "rep")),
    )
    return jax.shard_map(
        per_device, mesh=mesh, in_specs=in_specs, out_specs=out_specs, check_vma=False
    )
```

```python
import jax
import jax.numpy as jnp
from jax import lax
from jax.experimental import pallas as pl
from jax.experimental.pallas import tpu as pltpu
from jax.sharding import PartitionSpec as P

MESH = pl.DeviceIdType.MESH
BF = jnp.bfloat16
F32 = jnp.float32


def place():
    p = lax.axis_index("pts")
    return {
        "x": lax.div(p, 8),
        "y": lax.rem(lax.div(p, 2), 4),
        "c": lax.rem(p, 2),
        "z": lax.axis_index("rep"),
    }


def device_at(at):
    return ((at["x"] * 4 + at["y"]) * 2 + at["c"], at["z"])


def moved(at, axis, step):
    size = 2 if axis == "c" else 4
    return {**at, axis: lax.rem(at[axis] + step, size)}


def greet(at):
    barrier = pltpu.get_barrier_semaphore()
    friends = [("x", 1), ("x", 3), ("y", 1), ("y", 3), ("z", 1), ("z", 2), ("z", 3), ("c", 1)]
    for axis, step in friends:
        pl.semaphore_signal(
            barrier, inc=1, device_id=device_at(moved(at, axis, step)), device_id_type=MESH
        )
    pl.semaphore_wait(barrier, len(friends))


def whole(value):
    return slice(None) if value is None else value


def conv_view(ref, sel, h):
    r0, r1 = h
    return ref.at[
        whole(sel.get("z")), whole(sel.get("x")), whole(sel.get("y")), sel["c"], pl.ds(r0, r1 - r0), :
    ]


def wide_view(ref, sel, h):
    k0, k1 = h
    return ref.at[
        whole(sel.get("z")), pl.ds(k0, k1 - k0), whole(sel.get("x")), whole(sel.get("y")), sel["c"]
    ]


def tall_view(ref, sel, h):
    l0, l1 = h
    return ref.at[
        whole(sel.get("x")), whole(sel.get("y")), sel["c"], whole(sel.get("z")), :, pl.ds(l0, l1 - l0)
    ]


def flat_view(ref, sel, h):
    return ref.at[whole(sel.get("x")), whole(sel.get("y")), sel["c"]]


STREAMS = (
    ("cz", 0, conv_view, "xyz", ((0, 64), (64, 112))),
    ("cx", 0, conv_view, "yzx", ((112, 192), (192, 272))),
    ("cy", 0, conv_view, "zxy", ((272, 352), (352, 432))),
    ("m2", 2, tall_view, "zyx", ((0, 256), (256, 512))),
    ("m1", 1, wide_view, "xyz", ((0, 5), (5, 9))),
    ("vt", 3, flat_view, "xy", ((0, 16),)),
)
SLOTS = 40


def gather_kernel(conv, m1p, m2, vt, gc, g1, g2, gv, pre, m1b, prev, vb, sends, recvs, locs, presend, prerecv):
    at = place()
    greet(at)
    outs = (gc, g1, g2, gv)
    pending = []
    crossing = []

    def push(src, dst, k, to, keep=True):
        copy = pltpu.make_async_remote_copy(
            src_ref=src,
            dst_ref=dst,
            send_sem=sends.at[k[0], k[1]],
            recv_sem=recvs.at[k[0], k[1]],
            device_id=device_at(to),
            device_id_type=MESH,
        )
        copy.start()
        pending.append(copy)
        return copy

    def own_view(s, h):
        name, op, view, order, halves = s
        if op == 0:
            return conv.at[pl.ds(h[0], h[1] - h[0]), :]
        if op == 1:
            return m1b.at[pl.ds(h[0], h[1] - h[0])]
        if op == 2:
            return m2.at[:, pl.ds(h[0], h[1] - h[0])]
        return vb

    pre_copies = []
    for step in (1, 2, 3):
        to = moved(at, "z", step)
        for j, (src, dst) in enumerate(((m1p.at[to["z"]], pre.at[step]), (vt, prev.at[step]))):
            copy = pltpu.make_async_remote_copy(
                src_ref=src,
                dst_ref=dst,
                send_sem=presend.at[j, step],
                recv_sem=prerecv.at[j, step],
                device_id=device_at(to),
                device_id_type=MESH,
            )
            copy.start()
            pre_copies.append(copy)

    local_copies = {}

    def keep_own(i):
        name, op, view, order, halves = STREAMS[i]
        for j, h in enumerate(halves):
            copy = pltpu.make_async_copy(
                own_view(STREAMS[i], h), view(outs[op], at, h), locs.at[i, j]
            )
            copy.start()
            local_copies[(i, j)] = copy

    state = {}

    def block_sel(order, phase, index=None, axis=None):
        sel = {"c": at["c"]}
        for a in "xyz":
            if a in order and order.index(a) < phase:
                continue
            sel[a] = at[a]
        if axis is not None:
            sel[axis] = index
        return sel

    def begin(i, phase):
        name, op, view, order, halves = STREAMS[i]
        axis = order[phase]
        n = len(halves)
        sel = block_sel(order, phase)
        copies = {}
        for d, hs in ((1, range(n)), (3, reversed(range(n)))):
            for h in hs:
                dst = view(outs[op], sel, halves[h])
                src = own_view(STREAMS[i], halves[h]) if phase == 0 else dst
                k = (i, phase * 6 + (0 if d == 1 else 2) + h)
                copies[(d, h)] = push(src, dst, k, moved(at, axis, d))
        state[(i, phase)] = copies
        if phase == len(order) - 1:
            for h in range(n):
                dst = view(outs[op], sel, halves[h])
                crossing.append(push(dst, dst, (i, 20 + h), moved(at, "c", 1)))

    def relay(i, phase):
        name, op, view, order, halves = STREAMS[i]
        axis = order[phase]
        last = phase == len(order) - 1
        n = len(halves)
        copies = state[(i, phase)]
        base = phase * 6
        other = moved(at, "c", 1)
        for d in (1, 3):
            h = 0 if d == 1 else n - 1
            if n == 1 and d == 3:
                continue
            copies[(d, h)].wait_recv()
            sel = block_sel(order, phase, lax.rem(at[axis] + 4 - d, 4), axis)
            ref = view(outs[op], sel, halves[h])
            copies[(d, "f")] = push(ref, ref, (i, base + (4 if d == 1 else 5)), moved(at, axis, d))
            if last:
                crossing.append(push(ref, ref, (i, 22 + d), other))
        for d in (1, 3):
            for h in range(n):
                if h == (0 if d == 1 else n - 1) and not (n == 1 and d == 3):
                    continue
                copies[(d, h)].wait_recv()
                if last:
                    sel = block_sel(order, phase, lax.rem(at[axis] + 4 - d, 4), axis)
                    ref = view(outs[op], sel, halves[h])
                    crossing.append(push(ref, ref, (i, 26 + d), other))

    def finish(i, phase):
        name, op, view, order, halves = STREAMS[i]
        axis = order[phase]
        last = phase == len(order) - 1
        n = len(halves)
        copies = state[(i, phase)]
        other = moved(at, "c", 1)
        for d in (1, 3):
            if (d, "f") not in copies:
                continue
            copies[(d, "f")].wait_recv()
            if last:
                h = 0 if d == 1 else n - 1
                sel = block_sel(order, phase, lax.rem(at[axis] + 2, 4), axis)
                ref = view(outs[op], sel, halves[h])
                crossing.append(push(ref, ref, (i, 30 + d), other))

    early = (0, 1, 2, 3)
    for i in early:
        begin(i, 0)
        keep_own(i)
    for copy in pre_copies:
        copy.wait()
    mine = m1p.at[at["z"]]
    pre[0] = mine[...]

    def tile(k, _):
        pieces = [
            pre[lax.rem(at["z"] - s + 4, 4), k].astype(F32) for s in range(4)
        ]
        m1b[k] = jnp.concatenate(pieces, axis=0).astype(BF)
        return 0

    lax.fori_loop(0, 9, tile, 0)
    vb[...] = (
        vt[...].astype(F32) + prev[1].astype(F32) + prev[2].astype(F32) + prev[3].astype(F32)
    ).astype(BF)
    for i in (4, 5):
        begin(i, 0)
        keep_own(i)
    for phase in (0, 1, 2):
        live = [i for i in range(len(STREAMS)) if phase < len(STREAMS[i][3])]
        for i in live:
            relay(i, phase)
        for i in live:
            finish(i, phase)
            if phase == 0:
                for h in range(len(STREAMS[i][4])):
                    local_copies[(i, h)].wait()
            if phase + 1 < len(STREAMS[i][3]):
                begin(i, phase + 1)
    for copy in crossing:
        copy.wait_recv()
    for copy in pending:
        copy.wait_send()


ANY = pl.BlockSpec(memory_space=pl.ANY)
VM = pl.BlockSpec(memory_space=pltpu.VMEM)


def gather_weights(conv, m1p, m2, vt):
    shape = jax.ShapeDtypeStruct
    n = len(STREAMS)
    return pl.pallas_call(
        gather_kernel,
        out_shape=(
            shape((4, 4, 4, 2, 432, 128), BF),
            shape((4, 9, 4, 4, 2, 16, 128), BF),
            shape((4, 4, 2, 4, 16, 512), BF),
            shape((4, 4, 2, 16, 128), BF),
        ),
        in_specs=[ANY, VM, ANY, VM],
        out_specs=[ANY] * 4,
        scratch_shapes=[
            pltpu.VMEM((4, 9, 4, 128), BF),
            pltpu.VMEM((9, 16, 128), BF),
            pltpu.VMEM((4, 16, 128), BF),
            pltpu.VMEM((16, 128), BF),
            pltpu.SemaphoreType.DMA((n, SLOTS)),
            pltpu.SemaphoreType.DMA((n, SLOTS)),
            pltpu.SemaphoreType.DMA((n, 2)),
            pltpu.SemaphoreType.DMA((2, 4)),
            pltpu.SemaphoreType.DMA((2, 4)),
        ],
        compiler_params=pltpu.CompilerParams(collective_id=0, has_side_effects=True),
        name="gather_weights",
    )(conv, m1p, m2, vt)


RS_FRIENDS = [("x", 1), ("x", 2), ("x", 3), ("y", 1), ("y", 2), ("y", 3), ("z", 1), ("z", 2), ("z", 3), ("c", 1)]


def greet_all(at):
    barrier = pltpu.get_barrier_semaphore()
    for axis, step in RS_FRIENDS:
        pl.semaphore_signal(
            barrier, inc=1, device_id=device_at(moved(at, axis, step)), device_id_type=MESH
        )
    pl.semaphore_wait(barrier, len(RS_FRIENDS))


RS_STREAMS = (
    ("cz", 0, "zxycRL", {"R": 112, "L": 128}, "R", 0, "zyx", ((0, 64), (64, 112))),
    ("cx", 0, "zxycRL", {"R": 160, "L": 128}, "R", 112, "xzy", ((0, 80), (80, 160))),
    ("cy", 0, "zxycRL", {"R": 160, "L": 128}, "R", 272, "yxz", ((0, 80), (80, 160))),
    ("m2", 2, "xyczSL", {"S": 16, "L": 512}, "L", 0, "xyz", ((0, 256), (256, 512))),
    ("m1", 1, "zKxycSL", {"K": 9, "S": 16, "L": 128}, "K", 0, "zyx", ((0, 5), (5, 9))),
)
RS_ORDER = (4, 3, 0, 1, 2)


def cut_view(ref, layout, sel, cut=None, span=None, base=0):
    index = []
    for dim in layout:
        if dim in sel:
            index.append(sel[dim])
        elif dim == cut and span is not None:
            index.append(pl.ds(base + span[0], span[1] - span[0]))
        else:
            index.append(slice(None))
    return ref.at[tuple(index)]


def sizes_of(layout, plain):
    return tuple(plain[d] if d in plain else 4 for d in layout)


def rs_buffers():
    shapes = []
    for name, op, layout, plain, cut, base, order, halves in RS_STREAMS:
        inner = layout.replace("c", "")
        shapes += [sizes_of(inner, plain)] * 2
        left = inner
        for axis in order:
            left = left.replace(axis, "")
            for span in (halves[0], halves[1]):
                shapes.append(sizes_of(left, {**plain, cut: span[1] - span[0]}))
            shapes += [sizes_of(left, plain)] * 2
    return [pltpu.VMEM(s, BF) for s in shapes]


PER_STREAM = 14


def scatter_kernel(gc, g1, g2, gv, oc, o1, o2, ov, *scratch):
    bufs = scratch[: PER_STREAM * len(RS_STREAMS)]
    post, postr, vx, vr, sends, recvs, locs, vsend, vrecv, psend, precv = scratch[PER_STREAM * len(RS_STREAMS) :]
    at = place()
    greet_all(at)
    ops = (gc, g1, g2)
    pending = []
    other = moved(at, "c", 1)

    def push(src, dst, send, recv, to):
        copy = pltpu.make_async_remote_copy(
            src_ref=src, dst_ref=dst, send_sem=send, recv_sem=recv,
            device_id=device_at(to), device_id_type=MESH,
        )
        copy.start()
        pending.append(copy)
        return copy

    def stream(i):
        name, op, layout, plain, cut, base, order, halves = RS_STREAMS[i]
        mine = bufs[i * PER_STREAM : (i + 1) * PER_STREAM]
        return layout, layout.replace("c", ""), cut, base, order, halves, mine, ops[op], plain

    def add(dst, dst_layout, dst_sel, srcs, cut, span, plain):
        free = [d for d in dst_layout if d in "xyz" and d not in dst_sel]
        count = 4 ** len(free)

        def one(n, _):
            sel = dict(dst_sel)
            for k, d in enumerate(reversed(free)):
                sel[d] = lax.rem(lax.div(n, 4**k), 4)
            where = cut_view(dst, dst_layout, sel, cut, span)
            total = where[...].astype(F32)
            for src, src_layout, src_sel, src_span in srcs:
                full = {**{d: sel[d] for d in free}, **src_sel}
                total = total + cut_view(src, src_layout, full, cut, src_span)[...].astype(F32)
            where[...] = total.astype(BF)
            return 0

        if count == 1:
            one(0, 0)
        else:
            lax.fori_loop(0, count, one, 0)

    STEPS = (2, 1, 3, 0)

    def load(i):
        layout, inner, cut, base, order, halves, mine, src, plain = stream(i)
        axis = order[0]
        span = (0, plain[cut])
        copies = []
        for k, step in enumerate(STEPS):
            a = lax.rem(at[axis] + step, 4)
            theirs = cut_view(src, layout, {"c": other["c"], axis: a}, cut, span, base)
            here = cut_view(src, layout, {"c": at["c"], axis: a}, cut, span, base)
            sib = push(theirs, cut_view(mine[1], inner, {axis: a}), sends.at[i, k], recvs.at[i, k], other)
            loc = pltpu.make_async_copy(here, cut_view(mine[0], inner, {axis: a}), locs.at[i, k])
            loc.start()
            copies.append((sib, loc))
        return copies

    def start_phase(i, phase, loaded):
        layout, inner, cut, base, order, halves, mine, src, plain = stream(i)
        axis = order[phase]
        done = {a: at[a] for a in order[:phase]}
        left = "".join(d for d in inner if d not in order[: phase + 1])
        r0, r1, rp, rm = mine[2 + 4 * phase : 6 + 4 * phase]
        A = mine[0]
        slot = lambda k: (sends.at[i, 4 + phase * 6 + k], recvs.at[i, 4 + phase * 6 + k])
        span = (0, plain[cut])
        n = at[axis]
        up, down = moved(at, axis, 1), moved(at, axis, 3)
        view = lambda a, h: cut_view(A, inner, {**done, axis: a}, cut, h)
        got = {}
        for k, step in enumerate(STEPS):
            a = lax.rem(n + step, 4)
            if loaded is not None:
                sib, loc = loaded[k]
                sib.wait_recv()
                loc.wait()
                add(A, inner, {axis: a}, [(mine[1], inner, {axis: a}, span)], cut, span, plain)
            if step == 2:
                got["r0"] = push(view(a, halves[0]), r0, *slot(0), up)
                got["r1"] = push(view(a, halves[1]), r1, *slot(1), down)
            elif step == 1:
                got["p1"] = push(view(a, halves[1]), cut_view(rp, left, {}, cut, halves[1]), *slot(2), up)
            elif step == 3:
                got["m0"] = push(view(a, halves[0]), cut_view(rm, left, {}, cut, halves[0]), *slot(3), down)
        return got

    def middle(i, phase, got):
        layout, inner, cut, base, order, halves, mine, src, plain = stream(i)
        axis = order[phase]
        done = {a: at[a] for a in order[:phase]}
        left = "".join(d for d in inner if d not in order[: phase + 1])
        r0, r1, rp, rm = mine[2 + 4 * phase : 6 + 4 * phase]
        A = mine[0]
        slot = lambda k: (sends.at[i, 4 + phase * 6 + k], recvs.at[i, 4 + phase * 6 + k])
        up, down = moved(at, axis, 1), moved(at, axis, 3)
        view = lambda a, h: cut_view(A, inner, {**done, axis: a}, cut, h)
        local = lambda h: (0, h[1] - h[0])
        got["r0"].wait_recv()
        add(A, inner, {**done, axis: up[axis]}, [(r0, left, {}, local(halves[0]))], cut, halves[0], plain)
        got["p0"] = push(view(up[axis], halves[0]), cut_view(rp, left, {}, cut, halves[0]), *slot(4), up)
        got["r1"].wait_recv()
        add(A, inner, {**done, axis: down[axis]}, [(r1, left, {}, local(halves[1]))], cut, halves[1], plain)
        got["m1"] = push(view(down[axis], halves[1]), cut_view(rm, left, {}, cut, halves[1]), *slot(5), down)

    def close(i, phase, got):
        layout, inner, cut, base, order, halves, mine, src, plain = stream(i)
        axis = order[phase]
        done = {a: at[a] for a in order[: phase + 1]}
        left = "".join(d for d in inner if d not in order[: phase + 1])
        r0, r1, rp, rm = mine[2 + 4 * phase : 6 + 4 * phase]
        for k in ("p1", "m0", "p0", "m1"):
            got[k].wait_recv()
        span = (0, plain[cut])
        add(mine[0], inner, done, [(rp, left, {}, span), (rm, left, {}, span)], cut, span, plain)

    vstate = []

    def vector_step(k):
        axis, steps = (("c", (1,)), ("z", (1, 2, 3)), ("y", (1, 2, 3)), ("x", (1, 2, 3)))[k]
        copies = []
        for s in steps:
            to = moved(at, axis, s)
            if axis == "x":
                src, dst = vx.at[3, to["x"]], vr.at[3, s, 0]
            else:
                src, dst = (gv if k == 0 else vx.at[k]), vr.at[k, s]
            copies.append(push(src, dst, vsend.at[k, s], vrecv.at[k, s], to))
        return copies

    def vector_add(k, copies):
        for copy in copies:
            copy.wait_recv()
        if k == 3:
            total = vx[3, at["x"]]
            for s in (1, 2, 3):
                total = total + vr[3, s, 0]
            ov[...] = total
            return
        total = gv[...] if k == 0 else vx[k]
        for s in (1,) if k == 0 else (1, 2, 3):
            total = total + vr[k, s]
        vx[k + 1] = total

    vcopies = vector_step(0)
    loaded = {i: load(i) for i in RS_ORDER}
    state = {}
    for i in RS_ORDER:
        state[i] = start_phase(i, 0, loaded[i])
    for phase in range(3):
        vector_add(phase, vcopies)
        vcopies = vector_step(phase + 1)
        for i in RS_ORDER:
            middle(i, phase, state[i])
        for i in RS_ORDER:
            close(i, phase, state[i])
            if phase < 2:
                state[i] = start_phase(i, phase + 1, None)
    vector_add(3, vcopies)
    for i in (0, 1, 2):
        layout, inner, cut, base, order, halves, mine, src, plain = stream(i)
        oc[pl.ds(base, plain["R"]), :] = mine[0][at["z"], at["x"], at["y"]].astype(F32)
    o2[...] = bufs[3 * PER_STREAM][at["x"], at["y"], at["z"]].astype(F32)
    m1 = bufs[4 * PER_STREAM]
    wide = m1[at["z"], :, at["x"], at["y"]].astype(F32)
    for q in range(4):
        post[q] = wide[:, 4 * q : 4 * q + 4, :].astype(BF)
    copies = []
    for s in (1, 2, 3):
        to = moved(at, "z", s)
        copies.append(push(post.at[to["z"]], postr.at[s], psend.at[s], precv.at[s], to))
    o1[at["z"]] = post[at["z"]].astype(F32)
    for s in (1, 2, 3):
        copies[s - 1].wait_recv()
        o1[lax.rem(at["z"] + 4 - s, 4)] = postr[s].astype(F32)
    for copy in pending:
        copy.wait_send()


def scatter_grads(gc, g1, g2, gv):
    shape = jax.ShapeDtypeStruct
    n = len(RS_STREAMS)
    return pl.pallas_call(
        scatter_kernel,
        out_shape=(
            shape((432, 128), F32),
            shape((4, 9, 4, 128), F32),
            shape((16, 512), F32),
            shape((16, 128), F32),
        ),
        in_specs=[ANY, ANY, ANY, VM],
        out_specs=[VM] * 4,
        scratch_shapes=rs_buffers()
        + [
            pltpu.VMEM((4, 9, 4, 128), BF),
            pltpu.VMEM((4, 9, 4, 128), BF),
            pltpu.VMEM((4, 4, 16, 128), F32),
            pltpu.VMEM((4, 4, 4, 16, 128), F32),
            pltpu.SemaphoreType.DMA((n, 22)),
            pltpu.SemaphoreType.DMA((n, 22)),
            pltpu.SemaphoreType.DMA((n, 4)),
            pltpu.SemaphoreType.DMA((4, 4)),
            pltpu.SemaphoreType.DMA((4, 4)),
            pltpu.SemaphoreType.DMA((4,)),
            pltpu.SemaphoreType.DMA((4,)),
        ],
        compiler_params=pltpu.CompilerParams(
            collective_id=1, has_side_effects=True, vmem_limit_bytes=58 * 2**20
        ),
        name="scatter_grads",
    )(gc, g1, g2, gv)


SM = pl.BlockSpec(memory_space=pltpu.SMEM)
epsilon = 1e-05


def mm(a, b):
    return lax.dot_general(a, b, (((1,), (0,)), ((), ())), preferred_element_type=F32)


def mm_nt(a, b):
    return lax.dot_general(a, b, (((1,), (1,)), ((), ())), preferred_element_type=F32)


def mm_tn(a, b):
    return lax.dot_general(a, b, (((0,), (0,)), ((), ())), preferred_element_type=F32)


def wide_block(ref, first, count=4):
    return jnp.concatenate([ref[first + k] for k in range(count)], axis=1)


def put_wide(ref, first, value, count=4):
    for k in range(count):
        ref[first + k] = value[:, 128 * k : 128 * (k + 1)].astype(BF)


V_CONV, V_ENC, V_GAIN0, V_SHIFT0, V_GAIN1, V_SHIFT1, V_QUERY, V_VALUE, V_OUT, V_GAIN2, V_SHIFT2, V_RED = range(12)


def over_rows(body, step=64, rows=512):
    def one(n, _):
        body(pl.ds(pl.multiple_of(n * step, step), step))
        return 0

    lax.fori_loop(0, rows // step, one, 0)


def normalize(v):
    mean = jnp.mean(v, axis=-1, keepdims=True)
    centred = v - mean
    spread = jnp.mean(centred * centred, axis=-1, keepdims=True)
    rstd = lax.rsqrt(spread + epsilon)
    return centred * rstd, rstd


def norm_pull(hat, rstd, gain, grad):
    up = grad * gain
    a = jnp.mean(up, axis=-1, keepdims=True)
    b = jnp.mean(up * hat, axis=-1, keepdims=True)
    return rstd * (up - a - hat * b)


def total(v):
    return jnp.sum(v, axis=0, keepdims=True)


def gelu_both(u):
    cdf = 0.5 * (1.0 + lax.erf(u * 0.7071067811865476))
    pdf = 0.3989422804014327 * jnp.exp(-0.5 * u * u)
    return u * cdf, cdf + u * pdf


def three(v):
    hi = v.astype(BF).astype(F32)
    rest = v - hi
    mid = rest.astype(BF).astype(F32)
    return hi, mid, rest - mid


def block_kernel(
    length, conv, ordered, go, w1, w2, vec, xb,
    result, first_grad, conv_grad, g1, g2, gv,
    big, hat0, rstd0, first, hat1, rstd1, normed, normed_t, q, k, v, k_t, v_t,
    mixed_t, mixed, rows_a, rows_b, kx, xa, ya, hat2, rstd2, n2, n2_t,
    second, act, dh, da, acc, acc2, dn, d_mixed, dq_t, dk, dv,
):
    row = lambda n: vec[n : n + 1, :]
    gv[...] = jnp.zeros_like(gv)

    def gain(n, value):
        gv[n : n + 1, :] += total(value)

    big[...] = mm(conv[...], wide_block(w1, 0))

    def encode(r):
        hat, rstd = normalize(big[r, :] + row(V_ENC))
        hat0[r, :] = hat
        rstd0[r, :] = rstd
        here = ordered[r, :].astype(F32) + hat * row(V_GAIN0) + row(V_SHIFT0)
        first[r, :] = here
        hat, rstd = normalize(here)
        hat1[r, :] = hat
        rstd1[r, :] = rstd
        normed[r, :] = (hat * row(V_GAIN1) + row(V_SHIFT1)).astype(BF)

    over_rows(encode)
    normed_t[...] = normed[...].T
    q[...] = (0.25 * (mm(normed[...], wide_block(w1, 4)) + row(V_QUERY)).astype(BF).astype(F32)).astype(BF)
    k[...] = mm(normed[...], wide_block(w1, 8)).astype(BF)
    v[...] = (mm(normed[...], wide_block(w1, 12)) + row(V_VALUE)).astype(BF)
    k_t[...] = k[...].T
    v_t[...] = v[...].T

    lane = lax.broadcasted_iota(jnp.int32, (1, 128), 1)
    seat = lax.broadcasted_iota(jnp.int32, (512, 128), 0)
    spot = lax.broadcasted_iota(jnp.int32, (512, 128), 1)
    hidden_key = jnp.where((spot == 96) & (seat >= length[0]), -1e30, 0.0)
    kx[...] = jnp.where(spot < 96, 1.0, hidden_key).astype(BF)
    one_lane = jnp.where(spot == 96, 1.0, 0.0).astype(BF)
    rows_a[...] = jnp.zeros_like(rows_a)
    rows_b[...] = jnp.zeros_like(rows_b)

    def head_places(h):
        group = pl.ds(pl.multiple_of(lax.div(h, 8) * 128, 128), 128)
        mine = jnp.where(lax.div(lane, 16) == lax.rem(h, 8), 1.0, 0.0).astype(BF)
        extra = jnp.where((lax.rem(lane, 32) == h) & (lane < 96) | (lane == 96), 1.0, 0.0).astype(BF)
        return group, mine, extra, pl.ds(pl.multiple_of(h * 16, 16), 16)

    def forward_head(h):
        group, mine, extra, channels = head_places(h)
        keys = jnp.concatenate([k[:, group], kx[...]], axis=1)
        asks = jnp.concatenate([q[:, group] * mine, one_lane], axis=1)
        scores = mm_nt(keys, asks)
        peak = jnp.max(scores, axis=0, keepdims=True)
        e = jnp.exp(scores - peak)
        summed = total(e)
        mixed_t[channels, :] = mm(v_t[channels, :], e.astype(BF)) / summed
        lse = peak + jnp.log(summed)
        hi, mid, lo = three(-lse)
        rows_a[pl.ds(h, 1), :] = hi
        rows_a[pl.ds(h + 32, 1), :] = mid
        rows_a[pl.ds(h + 64, 1), :] = lo

    def forward_heads(n, _):
        for j in range(2):
            forward_head(n * 2 + j)
        return 0

    lax.fori_loop(0, 16, forward_heads, 0)
    rows_a[96:97, :] = jnp.ones((1, 512), F32)
    xa[...] = rows_a[...].T.astype(BF)
    mixed[...] = mixed_t[...].T.astype(BF)

    big[...] = mm(mixed[...], wide_block(w1, 16))

    def after(r):
        here = first[r, :] + big[r, :] + row(V_OUT)
        second[r, :] = here
        hat, rstd = normalize(here)
        hat2[r, :] = hat
        rstd2[r, :] = rstd
        n2[r, :] = (hat * row(V_GAIN2) + row(V_SHIFT2)).astype(BF)
        gain(V_RED, go[r, :].astype(F32))

    over_rows(after)
    n2_t[...] = n2[...].T
    acc[...] = jnp.zeros_like(acc)
    acc2[...] = jnp.zeros_like(acc2)

    def chunk(c, _):
        up = jnp.concatenate([w1[20 + 4 * c + j] for j in range(4)], axis=1)
        span = pl.ds(pl.multiple_of(c * 512, 512), 512)
        down = w2[span, :]
        big[...] = mm(n2[...], up)
        da[...] = mm_nt(go[...], down)

        def gelu_rows(r):
            value, slope = gelu_both(big[r, :] + xb[pl.ds(c, 1), :])
            act[r, :] = value.astype(BF)
            low = (da[r, :] * slope).astype(BF)
            dh[r, :] = low
            gv[pl.ds(12 + c, 1), :] += total(low.astype(F32))

        over_rows(gelu_rows, 32)
        acc[...] += mm(act[...], down)
        acc2[...] += mm_nt(dh[...], up)
        g2[span, :] = mm_tn(act[...], go[...]).astype(BF)
        grad_up = mm(n2_t[...], dh[...])
        for j in range(4):
            g1[20 + 4 * c + j] = grad_up[:, 128 * j : 128 * (j + 1)].astype(BF)
        return 0

    lax.fori_loop(0, 4, chunk, 0)

    def before_mlp(r):
        result[r, :] = (second[r, :] + acc[r, :] + row(V_RED)).astype(BF)
        grad = acc2[r, :]
        hat = hat2[r, :]
        gain(V_GAIN2, grad * hat)
        gain(V_SHIFT2, grad)
        here = go[r, :].astype(F32) + norm_pull(hat, rstd2[r, :], row(V_GAIN2), grad)
        second[r, :] = here
        low = here.astype(BF)
        dn[r, :] = low
        gain(V_OUT, low.astype(F32))

    over_rows(before_mlp)
    put_wide(g1, 16, mm_tn(mixed[...], dn[...]))
    d_mixed[...] = mm_nt(dn[...], wide_block(w1, 16)).astype(BF)
    big[...] = d_mixed[...].astype(F32).T

    def inner(h, _):
        channels = pl.ds(pl.multiple_of(h * 16, 16), 16)
        hi, mid, lo = three(-total(big[channels, :] * mixed_t[channels, :]))
        rows_b[pl.ds(h, 1), :] = hi
        rows_b[pl.ds(h + 32, 1), :] = mid
        rows_b[pl.ds(h + 64, 1), :] = lo
        return 0

    lax.fori_loop(0, 32, inner, 0)
    ya[...] = rows_b[...].T.astype(BF)
    dk[...] = jnp.zeros_like(dk)
    dv[...] = jnp.zeros_like(dv)
    ones = jnp.where(spot < 96, 1.0, 0.0).astype(BF)

    def backward_head(h):
        group, mine, extra, channels = head_places(h)
        q_h = q[:, group] * mine
        m_h = d_mixed[:, group] * mine
        keys = jnp.concatenate([k[:, group], kx[...]], axis=1)
        p = jnp.exp(mm_nt(keys, jnp.concatenate([q_h, xa[...] * extra], axis=1)))
        values = jnp.concatenate([v[:, group], ones], axis=1)
        slope = mm_nt(values, jnp.concatenate([m_h, ya[...] * extra], axis=1))
        ds = (p * slope).astype(BF)
        dv[:, group] += mm(p.astype(BF), m_h)
        dk[:, group] += mm(ds, q_h)
        dq_t[channels, :] = mm(k_t[channels, :], ds)

    def backward_heads(n, _):
        for j in range(2):
            backward_head(n * 2 + j)
        return 0

    lax.fori_loop(0, 16, backward_heads, 0)
    q[...] = (0.25 * dq_t[...].T).astype(BF)
    k[...] = dk[...].astype(BF)
    v[...] = dv[...].astype(BF)
    gain(V_QUERY, q[...].astype(F32))
    gain(V_VALUE, v[...].astype(F32))
    put_wide(g1, 4, mm(normed_t[...], q[...]))
    put_wide(g1, 8, mm(normed_t[...], k[...]))
    put_wide(g1, 12, mm(normed_t[...], v[...]))
    acc2[...] = (
        mm_nt(q[...], wide_block(w1, 4)) + mm_nt(k[...], wide_block(w1, 8)) + mm_nt(v[...], wide_block(w1, 12))
    )

    def before_attention(r):
        grad = acc2[r, :]
        hat = hat1[r, :]
        gain(V_GAIN1, grad * hat)
        gain(V_SHIFT1, grad)
        here = second[r, :] + norm_pull(hat, rstd1[r, :], row(V_GAIN1), grad)
        first_grad[r, :] = here
        hat = hat0[r, :]
        gain(V_GAIN0, here * hat)
        gain(V_SHIFT0, here)
        low = norm_pull(hat, rstd0[r, :], row(V_GAIN0), here).astype(BF)
        dn[r, :] = low
        gain(V_ENC, low.astype(F32))

    over_rows(before_attention)
    put_wide(g1, 0, mm_tn(conv[...], dn[...]))
    conv_grad[...] = mm_nt(dn[...], wide_block(w1, 0)).astype(BF)
    gain(V_CONV, conv_grad[...].astype(F32))


def block(length, conv, ordered, go, w1, w2, vec, xb):
    shape = jax.ShapeDtypeStruct
    full = (512, 512)
    f, b, col = pltpu.VMEM(full, F32), pltpu.VMEM(full, BF), pltpu.VMEM((512, 1), F32)
    rows, lanes = pltpu.VMEM((128, 512), F32), pltpu.VMEM((512, 128), BF)
    return pl.pallas_call(
        block_kernel,
        out_shape=(
            shape(full, BF),
            shape(full, F32),
            shape(full, BF),
            shape((36, 512, 128), BF),
            shape((2048, 512), BF),
            shape((16, 512), F32),
        ),
        in_specs=[SM] + [VM] * 7,
        out_specs=[VM] * 6,
        scratch_shapes=[
            f, f, col, f, f, col, b, b, b, b, b, b, b,
            f, b, rows, rows, lanes, lanes, lanes, f, col, b, b,
            f, b, b, f, f, f, b, b, f, f, f,
        ],
        compiler_params=pltpu.CompilerParams(vmem_limit_bytes=60 * 2**20),
        name="block",
    )(length, conv, ordered, go, w1, w2, vec, xb)


def spread_columns(columns, j, b):
    seat = lax.broadcasted_iota(jnp.int32, (256, 512), 1)
    return jnp.where(seat == columns[256 * b : 256 * (b + 1), j : j + 1], 1.0, 0.0).astype(BF)


def spread_rows(picks, j, b):
    seat = lax.broadcasted_iota(jnp.int32, (512, 256), 0)
    return jnp.where(seat == picks[j : j + 1, 256 * b : 256 * (b + 1)], 1.0, 0.0).astype(BF)


def conv_kernel(columns, extended, w, bias, conv, picked, acc):
    step = pl.program_id(0)

    @pl.when(step == 0)
    def _():
        acc[...] = jnp.zeros_like(acc)

    for j in range(3):
        for b in range(2):
            window = extended[256 * b : 256 * b + 512, :]
            picked[j, 256 * b : 256 * (b + 1), :] = mm(spread_columns(columns.at[0], j, b), window).astype(BF)
    parts = [mm(picked[j], jnp.concatenate([w[n, j] for n in range(4)], axis=1)) for j in range(3)]
    acc[...] += parts[0] + parts[1] + parts[2]

    @pl.when(step == 8)
    def _():
        conv[...] = (acc[...] + bias[...]).astype(BF)


def conv_forward(columns, extended, w, bias):
    shape = jax.ShapeDtypeStruct
    return pl.pallas_call(
        conv_kernel,
        grid=(9,),
        out_shape=(shape((512, 512), BF), shape((27, 512, 512), BF)),
        in_specs=[
            pl.BlockSpec((1, 512, 3), lambda i: (i, 0, 0)),
            pl.BlockSpec((768, 512), lambda i: (0, 0)),
            pl.BlockSpec((4, 3, 512, 128), lambda i: (0, i, 0, 0)),
            pl.BlockSpec((1, 512), lambda i: (0, 0)),
        ],
        out_specs=[
            pl.BlockSpec((512, 512), lambda i: (0, 0)),
            pl.BlockSpec((3, 512, 512), lambda i: (i, 0, 0)),
        ],
        scratch_shapes=[pltpu.VMEM((512, 512), F32)],
        compiler_params=pltpu.CompilerParams(vmem_limit_bytes=56 * 2**20),
        name="conv_forward",
    )(columns, extended, w, bias)


def conv_back_kernel(picks, grad, w, picked, spread, kernel_grad):
    step = pl.program_id(0)

    @pl.when(step == 0)
    def _():
        spread[...] = jnp.zeros_like(spread)

    g = grad[...]
    back = [mm_nt(g, jnp.concatenate([w[n, j] for n in range(4)], axis=1)).astype(BF) for j in range(3)]
    for b in range(2):
        hot = jnp.concatenate([spread_rows(picks.at[0], j, b) for j in range(3)], axis=1)
        terms = jnp.concatenate([back[j][256 * b : 256 * (b + 1), :] for j in range(3)], axis=0)
        spread[256 * b : 256 * b + 512, :] += mm(hot, terms)
    for j in range(3):
        product = mm_tn(picked[j], g)
        for n in range(4):
            kernel_grad[n, j] = product[:, 128 * n : 128 * (n + 1)].astype(BF)


def conv_back(picks, grad, w, picked):
    shape = jax.ShapeDtypeStruct
    return pl.pallas_call(
        conv_back_kernel,
        grid=(9,),
        out_shape=(shape((768, 512), F32), shape((4, 27, 512, 128), BF)),
        in_specs=[
            pl.BlockSpec((1, 3, 512), lambda i: (i, 0, 0)),
            pl.BlockSpec((512, 512), lambda i: (0, 0)),
            pl.BlockSpec((4, 3, 512, 128), lambda i: (0, i, 0, 0)),
            pl.BlockSpec((3, 512, 512), lambda i: (i, 0, 0)),
        ],
        out_specs=[
            pl.BlockSpec((768, 512), lambda i: (0, 0)),
            pl.BlockSpec((4, 3, 512, 128), lambda i: (0, i, 0, 0)),
        ],
        compiler_params=pltpu.CompilerParams(vmem_limit_bytes=56 * 2**20),
        name="conv_back",
    )(picks, grad, w, picked)


def with_halo(cells, width):
    count = lax.axis_size(("pts", "rep"))
    head, tail = cells[:width], cells[cells.shape[0] - width :]
    return (
        lax.ppermute(tail, ("pts", "rep"), [(i, i + 1) for i in range(count - 1)]),
        lax.ppermute(head, ("pts", "rep"), [(i + 1, i) for i in range(count - 1)]),
    )


def rank_within(labels, count):
    onehot = (labels[:, None] == jnp.arange(count, dtype=jnp.int32)[None, :]).astype(jnp.int32)
    before = jnp.cumsum(onehot, axis=0) - onehot
    return jnp.sum(before * onehot, axis=1)


def per_device(
    points,
    perm,
    inverse,
    lengths,
    neighbours,
    conv_weight,
    conv_bias,
    encode_weight,
    encode_bias,
    encode_gain,
    encode_shift,
    before_gain,
    before_shift,
    triple_weight,
    query_bias,
    value_bias,
    output_weight,
    output_bias,
    second_gain,
    second_shift,
    expand_weight,
    expand_bias,
    reduce_weight,
    reduce_bias,
    grad_out,
):
    rows, width = points.shape
    devices = lax.axis_size(("pts", "rep"))
    capacity = 2 * rows // devices
    halo_rows = rows // 4
    device = lax.axis_index(("pts", "rep"))
    pts, rep = lax.axis_index("pts"), lax.axis_index("rep")
    lane = lax.rem(pts, 8) * 16 + rep * 4
    wide_piece = jnp.concatenate([encode_weight, triple_weight, output_weight, expand_weight], axis=1)
    wide_piece = wide_piece.reshape(4, 36, 128).transpose(1, 0, 2).reshape(4, 9, 4, 128)
    vector_piece = jnp.concatenate(
        [
            jnp.stack(
                [
                    conv_bias,
                    encode_bias,
                    encode_gain,
                    encode_shift,
                    before_gain,
                    before_shift,
                    query_bias,
                    value_bias,
                    output_bias,
                    second_gain,
                    second_shift,
                    reduce_bias,
                ]
            ),
            expand_bias.reshape(4, 4),
        ],
        axis=0,
    )
    vector_tile = lax.dynamic_update_slice(jnp.zeros((16, 128), BF), vector_piece, (0, lane))
    got_conv, got_wide, got_tall, got_vectors = gather_weights(
        conv_weight, wide_piece, reduce_weight, vector_tile
    )
    kernel = got_conv.reshape(4, 27, 512, 128)
    wide = got_wide.reshape(36, 512, 128)
    tall = got_tall.reshape(2048, 512)
    vectors = got_vectors.reshape(4, 8, 16, 128).astype(F32).sum(axis=1)
    vectors = vectors.transpose(1, 0, 2).reshape(16, 512)
    full_expand_bias = vectors[12:].reshape(4, 128, 4).transpose(1, 0, 2).reshape(4, 512)

    destination = inverse // rows
    send_index = destination * capacity + rank_within(destination, devices)
    outgoing = jnp.zeros((devices * capacity, width), jnp.bfloat16).at[send_index].set(points)
    incoming = lax.all_to_all(
        outgoing.reshape(devices, capacity, width),
        ("pts", "rep"),
        split_axis=0,
        concat_axis=0,
        tiled=True,
    )
    incoming = incoming.reshape(devices * capacity, width)
    source = perm // rows
    same_source = source[:, None] == source[None, :]
    earlier = perm[None, :] < perm[:, None]
    take_index = source * capacity + jnp.sum(same_source & earlier, axis=1)
    ordered = incoming[take_index]
    before, after = with_halo(ordered, halo_rows)
    extended = jnp.concatenate([before, ordered, after], axis=0)
    token = jnp.arange(rows, dtype=jnp.int32)[None, :]
    local = jnp.where(
        neighbours >= 0, neighbours - (device * rows - halo_rows) - token // 256 * 256, -1
    )
    picks = local.reshape(9, 3, rows)

    conv, picked = conv_forward(picks.transpose(0, 2, 1), extended, kernel, vectors[:1])
    result, grad_first, grad_conv, grad_wide, grad_tall, vector_grads = block(
        lengths, conv, ordered, grad_out, wide, tall, vectors, full_expand_bias
    )
    grad_extended, grad_kernel = conv_back(picks, grad_conv, kernel, picked)

    rim_terms = jnp.concatenate(
        [grad_extended[:halo_rows], grad_extended[rows + halo_rows :]], axis=0
    )
    from_before, from_after = with_halo(rim_terms, halo_rows)
    grad_ordered = grad_first + grad_extended[halo_rows : halo_rows + rows]
    grad_ordered = grad_ordered.at[:halo_rows].add(from_before)
    grad_ordered = grad_ordered.at[rows - halo_rows :].add(from_after)
    returning = (
        jnp.zeros((devices * capacity, width), jnp.bfloat16)
        .at[take_index]
        .set(grad_ordered.astype(jnp.bfloat16))
    )
    arrived = lax.all_to_all(
        returning.reshape(devices, capacity, width),
        ("pts", "rep"),
        split_axis=0,
        concat_axis=0,
        tiled=True,
    )
    points_grad = arrived.reshape(devices * capacity, width)[send_index]

    natural = vector_grads[12:].reshape(128, 4, 4).transpose(1, 0, 2).reshape(4, 512)
    vector_grads = jnp.concatenate([vector_grads[:12], natural], axis=0)
    kernel_out, wide_out, tall_out, vector_out = scatter_grads(
        grad_kernel.reshape(4, 4, 4, 2, 432, 128),
        grad_wide.reshape(4, 9, 4, 4, 2, 16, 128),
        grad_tall.reshape(4, 4, 2, 4, 16, 512),
        vector_grads.reshape(16, 4, 128).transpose(1, 0, 2),
    )
    wide_out = wide_out.reshape(36, 4, 128).transpose(1, 0, 2).reshape(4, 4608)
    vector_out = lax.dynamic_slice(vector_out, (0, lane), (16, 4))
    reduced = (
        vector_out[V_CONV],
        wide_out[:, :512],
        vector_out[V_ENC],
        vector_out[V_GAIN0],
        vector_out[V_SHIFT0],
        vector_out[V_GAIN1],
        vector_out[V_SHIFT1],
        wide_out[:, 512:2048],
        vector_out[V_QUERY],
        vector_out[V_VALUE],
        wide_out[:, 2048:2560],
        vector_out[V_OUT],
        vector_out[V_GAIN2],
        vector_out[V_SHIFT2],
        wide_out[:, 2560:],
        vector_out[12:].reshape(16),
        tall_out,
        vector_out[V_RED],
    )
    return (result, points_grad, kernel_out) + reduced


def solution(mesh):
    in_specs = (
        P(("pts", "rep"), None),
        P(("pts", "rep")),
        P(("pts", "rep")),
        P(("pts", "rep")),
        P(None, ("pts", "rep")),
        P("pts", "rep"),
        P(("pts", "rep")),
        P(("pts", "rep"), None),
        P(("pts", "rep")),
        P(("pts", "rep")),
        P(("pts", "rep")),
        P(("pts", "rep")),
        P(("pts", "rep")),
        P(("pts", "rep"), None),
        P(("pts", "rep")),
        P(("pts", "rep")),
        P(("pts", "rep"), None),
        P(("pts", "rep")),
        P(("pts", "rep")),
        P(("pts", "rep")),
        P(("pts", "rep"), None),
        P(("pts", "rep")),
        P(("pts", "rep"), None),
        P(("pts", "rep")),
        P(("pts", "rep"), None),
    )
    out_specs = (
        P(("pts", "rep"), None),
        P(("pts", "rep"), None),
        P("pts", "rep"),
        P(("pts", "rep")),
        P(("pts", "rep"), None),
        P(("pts", "rep")),
        P(("pts", "rep")),
        P(("pts", "rep")),
        P(("pts", "rep")),
        P(("pts", "rep")),
        P(("pts", "rep"), None),
        P(("pts", "rep")),
        P(("pts", "rep")),
        P(("pts", "rep"), None),
        P(("pts", "rep")),
        P(("pts", "rep")),
        P(("pts", "rep")),
        P(("pts", "rep"), None),
        P(("pts", "rep")),
        P(("pts", "rep"), None),
        P(("pts", "rep")),
    )
    return jax.shard_map(
        per_device, mesh=mesh, in_specs=in_specs, out_specs=out_specs, check_vma=False
    )
```

```python
import jax
import jax.numpy as jnp
from jax import lax
from jax.experimental import pallas as pl
from jax.experimental.pallas import tpu as pltpu
from jax.sharding import PartitionSpec as P

MESH = pl.DeviceIdType.MESH
BF = jnp.bfloat16
F32 = jnp.float32


def place():
    p = lax.axis_index("pts")
    return {
        "x": lax.div(p, 8),
        "y": lax.rem(lax.div(p, 2), 4),
        "c": lax.rem(p, 2),
        "z": lax.axis_index("rep"),
    }


def device_at(at):
    return ((at["x"] * 4 + at["y"]) * 2 + at["c"], at["z"])


def moved(at, axis, step):
    size = 2 if axis == "c" else 4
    return {**at, axis: lax.rem(at[axis] + step, size)}


def greet(at):
    barrier = pltpu.get_barrier_semaphore()
    friends = [("x", 1), ("x", 3), ("y", 1), ("y", 3), ("z", 1), ("z", 2), ("z", 3), ("c", 1)]
    for axis, step in friends:
        pl.semaphore_signal(
            barrier, inc=1, device_id=device_at(moved(at, axis, step)), device_id_type=MESH
        )
    pl.semaphore_wait(barrier, len(friends))


def whole(value):
    return slice(None) if value is None else value


def conv_view(ref, sel, h):
    r0, r1 = h
    return ref.at[
        whole(sel.get("z")), whole(sel.get("x")), whole(sel.get("y")), sel["c"], pl.ds(r0, r1 - r0), :
    ]


def wide_view(ref, sel, h):
    k0, k1 = h
    return ref.at[
        whole(sel.get("z")), pl.ds(k0, k1 - k0), whole(sel.get("x")), whole(sel.get("y")), sel["c"]
    ]


def tall_view(ref, sel, h):
    l0, l1 = h
    return ref.at[
        whole(sel.get("x")), whole(sel.get("y")), sel["c"], whole(sel.get("z")), :, pl.ds(l0, l1 - l0)
    ]


def flat_view(ref, sel, h):
    return ref.at[whole(sel.get("x")), whole(sel.get("y")), sel["c"]]


STREAMS = (
    ("cz", 0, conv_view, "xyz", ((0, 64), (64, 112))),
    ("cx", 0, conv_view, "yzx", ((112, 192), (192, 272))),
    ("cy", 0, conv_view, "zxy", ((272, 352), (352, 432))),
    ("m2", 2, tall_view, "zyx", ((0, 256), (256, 512))),
    ("m1", 1, wide_view, "xyz", ((0, 5), (5, 9))),
    ("vt", 3, flat_view, "xy", ((0, 16),)),
)
SLOTS = 40


def gather_kernel(conv, m1p, m2, vt, gc, g1, g2, gv, pre, m1b, prev, vb, sends, recvs, locs, presend, prerecv):
    at = place()
    greet(at)
    outs = (gc, g1, g2, gv)
    pending = []
    crossing = []

    def push(src, dst, k, to, keep=True):
        copy = pltpu.make_async_remote_copy(
            src_ref=src,
            dst_ref=dst,
            send_sem=sends.at[k[0], k[1]],
            recv_sem=recvs.at[k[0], k[1]],
            device_id=device_at(to),
            device_id_type=MESH,
        )
        copy.start()
        pending.append(copy)
        return copy

    def own_view(s, h):
        name, op, view, order, halves = s
        if op == 0:
            return conv.at[pl.ds(h[0], h[1] - h[0]), :]
        if op == 1:
            return m1b.at[pl.ds(h[0], h[1] - h[0])]
        if op == 2:
            return m2.at[:, pl.ds(h[0], h[1] - h[0])]
        return vb

    pre_copies = []
    for step in (1, 2, 3):
        to = moved(at, "z", step)
        for j, (src, dst) in enumerate(((m1p.at[to["z"]], pre.at[step]), (vt, prev.at[step]))):
            copy = pltpu.make_async_remote_copy(
                src_ref=src,
                dst_ref=dst,
                send_sem=presend.at[j, step],
                recv_sem=prerecv.at[j, step],
                device_id=device_at(to),
                device_id_type=MESH,
            )
            copy.start()
            pre_copies.append(copy)

    local_copies = {}

    def keep_own(i):
        name, op, view, order, halves = STREAMS[i]
        for j, h in enumerate(halves):
            copy = pltpu.make_async_copy(
                own_view(STREAMS[i], h), view(outs[op], at, h), locs.at[i, j]
            )
            copy.start()
            local_copies[(i, j)] = copy

    state = {}

    def block_sel(order, phase, index=None, axis=None):
        sel = {"c": at["c"]}
        for a in "xyz":
            if a in order and order.index(a) < phase:
                continue
            sel[a] = at[a]
        if axis is not None:
            sel[axis] = index
        return sel

    def begin(i, phase):
        name, op, view, order, halves = STREAMS[i]
        axis = order[phase]
        n = len(halves)
        sel = block_sel(order, phase)
        copies = {}
        for d, hs in ((1, range(n)), (3, reversed(range(n)))):
            for h in hs:
                dst = view(outs[op], sel, halves[h])
                src = own_view(STREAMS[i], halves[h]) if phase == 0 else dst
                k = (i, phase * 6 + (0 if d == 1 else 2) + h)
                copies[(d, h)] = push(src, dst, k, moved(at, axis, d))
        state[(i, phase)] = copies
        if phase == len(order) - 1:
            for h in range(n):
                dst = view(outs[op], sel, halves[h])
                crossing.append(push(dst, dst, (i, 20 + h), moved(at, "c", 1)))

    def relay(i, phase):
        name, op, view, order, halves = STREAMS[i]
        axis = order[phase]
        last = phase == len(order) - 1
        n = len(halves)
        copies = state[(i, phase)]
        base = phase * 6
        other = moved(at, "c", 1)
        for d in (1, 3):
            h = 0 if d == 1 else n - 1
            if n == 1 and d == 3:
                continue
            copies[(d, h)].wait_recv()
            sel = block_sel(order, phase, lax.rem(at[axis] + 4 - d, 4), axis)
            ref = view(outs[op], sel, halves[h])
            copies[(d, "f")] = push(ref, ref, (i, base + (4 if d == 1 else 5)), moved(at, axis, d))
            if last:
                crossing.append(push(ref, ref, (i, 22 + d), other))
        for d in (1, 3):
            for h in range(n):
                if h == (0 if d == 1 else n - 1) and not (n == 1 and d == 3):
                    continue
                copies[(d, h)].wait_recv()
                if last:
                    sel = block_sel(order, phase, lax.rem(at[axis] + 4 - d, 4), axis)
                    ref = view(outs[op], sel, halves[h])
                    crossing.append(push(ref, ref, (i, 26 + d), other))

    def finish(i, phase):
        name, op, view, order, halves = STREAMS[i]
        axis = order[phase]
        last = phase == len(order) - 1
        n = len(halves)
        copies = state[(i, phase)]
        other = moved(at, "c", 1)
        for d in (1, 3):
            if (d, "f") not in copies:
                continue
            copies[(d, "f")].wait_recv()
            if last:
                h = 0 if d == 1 else n - 1
                sel = block_sel(order, phase, lax.rem(at[axis] + 2, 4), axis)
                ref = view(outs[op], sel, halves[h])
                crossing.append(push(ref, ref, (i, 30 + d), other))

    early = (0, 1, 2, 3)
    for i in early:
        begin(i, 0)
        keep_own(i)
    for copy in pre_copies:
        copy.wait()
    mine = m1p.at[at["z"]]
    pre[0] = mine[...]

    def tile(k, _):
        pieces = [
            pre[lax.rem(at["z"] - s + 4, 4), k].astype(F32) for s in range(4)
        ]
        m1b[k] = jnp.concatenate(pieces, axis=0).astype(BF)
        return 0

    lax.fori_loop(0, 9, tile, 0)
    vb[...] = (
        vt[...].astype(F32) + prev[1].astype(F32) + prev[2].astype(F32) + prev[3].astype(F32)
    ).astype(BF)
    for i in (4, 5):
        begin(i, 0)
        keep_own(i)
    for phase in (0, 1, 2):
        live = [i for i in range(len(STREAMS)) if phase < len(STREAMS[i][3])]
        for i in live:
            relay(i, phase)
        for i in live:
            finish(i, phase)
            if phase == 0:
                for h in range(len(STREAMS[i][4])):
                    local_copies[(i, h)].wait()
            if phase + 1 < len(STREAMS[i][3]):
                begin(i, phase + 1)
    for copy in crossing:
        copy.wait_recv()
    for copy in pending:
        copy.wait_send()


ANY = pl.BlockSpec(memory_space=pl.ANY)
VM = pl.BlockSpec(memory_space=pltpu.VMEM)


def gather_weights(conv, m1p, m2, vt):
    shape = jax.ShapeDtypeStruct
    n = len(STREAMS)
    return pl.pallas_call(
        gather_kernel,
        out_shape=(
            shape((4, 4, 4, 2, 432, 128), BF),
            shape((4, 9, 4, 4, 2, 16, 128), BF),
            shape((4, 4, 2, 4, 16, 512), BF),
            shape((4, 4, 2, 16, 128), BF),
        ),
        in_specs=[ANY, VM, ANY, VM],
        out_specs=[ANY] * 4,
        scratch_shapes=[
            pltpu.VMEM((4, 9, 4, 128), BF),
            pltpu.VMEM((9, 16, 128), BF),
            pltpu.VMEM((4, 16, 128), BF),
            pltpu.VMEM((16, 128), BF),
            pltpu.SemaphoreType.DMA((n, SLOTS)),
            pltpu.SemaphoreType.DMA((n, SLOTS)),
            pltpu.SemaphoreType.DMA((n, 2)),
            pltpu.SemaphoreType.DMA((2, 4)),
            pltpu.SemaphoreType.DMA((2, 4)),
        ],
        compiler_params=pltpu.CompilerParams(collective_id=0, has_side_effects=True),
        name="gather_weights",
    )(conv, m1p, m2, vt)


SM = pl.BlockSpec(memory_space=pltpu.SMEM)
epsilon = 1e-05


def mm(a, b):
    return lax.dot_general(a, b, (((1,), (0,)), ((), ())), preferred_element_type=F32)


def mm_nt(a, b):
    return lax.dot_general(a, b, (((1,), (1,)), ((), ())), preferred_element_type=F32)


def mm_tn(a, b):
    return lax.dot_general(a, b, (((0,), (0,)), ((), ())), preferred_element_type=F32)


def wide_block(ref, first, count=4):
    return jnp.concatenate([ref[first + k] for k in range(count)], axis=1)


def put_wide(ref, first, value, count=4):
    for k in range(count):
        ref[first + k] = value[:, 128 * k : 128 * (k + 1)].astype(BF)


V_CONV, V_ENC, V_GAIN0, V_SHIFT0, V_GAIN1, V_SHIFT1, V_QUERY, V_VALUE, V_OUT, V_GAIN2, V_SHIFT2, V_RED = range(12)


def over_rows(body, step=64, rows=512):
    def one(n, _):
        body(pl.ds(pl.multiple_of(n * step, step), step))
        return 0

    lax.fori_loop(0, rows // step, one, 0)


def normalize(v):
    mean = jnp.mean(v, axis=-1, keepdims=True)
    centred = v - mean
    spread = jnp.mean(centred * centred, axis=-1, keepdims=True)
    rstd = lax.rsqrt(spread + epsilon)
    return centred * rstd, rstd


def norm_pull(hat, rstd, gain, grad):
    up = grad * gain
    a = jnp.mean(up, axis=-1, keepdims=True)
    b = jnp.mean(up * hat, axis=-1, keepdims=True)
    return rstd * (up - a - hat * b)


def total(v):
    return jnp.sum(v, axis=0, keepdims=True)


def gelu_both(u):
    cdf = 0.5 * (1.0 + lax.erf(u * 0.7071067811865476))
    pdf = 0.3989422804014327 * jnp.exp(-0.5 * u * u)
    return u * cdf, cdf + u * pdf


def three(v):
    hi = v.astype(BF).astype(F32)
    rest = v - hi
    mid = rest.astype(BF).astype(F32)
    return hi, mid, rest - mid


def block_kernel(
    length, conv, ordered, go, w1, w2, vec, xb,
    result, first_grad, conv_grad, g1, g2, gv,
    big, hat0, rstd0, first, hat1, rstd1, normed, normed_t, q, k, v, k_t, v_t,
    mixed_t, mixed, rows_a, rows_b, kx, xa, ya, hat2, rstd2, n2, n2_t,
    second, act, dh, da, acc, acc2, dn, d_mixed, dq_t, dk, dv,
):
    row = lambda n: vec[n : n + 1, :]
    gv[...] = jnp.zeros_like(gv)

    def gain(n, value):
        gv[n : n + 1, :] += total(value)

    big[...] = mm(conv[...], wide_block(w1, 0))

    def encode(r):
        hat, rstd = normalize(big[r, :] + row(V_ENC))
        hat0[r, :] = hat
        rstd0[r, :] = rstd
        here = ordered[r, :].astype(F32) + hat * row(V_GAIN0) + row(V_SHIFT0)
        first[r, :] = here
        hat, rstd = normalize(here)
        hat1[r, :] = hat
        rstd1[r, :] = rstd
        normed[r, :] = (hat * row(V_GAIN1) + row(V_SHIFT1)).astype(BF)

    over_rows(encode)
    normed_t[...] = normed[...].T
    q[...] = (0.25 * (mm(normed[...], wide_block(w1, 4)) + row(V_QUERY)).astype(BF).astype(F32)).astype(BF)
    k[...] = mm(normed[...], wide_block(w1, 8)).astype(BF)
    v[...] = (mm(normed[...], wide_block(w1, 12)) + row(V_VALUE)).astype(BF)
    k_t[...] = k[...].T
    v_t[...] = v[...].T

    lane = lax.broadcasted_iota(jnp.int32, (1, 128), 1)
    seat = lax.broadcasted_iota(jnp.int32, (512, 128), 0)
    spot = lax.broadcasted_iota(jnp.int32, (512, 128), 1)
    hidden_key = jnp.where((spot == 96) & (seat >= length[0]), -1e30, 0.0)
    kx[...] = jnp.where(spot < 96, 1.0, hidden_key).astype(BF)
    one_lane = jnp.where(spot == 96, 1.0, 0.0).astype(BF)
    rows_a[...] = jnp.zeros_like(rows_a)
    rows_b[...] = jnp.zeros_like(rows_b)

    def head_places(h):
        group = pl.ds(pl.multiple_of(lax.div(h, 8) * 128, 128), 128)
        mine = jnp.where(lax.div(lane, 16) == lax.rem(h, 8), 1.0, 0.0).astype(BF)
        extra = jnp.where((lax.rem(lane, 32) == h) & (lane < 96) | (lane == 96), 1.0, 0.0).astype(BF)
        return group, mine, extra, pl.ds(pl.multiple_of(h * 16, 16), 16)

    def forward_head(h):
        group, mine, extra, channels = head_places(h)
        keys = jnp.concatenate([k[:, group], kx[...]], axis=1)
        asks = jnp.concatenate([q[:, group] * mine, one_lane], axis=1)
        scores = mm_nt(keys, asks)
        peak = jnp.max(scores, axis=0, keepdims=True)
        e = jnp.exp(scores - peak)
        summed = total(e)
        mixed_t[channels, :] = mm(v_t[channels, :], e.astype(BF)) / summed
        lse = peak + jnp.log(summed)
        hi, mid, lo = three(-lse)
        rows_a[pl.ds(h, 1), :] = hi
        rows_a[pl.ds(h + 32, 1), :] = mid
        rows_a[pl.ds(h + 64, 1), :] = lo

    def forward_heads(n, _):
        for j in range(2):
            forward_head(n * 2 + j)
        return 0

    lax.fori_loop(0, 16, forward_heads, 0)
    rows_a[96:97, :] = jnp.ones((1, 512), F32)
    xa[...] = rows_a[...].T.astype(BF)
    mixed[...] = mixed_t[...].T.astype(BF)

    big[...] = mm(mixed[...], wide_block(w1, 16))

    def after(r):
        here = first[r, :] + big[r, :] + row(V_OUT)
        second[r, :] = here
        hat, rstd = normalize(here)
        hat2[r, :] = hat
        rstd2[r, :] = rstd
        n2[r, :] = (hat * row(V_GAIN2) + row(V_SHIFT2)).astype(BF)
        gain(V_RED, go[r, :].astype(F32))

    over_rows(after)
    n2_t[...] = n2[...].T
    acc[...] = jnp.zeros_like(acc)
    acc2[...] = jnp.zeros_like(acc2)

    def chunk(c, _):
        up = jnp.concatenate([w1[20 + 4 * c + j] for j in range(4)], axis=1)
        span = pl.ds(pl.multiple_of(c * 512, 512), 512)
        down = w2[span, :]
        big[...] = mm(n2[...], up)
        da[...] = mm_nt(go[...], down)

        def gelu_rows(r):
            value, slope = gelu_both(big[r, :] + xb[pl.ds(c, 1), :])
            act[r, :] = value.astype(BF)
            low = (da[r, :] * slope).astype(BF)
            dh[r, :] = low
            gv[pl.ds(12 + c, 1), :] += total(low.astype(F32))

        over_rows(gelu_rows, 32)
        acc[...] += mm(act[...], down)
        acc2[...] += mm_nt(dh[...], up)
        g2[span, :] = mm_tn(act[...], go[...]).astype(BF)
        grad_up = mm(n2_t[...], dh[...])
        for j in range(4):
            g1[20 + 4 * c + j] = grad_up[:, 128 * j : 128 * (j + 1)].astype(BF)
        return 0

    lax.fori_loop(0, 4, chunk, 0)

    def before_mlp(r):
        result[r, :] = (second[r, :] + acc[r, :] + row(V_RED)).astype(BF)
        grad = acc2[r, :]
        hat = hat2[r, :]
        gain(V_GAIN2, grad * hat)
        gain(V_SHIFT2, grad)
        here = go[r, :].astype(F32) + norm_pull(hat, rstd2[r, :], row(V_GAIN2), grad)
        second[r, :] = here
        low = here.astype(BF)
        dn[r, :] = low
        gain(V_OUT, low.astype(F32))

    over_rows(before_mlp)
    put_wide(g1, 16, mm_tn(mixed[...], dn[...]))
    d_mixed[...] = mm_nt(dn[...], wide_block(w1, 16)).astype(BF)
    big[...] = d_mixed[...].astype(F32).T

    def inner(h, _):
        channels = pl.ds(pl.multiple_of(h * 16, 16), 16)
        hi, mid, lo = three(-total(big[channels, :] * mixed_t[channels, :]))
        rows_b[pl.ds(h, 1), :] = hi
        rows_b[pl.ds(h + 32, 1), :] = mid
        rows_b[pl.ds(h + 64, 1), :] = lo
        return 0

    lax.fori_loop(0, 32, inner, 0)
    ya[...] = rows_b[...].T.astype(BF)
    dk[...] = jnp.zeros_like(dk)
    dv[...] = jnp.zeros_like(dv)
    ones = jnp.where(spot < 96, 1.0, 0.0).astype(BF)

    def backward_head(h):
        group, mine, extra, channels = head_places(h)
        q_h = q[:, group] * mine
        m_h = d_mixed[:, group] * mine
        keys = jnp.concatenate([k[:, group], kx[...]], axis=1)
        p = jnp.exp(mm_nt(keys, jnp.concatenate([q_h, xa[...] * extra], axis=1)))
        values = jnp.concatenate([v[:, group], ones], axis=1)
        slope = mm_nt(values, jnp.concatenate([m_h, ya[...] * extra], axis=1))
        ds = (p * slope).astype(BF)
        dv[:, group] += mm(p.astype(BF), m_h)
        dk[:, group] += mm(ds, q_h)
        dq_t[channels, :] = mm(k_t[channels, :], ds)

    def backward_heads(n, _):
        for j in range(2):
            backward_head(n * 2 + j)
        return 0

    lax.fori_loop(0, 16, backward_heads, 0)
    q[...] = (0.25 * dq_t[...].T).astype(BF)
    k[...] = dk[...].astype(BF)
    v[...] = dv[...].astype(BF)
    gain(V_QUERY, q[...].astype(F32))
    gain(V_VALUE, v[...].astype(F32))
    put_wide(g1, 4, mm(normed_t[...], q[...]))
    put_wide(g1, 8, mm(normed_t[...], k[...]))
    put_wide(g1, 12, mm(normed_t[...], v[...]))
    acc2[...] = (
        mm_nt(q[...], wide_block(w1, 4)) + mm_nt(k[...], wide_block(w1, 8)) + mm_nt(v[...], wide_block(w1, 12))
    )

    def before_attention(r):
        grad = acc2[r, :]
        hat = hat1[r, :]
        gain(V_GAIN1, grad * hat)
        gain(V_SHIFT1, grad)
        here = second[r, :] + norm_pull(hat, rstd1[r, :], row(V_GAIN1), grad)
        first_grad[r, :] = here
        hat = hat0[r, :]
        gain(V_GAIN0, here * hat)
        gain(V_SHIFT0, here)
        low = norm_pull(hat, rstd0[r, :], row(V_GAIN0), here).astype(BF)
        dn[r, :] = low
        gain(V_ENC, low.astype(F32))

    over_rows(before_attention)
    put_wide(g1, 0, mm_tn(conv[...], dn[...]))
    conv_grad[...] = mm_nt(dn[...], wide_block(w1, 0)).astype(BF)
    gain(V_CONV, conv_grad[...].astype(F32))


def block(length, conv, ordered, go, w1, w2, vec, xb):
    shape = jax.ShapeDtypeStruct
    full = (512, 512)
    f, b, col = pltpu.VMEM(full, F32), pltpu.VMEM(full, BF), pltpu.VMEM((512, 1), F32)
    rows, lanes = pltpu.VMEM((128, 512), F32), pltpu.VMEM((512, 128), BF)
    return pl.pallas_call(
        block_kernel,
        out_shape=(
            shape(full, BF),
            shape(full, F32),
            shape(full, BF),
            shape((36, 512, 128), BF),
            shape((2048, 512), BF),
            shape((16, 512), F32),
        ),
        in_specs=[SM] + [VM] * 7,
        out_specs=[VM] * 6,
        scratch_shapes=[
            f, f, col, f, f, col, b, b, b, b, b, b, b,
            f, b, rows, rows, lanes, lanes, lanes, f, col, b, b,
            f, b, b, f, f, f, b, b, f, f, f,
        ],
        compiler_params=pltpu.CompilerParams(vmem_limit_bytes=60 * 2**20),
        name="block",
    )(length, conv, ordered, go, w1, w2, vec, xb)


def spread_columns(columns, j, b):
    seat = lax.broadcasted_iota(jnp.int32, (256, 512), 1)
    return jnp.where(seat == columns[256 * b : 256 * (b + 1), j : j + 1], 1.0, 0.0).astype(BF)


def spread_rows(picks, j, b):
    seat = lax.broadcasted_iota(jnp.int32, (512, 256), 0)
    return jnp.where(seat == picks[j : j + 1, 256 * b : 256 * (b + 1)], 1.0, 0.0).astype(BF)


def conv_kernel(columns, extended, w, bias, conv, picked, acc):
    step = pl.program_id(0)

    @pl.when(step == 0)
    def _():
        acc[...] = jnp.zeros_like(acc)

    for j in range(3):
        for b in range(2):
            window = extended[256 * b : 256 * b + 512, :]
            picked[j, 256 * b : 256 * (b + 1), :] = mm(spread_columns(columns.at[0], j, b), window).astype(BF)
    parts = [mm(picked[j], jnp.concatenate([w[n, j] for n in range(4)], axis=1)) for j in range(3)]
    acc[...] += parts[0] + parts[1] + parts[2]

    @pl.when(step == 8)
    def _():
        conv[...] = (acc[...] + bias[...]).astype(BF)


def conv_forward(columns, extended, w, bias):
    shape = jax.ShapeDtypeStruct
    return pl.pallas_call(
        conv_kernel,
        grid=(9,),
        out_shape=(shape((512, 512), BF), shape((27, 512, 512), BF)),
        in_specs=[
            pl.BlockSpec((1, 512, 3), lambda i: (i, 0, 0)),
            pl.BlockSpec((768, 512), lambda i: (0, 0)),
            pl.BlockSpec((4, 3, 512, 128), lambda i: (0, i, 0, 0)),
            pl.BlockSpec((1, 512), lambda i: (0, 0)),
        ],
        out_specs=[
            pl.BlockSpec((512, 512), lambda i: (0, 0)),
            pl.BlockSpec((3, 512, 512), lambda i: (i, 0, 0)),
        ],
        scratch_shapes=[pltpu.VMEM((512, 512), F32)],
        compiler_params=pltpu.CompilerParams(vmem_limit_bytes=56 * 2**20),
        name="conv_forward",
    )(columns, extended, w, bias)


BACK_FRIENDS = [("x", 1), ("x", 2), ("x", 3), ("y", 1), ("y", 2), ("y", 3), ("z", 1), ("z", 2), ("z", 3), ("c", 1)]


def line_neighbour(at, step):
    linear = lax.rem(((at["x"] * 4 + at["y"]) * 2 + at["c"]) * 4 + at["z"] + step, 128)
    return (lax.div(linear, 4), lax.rem(linear, 4))


def greet_for_back(at):
    barrier = pltpu.get_barrier_semaphore()
    ids = [device_at(moved(at, axis, step)) for axis, step in BACK_FRIENDS]
    ids += [line_neighbour(at, 1), line_neighbour(at, 127)]
    for device in ids:
        pl.semaphore_signal(barrier, inc=1, device_id=device, device_id_type=MESH)
    pl.semaphore_wait(barrier, len(ids))


CHAINS = (
    ("cz", "zxycRL", {"R": 112, "L": 128}, "R", 0, "zyx", ((0, 64), (64, 112))),
    ("cx", "zxycRL", {"R": 160, "L": 128}, "R", 112, "xzy", ((0, 80), (80, 160))),
    ("cy", "zxycRL", {"R": 160, "L": 128}, "R", 272, "yxz", ((0, 80), (80, 160))),
    ("m2", "xyczSL", {"S": 16, "L": 512}, "L", 0, "xyz", ((0, 256), (256, 512))),
    ("m1", "zKxycSL", {"K": 9, "S": 16, "L": 128}, "K", 0, "zyx", ((0, 5), (5, 9))),
)
CONV_CHAINS, MORE_CHAINS = (0, 1, 2), (4, 3)


def cut_view(ref, layout, sel, cut=None, span=None, base=0):
    index = []
    for dim in layout:
        if dim in sel:
            index.append(sel[dim])
        elif dim == cut and span is not None:
            index.append(pl.ds(base + span[0], span[1] - span[0]))
        else:
            index.append(slice(None))
    return ref.at[tuple(index)]


def sizes_of(layout, plain):
    return tuple(plain[d] if d in plain else 4 for d in layout)


def landing_shapes(i):
    name, layout, plain, cut, base, order, halves = CHAINS[i]
    left = layout.replace("c", "")
    shapes = []
    for axis in order:
        left = left.replace(axis, "")
        for span in halves:
            shapes.append(sizes_of(left, {**plain, cut: span[1] - span[0]}))
        shapes += [sizes_of(left, plain)] * 2
    return shapes


STEPS = (2, 1, 3, 0)


def back_kernel(
    grad, first_grad, take, picks, w, picked, g1, g2, gv,
    returning, oc, o1, o2, ov,
    kernel_grad, theirs, spread, p_buf, w_buf, rims, landed, own1, sib1, own2, sib2, *rest,
):
    count = 12 * len(CHAINS)
    landing, rest = rest[:count], rest[count:]
    post, postr, vx, vr, p_sem, w_sem, xy_send, xy_recv, sends, recvs, locs, vsend, vrecv, psend, precv, rim_s, rim_r = rest
    at = place()
    greet_for_back(at)
    other = moved(at, "c", 1)
    pending = []
    tiles = kernel_grad.reshape((4, 4, 4, 2, 432, 128))

    def remote(src, dst, send, recv, device):
        return pltpu.make_async_remote_copy(
            src_ref=src, dst_ref=dst, send_sem=send, recv_sem=recv,
            device_id=device, device_id_type=MESH,
        )

    def push(src, dst, send, recv, to):
        copy = remote(src, dst, send, recv, device_at(to))
        copy.start()
        pending.append(copy)
        return copy

    stores = {
        0: (tiles, "zxycRL", {"c": at["c"]}),
        1: (tiles, "zxycRL", {"c": at["c"]}),
        2: (tiles, "zxycRL", {"c": at["c"]}),
        3: (own2, "xyzSL", {}),
        4: (own1, "zKxySL", {}),
    }

    def view(i, sel, span):
        name, layout, plain, cut, base, order, halves = CHAINS[i]
        ref, inner, fixed = stores[i]
        return cut_view(ref, inner, {**fixed, **sel}, cut, span, base)

    def add(i, sel, srcs, span):
        name, layout, plain, cut, base, order, halves = CHAINS[i]
        ref, inner, fixed = stores[i]
        free = [d for d in inner if d in "xyz" and d not in sel]
        count = 4 ** len(free)

        def one(n, _):
            here = dict(sel)
            for k, d in enumerate(reversed(free)):
                here[d] = lax.rem(lax.div(n, 4**k), 4)
            where = view(i, here, span)
            total = where[...].astype(F32)
            for src, src_layout, src_sel, src_span in srcs:
                full = {**{d: here[d] for d in free}, **src_sel}
                total = total + cut_view(src, src_layout, full, cut, src_span)[...].astype(F32)
            where[...] = total.astype(BF)
            return 0

        if count == 1:
            one(0, 0)
        else:
            lax.fori_loop(0, count, one, 0)

    def load(i, src, own, sib):
        name, layout, plain, cut, base, order, halves = CHAINS[i]
        inner, axis, span = layout.replace("c", ""), order[0], (0, plain[cut])
        copies = []
        for k, step in enumerate(STEPS):
            a = lax.rem(at[axis] + step, 4)
            far = cut_view(src, layout, {"c": other["c"], axis: a}, cut, span)
            near = cut_view(src, layout, {"c": at["c"], axis: a}, cut, span)
            crossing = push(far, cut_view(sib, inner, {axis: a}), sends.at[i, k], recvs.at[i, k], other)
            local = pltpu.make_async_copy(near, cut_view(own, inner, {axis: a}), locs.at[i, k])
            local.start()
            copies.append((crossing, local))
        return copies

    def names(i, phase):
        name, layout, plain, cut, base, order, halves = CHAINS[i]
        inner = layout.replace("c", "")
        axis = order[phase]
        done = {a: at[a] for a in order[:phase]}
        left = "".join(d for d in inner if d not in order[: phase + 1])
        buffers = landing[i * 12 + 4 * phase : i * 12 + 4 * phase + 4]
        slot = lambda k: (sends.at[i, 4 + phase * 6 + k], recvs.at[i, 4 + phase * 6 + k])
        return inner, axis, done, left, buffers, slot, cut, halves, (0, plain[cut])

    def start(i, phase, loaded=None, sib=None):
        inner, axis, done, left, (r0, r1, rp, rm), slot, cut, halves, span = names(i, phase)
        up, down = moved(at, axis, 1), moved(at, axis, 3)
        got = {}
        for k, step in enumerate(STEPS):
            a = lax.rem(at[axis] + step, 4)
            if loaded is not None:
                crossing, local = loaded[k]
                crossing.wait_recv()
                local.wait()
                add(i, {axis: a}, [(sib, inner, {axis: a}, span)], span)
            part = lambda h: view(i, {**done, axis: a}, h)
            if step == 2:
                got["r0"] = push(part(halves[0]), r0, *slot(0), up)
                got["r1"] = push(part(halves[1]), r1, *slot(1), down)
            elif step == 1:
                got["p1"] = push(part(halves[1]), cut_view(rp, left, {}, cut, halves[1]), *slot(2), up)
            elif step == 3:
                got["m0"] = push(part(halves[0]), cut_view(rm, left, {}, cut, halves[0]), *slot(3), down)
        return got

    def middle(i, phase, got):
        inner, axis, done, left, (r0, r1, rp, rm), slot, cut, halves, span = names(i, phase)
        up, down = moved(at, axis, 1), moved(at, axis, 3)
        for key, h, buf, land, to, k in (("r0", 0, r0, rp, up, 4), ("r1", 1, r1, rm, down, 5)):
            half = halves[h]
            got[key].wait_recv()
            sel = {**done, axis: to[axis]}
            add(i, sel, [(buf, left, {}, (0, half[1] - half[0]))], half)
            got[k] = push(view(i, sel, half), cut_view(land, left, {}, cut, half), *slot(k), to)

    def close(i, phase, got):
        inner, axis, done, left, (r0, r1, rp, rm), slot, cut, halves, span = names(i, phase)
        for k in ("p1", "m0", 4, 5):
            got[k].wait_recv()
        add(i, {**done, axis: at[axis]}, [(rp, left, {}, span), (rm, left, {}, span)], span)

    def vector_step(k):
        axis, steps = (("c", (1,)), ("z", (1, 2, 3)), ("y", (1, 2, 3)), ("x", (1, 2, 3)))[k]
        copies = []
        for s in steps:
            to = moved(at, axis, s)
            if axis == "x":
                src, dst = vx.at[3, to["x"]], vr.at[3, s, 0]
            else:
                src, dst = (gv if k == 0 else vx.at[k]), vr.at[k, s]
            copies.append(push(src, dst, vsend.at[k, s], vrecv.at[k, s], to))
        return copies

    def vector_add(k, copies):
        for copy in copies:
            copy.wait_recv()
        if k == 3:
            ov[...] = vx[3, at["x"]] + vr[3, 1, 0] + vr[3, 2, 0] + vr[3, 3, 0]
            return
        sum_now = gv[...] if k == 0 else vx[k]
        for s in (1,) if k == 0 else (1, 2, 3):
            sum_now = sum_now + vr[k, s]
        vx[k + 1] = sum_now

    def p_copy(u):
        slot = lax.rem(u, 2)
        return pltpu.make_async_copy(picked.at[pl.ds(u * 3, 3)], p_buf.at[slot], p_sem.at[slot])

    def w_copy(u):
        slot = lax.rem(u, 2)
        return pltpu.make_async_copy(w.at[:, pl.ds(u * 3, 3)], w_buf.at[slot], w_sem.at[slot])

    def xy_copy(n):
        x, y = lax.div(n, 4), lax.rem(n, 4)
        return remote(
            tiles.at[:, x, y, other["c"]], theirs.at[:, x, y], xy_send.at[n], xy_recv.at[n], device_at(other)
        )

    def weight_unit(u, _):
        @pl.when(u < 8)
        def _():
            p_copy(u + 1).start()

        p_copy(u).wait()
        for j in range(3):
            product = mm_tn(p_buf[lax.rem(u, 2), j], grad[...])
            span = pl.ds(pl.multiple_of(u * 1536 + j * 512, 512), 512)
            for n in range(4):
                kernel_grad[n, span, :] = product[:, 128 * n : 128 * (n + 1)].astype(BF)
        ready, ready_next = lax.div(u * 16, 9), lax.div((u + 1) * 16, 9)
        for j in range(2):
            @pl.when(ready + j < ready_next)
            def _():
                xy_copy(ready + j).start()

        return 0

    def row_unit(u, _):
        @pl.when(u < 8)
        def _():
            w_copy(u + 1).start()

        w_copy(u).wait()
        slot = lax.rem(u, 2)
        g = grad[...]
        back = [
            mm_nt(g, jnp.concatenate([w_buf[slot, n, j] for n in range(4)], axis=1)).astype(BF)
            for j in range(3)
        ]
        for b in range(2):
            hot = jnp.concatenate([spread_rows(picks.at[u], j, b) for j in range(3)], axis=1)
            terms = jnp.concatenate([back[j][256 * b : 256 * (b + 1), :] for j in range(3)], axis=0)
            spread[256 * b : 256 * b + 512, :] += mm(hot, terms)
        return 0

    p_copy(0).start()
    vectors = vector_step(0)
    state = {}
    loaded = {4: load(4, g1, own1, sib1), 3: load(3, g2, own2, sib2)}
    w_copy(0).start()
    spread[...] = jnp.zeros_like(spread)
    lax.fori_loop(0, 3, weight_unit, 0)
    for i in MORE_CHAINS:
        state[i] = start(i, 0, loaded[i], {4: sib1, 3: sib2}[i])
    vector_add(0, vectors)
    vectors = vector_step(1)
    lax.fori_loop(3, 6, weight_unit, 0)
    for i in MORE_CHAINS:
        middle(i, 0, state[i])
    lax.fori_loop(6, 9, weight_unit, 0)
    vector_add(1, vectors)
    vectors = vector_step(2)
    for i in MORE_CHAINS:
        close(i, 0, state[i])
        state[i] = start(i, 1)
    for n in range(16):
        xy_copy(n).wait_recv()

    def join(n, _):
        z, x, y = lax.div(n, 16), lax.rem(lax.div(n, 4), 4), lax.rem(n, 4)
        where = tiles.at[z, x, y, at["c"]]
        where[...] = (where[...].astype(F32) + theirs[z, x, y].astype(F32)).astype(BF)
        return 0

    lax.fori_loop(0, 64, join, 0)
    for i in CONV_CHAINS:
        state[i] = start(i, 0)
    for i in MORE_CHAINS:
        middle(i, 1, state[i])
    lax.fori_loop(0, 3, row_unit, 0)
    vector_add(2, vectors)
    vectors = vector_step(3)
    for i in MORE_CHAINS:
        close(i, 1, state[i])
        state[i] = start(i, 2)
    lax.fori_loop(3, 5, row_unit, 0)
    for i in CONV_CHAINS:
        middle(i, 0, state[i])
    for i in MORE_CHAINS:
        middle(i, 2, state[i])
    lax.fori_loop(5, 9, row_unit, 0)
    rims[0] = spread[0:128, :].astype(BF)
    rims[1] = spread[640:768, :].astype(BF)
    rim_copies = []
    for j, step in ((0, 127), (1, 1)):
        copy = remote(rims.at[j], landed.at[j], rim_s.at[j], rim_r.at[j], line_neighbour(at, step))
        copy.start()
        pending.append(copy)
        rim_copies.append(copy)
    for i in CONV_CHAINS:
        close(i, 0, state[i])
        state[i] = start(i, 1)
    for i in MORE_CHAINS:
        close(i, 2, state[i])
    vector_add(3, vectors)
    o2[...] = own2[at["x"], at["y"], at["z"]].astype(F32)
    wide = own1[at["z"], :, at["x"], at["y"]].astype(F32)
    for n in range(4):
        post[n] = wide[:, 4 * n : 4 * n + 4, :].astype(BF)
    swaps = []
    for s in (1, 2, 3):
        to = moved(at, "z", s)
        swaps.append(push(post.at[to["z"]], postr.at[s], psend.at[s], precv.at[s], to))
    for copy in rim_copies:
        copy.wait_recv()
    spread[512:640, :] += landed[0].astype(F32)
    spread[128:256, :] += landed[1].astype(F32)
    ordered_grad = (first_grad[...] + spread[128:640, :]).astype(BF)
    for n in range(4):
        seat = lax.broadcasted_iota(jnp.int32, (256, 512), 0) + 256 * n
        hot = jnp.where(seat == take[...], 1.0, 0.0).astype(BF)
        returning[256 * n : 256 * (n + 1), :] = mm(hot, ordered_grad).astype(BF)
    for i in CONV_CHAINS:
        middle(i, 1, state[i])
    for i in CONV_CHAINS:
        close(i, 1, state[i])
        state[i] = start(i, 2)
    o1[at["z"]] = post[at["z"]].astype(F32)
    for s in (1, 2, 3):
        swaps[s - 1].wait_recv()
        o1[lax.rem(at["z"] + 4 - s, 4)] = postr[s].astype(F32)
    for i in CONV_CHAINS:
        middle(i, 2, state[i])
    for i in CONV_CHAINS:
        close(i, 2, state[i])
        name, layout, plain, cut, base, order, halves = CHAINS[i]
        oc[pl.ds(base, plain["R"]), :] = tiles[at["z"], at["x"], at["y"], at["c"], pl.ds(base, plain["R"]), :].astype(F32)
    for copy in pending:
        copy.wait_send()
    for n in range(16):
        xy_copy(n).wait_send()


def back_scatter(grad, first_grad, take, picks, w, picked, g1, g2, gv):
    shape = jax.ShapeDtypeStruct
    n = len(CHAINS)
    dma = pltpu.SemaphoreType.DMA
    own1, own2 = (4, 9, 4, 4, 16, 128), (4, 4, 4, 16, 512)
    landing = [s for i in range(n) for s in landing_shapes(i)]
    return pl.pallas_call(
        back_kernel,
        out_shape=(
            shape((1024, 512), BF),
            shape((432, 128), F32),
            shape((4, 9, 4, 128), F32),
            shape((16, 512), F32),
            shape((16, 128), F32),
        ),
        in_specs=[VM, VM, VM, VM, ANY, ANY, ANY, ANY, VM],
        out_specs=[VM] * 5,
        scratch_shapes=[
            pltpu.VMEM((4, 13824, 128), BF),
            pltpu.VMEM((4, 4, 4, 432, 128), BF),
            pltpu.VMEM((768, 512), F32),
            pltpu.VMEM((2, 3, 512, 512), BF),
            pltpu.VMEM((2, 4, 3, 512, 128), BF),
            pltpu.VMEM((2, 128, 512), BF),
            pltpu.VMEM((2, 128, 512), BF),
            pltpu.VMEM(own1, BF),
            pltpu.VMEM(own1, BF),
            pltpu.VMEM(own2, BF),
            pltpu.VMEM(own2, BF),
        ]
        + [pltpu.VMEM(s, BF) for s in landing]
        + [
            pltpu.VMEM((4, 9, 4, 128), BF),
            pltpu.VMEM((4, 9, 4, 128), BF),
            pltpu.VMEM((4, 4, 16, 128), F32),
            pltpu.VMEM((4, 4, 4, 16, 128), F32),
            dma((2,)),
            dma((2,)),
            dma((16,)),
            dma((16,)),
            dma((n, 22)),
            dma((n, 22)),
            dma((n, 4)),
            dma((4, 4)),
            dma((4, 4)),
            dma((4,)),
            dma((4,)),
            dma((2,)),
            dma((2,)),
        ],
        compiler_params=pltpu.CompilerParams(
            collective_id=1, has_side_effects=True, vmem_limit_bytes=62 * 2**20
        ),
        name="back_scatter",
    )(grad, first_grad, take, picks, w, picked, g1, g2, gv)


def with_halo(cells, width):
    count = lax.axis_size(("pts", "rep"))
    head, tail = cells[:width], cells[cells.shape[0] - width :]
    return (
        lax.ppermute(tail, ("pts", "rep"), [(i, i + 1) for i in range(count - 1)]),
        lax.ppermute(head, ("pts", "rep"), [(i + 1, i) for i in range(count - 1)]),
    )


def rank_within(labels, count):
    onehot = (labels[:, None] == jnp.arange(count, dtype=jnp.int32)[None, :]).astype(jnp.int32)
    before = jnp.cumsum(onehot, axis=0) - onehot
    return jnp.sum(before * onehot, axis=1)


def per_device(
    points,
    perm,
    inverse,
    lengths,
    neighbours,
    conv_weight,
    conv_bias,
    encode_weight,
    encode_bias,
    encode_gain,
    encode_shift,
    before_gain,
    before_shift,
    triple_weight,
    query_bias,
    value_bias,
    output_weight,
    output_bias,
    second_gain,
    second_shift,
    expand_weight,
    expand_bias,
    reduce_weight,
    reduce_bias,
    grad_out,
):
    rows, width = points.shape
    devices = lax.axis_size(("pts", "rep"))
    capacity = 2 * rows // devices
    halo_rows = rows // 4
    device = lax.axis_index(("pts", "rep"))
    pts, rep = lax.axis_index("pts"), lax.axis_index("rep")
    lane = lax.rem(pts, 8) * 16 + rep * 4
    wide_piece = jnp.concatenate([encode_weight, triple_weight, output_weight, expand_weight], axis=1)
    wide_piece = wide_piece.reshape(4, 36, 128).transpose(1, 0, 2).reshape(4, 9, 4, 128)
    vector_piece = jnp.concatenate(
        [
            jnp.stack(
                [
                    conv_bias,
                    encode_bias,
                    encode_gain,
                    encode_shift,
                    before_gain,
                    before_shift,
                    query_bias,
                    value_bias,
                    output_bias,
                    second_gain,
                    second_shift,
                    reduce_bias,
                ]
            ),
            expand_bias.reshape(4, 4),
        ],
        axis=0,
    )
    vector_tile = lax.dynamic_update_slice(jnp.zeros((16, 128), BF), vector_piece, (0, lane))
    got_conv, got_wide, got_tall, got_vectors = gather_weights(
        conv_weight, wide_piece, reduce_weight, vector_tile
    )
    kernel = got_conv.reshape(4, 27, 512, 128)
    wide = got_wide.reshape(36, 512, 128)
    tall = got_tall.reshape(2048, 512)
    vectors = got_vectors.reshape(4, 8, 16, 128).astype(F32).sum(axis=1)
    vectors = vectors.transpose(1, 0, 2).reshape(16, 512)
    full_expand_bias = vectors[12:].reshape(4, 128, 4).transpose(1, 0, 2).reshape(4, 512)

    destination = inverse // rows
    send_index = destination * capacity + rank_within(destination, devices)
    outgoing = jnp.zeros((devices * capacity, width), jnp.bfloat16).at[send_index].set(points)
    incoming = lax.all_to_all(
        outgoing.reshape(devices, capacity, width),
        ("pts", "rep"),
        split_axis=0,
        concat_axis=0,
        tiled=True,
    )
    incoming = incoming.reshape(devices * capacity, width)
    source = perm // rows
    same_source = source[:, None] == source[None, :]
    earlier = perm[None, :] < perm[:, None]
    take_index = source * capacity + jnp.sum(same_source & earlier, axis=1)
    ordered = incoming[take_index]
    before, after = with_halo(ordered, halo_rows)
    extended = jnp.concatenate([before, ordered, after], axis=0)
    token = jnp.arange(rows, dtype=jnp.int32)[None, :]
    local = jnp.where(
        neighbours >= 0, neighbours - (device * rows - halo_rows) - token // 256 * 256, -1
    )
    picks = local.reshape(9, 3, rows)

    conv, picked = conv_forward(picks.transpose(0, 2, 1), extended, kernel, vectors[:1])
    result, grad_first, grad_conv, grad_wide, grad_tall, vector_grads = block(
        lengths, conv, ordered, grad_out, wide, tall, vectors, full_expand_bias
    )
    natural = vector_grads[12:].reshape(128, 4, 4).transpose(1, 0, 2).reshape(4, 512)
    vector_grads = jnp.concatenate([vector_grads[:12], natural], axis=0)
    returning, kernel_out, wide_out, tall_out, vector_out = back_scatter(
        grad_conv,
        grad_first,
        take_index.reshape(1, rows),
        picks,
        kernel,
        picked,
        grad_wide.reshape(4, 9, 4, 4, 2, 16, 128),
        grad_tall.reshape(4, 4, 2, 4, 16, 512),
        vector_grads.reshape(16, 4, 128).transpose(1, 0, 2),
    )
    arrived = lax.all_to_all(
        returning.reshape(devices, capacity, width),
        ("pts", "rep"),
        split_axis=0,
        concat_axis=0,
        tiled=True,
    )
    points_grad = arrived.reshape(devices * capacity, width)[send_index]

    wide_out = wide_out.reshape(36, 4, 128).transpose(1, 0, 2).reshape(4, 4608)
    vector_out = lax.dynamic_slice(vector_out, (0, lane), (16, 4))
    reduced = (
        vector_out[V_CONV],
        wide_out[:, :512],
        vector_out[V_ENC],
        vector_out[V_GAIN0],
        vector_out[V_SHIFT0],
        vector_out[V_GAIN1],
        vector_out[V_SHIFT1],
        wide_out[:, 512:2048],
        vector_out[V_QUERY],
        vector_out[V_VALUE],
        wide_out[:, 2048:2560],
        vector_out[V_OUT],
        vector_out[V_GAIN2],
        vector_out[V_SHIFT2],
        wide_out[:, 2560:],
        vector_out[12:].reshape(16),
        tall_out,
        vector_out[V_RED],
    )
    return (result, points_grad, kernel_out) + reduced


def solution(mesh):
    in_specs = (
        P(("pts", "rep"), None),
        P(("pts", "rep")),
        P(("pts", "rep")),
        P(("pts", "rep")),
        P(None, ("pts", "rep")),
        P("pts", "rep"),
        P(("pts", "rep")),
        P(("pts", "rep"), None),
        P(("pts", "rep")),
        P(("pts", "rep")),
        P(("pts", "rep")),
        P(("pts", "rep")),
        P(("pts", "rep")),
        P(("pts", "rep"), None),
        P(("pts", "rep")),
        P(("pts", "rep")),
        P(("pts", "rep"), None),
        P(("pts", "rep")),
        P(("pts", "rep")),
        P(("pts", "rep")),
        P(("pts", "rep"), None),
        P(("pts", "rep")),
        P(("pts", "rep"), None),
        P(("pts", "rep")),
        P(("pts", "rep"), None),
    )
    out_specs = (
        P(("pts", "rep"), None),
        P(("pts", "rep"), None),
        P("pts", "rep"),
        P(("pts", "rep")),
        P(("pts", "rep"), None),
        P(("pts", "rep")),
        P(("pts", "rep")),
        P(("pts", "rep")),
        P(("pts", "rep")),
        P(("pts", "rep")),
        P(("pts", "rep"), None),
        P(("pts", "rep")),
        P(("pts", "rep")),
        P(("pts", "rep"), None),
        P(("pts", "rep")),
        P(("pts", "rep")),
        P(("pts", "rep")),
        P(("pts", "rep"), None),
        P(("pts", "rep")),
        P(("pts", "rep"), None),
        P(("pts", "rep")),
    )
    return jax.shard_map(
        per_device, mesh=mesh, in_specs=in_specs, out_specs=out_specs, check_vma=False
    )
```

```python
import jax
import jax.numpy as jnp
from jax import lax
from jax.experimental import pallas as pl
from jax.experimental.pallas import tpu as pltpu
from jax.sharding import PartitionSpec as P

MESH = pl.DeviceIdType.MESH
BF = jnp.bfloat16
F32 = jnp.float32


def place():
    p = lax.axis_index("pts")
    return {
        "x": lax.div(p, 8),
        "y": lax.rem(lax.div(p, 2), 4),
        "c": lax.rem(p, 2),
        "z": lax.axis_index("rep"),
    }


def device_at(at):
    return ((at["x"] * 4 + at["y"]) * 2 + at["c"], at["z"])


def moved(at, axis, step):
    size = 2 if axis == "c" else 4
    return {**at, axis: lax.rem(at[axis] + step, size)}


def whole(value):
    return slice(None) if value is None else value


def conv_view(ref, sel, h):
    r0, r1 = h
    return ref.at[
        whole(sel.get("z")), whole(sel.get("x")), whole(sel.get("y")), sel["c"], pl.ds(r0, r1 - r0), :
    ]


def wide_view(ref, sel, h):
    k0, k1 = h
    return ref.at[
        whole(sel.get("z")), pl.ds(k0, k1 - k0), whole(sel.get("x")), whole(sel.get("y")), sel["c"]
    ]


def tall_view(ref, sel, h):
    l0, l1 = h
    return ref.at[
        whole(sel.get("x")), whole(sel.get("y")), sel["c"], whole(sel.get("z")), :, pl.ds(l0, l1 - l0)
    ]


def flat_view(ref, sel, h):
    return ref.at[whole(sel.get("x")), whole(sel.get("y")), sel["c"]]


STREAMS = (
    ("cz", 0, conv_view, "xyz", ((0, 64), (64, 112))),
    ("cx", 0, conv_view, "yzx", ((112, 192), (192, 272))),
    ("cy", 0, conv_view, "zxy", ((272, 352), (352, 432))),
    ("m2", 2, tall_view, "zyx", ((0, 256), (256, 512))),
    ("m1", 1, wide_view, "xyz", ((0, 5), (5, 9))),
    ("vt", 3, flat_view, "xy", ((0, 16),)),
)
SLOTS = 40


VM = pl.BlockSpec(memory_space=pltpu.VMEM)
ANY = pl.BlockSpec(memory_space=pl.ANY)
SM = pl.BlockSpec(memory_space=pltpu.SMEM)
epsilon = 1e-05


def mm(a, b):
    return lax.dot_general(a, b, (((1,), (0,)), ((), ())), preferred_element_type=F32)


def mm_nt(a, b):
    return lax.dot_general(a, b, (((1,), (1,)), ((), ())), preferred_element_type=F32)


def mm_tn(a, b):
    return lax.dot_general(a, b, (((0,), (0,)), ((), ())), preferred_element_type=F32)


def wide_block(ref, first, count=4):
    return jnp.concatenate([ref[first + k] for k in range(count)], axis=1)


def put_wide(ref, first, value, count=4):
    for k in range(count):
        ref[first + k] = value[:, 128 * k : 128 * (k + 1)].astype(BF)


V_CONV, V_ENC, V_GAIN0, V_SHIFT0, V_GAIN1, V_SHIFT1, V_QUERY, V_VALUE, V_OUT, V_GAIN2, V_SHIFT2, V_RED = range(12)


def over_rows(body, step=64, rows=512):
    def one(n, _):
        body(pl.ds(pl.multiple_of(n * step, step), step))
        return 0

    lax.fori_loop(0, rows // step, one, 0)


def normalize(v):
    mean = jnp.mean(v, axis=-1, keepdims=True)
    centred = v - mean
    spread = jnp.mean(centred * centred, axis=-1, keepdims=True)
    rstd = lax.rsqrt(spread + epsilon)
    return centred * rstd, rstd


def norm_pull(hat, rstd, gain, grad):
    up = grad * gain
    a = jnp.mean(up, axis=-1, keepdims=True)
    b = jnp.mean(up * hat, axis=-1, keepdims=True)
    return rstd * (up - a - hat * b)


def total(v):
    return jnp.sum(v, axis=0, keepdims=True)


def gelu_both(u):
    cdf = 0.5 * (1.0 + lax.erf(u * 0.7071067811865476))
    pdf = 0.3989422804014327 * jnp.exp(-0.5 * u * u)
    return u * cdf, cdf + u * pdf


def three(v):
    hi = v.astype(BF).astype(F32)
    rest = v - hi
    mid = rest.astype(BF).astype(F32)
    return hi, mid, rest - mid


def block_kernel(
    length, conv, ordered, go, w1, w2, vec, xb,
    result, first_grad, conv_grad, g1, g2, gv,
    big, hat0, rstd0, first, hat1, rstd1, normed, normed_t, q, k, v, k_t, v_t,
    mixed_t, mixed, rows_a, rows_b, kx, xa, ya, hat2, rstd2, n2, n2_t,
    second, act, dh, da, acc, acc2, dn, d_mixed, dq_t, dk, dv,
):
    row = lambda n: vec[n : n + 1, :]
    gv[...] = jnp.zeros_like(gv)

    def gain(n, value):
        gv[n : n + 1, :] += total(value)

    big[...] = mm(conv[...], wide_block(w1, 0))

    def encode(r):
        hat, rstd = normalize(big[r, :] + row(V_ENC))
        hat0[r, :] = hat
        rstd0[r, :] = rstd
        here = ordered[r, :].astype(F32) + hat * row(V_GAIN0) + row(V_SHIFT0)
        first[r, :] = here
        hat, rstd = normalize(here)
        hat1[r, :] = hat
        rstd1[r, :] = rstd
        normed[r, :] = (hat * row(V_GAIN1) + row(V_SHIFT1)).astype(BF)

    over_rows(encode)
    normed_t[...] = normed[...].T
    q[...] = (0.25 * (mm(normed[...], wide_block(w1, 4)) + row(V_QUERY)).astype(BF).astype(F32)).astype(BF)
    k[...] = mm(normed[...], wide_block(w1, 8)).astype(BF)
    v[...] = (mm(normed[...], wide_block(w1, 12)) + row(V_VALUE)).astype(BF)
    k_t[...] = k[...].T
    v_t[...] = v[...].T

    lane = lax.broadcasted_iota(jnp.int32, (1, 128), 1)
    seat = lax.broadcasted_iota(jnp.int32, (512, 128), 0)
    spot = lax.broadcasted_iota(jnp.int32, (512, 128), 1)
    hidden_key = jnp.where((spot == 96) & (seat >= length[0]), -1e30, 0.0)
    kx[...] = jnp.where(spot < 96, 1.0, hidden_key).astype(BF)
    one_lane = jnp.where(spot == 96, 1.0, 0.0).astype(BF)
    rows_a[...] = jnp.zeros_like(rows_a)
    rows_b[...] = jnp.zeros_like(rows_b)

    def head_places(h):
        group = pl.ds(pl.multiple_of(lax.div(h, 8) * 128, 128), 128)
        mine = jnp.where(lax.div(lane, 16) == lax.rem(h, 8), 1.0, 0.0).astype(BF)
        extra = jnp.where((lax.rem(lane, 32) == h) & (lane < 96) | (lane == 96), 1.0, 0.0).astype(BF)
        return group, mine, extra, pl.ds(pl.multiple_of(h * 16, 16), 16)

    def forward_head(h):
        group, mine, extra, channels = head_places(h)
        keys = jnp.concatenate([k[:, group], kx[...]], axis=1)
        asks = jnp.concatenate([q[:, group] * mine, one_lane], axis=1)
        scores = mm_nt(keys, asks)
        peak = jnp.max(scores, axis=0, keepdims=True)
        e = jnp.exp(scores - peak)
        summed = total(e)
        mixed_t[channels, :] = mm(v_t[channels, :], e.astype(BF)) / summed
        lse = peak + jnp.log(summed)
        hi, mid, lo = three(-lse)
        rows_a[pl.ds(h, 1), :] = hi
        rows_a[pl.ds(h + 32, 1), :] = mid
        rows_a[pl.ds(h + 64, 1), :] = lo

    def forward_heads(n, _):
        for j in range(2):
            forward_head(n * 2 + j)
        return 0

    lax.fori_loop(0, 16, forward_heads, 0)
    rows_a[96:97, :] = jnp.ones((1, 512), F32)
    xa[...] = rows_a[...].T.astype(BF)
    mixed[...] = mixed_t[...].T.astype(BF)

    big[...] = mm(mixed[...], wide_block(w1, 16))

    def after(r):
        here = first[r, :] + big[r, :] + row(V_OUT)
        second[r, :] = here
        hat, rstd = normalize(here)
        hat2[r, :] = hat
        rstd2[r, :] = rstd
        n2[r, :] = (hat * row(V_GAIN2) + row(V_SHIFT2)).astype(BF)
        gain(V_RED, go[r, :].astype(F32))

    over_rows(after)
    n2_t[...] = n2[...].T
    acc[...] = jnp.zeros_like(acc)
    acc2[...] = jnp.zeros_like(acc2)

    def chunk(c, _):
        up = jnp.concatenate([w1[20 + 4 * c + j] for j in range(4)], axis=1)
        span = pl.ds(pl.multiple_of(c * 512, 512), 512)
        down = w2[span, :]
        big[...] = mm(n2[...], up)
        da[...] = mm_nt(go[...], down)

        def gelu_rows(r):
            value, slope = gelu_both(big[r, :] + xb[pl.ds(c, 1), :])
            act[r, :] = value.astype(BF)
            low = (da[r, :] * slope).astype(BF)
            dh[r, :] = low
            gv[pl.ds(12 + c, 1), :] += total(low.astype(F32))

        over_rows(gelu_rows, 32)
        acc[...] += mm(act[...], down)
        acc2[...] += mm_nt(dh[...], up)
        g2[span, :] = mm_tn(act[...], go[...]).astype(BF)
        grad_up = mm(n2_t[...], dh[...])
        for j in range(4):
            g1[20 + 4 * c + j] = grad_up[:, 128 * j : 128 * (j + 1)].astype(BF)
        return 0

    lax.fori_loop(0, 4, chunk, 0)

    def before_mlp(r):
        result[r, :] = (second[r, :] + acc[r, :] + row(V_RED)).astype(BF)
        grad = acc2[r, :]
        hat = hat2[r, :]
        gain(V_GAIN2, grad * hat)
        gain(V_SHIFT2, grad)
        here = go[r, :].astype(F32) + norm_pull(hat, rstd2[r, :], row(V_GAIN2), grad)
        second[r, :] = here
        low = here.astype(BF)
        dn[r, :] = low
        gain(V_OUT, low.astype(F32))

    over_rows(before_mlp)
    put_wide(g1, 16, mm_tn(mixed[...], dn[...]))
    d_mixed[...] = mm_nt(dn[...], wide_block(w1, 16)).astype(BF)
    big[...] = d_mixed[...].astype(F32).T

    def inner(h, _):
        channels = pl.ds(pl.multiple_of(h * 16, 16), 16)
        hi, mid, lo = three(-total(big[channels, :] * mixed_t[channels, :]))
        rows_b[pl.ds(h, 1), :] = hi
        rows_b[pl.ds(h + 32, 1), :] = mid
        rows_b[pl.ds(h + 64, 1), :] = lo
        return 0

    lax.fori_loop(0, 32, inner, 0)
    ya[...] = rows_b[...].T.astype(BF)
    dk[...] = jnp.zeros_like(dk)
    dv[...] = jnp.zeros_like(dv)
    ones = jnp.where(spot < 96, 1.0, 0.0).astype(BF)

    def backward_head(h):
        group, mine, extra, channels = head_places(h)
        q_h = q[:, group] * mine
        m_h = d_mixed[:, group] * mine
        keys = jnp.concatenate([k[:, group], kx[...]], axis=1)
        p = jnp.exp(mm_nt(keys, jnp.concatenate([q_h, xa[...] * extra], axis=1)))
        values = jnp.concatenate([v[:, group], ones], axis=1)
        slope = mm_nt(values, jnp.concatenate([m_h, ya[...] * extra], axis=1))
        ds = (p * slope).astype(BF)
        dv[:, group] += mm(p.astype(BF), m_h)
        dk[:, group] += mm(ds, q_h)
        dq_t[channels, :] = mm(k_t[channels, :], ds)

    def backward_heads(n, _):
        for j in range(2):
            backward_head(n * 2 + j)
        return 0

    lax.fori_loop(0, 16, backward_heads, 0)
    q[...] = (0.25 * dq_t[...].T).astype(BF)
    k[...] = dk[...].astype(BF)
    v[...] = dv[...].astype(BF)
    gain(V_QUERY, q[...].astype(F32))
    gain(V_VALUE, v[...].astype(F32))
    put_wide(g1, 4, mm(normed_t[...], q[...]))
    put_wide(g1, 8, mm(normed_t[...], k[...]))
    put_wide(g1, 12, mm(normed_t[...], v[...]))
    acc2[...] = (
        mm_nt(q[...], wide_block(w1, 4)) + mm_nt(k[...], wide_block(w1, 8)) + mm_nt(v[...], wide_block(w1, 12))
    )

    def before_attention(r):
        grad = acc2[r, :]
        hat = hat1[r, :]
        gain(V_GAIN1, grad * hat)
        gain(V_SHIFT1, grad)
        here = second[r, :] + norm_pull(hat, rstd1[r, :], row(V_GAIN1), grad)
        first_grad[r, :] = here
        hat = hat0[r, :]
        gain(V_GAIN0, here * hat)
        gain(V_SHIFT0, here)
        low = norm_pull(hat, rstd0[r, :], row(V_GAIN0), here).astype(BF)
        dn[r, :] = low
        gain(V_ENC, low.astype(F32))

    over_rows(before_attention)
    put_wide(g1, 0, mm_tn(conv[...], dn[...]))
    conv_grad[...] = mm_nt(dn[...], wide_block(w1, 0)).astype(BF)
    gain(V_CONV, conv_grad[...].astype(F32))


def block(length, conv, ordered, go, w1, w2, vec, xb):
    shape = jax.ShapeDtypeStruct
    full = (512, 512)
    f, b, col = pltpu.VMEM(full, F32), pltpu.VMEM(full, BF), pltpu.VMEM((512, 1), F32)
    rows, lanes = pltpu.VMEM((128, 512), F32), pltpu.VMEM((512, 128), BF)
    return pl.pallas_call(
        block_kernel,
        out_shape=(
            shape(full, BF),
            shape(full, F32),
            shape(full, BF),
            shape((36, 512, 128), BF),
            shape((2048, 512), BF),
            shape((16, 512), F32),
        ),
        in_specs=[SM] + [VM] * 7,
        out_specs=[VM] * 6,
        scratch_shapes=[
            f, f, col, f, f, col, b, b, b, b, b, b, b,
            f, b, rows, rows, lanes, lanes, lanes, f, col, b, b,
            f, b, b, f, f, f, b, b, f, f, f,
        ],
        compiler_params=pltpu.CompilerParams(vmem_limit_bytes=60 * 2**20),
        name="block",
    )(length, conv, ordered, go, w1, w2, vec, xb)


def spread_rows(picks, j, b):
    seat = lax.broadcasted_iota(jnp.int32, (512, 256), 0)
    return jnp.where(seat == picks[j : j + 1, 256 * b : 256 * (b + 1)], 1.0, 0.0).astype(BF)


def line_neighbour(at, step):
    linear = lax.rem(((at["x"] * 4 + at["y"]) * 2 + at["c"]) * 4 + at["z"] + step, 128)
    return (lax.div(linear, 4), lax.rem(linear, 4))


def meet_all(me):
    barrier = pltpu.get_barrier_semaphore()

    def tell(s, _):
        pl.semaphore_signal(barrier, inc=1, device_id=device_after(me, s), device_id_type=MESH)
        return 0

    lax.fori_loop(1, 128, tell, 0)


def device_after(me, s):
    linear = lax.rem(me + s, 128)
    return (lax.div(linear, 4), lax.rem(linear, 4))


def deal(rows, landing, me, send, recv):
    def one(s, _):
        pltpu.make_async_remote_copy(
            src_ref=rows.at[lax.rem(me + s, 128)],
            dst_ref=landing.at[me],
            send_sem=send,
            recv_sem=recv,
            device_id=device_after(me, s),
            device_id_type=MESH,
        ).start()
        return 0

    lax.fori_loop(1, 128, one, 0)
    landing[me] = rows[me]


def dealt(rows, landing, me, send, recv):
    return pltpu.make_async_remote_copy(
        src_ref=rows.at[pl.ds(0, 127)],
        dst_ref=landing.at[pl.ds(0, 127)],
        send_sem=send,
        recv_sem=recv,
        device_id=device_after(me, 1),
        device_id_type=MESH,
    )


def fold_rows(index, rows, out):
    for n in range(4):
        seat = lax.broadcasted_iota(jnp.int32, (256, 512), 0) + 256 * n
        hot = jnp.where(seat == index, 1.0, 0.0).astype(BF)
        out[32 * n : 32 * (n + 1)] = mm(hot, rows).reshape(32, 8, 512).astype(BF)


def unfold_rows(index, blocks):
    seat = lax.broadcasted_iota(jnp.int32, (1024, 512), 0)
    hot = jnp.where(seat == index, 1.0, 0.0).astype(BF)
    return mm_tn(hot, blocks[...].astype(F32).reshape(1024, 512).astype(BF)).astype(BF)


def column_of(row):
    return jnp.broadcast_to(row, (128, 512)).T[:, 0:1]


def front_kernel(
    conv, m1p, m2, vt, points, inverse, perm, neighbours,
    gc, g1, g2, picked, conv_low, ordered, vectors, natural, take, send, picks,
    outgoing, incoming,
    extended, all_picks, acc, w_buf, pick_cols, pre, m1b, prev, vb, gv,
    sends, recvs, locs, presend, prerecv, halo_s, halo_r, p_sem, w_sem, deal_s, deal_r,
):
    at = place()
    width = 512
    me = ((at["x"] * 4 + at["y"]) * 2 + at["c"]) * 4 + at["z"]
    meet_all(me)
    home = lax.div(inverse[...], width)
    row_id = lax.broadcasted_iota(jnp.int32, (width, width), 0)
    lane_id = lax.broadcasted_iota(jnp.int32, (width, width), 1)
    ahead = jnp.where((column_of(home.astype(F32)) == home.astype(F32)) & (row_id < lane_id), 1.0, 0.0)
    send[...] = home * 8 + total(ahead).astype(jnp.int32)
    fold_rows(send[...], points[...], outgoing)
    pl.semaphore_wait(pltpu.get_barrier_semaphore(), 127)
    outs = (gc, g1, g2, gv)
    other = moved(at, "c", 1)
    pending = []
    crossing = {i: [] for i in range(len(STREAMS))}

    def remote(src, dst, send, recv, device):
        copy = pltpu.make_async_remote_copy(
            src_ref=src, dst_ref=dst, send_sem=send, recv_sem=recv,
            device_id=device, device_id_type=MESH,
        )
        copy.start()
        pending.append(copy)
        return copy

    def push(src, dst, i, k, to):
        return remote(src, dst, sends.at[i, k], recvs.at[i, k], device_at(to))

    def cross(ref, i, k):
        crossing[i].append(push(ref, ref, i, k, other))

    def own_view(i, h):
        name, op, view, order, halves = STREAMS[i]
        if op == 0:
            return conv.at[pl.ds(h[0], h[1] - h[0]), :]
        if op == 1:
            return m1b.at[pl.ds(h[0], h[1] - h[0])]
        if op == 2:
            return m2.at[:, pl.ds(h[0], h[1] - h[0])]
        return vb

    local_copies = {}

    def keep_own(i):
        name, op, view, order, halves = STREAMS[i]
        for j, h in enumerate(halves):
            copy = pltpu.make_async_copy(own_view(i, h), view(outs[op], at, h), locs.at[i, j])
            copy.start()
            local_copies[(i, j)] = copy

    state = {}

    def block_sel(order, phase, index=None):
        sel = {"c": at["c"]}
        for a in "xyz":
            if a in order and order.index(a) < phase:
                continue
            sel[a] = at[a]
        if index is not None:
            sel[order[phase]] = index
        return sel

    def begin(i, phase):
        name, op, view, order, halves = STREAMS[i]
        axis = order[phase]
        n = len(halves)
        sel = block_sel(order, phase)
        copies = {}
        for d, hs in ((1, range(n)), (3, reversed(range(n)))):
            for h in hs:
                dst = view(outs[op], sel, halves[h])
                src = own_view(i, halves[h]) if phase == 0 else dst
                copies[(d, h)] = push(src, dst, i, phase * 6 + (0 if d == 1 else 2) + h, moved(at, axis, d))
        state[(i, phase)] = copies
        if phase == len(order) - 1:
            for h in range(n):
                cross(view(outs[op], sel, halves[h]), i, 20 + h)

    def relay(i, phase):
        name, op, view, order, halves = STREAMS[i]
        axis = order[phase]
        last = phase == len(order) - 1
        n = len(halves)
        copies = state[(i, phase)]
        for d in (1, 3) if n == 2 else (1,):
            h = 0 if d == 1 else n - 1
            copies[(d, h)].wait_recv()
            ref = view(outs[op], block_sel(order, phase, lax.rem(at[axis] + 4 - d, 4)), halves[h])
            copies[(d, "f")] = push(ref, ref, i, phase * 6 + (4 if d == 1 else 5), moved(at, axis, d))
            if last:
                cross(ref, i, 22 + d)

    def finish(i, phase):
        name, op, view, order, halves = STREAMS[i]
        axis = order[phase]
        last = phase == len(order) - 1
        n = len(halves)
        copies = state[(i, phase)]
        for d in (1, 3):
            for h in range(n):
                if h == (0 if d == 1 else n - 1) and not (n == 1 and d == 3):
                    continue
                copies[(d, h)].wait_recv()
                if last:
                    sel = block_sel(order, phase, lax.rem(at[axis] + 4 - d, 4))
                    cross(view(outs[op], sel, halves[h]), i, 26 + d)
        for d in (1, 3):
            if (d, "f") not in copies:
                continue
            copies[(d, "f")].wait_recv()
            if last:
                h = 0 if d == 1 else n - 1
                sel = block_sel(order, phase, lax.rem(at[axis] + 2, 4))
                cross(view(outs[op], sel, halves[h]), i, 30 + d)
        if phase == 0:
            for h in range(n):
                local_copies[(i, h)].wait()

    pre_copies = []
    for step in (1, 2, 3):
        to = moved(at, "z", step)
        for j, (src, dst) in enumerate(((m1p.at[to["z"]], pre.at[step]), (vt, prev.at[step]))):
            pre_copies.append(remote(src, dst, presend.at[j, step], prerecv.at[j, step], device_at(to)))
    first, more = (0, 1, 2), (3, 4, 5)
    for i in first:
        begin(i, 0)
        keep_own(i)

    deal(outgoing, incoming, me, deal_s, deal_r)
    source = lax.div(perm[...], width)
    column = column_of(perm[...].astype(F32))
    source_column = lax.div(column.astype(jnp.int32), width)
    ahead = jnp.where((source_column == source) & (column < perm[...].astype(F32)), 1.0, 0.0)
    take[...] = source * 8 + total(ahead).astype(jnp.int32)
    token = lax.broadcasted_iota(jnp.int32, (1, width), 1)
    shift = me * width - 128 + lax.div(token, 256) * 256

    def pick_rows(u, _):
        local = jnp.where(neighbours[u] >= 0, neighbours[u] - shift, -1)
        picks[u] = local
        pick_cols[u] = jnp.concatenate([local, local, local[0:2]], axis=0).astype(F32)
        return 0

    lax.fori_loop(0, 9, pick_rows, 0)
    acc[...] = jnp.zeros_like(acc)
    for copy in pre_copies:
        copy.wait_recv()
    pre[0] = m1p[at["z"]]

    def tile(k, _):
        pieces = [pre[lax.rem(at["z"] - s + 4, 4), k].astype(F32) for s in range(4)]
        m1b[k] = jnp.concatenate(pieces, axis=0).astype(BF)
        return 0

    lax.fori_loop(0, 9, tile, 0)
    vb[...] = (
        vt[...].astype(F32) + prev[1].astype(F32) + prev[2].astype(F32) + prev[3].astype(F32)
    ).astype(BF)
    for i in first:
        relay(i, 0)
    for i in first:
        finish(i, 0)
        begin(i, 1)
    dealt(outgoing, incoming, me, deal_s, deal_r).wait_recv()
    mine = unfold_rows(take[...], incoming)
    ordered[...] = mine
    extended[128:640, :] = mine
    halos = []
    for j, (src, dst, step) in enumerate(((128, 640, 127), (512, 0, 1))):
        halos.append(
            remote(
                extended.at[pl.ds(src, 128), :], extended.at[pl.ds(dst, 128), :],
                halo_s.at[j], halo_r.at[j], line_neighbour(at, step),
            )
        )
    for i in more:
        begin(i, 0)
        keep_own(i)
    for copy in halos:
        copy.wait_recv()

    def p_copy(u):
        return pltpu.make_async_copy(all_picks.at[pl.ds(u * 3, 3)], picked.at[pl.ds(u * 3, 3)], p_sem.at[u])

    def pick_unit(u, _):
        columns = pick_cols[u].T
        for j in range(3):
            for b in range(2):
                seat = lax.broadcasted_iota(jnp.int32, (256, 512), 1).astype(F32)
                hot = jnp.where(seat == columns[256 * b : 256 * (b + 1), j : j + 1], 1.0, 0.0).astype(BF)
                window = extended[256 * b : 256 * b + 512, :]
                all_picks[u * 3 + j, 256 * b : 256 * (b + 1), :] = mm(hot, window).astype(BF)
        p_copy(u).start()
        return 0

    def w_copy(u):
        slot = lax.rem(u, 2)
        return pltpu.make_async_copy(
            gc.reshape((4, 27, 512, 128)).at[:, pl.ds(u * 3, 3)], w_buf.at[slot], w_sem.at[slot]
        )

    def conv_unit(u, _):
        @pl.when(u < 8)
        def _():
            w_copy(u + 1).start()

        w_copy(u).wait()
        slot = lax.rem(u, 2)
        parts = [
            mm(all_picks[u * 3 + j], jnp.concatenate([w_buf[slot, n, j] for n in range(4)], axis=1))
            for j in range(3)
        ]
        acc[...] += parts[0] + parts[1] + parts[2]
        return 0

    lax.fori_loop(0, 1, pick_unit, 0)
    for i in first:
        relay(i, 1)
    for i in more:
        relay(i, 0)
    for i in first:
        finish(i, 1)
        begin(i, 2)
    for i in more:
        finish(i, 0)
        begin(i, 1)
    lax.fori_loop(1, 4, pick_unit, 0)
    for i in more:
        relay(i, 1)
    lax.fori_loop(4, 6, pick_unit, 0)
    for i in first:
        relay(i, 2)
    for i in more:
        finish(i, 1)
        if len(STREAMS[i][3]) > 2:
            begin(i, 2)
    lax.fori_loop(6, 9, pick_unit, 0)
    for i in first:
        finish(i, 2)
    for i in first:
        for copy in crossing[i]:
            copy.wait_recv()
    w_copy(0).start()
    lax.fori_loop(0, 2, conv_unit, 0)
    for i in (3, 4):
        relay(i, 2)
    lax.fori_loop(2, 7, conv_unit, 0)
    for i in (3, 4):
        finish(i, 2)
    lax.fori_loop(7, 9, conv_unit, 0)
    for i in more:
        for copy in crossing[i]:
            copy.wait_recv()
    chunks = []
    for x in range(4):
        chunk = jnp.zeros((16, 128), F32)
        for y in range(4):
            for c in range(2):
                chunk = chunk + gv[x, y, c].astype(F32)
        chunks.append(chunk)
    together = jnp.concatenate(chunks, axis=1)
    vectors[...] = together
    lane = lax.broadcasted_iota(jnp.int32, (128, width), 1)
    from_lane = lax.broadcasted_iota(jnp.int32, (128, width), 0)
    shuffle = jnp.where(from_lane == lax.div(lane, 16) * 4 + lax.rem(lane, 4), 1.0, 0.0).astype(BF)
    which = lax.div(lax.rem(lax.broadcasted_iota(jnp.int32, (4, width), 1), 16), 4)
    group = lax.broadcasted_iota(jnp.int32, (4, width), 0)
    for x in range(4):
        spreaded = mm(chunks[x].astype(BF), shuffle)[12:16, :]
        natural[x : x + 1, :] = total(jnp.where(which == group, spreaded, 0.0))
    conv_low[...] = (acc[...] + together[0:1, :]).astype(BF)
    for copy in pending:
        copy.wait_send()
    dealt(outgoing, incoming, me, deal_s, deal_r).wait_send()

    def stored(u, _):
        p_copy(u).wait()
        return 0

    lax.fori_loop(0, 9, stored, 0)


def front(conv, m1p, m2, vt, points, inverse, perm, neighbours):
    shape = jax.ShapeDtypeStruct
    n = len(STREAMS)
    dma = pltpu.SemaphoreType.DMA
    return pl.pallas_call(
        front_kernel,
        out_shape=(
            shape((4, 4, 4, 2, 432, 128), BF),
            shape((4, 9, 4, 4, 2, 16, 128), BF),
            shape((4, 4, 2, 4, 16, 512), BF),
            shape((27, 512, 512), BF),
            shape((512, 512), BF),
            shape((512, 512), BF),
            shape((16, 512), F32),
            shape((4, 512), F32),
            shape((1, 512), jnp.int32),
            shape((1, 512), jnp.int32),
            shape((9, 3, 512), jnp.int32),
        ),
        in_specs=[ANY, VM, ANY] + [VM] * 5,
        out_specs=[ANY] * 4 + [VM] * 7,
        scratch_shapes=[
            pltpu.VMEM((128, 8, 512), BF),
            pltpu.VMEM((128, 8, 512), BF),
            pltpu.VMEM((768, 512), BF),
            pltpu.VMEM((27, 512, 512), BF),
            pltpu.VMEM((512, 512), F32),
            pltpu.VMEM((2, 4, 3, 512, 128), BF),
            pltpu.VMEM((9, 8, 512), F32),
            pltpu.VMEM((4, 9, 4, 128), BF),
            pltpu.VMEM((9, 16, 128), BF),
            pltpu.VMEM((4, 16, 128), BF),
            pltpu.VMEM((16, 128), BF),
            pltpu.VMEM((4, 4, 2, 16, 128), BF),
            dma((n, SLOTS)),
            dma((n, SLOTS)),
            dma((n, 2)),
            dma((2, 4)),
            dma((2, 4)),
            dma((2,)),
            dma((2,)),
            dma((9,)),
            dma((2,)),
            dma,
            dma,
        ],
        compiler_params=pltpu.CompilerParams(
            collective_id=0, has_side_effects=True, vmem_limit_bytes=48 * 2**20
        ),
        name="front",
    )(conv, m1p, m2, vt, points, inverse, perm, neighbours)


CHAINS = (
    ("cz", "zxycRL", {"R": 112, "L": 128}, "R", 0, "zyx", ((0, 64), (64, 112))),
    ("cx", "zxycRL", {"R": 160, "L": 128}, "R", 112, "xzy", ((0, 80), (80, 160))),
    ("cy", "zxycRL", {"R": 160, "L": 128}, "R", 272, "yxz", ((0, 80), (80, 160))),
    ("m2", "xyczSL", {"S": 16, "L": 512}, "L", 0, "xyz", ((0, 256), (256, 512))),
    ("m1", "zKxycSL", {"K": 9, "S": 16, "L": 128}, "K", 0, "zyx", ((0, 5), (5, 9))),
)
CONV_CHAINS, MORE_CHAINS = (0, 1, 2), (4, 3)


def cut_view(ref, layout, sel, cut=None, span=None, base=0):
    index = []
    for dim in layout:
        if dim in sel:
            index.append(sel[dim])
        elif dim == cut and span is not None:
            index.append(pl.ds(base + span[0], span[1] - span[0]))
        else:
            index.append(slice(None))
    return ref.at[tuple(index)]


def sizes_of(layout, plain):
    return tuple(plain[d] if d in plain else 4 for d in layout)


def landing_shapes(i):
    name, layout, plain, cut, base, order, halves = CHAINS[i]
    left = layout.replace("c", "")
    shapes = []
    for axis in order:
        left = left.replace(axis, "")
        for span in halves:
            shapes.append(sizes_of(left, {**plain, cut: span[1] - span[0]}))
        shapes += [sizes_of(left, plain)] * 2
    return shapes


STEPS = (2, 1, 3, 0)


def back_kernel(
    grad, first_grad, take, send, picks, w, picked, g1, g2, gv,
    points_grad, oc, o1, o2, ov,
    returning, arrived,
    kernel_grad, theirs, spread, p_buf, w_buf, rims, landed, own1, sib1, own2, sib2, *rest,
):
    count = 12 * len(CHAINS)
    landing, rest = rest[:count], rest[count:]
    post, postr, vx, vr, p_sem, w_sem, xy_send, xy_recv, sends, recvs, locs, vsend, vrecv, psend, precv, rim_s, rim_r, deal_s, deal_r = rest
    at = place()
    me = ((at["x"] * 4 + at["y"]) * 2 + at["c"]) * 4 + at["z"]
    meet_all(me)
    other = moved(at, "c", 1)
    pending = []
    tiles = kernel_grad.reshape((4, 4, 4, 2, 432, 128))

    def remote(src, dst, send, recv, device):
        return pltpu.make_async_remote_copy(
            src_ref=src, dst_ref=dst, send_sem=send, recv_sem=recv,
            device_id=device, device_id_type=MESH,
        )

    def push(src, dst, send, recv, to):
        copy = remote(src, dst, send, recv, device_at(to))
        copy.start()
        pending.append(copy)
        return copy

    stores = {
        0: (tiles, "zxycRL", {"c": at["c"]}),
        1: (tiles, "zxycRL", {"c": at["c"]}),
        2: (tiles, "zxycRL", {"c": at["c"]}),
        3: (own2, "xyzSL", {}),
        4: (own1, "zKxySL", {}),
    }

    def view(i, sel, span):
        name, layout, plain, cut, base, order, halves = CHAINS[i]
        ref, inner, fixed = stores[i]
        return cut_view(ref, inner, {**fixed, **sel}, cut, span, base)

    def add(i, sel, srcs, span):
        name, layout, plain, cut, base, order, halves = CHAINS[i]
        ref, inner, fixed = stores[i]
        free = [d for d in inner if d in "xyz" and d not in sel]
        count = 4 ** len(free)

        def one(n, _):
            here = dict(sel)
            for k, d in enumerate(reversed(free)):
                here[d] = lax.rem(lax.div(n, 4**k), 4)
            where = view(i, here, span)
            total = where[...].astype(F32)
            for src, src_layout, src_sel, src_span in srcs:
                full = {**{d: here[d] for d in free}, **src_sel}
                total = total + cut_view(src, src_layout, full, cut, src_span)[...].astype(F32)
            where[...] = total.astype(BF)
            return 0

        if count == 1:
            one(0, 0)
        else:
            lax.fori_loop(0, count, one, 0)

    def load(i, src, own, sib):
        name, layout, plain, cut, base, order, halves = CHAINS[i]
        inner, axis, span = layout.replace("c", ""), order[0], (0, plain[cut])
        copies = []
        for k, step in enumerate(STEPS):
            a = lax.rem(at[axis] + step, 4)
            far = cut_view(src, layout, {"c": other["c"], axis: a}, cut, span)
            near = cut_view(src, layout, {"c": at["c"], axis: a}, cut, span)
            crossing = push(far, cut_view(sib, inner, {axis: a}), sends.at[i, k], recvs.at[i, k], other)
            local = pltpu.make_async_copy(near, cut_view(own, inner, {axis: a}), locs.at[i, k])
            local.start()
            copies.append((crossing, local))
        return copies

    def names(i, phase):
        name, layout, plain, cut, base, order, halves = CHAINS[i]
        inner = layout.replace("c", "")
        axis = order[phase]
        done = {a: at[a] for a in order[:phase]}
        left = "".join(d for d in inner if d not in order[: phase + 1])
        buffers = landing[i * 12 + 4 * phase : i * 12 + 4 * phase + 4]
        slot = lambda k: (sends.at[i, 4 + phase * 6 + k], recvs.at[i, 4 + phase * 6 + k])
        return inner, axis, done, left, buffers, slot, cut, halves, (0, plain[cut])

    def start(i, phase, loaded=None, sib=None):
        inner, axis, done, left, (r0, r1, rp, rm), slot, cut, halves, span = names(i, phase)
        up, down = moved(at, axis, 1), moved(at, axis, 3)
        got = {}
        for k, step in enumerate(STEPS):
            a = lax.rem(at[axis] + step, 4)
            if loaded is not None:
                crossing, local = loaded[k]
                crossing.wait_recv()
                local.wait()
                add(i, {axis: a}, [(sib, inner, {axis: a}, span)], span)
            part = lambda h: view(i, {**done, axis: a}, h)
            if step == 2:
                got["r0"] = push(part(halves[0]), r0, *slot(0), up)
                got["r1"] = push(part(halves[1]), r1, *slot(1), down)
            elif step == 1:
                got["p1"] = push(part(halves[1]), cut_view(rp, left, {}, cut, halves[1]), *slot(2), up)
            elif step == 3:
                got["m0"] = push(part(halves[0]), cut_view(rm, left, {}, cut, halves[0]), *slot(3), down)
        return got

    def middle(i, phase, got):
        inner, axis, done, left, (r0, r1, rp, rm), slot, cut, halves, span = names(i, phase)
        up, down = moved(at, axis, 1), moved(at, axis, 3)
        for key, h, buf, land, to, k in (("r0", 0, r0, rp, up, 4), ("r1", 1, r1, rm, down, 5)):
            half = halves[h]
            got[key].wait_recv()
            sel = {**done, axis: to[axis]}
            add(i, sel, [(buf, left, {}, (0, half[1] - half[0]))], half)
            got[k] = push(view(i, sel, half), cut_view(land, left, {}, cut, half), *slot(k), to)

    def close(i, phase, got):
        inner, axis, done, left, (r0, r1, rp, rm), slot, cut, halves, span = names(i, phase)
        for k in ("p1", "m0", 4, 5):
            got[k].wait_recv()
        add(i, {**done, axis: at[axis]}, [(rp, left, {}, span), (rm, left, {}, span)], span)

    def vector_step(k):
        axis, steps = (("c", (1,)), ("z", (1, 2, 3)), ("y", (1, 2, 3)), ("x", (1, 2, 3)))[k]
        copies = []
        for s in steps:
            to = moved(at, axis, s)
            if axis == "x":
                src, dst = vx.at[3, to["x"]], vr.at[3, s, 0]
            else:
                src, dst = (gv if k == 0 else vx.at[k]), vr.at[k, s]
            copies.append(push(src, dst, vsend.at[k, s], vrecv.at[k, s], to))
        return copies

    def vector_add(k, copies):
        for copy in copies:
            copy.wait_recv()
        if k == 3:
            ov[...] = vx[3, at["x"]] + vr[3, 1, 0] + vr[3, 2, 0] + vr[3, 3, 0]
            return
        sum_now = gv[...] if k == 0 else vx[k]
        for s in (1,) if k == 0 else (1, 2, 3):
            sum_now = sum_now + vr[k, s]
        vx[k + 1] = sum_now

    def p_copy(u):
        slot = lax.rem(u, 2)
        return pltpu.make_async_copy(picked.at[pl.ds(u * 3, 3)], p_buf.at[slot], p_sem.at[slot])

    def w_copy(u):
        slot = lax.rem(u, 2)
        return pltpu.make_async_copy(w.at[:, pl.ds(u * 3, 3)], w_buf.at[slot], w_sem.at[slot])

    def xy_copy(n):
        x, y = lax.div(n, 4), lax.rem(n, 4)
        return remote(
            tiles.at[:, x, y, other["c"]], theirs.at[:, x, y], xy_send.at[n], xy_recv.at[n], device_at(other)
        )

    def weight_unit(u, _):
        @pl.when(u < 8)
        def _():
            p_copy(u + 1).start()

        p_copy(u).wait()
        for j in range(3):
            product = mm_tn(p_buf[lax.rem(u, 2), j], grad[...])
            span = pl.ds(pl.multiple_of(u * 1536 + j * 512, 512), 512)
            for n in range(4):
                kernel_grad[n, span, :] = product[:, 128 * n : 128 * (n + 1)].astype(BF)
        ready, ready_next = lax.div(u * 16, 9), lax.div((u + 1) * 16, 9)
        for j in range(2):
            @pl.when(ready + j < ready_next)
            def _():
                xy_copy(ready + j).start()

        return 0

    def row_unit(u, _):
        @pl.when(u < 8)
        def _():
            w_copy(u + 1).start()

        w_copy(u).wait()
        slot = lax.rem(u, 2)
        g = grad[...]
        back = [
            mm_nt(g, jnp.concatenate([w_buf[slot, n, j] for n in range(4)], axis=1)).astype(BF)
            for j in range(3)
        ]
        for b in range(2):
            hot = jnp.concatenate([spread_rows(picks.at[u], j, b) for j in range(3)], axis=1)
            terms = jnp.concatenate([back[j][256 * b : 256 * (b + 1), :] for j in range(3)], axis=0)
            spread[256 * b : 256 * b + 512, :] += mm(hot, terms)
        return 0

    p_copy(0).start()
    spread[...] = jnp.zeros_like(spread)
    pl.semaphore_wait(pltpu.get_barrier_semaphore(), 127)
    vectors = vector_step(0)
    state = {}
    loaded = {4: load(4, g1, own1, sib1), 3: load(3, g2, own2, sib2)}
    w_copy(0).start()
    lax.fori_loop(0, 3, weight_unit, 0)
    for i in MORE_CHAINS:
        state[i] = start(i, 0, loaded[i], {4: sib1, 3: sib2}[i])
    vector_add(0, vectors)
    vectors = vector_step(1)
    lax.fori_loop(3, 6, weight_unit, 0)
    for i in MORE_CHAINS:
        middle(i, 0, state[i])
    lax.fori_loop(6, 9, weight_unit, 0)
    vector_add(1, vectors)
    vectors = vector_step(2)
    for i in MORE_CHAINS:
        close(i, 0, state[i])
        state[i] = start(i, 1)
    for n in range(16):
        xy_copy(n).wait_recv()

    def join(n, _):
        z, x, y = lax.div(n, 16), lax.rem(lax.div(n, 4), 4), lax.rem(n, 4)
        where = tiles.at[z, x, y, at["c"]]
        where[...] = (where[...].astype(F32) + theirs[z, x, y].astype(F32)).astype(BF)
        return 0

    lax.fori_loop(0, 64, join, 0)
    for i in CONV_CHAINS:
        state[i] = start(i, 0)
    for i in MORE_CHAINS:
        middle(i, 1, state[i])
    lax.fori_loop(0, 3, row_unit, 0)
    vector_add(2, vectors)
    vectors = vector_step(3)
    for i in MORE_CHAINS:
        close(i, 1, state[i])
        state[i] = start(i, 2)
    lax.fori_loop(3, 5, row_unit, 0)
    for i in CONV_CHAINS:
        middle(i, 0, state[i])
    for i in MORE_CHAINS:
        middle(i, 2, state[i])
    lax.fori_loop(5, 9, row_unit, 0)
    rims[0] = spread[0:128, :].astype(BF)
    rims[1] = spread[640:768, :].astype(BF)
    rim_copies = []
    for j, step in ((0, 127), (1, 1)):
        copy = remote(rims.at[j], landed.at[j], rim_s.at[j], rim_r.at[j], line_neighbour(at, step))
        copy.start()
        pending.append(copy)
        rim_copies.append(copy)
    for i in CONV_CHAINS:
        close(i, 0, state[i])
        state[i] = start(i, 1)
    for i in MORE_CHAINS:
        close(i, 2, state[i])
    vector_add(3, vectors)
    o2[...] = own2[at["x"], at["y"], at["z"]].astype(F32)
    wide = own1[at["z"], :, at["x"], at["y"]].astype(F32)
    for n in range(4):
        post[n] = wide[:, 4 * n : 4 * n + 4, :].astype(BF)
    swaps = []
    for s in (1, 2, 3):
        to = moved(at, "z", s)
        swaps.append(push(post.at[to["z"]], postr.at[s], psend.at[s], precv.at[s], to))
    for copy in rim_copies:
        copy.wait_recv()
    spread[512:640, :] += landed[0].astype(F32)
    spread[128:256, :] += landed[1].astype(F32)
    ordered_grad = (first_grad[...] + spread[128:640, :]).astype(BF)
    fold_rows(take[...], ordered_grad, returning)
    deal(returning, arrived, me, deal_s, deal_r)
    for i in CONV_CHAINS:
        middle(i, 1, state[i])
    for i in CONV_CHAINS:
        close(i, 1, state[i])
        state[i] = start(i, 2)
    o1[at["z"]] = post[at["z"]].astype(F32)
    for s in (1, 2, 3):
        swaps[s - 1].wait_recv()
        o1[lax.rem(at["z"] + 4 - s, 4)] = postr[s].astype(F32)
    for i in CONV_CHAINS:
        middle(i, 2, state[i])
    for i in CONV_CHAINS:
        close(i, 2, state[i])
        name, layout, plain, cut, base, order, halves = CHAINS[i]
        oc[pl.ds(base, plain["R"]), :] = tiles[at["z"], at["x"], at["y"], at["c"], pl.ds(base, plain["R"]), :].astype(F32)
    dealt(returning, arrived, me, deal_s, deal_r).wait_recv()
    points_grad[...] = unfold_rows(send[...], arrived)
    for copy in pending:
        copy.wait_send()
    for n in range(16):
        xy_copy(n).wait_send()
    dealt(returning, arrived, me, deal_s, deal_r).wait_send()


def back_scatter(grad, first_grad, take, send, picks, w, picked, g1, g2, gv):
    shape = jax.ShapeDtypeStruct
    n = len(CHAINS)
    dma = pltpu.SemaphoreType.DMA
    own1, own2 = (4, 9, 4, 4, 16, 128), (4, 4, 4, 16, 512)
    landing = [s for i in range(n) for s in landing_shapes(i)]
    return pl.pallas_call(
        back_kernel,
        out_shape=(
            shape((512, 512), BF),
            shape((432, 128), F32),
            shape((4, 9, 4, 128), F32),
            shape((16, 512), F32),
            shape((16, 128), F32),
        ),
        in_specs=[VM, VM, VM, VM, VM, ANY, ANY, ANY, ANY, VM],
        out_specs=[VM] * 5,
        scratch_shapes=[
            pltpu.VMEM((128, 8, 512), BF),
            pltpu.VMEM((128, 8, 512), BF),
            pltpu.VMEM((4, 13824, 128), BF),
            pltpu.VMEM((4, 4, 4, 432, 128), BF),
            pltpu.VMEM((768, 512), F32),
            pltpu.VMEM((2, 3, 512, 512), BF),
            pltpu.VMEM((2, 4, 3, 512, 128), BF),
            pltpu.VMEM((2, 128, 512), BF),
            pltpu.VMEM((2, 128, 512), BF),
            pltpu.VMEM(own1, BF),
            pltpu.VMEM(own1, BF),
            pltpu.VMEM(own2, BF),
            pltpu.VMEM(own2, BF),
        ]
        + [pltpu.VMEM(s, BF) for s in landing]
        + [
            pltpu.VMEM((4, 9, 4, 128), BF),
            pltpu.VMEM((4, 9, 4, 128), BF),
            pltpu.VMEM((4, 4, 16, 128), F32),
            pltpu.VMEM((4, 4, 4, 16, 128), F32),
            dma((2,)),
            dma((2,)),
            dma((16,)),
            dma((16,)),
            dma((n, 22)),
            dma((n, 22)),
            dma((n, 4)),
            dma((4, 4)),
            dma((4, 4)),
            dma((4,)),
            dma((4,)),
            dma((2,)),
            dma((2,)),
            dma,
            dma,
        ],
        compiler_params=pltpu.CompilerParams(
            collective_id=1, has_side_effects=True, vmem_limit_bytes=62 * 2**20
        ),
        name="back_scatter",
    )(grad, first_grad, take, send, picks, w, picked, g1, g2, gv)


def per_device(
    points,
    perm,
    inverse,
    lengths,
    neighbours,
    conv_weight,
    conv_bias,
    encode_weight,
    encode_bias,
    encode_gain,
    encode_shift,
    before_gain,
    before_shift,
    triple_weight,
    query_bias,
    value_bias,
    output_weight,
    output_bias,
    second_gain,
    second_shift,
    expand_weight,
    expand_bias,
    reduce_weight,
    reduce_bias,
    grad_out,
):
    pts, rep = lax.axis_index("pts"), lax.axis_index("rep")
    lane = lax.rem(pts, 8) * 16 + rep * 4
    wide_piece = jnp.concatenate([encode_weight, triple_weight, output_weight, expand_weight], axis=1)
    wide_piece = wide_piece.reshape(4, 36, 128).transpose(1, 0, 2).reshape(4, 9, 4, 128)
    vector_piece = jnp.concatenate(
        [
            jnp.stack(
                [
                    conv_bias,
                    encode_bias,
                    encode_gain,
                    encode_shift,
                    before_gain,
                    before_shift,
                    query_bias,
                    value_bias,
                    output_bias,
                    second_gain,
                    second_shift,
                    reduce_bias,
                ]
            ),
            expand_bias.reshape(4, 4),
        ],
        axis=0,
    )
    vector_tile = lax.dynamic_update_slice(jnp.zeros((16, 128), BF), vector_piece, (0, lane))
    kernel, wide, tall, picked, conv, ordered, vectors, wide_bias, take, send, picks = front(
        conv_weight,
        wide_piece,
        reduce_weight,
        vector_tile,
        points,
        inverse.reshape(1, 512),
        perm.reshape(1, 512),
        neighbours.reshape(9, 3, 512),
    )
    result, grad_first, grad_conv, grad_wide, grad_tall, vector_grads = block(
        lengths,
        conv,
        ordered,
        grad_out,
        wide.reshape(36, 512, 128),
        tall.reshape(2048, 512),
        vectors,
        wide_bias,
    )
    natural = vector_grads[12:].reshape(128, 4, 4).transpose(1, 0, 2).reshape(4, 512)
    vector_grads = jnp.concatenate([vector_grads[:12], natural], axis=0)
    points_grad, kernel_out, wide_out, tall_out, vector_out = back_scatter(
        grad_conv,
        grad_first,
        take,
        send,
        picks,
        kernel.reshape(4, 27, 512, 128),
        picked,
        grad_wide.reshape(4, 9, 4, 4, 2, 16, 128),
        grad_tall.reshape(4, 4, 2, 4, 16, 512),
        vector_grads.reshape(16, 4, 128).transpose(1, 0, 2),
    )
    wide_out = wide_out.reshape(36, 4, 128).transpose(1, 0, 2).reshape(4, 4608)
    vector_out = lax.dynamic_slice(vector_out, (0, lane), (16, 4))
    reduced = (
        vector_out[V_CONV],
        wide_out[:, :512],
        vector_out[V_ENC],
        vector_out[V_GAIN0],
        vector_out[V_SHIFT0],
        vector_out[V_GAIN1],
        vector_out[V_SHIFT1],
        wide_out[:, 512:2048],
        vector_out[V_QUERY],
        vector_out[V_VALUE],
        wide_out[:, 2048:2560],
        vector_out[V_OUT],
        vector_out[V_GAIN2],
        vector_out[V_SHIFT2],
        wide_out[:, 2560:],
        vector_out[12:].reshape(16),
        tall_out,
        vector_out[V_RED],
    )
    return (result, points_grad, kernel_out) + reduced


def solution(mesh):
    in_specs = (
        P(("pts", "rep"), None),
        P(("pts", "rep")),
        P(("pts", "rep")),
        P(("pts", "rep")),
        P(None, ("pts", "rep")),
        P("pts", "rep"),
        P(("pts", "rep")),
        P(("pts", "rep"), None),
        P(("pts", "rep")),
        P(("pts", "rep")),
        P(("pts", "rep")),
        P(("pts", "rep")),
        P(("pts", "rep")),
        P(("pts", "rep"), None),
        P(("pts", "rep")),
        P(("pts", "rep")),
        P(("pts", "rep"), None),
        P(("pts", "rep")),
        P(("pts", "rep")),
        P(("pts", "rep")),
        P(("pts", "rep"), None),
        P(("pts", "rep")),
        P(("pts", "rep"), None),
        P(("pts", "rep")),
        P(("pts", "rep"), None),
    )
    out_specs = (
        P(("pts", "rep"), None),
        P(("pts", "rep"), None),
        P("pts", "rep"),
        P(("pts", "rep")),
        P(("pts", "rep"), None),
        P(("pts", "rep")),
        P(("pts", "rep")),
        P(("pts", "rep")),
        P(("pts", "rep")),
        P(("pts", "rep")),
        P(("pts", "rep"), None),
        P(("pts", "rep")),
        P(("pts", "rep")),
        P(("pts", "rep"), None),
        P(("pts", "rep")),
        P(("pts", "rep")),
        P(("pts", "rep")),
        P(("pts", "rep"), None),
        P(("pts", "rep")),
        P(("pts", "rep"), None),
        P(("pts", "rep")),
    )
    return jax.shard_map(
        per_device, mesh=mesh, in_specs=in_specs, out_specs=out_specs, check_vma=False
    )
```

```python
import jax
import jax.numpy as jnp
from jax import lax
from jax.experimental import pallas as pl
from jax.experimental.pallas import tpu as pltpu
from jax.sharding import PartitionSpec as P

MESH = pl.DeviceIdType.MESH
BF = jnp.bfloat16
F32 = jnp.float32


def place():
    p = lax.axis_index("pts")
    return {
        "x": lax.div(p, 8),
        "y": lax.rem(lax.div(p, 2), 4),
        "c": lax.rem(p, 2),
        "z": lax.axis_index("rep"),
    }


def device_at(at):
    return ((at["x"] * 4 + at["y"]) * 2 + at["c"], at["z"])


def moved(at, axis, step):
    size = 2 if axis == "c" else 4
    return {**at, axis: lax.rem(at[axis] + step, size)}


def whole(value):
    return slice(None) if value is None else value


def conv_view(ref, sel, h):
    r0, r1 = h
    return ref.at[
        whole(sel.get("z")), whole(sel.get("x")), whole(sel.get("y")), sel["c"], pl.ds(r0, r1 - r0), :
    ]


def wide_view(ref, sel, h):
    k0, k1 = h
    return ref.at[
        whole(sel.get("z")), pl.ds(k0, k1 - k0), whole(sel.get("x")), whole(sel.get("y")), sel["c"]
    ]


def tall_view(ref, sel, h):
    l0, l1 = h
    return ref.at[
        whole(sel.get("x")), whole(sel.get("y")), sel["c"], whole(sel.get("z")), :, pl.ds(l0, l1 - l0)
    ]


def flat_view(ref, sel, h):
    return ref.at[whole(sel.get("x")), whole(sel.get("y")), sel["c"]]


STREAMS = (
    ("cz", 0, conv_view, "xyz", ((0, 32), (32, 64))),
    ("cx", 0, conv_view, "yzx", ((64, 144), (144, 224))),
    ("cy", 0, conv_view, "zxy", ((224, 336), (336, 432))),
    ("m2", 2, tall_view, "zyx", ((0, 256), (256, 512))),
    ("m1", 1, wide_view, "xyz", ((0, 5), (5, 9))),
    ("vt", 3, flat_view, "xy", ((0, 16),)),
)
SLOTS = 40


VM = pl.BlockSpec(memory_space=pltpu.VMEM)
ANY = pl.BlockSpec(memory_space=pl.ANY)
SM = pl.BlockSpec(memory_space=pltpu.SMEM)
epsilon = 1e-05


def mm(a, b):
    return lax.dot_general(a, b, (((1,), (0,)), ((), ())), preferred_element_type=F32)


def mm_nt(a, b):
    return lax.dot_general(a, b, (((1,), (1,)), ((), ())), preferred_element_type=F32)


def mm_tn(a, b):
    return lax.dot_general(a, b, (((0,), (0,)), ((), ())), preferred_element_type=F32)


def wide_block(ref, first, count=4):
    return jnp.concatenate([ref[first + k] for k in range(count)], axis=1)


def put_wide(ref, first, value, count=4):
    for k in range(count):
        ref[first + k] = value[:, 128 * k : 128 * (k + 1)].astype(BF)


V_CONV, V_ENC, V_GAIN0, V_SHIFT0, V_GAIN1, V_SHIFT1, V_QUERY, V_VALUE, V_OUT, V_GAIN2, V_SHIFT2, V_RED = range(12)


def over_rows(body, step=64, rows=512):
    def one(n, _):
        body(pl.ds(pl.multiple_of(n * step, step), step))
        return 0

    lax.fori_loop(0, rows // step, one, 0)


def normalize(v):
    mean = jnp.mean(v, axis=-1, keepdims=True)
    centred = v - mean
    spread = jnp.mean(centred * centred, axis=-1, keepdims=True)
    rstd = lax.rsqrt(spread + epsilon)
    return centred * rstd, rstd


def norm_pull(hat, rstd, gain, grad):
    up = grad * gain
    a = jnp.mean(up, axis=-1, keepdims=True)
    b = jnp.mean(up * hat, axis=-1, keepdims=True)
    return rstd * (up - a - hat * b)


def total(v):
    return jnp.sum(v, axis=0, keepdims=True)


def gelu_both(u):
    cdf = 0.5 * (1.0 + lax.erf(u * 0.7071067811865476))
    pdf = 0.3989422804014327 * jnp.exp(-0.5 * u * u)
    return u * cdf, cdf + u * pdf


def three(v):
    hi = v.astype(BF).astype(F32)
    rest = v - hi
    mid = rest.astype(BF).astype(F32)
    return hi, mid, rest - mid


def block_kernel(
    length, conv, ordered, go, w1, w2, vec, xb,
    result, first_grad, conv_grad, g1, g2, gv,
    big, hat0, rstd0, first, hat1, rstd1, normed, normed_t, q, k, v, k_t, v_t,
    mixed_t, mixed, rows_a, rows_b, kx, xa, ya, hat2, rstd2, n2, n2_t,
    second, act, dh, da, acc, acc2, dn, d_mixed, dq_t, dk, dv,
):
    row = lambda n: vec[n : n + 1, :]
    gv[...] = jnp.zeros_like(gv)

    def gain(n, value):
        gv[n : n + 1, :] += total(value)

    big[...] = mm(conv[...], wide_block(w1, 0))

    def encode(r):
        hat, rstd = normalize(big[r, :] + row(V_ENC))
        hat0[r, :] = hat
        rstd0[r, :] = rstd
        here = ordered[r, :].astype(F32) + hat * row(V_GAIN0) + row(V_SHIFT0)
        first[r, :] = here
        hat, rstd = normalize(here)
        hat1[r, :] = hat
        rstd1[r, :] = rstd
        normed[r, :] = (hat * row(V_GAIN1) + row(V_SHIFT1)).astype(BF)

    over_rows(encode)
    normed_t[...] = normed[...].T
    q[...] = (0.25 * (mm(normed[...], wide_block(w1, 4)) + row(V_QUERY)).astype(BF).astype(F32)).astype(BF)
    k[...] = mm(normed[...], wide_block(w1, 8)).astype(BF)
    v[...] = (mm(normed[...], wide_block(w1, 12)) + row(V_VALUE)).astype(BF)
    k_t[...] = k[...].T
    v_t[...] = v[...].T

    lane = lax.broadcasted_iota(jnp.int32, (1, 128), 1)
    seat = lax.broadcasted_iota(jnp.int32, (512, 128), 0)
    spot = lax.broadcasted_iota(jnp.int32, (512, 128), 1)
    hidden_key = jnp.where((spot == 96) & (seat >= length[0]), -1e30, 0.0)
    kx[...] = jnp.where(spot < 96, 1.0, hidden_key).astype(BF)
    one_lane = jnp.where(spot == 96, 1.0, 0.0).astype(BF)
    rows_a[...] = jnp.zeros_like(rows_a)
    rows_b[...] = jnp.zeros_like(rows_b)

    def head_places(h):
        group = pl.ds(pl.multiple_of(lax.div(h, 8) * 128, 128), 128)
        mine = jnp.where(lax.div(lane, 16) == lax.rem(h, 8), 1.0, 0.0).astype(BF)
        extra = jnp.where((lax.rem(lane, 32) == h) & (lane < 96) | (lane == 96), 1.0, 0.0).astype(BF)
        return group, mine, extra, pl.ds(pl.multiple_of(h * 16, 16), 16)

    def forward_head(h):
        group, mine, extra, channels = head_places(h)
        keys = jnp.concatenate([k[:, group], kx[...]], axis=1)
        asks = jnp.concatenate([q[:, group] * mine, one_lane], axis=1)
        scores = mm_nt(keys, asks)
        peak = jnp.max(scores, axis=0, keepdims=True)
        e = jnp.exp(scores - peak)
        summed = total(e)
        mixed_t[channels, :] = mm(v_t[channels, :], e.astype(BF)) / summed
        lse = peak + jnp.log(summed)
        hi, mid, lo = three(-lse)
        rows_a[pl.ds(h, 1), :] = hi
        rows_a[pl.ds(h + 32, 1), :] = mid
        rows_a[pl.ds(h + 64, 1), :] = lo

    def forward_heads(n, _):
        for j in range(2):
            forward_head(n * 2 + j)
        return 0

    lax.fori_loop(0, 16, forward_heads, 0)
    rows_a[96:97, :] = jnp.ones((1, 512), F32)
    xa[...] = rows_a[...].T.astype(BF)
    mixed[...] = mixed_t[...].T.astype(BF)

    big[...] = mm(mixed[...], wide_block(w1, 16))

    def after(r):
        here = first[r, :] + big[r, :] + row(V_OUT)
        second[r, :] = here
        hat, rstd = normalize(here)
        hat2[r, :] = hat
        rstd2[r, :] = rstd
        n2[r, :] = (hat * row(V_GAIN2) + row(V_SHIFT2)).astype(BF)
        gain(V_RED, go[r, :].astype(F32))

    over_rows(after)
    n2_t[...] = n2[...].T
    acc[...] = jnp.zeros_like(acc)
    acc2[...] = jnp.zeros_like(acc2)

    def chunk(c, _):
        up = jnp.concatenate([w1[20 + 4 * c + j] for j in range(4)], axis=1)
        span = pl.ds(pl.multiple_of(c * 512, 512), 512)
        down = w2[span, :]
        big[...] = mm(n2[...], up)
        da[...] = mm_nt(go[...], down)

        def gelu_rows(r):
            value, slope = gelu_both(big[r, :] + xb[pl.ds(c, 1), :])
            act[r, :] = value.astype(BF)
            low = (da[r, :] * slope).astype(BF)
            dh[r, :] = low
            gv[pl.ds(12 + c, 1), :] += total(low.astype(F32))

        over_rows(gelu_rows, 32)
        acc[...] += mm(act[...], down)
        acc2[...] += mm_nt(dh[...], up)
        g2[span, :] = mm_tn(act[...], go[...]).astype(BF)
        grad_up = mm(n2_t[...], dh[...])
        for j in range(4):
            g1[20 + 4 * c + j] = grad_up[:, 128 * j : 128 * (j + 1)].astype(BF)
        return 0

    lax.fori_loop(0, 4, chunk, 0)

    def before_mlp(r):
        result[r, :] = (second[r, :] + acc[r, :] + row(V_RED)).astype(BF)
        grad = acc2[r, :]
        hat = hat2[r, :]
        gain(V_GAIN2, grad * hat)
        gain(V_SHIFT2, grad)
        here = go[r, :].astype(F32) + norm_pull(hat, rstd2[r, :], row(V_GAIN2), grad)
        second[r, :] = here
        low = here.astype(BF)
        dn[r, :] = low
        gain(V_OUT, low.astype(F32))

    over_rows(before_mlp)
    put_wide(g1, 16, mm_tn(mixed[...], dn[...]))
    d_mixed[...] = mm_nt(dn[...], wide_block(w1, 16)).astype(BF)
    big[...] = d_mixed[...].astype(F32).T

    def inner(h, _):
        channels = pl.ds(pl.multiple_of(h * 16, 16), 16)
        hi, mid, lo = three(-total(big[channels, :] * mixed_t[channels, :]))
        rows_b[pl.ds(h, 1), :] = hi
        rows_b[pl.ds(h + 32, 1), :] = mid
        rows_b[pl.ds(h + 64, 1), :] = lo
        return 0

    lax.fori_loop(0, 32, inner, 0)
    ya[...] = rows_b[...].T.astype(BF)
    dk[...] = jnp.zeros_like(dk)
    dv[...] = jnp.zeros_like(dv)
    ones = jnp.where(spot < 96, 1.0, 0.0).astype(BF)

    def backward_head(h):
        group, mine, extra, channels = head_places(h)
        q_h = q[:, group] * mine
        m_h = d_mixed[:, group] * mine
        keys = jnp.concatenate([k[:, group], kx[...]], axis=1)
        p = jnp.exp(mm_nt(keys, jnp.concatenate([q_h, xa[...] * extra], axis=1)))
        values = jnp.concatenate([v[:, group], ones], axis=1)
        slope = mm_nt(values, jnp.concatenate([m_h, ya[...] * extra], axis=1))
        ds = (p * slope).astype(BF)
        dv[:, group] += mm(p.astype(BF), m_h)
        dk[:, group] += mm(ds, q_h)
        dq_t[channels, :] = mm(k_t[channels, :], ds)

    def backward_heads(n, _):
        for j in range(2):
            backward_head(n * 2 + j)
        return 0

    lax.fori_loop(0, 16, backward_heads, 0)
    q[...] = (0.25 * dq_t[...].T).astype(BF)
    k[...] = dk[...].astype(BF)
    v[...] = dv[...].astype(BF)
    gain(V_QUERY, q[...].astype(F32))
    gain(V_VALUE, v[...].astype(F32))
    put_wide(g1, 4, mm(normed_t[...], q[...]))
    put_wide(g1, 8, mm(normed_t[...], k[...]))
    put_wide(g1, 12, mm(normed_t[...], v[...]))
    acc2[...] = (
        mm_nt(q[...], wide_block(w1, 4)) + mm_nt(k[...], wide_block(w1, 8)) + mm_nt(v[...], wide_block(w1, 12))
    )

    def before_attention(r):
        grad = acc2[r, :]
        hat = hat1[r, :]
        gain(V_GAIN1, grad * hat)
        gain(V_SHIFT1, grad)
        here = second[r, :] + norm_pull(hat, rstd1[r, :], row(V_GAIN1), grad)
        first_grad[r, :] = here
        hat = hat0[r, :]
        gain(V_GAIN0, here * hat)
        gain(V_SHIFT0, here)
        low = norm_pull(hat, rstd0[r, :], row(V_GAIN0), here).astype(BF)
        dn[r, :] = low
        gain(V_ENC, low.astype(F32))

    over_rows(before_attention)
    put_wide(g1, 0, mm_tn(conv[...], dn[...]))
    conv_grad[...] = mm_nt(dn[...], wide_block(w1, 0)).astype(BF)
    gain(V_CONV, conv_grad[...].astype(F32))


def block(length, conv, ordered, go, w1, w2, vec, xb):
    shape = jax.ShapeDtypeStruct
    full = (512, 512)
    f, b, col = pltpu.VMEM(full, F32), pltpu.VMEM(full, BF), pltpu.VMEM((512, 1), F32)
    rows, lanes = pltpu.VMEM((128, 512), F32), pltpu.VMEM((512, 128), BF)
    return pl.pallas_call(
        block_kernel,
        out_shape=(
            shape(full, BF),
            shape(full, F32),
            shape(full, BF),
            shape((36, 512, 128), BF),
            shape((2048, 512), BF),
            shape((16, 512), F32),
        ),
        in_specs=[SM] + [VM] * 7,
        out_specs=[VM] * 6,
        scratch_shapes=[
            f, f, col, f, f, col, b, b, b, b, b, b, b,
            f, b, rows, rows, lanes, lanes, lanes, f, col, b, b,
            f, b, b, f, f, f, b, b, f, f, f,
        ],
        compiler_params=pltpu.CompilerParams(vmem_limit_bytes=60 * 2**20),
        name="block",
    )(length, conv, ordered, go, w1, w2, vec, xb)


def spread_rows(picks, j, b):
    seat = lax.broadcasted_iota(jnp.int32, (512, 256), 0)
    return jnp.where(seat == picks[j : j + 1, 256 * b : 256 * (b + 1)], 1.0, 0.0).astype(BF)


def line_neighbour(at, step):
    linear = lax.rem(((at["x"] * 4 + at["y"]) * 2 + at["c"]) * 4 + at["z"] + step, 128)
    return (lax.div(linear, 4), lax.rem(linear, 4))


def meet_lines(at):
    barrier = pltpu.get_barrier_semaphore()
    for axis, steps in (("x", (1, 2, 3)), ("y", (1, 2, 3)), ("z", (1, 2, 3)), ("c", (1,))):
        for s in steps:
            pl.semaphore_signal(
                barrier, inc=1, device_id=device_at(moved(at, axis, s)), device_id_type=MESH
            )
    pl.semaphore_wait(barrier, 10)


def tell_line(at, axis, sem):
    for s in (1,) if axis == "c" else (1, 2, 3):
        pl.semaphore_signal(sem, inc=1, device_id=device_at(moved(at, axis, s)), device_id_type=MESH)


def device_after(me, s):
    linear = lax.rem(me + s, 128)
    return (lax.div(linear, 4), lax.rem(linear, 4))


def deal(rows, landing, me, send, recv):
    def one(s, _):
        pltpu.make_async_remote_copy(
            src_ref=rows.at[lax.rem(me + s, 128)],
            dst_ref=landing.at[me],
            send_sem=send,
            recv_sem=recv,
            device_id=device_after(me, s),
            device_id_type=MESH,
        ).start()
        return 0

    lax.fori_loop(1, 128, one, 0)
    landing[me] = rows[me]


def dealt(rows, landing, me, send, recv):
    return pltpu.make_async_remote_copy(
        src_ref=rows.at[pl.ds(0, 127)],
        dst_ref=landing.at[pl.ds(0, 127)],
        send_sem=send,
        recv_sem=recv,
        device_id=device_after(me, 1),
        device_id_type=MESH,
    )


def fold_rows(index, rows, out):
    for n in range(4):
        seat = lax.broadcasted_iota(jnp.int32, (256, 512), 0) + 256 * n
        hot = jnp.where(seat == index, 1.0, 0.0).astype(BF)
        out[32 * n : 32 * (n + 1)] = mm(hot, rows).reshape(32, 8, 512).astype(BF)


def unfold_rows(index, blocks):
    seat = lax.broadcasted_iota(jnp.int32, (1024, 512), 0)
    hot = jnp.where(seat == index, 1.0, 0.0).astype(BF)
    return mm_tn(hot, blocks[...].astype(F32).reshape(1024, 512).astype(BF)).astype(BF)


def column_of(row):
    return jnp.broadcast_to(row, (128, 512)).T[:, 0:1]


def front_kernel(
    conv, m1p, m2, vt, points, inverse, perm, neighbours,
    gc, g1, g2, picked, conv_low, ordered, vectors, natural, take, send, picks,
    outgoing, incoming,
    extended, all_picks, acc, w_buf, pick_cols, pre, m1b, prev, vb, gv,
    sends, recvs, locs, presend, prerecv, halo_s, halo_r, p_sem, w_sem, deal_s, deal_r, met,
):
    at = place()
    width = 512
    me = ((at["x"] * 4 + at["y"]) * 2 + at["c"]) * 4 + at["z"]
    meet_lines(at)
    tell_line(at, "x", met.at[0])
    outs = (gc, g1, g2, gv)
    other = moved(at, "c", 1)
    pending = []
    crossing = {i: [] for i in range(len(STREAMS))}

    def remote(src, dst, send, recv, device):
        copy = pltpu.make_async_remote_copy(
            src_ref=src, dst_ref=dst, send_sem=send, recv_sem=recv,
            device_id=device, device_id_type=MESH,
        )
        copy.start()
        pending.append(copy)
        return copy

    def push(src, dst, i, k, to):
        return remote(src, dst, sends.at[i, k], recvs.at[i, k], device_at(to))

    def cross(ref, i, k):
        crossing[i].append(push(ref, ref, i, k, other))

    def own_view(i, h):
        name, op, view, order, halves = STREAMS[i]
        if op == 0:
            return conv.at[pl.ds(h[0], h[1] - h[0]), :]
        if op == 1:
            return m1b.at[pl.ds(h[0], h[1] - h[0])]
        if op == 2:
            return m2.at[:, pl.ds(h[0], h[1] - h[0])]
        return vb

    local_copies = {}

    def keep_own(i):
        name, op, view, order, halves = STREAMS[i]
        for j, h in enumerate(halves):
            copy = pltpu.make_async_copy(own_view(i, h), view(outs[op], at, h), locs.at[i, j])
            copy.start()
            local_copies[(i, j)] = copy

    state = {}

    def block_sel(order, phase, index=None):
        sel = {"c": at["c"]}
        for a in "xyz":
            if a in order and order.index(a) < phase:
                continue
            sel[a] = at[a]
        if index is not None:
            sel[order[phase]] = index
        return sel

    def begin(i, phase):
        name, op, view, order, halves = STREAMS[i]
        axis = order[phase]
        n = len(halves)
        sel = block_sel(order, phase)
        copies = {}
        if phase == 0:
            span = (halves[0][0], halves[-1][1])
            for d in (1, 3, 2):
                copies[d] = push(own_view(i, span), view(outs[op], sel, span), i, d, moved(at, axis, d))
        else:
            for d, hs in ((1, range(n)), (3, reversed(range(n)))):
                for h in hs:
                    ref = view(outs[op], sel, halves[h])
                    copies[(d, h)] = push(ref, ref, i, phase * 6 + (0 if d == 1 else 2) + h, moved(at, axis, d))
        state[(i, phase)] = copies
        if phase == len(order) - 1:
            for h in range(n):
                cross(view(outs[op], sel, halves[h]), i, 20 + h)

    def relay(i, phase):
        name, op, view, order, halves = STREAMS[i]
        axis = order[phase]
        last = phase == len(order) - 1
        n = len(halves)
        copies = state[(i, phase)]
        for d in (1, 3) if n == 2 else (1,):
            h = 0 if d == 1 else n - 1
            copies[(d, h)].wait_recv()
            ref = view(outs[op], block_sel(order, phase, lax.rem(at[axis] + 4 - d, 4)), halves[h])
            copies[(d, "f")] = push(ref, ref, i, phase * 6 + (4 if d == 1 else 5), moved(at, axis, d))
            if last:
                cross(ref, i, 22 + d)

    def finish(i, phase):
        name, op, view, order, halves = STREAMS[i]
        axis = order[phase]
        last = phase == len(order) - 1
        n = len(halves)
        copies = state[(i, phase)]
        if phase == 0:
            for d in (1, 3, 2):
                copies[d].wait_recv()
            for h in range(n):
                local_copies[(i, h)].wait()
            return
        for d in (1, 3):
            for h in range(n):
                if h == (0 if d == 1 else n - 1) and not (n == 1 and d == 3):
                    continue
                copies[(d, h)].wait_recv()
                if last:
                    sel = block_sel(order, phase, lax.rem(at[axis] + 4 - d, 4))
                    cross(view(outs[op], sel, halves[h]), i, 26 + d)
        for d in (1, 3):
            if (d, "f") not in copies:
                continue
            copies[(d, "f")].wait_recv()
            if last:
                h = 0 if d == 1 else n - 1
                sel = block_sel(order, phase, lax.rem(at[axis] + 2, 4))
                cross(view(outs[op], sel, halves[h]), i, 30 + d)

    pre_copies = []
    for step in (1, 2, 3):
        to = moved(at, "z", step)
        for j, (src, dst) in enumerate(((m1p.at[to["z"]], pre.at[step]), (vt, prev.at[step]))):
            pre_copies.append(remote(src, dst, presend.at[j, step], prerecv.at[j, step], device_at(to)))
    first, more = (0, 1, 2), (3, 4, 5)
    for i in (0, 1, 2, 3):
        begin(i, 0)
        keep_own(i)
    home = lax.div(inverse[...], width)
    row_id = lax.broadcasted_iota(jnp.int32, (width, width), 0)
    lane_id = lax.broadcasted_iota(jnp.int32, (width, width), 1)
    ahead = jnp.where((column_of(home.astype(F32)) == home.astype(F32)) & (row_id < lane_id), 1.0, 0.0)
    send[...] = home * 8 + total(ahead).astype(jnp.int32)
    pl.semaphore_wait(met.at[0], 3)
    tell_line(at, "y", met.at[1])
    fold_rows(send[...], points[...], outgoing)
    pl.semaphore_wait(met.at[1], 3)
    tell_line(at, "c", met.at[2])
    for copy in pre_copies:
        copy.wait_recv()
    pre[0] = m1p[at["z"]]

    def tile(k, _):
        pieces = [pre[lax.rem(at["z"] - s + 4, 4), k].astype(F32) for s in range(4)]
        m1b[k] = jnp.concatenate(pieces, axis=0).astype(BF)
        return 0

    lax.fori_loop(0, 9, tile, 0)
    vb[...] = (
        vt[...].astype(F32) + prev[1].astype(F32) + prev[2].astype(F32) + prev[3].astype(F32)
    ).astype(BF)
    for i in (4, 5):
        begin(i, 0)
        keep_own(i)
    pl.semaphore_wait(met.at[2], 1)
    deal(outgoing, incoming, me, deal_s, deal_r)
    for i in first + more:
        finish(i, 0)
        begin(i, 1)
    source = lax.div(perm[...], width)
    column = column_of(perm[...].astype(F32))
    source_column = lax.div(column.astype(jnp.int32), width)
    ahead = jnp.where((source_column == source) & (column < perm[...].astype(F32)), 1.0, 0.0)
    take[...] = source * 8 + total(ahead).astype(jnp.int32)
    token = lax.broadcasted_iota(jnp.int32, (1, width), 1)
    shift = me * width - 128 + lax.div(token, 256) * 256

    def pick_rows(u, _):
        local = jnp.where(neighbours[u] >= 0, neighbours[u] - shift, -1)
        picks[u] = local
        pick_cols[u] = jnp.concatenate([local, local, local[0:2]], axis=0).astype(F32)
        return 0

    lax.fori_loop(0, 9, pick_rows, 0)
    for i in first + more:
        relay(i, 1)
    for i in first:
        finish(i, 1)
        begin(i, 2)
    acc[...] = jnp.zeros_like(acc)
    for i in more:
        finish(i, 1)
    dealt(outgoing, incoming, me, deal_s, deal_r).wait_recv()
    mine = unfold_rows(take[...], incoming)
    ordered[...] = mine
    extended[128:640, :] = mine
    halos = []
    for j, (src, dst, step) in enumerate(((128, 640, 127), (512, 0, 1))):
        halos.append(
            remote(
                extended.at[pl.ds(src, 128), :], extended.at[pl.ds(dst, 128), :],
                halo_s.at[j], halo_r.at[j], line_neighbour(at, step),
            )
        )

    def p_copy(u):
        return pltpu.make_async_copy(all_picks.at[pl.ds(u * 3, 3)], picked.at[pl.ds(u * 3, 3)], p_sem.at[u])

    def pick_unit(u, _):
        columns = pick_cols[u].T
        for j in range(3):
            for b in range(2):
                seat = lax.broadcasted_iota(jnp.int32, (256, 512), 1).astype(F32)
                hot = jnp.where(seat == columns[256 * b : 256 * (b + 1), j : j + 1], 1.0, 0.0).astype(BF)
                window = extended[256 * b : 256 * b + 512, :]
                all_picks[u * 3 + j, 256 * b : 256 * (b + 1), :] = mm(hot, window).astype(BF)
        p_copy(u).start()
        return 0

    def w_copy(u):
        slot = lax.rem(u, 2)
        return pltpu.make_async_copy(
            gc.reshape((4, 27, 512, 128)).at[:, pl.ds(u * 3, 3)], w_buf.at[slot], w_sem.at[slot]
        )

    def conv_unit(u, _):
        @pl.when(u < 8)
        def _():
            w_copy(u + 1).start()

        w_copy(u).wait()
        slot = lax.rem(u, 2)
        parts = [
            mm(all_picks[u * 3 + j], jnp.concatenate([w_buf[slot, n, j] for n in range(4)], axis=1))
            for j in range(3)
        ]
        acc[...] += parts[0] + parts[1] + parts[2]
        return 0

    for i in first:
        relay(i, 2)
    for i in (3, 4):
        begin(i, 2)
    for copy in halos:
        copy.wait_recv()
    lax.fori_loop(0, 5, pick_unit, 0)
    for i in (3, 4):
        relay(i, 2)
    lax.fori_loop(5, 9, pick_unit, 0)
    for i in first:
        finish(i, 2)
    for i in first:
        for copy in crossing[i]:
            copy.wait_recv()
    w_copy(0).start()
    lax.fori_loop(0, 6, conv_unit, 0)
    for i in (3, 4):
        finish(i, 2)
    lax.fori_loop(6, 9, conv_unit, 0)
    for i in more:
        for copy in crossing[i]:
            copy.wait_recv()
    chunks = []
    for x in range(4):
        chunk = jnp.zeros((16, 128), F32)
        for y in range(4):
            for c in range(2):
                chunk = chunk + gv[x, y, c].astype(F32)
        chunks.append(chunk)
    together = jnp.concatenate(chunks, axis=1)
    vectors[...] = together
    lane = lax.broadcasted_iota(jnp.int32, (128, width), 1)
    from_lane = lax.broadcasted_iota(jnp.int32, (128, width), 0)
    shuffle = jnp.where(from_lane == lax.div(lane, 16) * 4 + lax.rem(lane, 4), 1.0, 0.0).astype(BF)
    which = lax.div(lax.rem(lax.broadcasted_iota(jnp.int32, (4, width), 1), 16), 4)
    group = lax.broadcasted_iota(jnp.int32, (4, width), 0)
    for x in range(4):
        spreaded = mm(chunks[x].astype(BF), shuffle)[12:16, :]
        natural[x : x + 1, :] = total(jnp.where(which == group, spreaded, 0.0))
    conv_low[...] = (acc[...] + together[0:1, :]).astype(BF)
    for copy in pending:
        copy.wait_send()
    dealt(outgoing, incoming, me, deal_s, deal_r).wait_send()

    def stored(u, _):
        p_copy(u).wait()
        return 0

    lax.fori_loop(0, 9, stored, 0)


def front(conv, m1p, m2, vt, points, inverse, perm, neighbours):
    shape = jax.ShapeDtypeStruct
    n = len(STREAMS)
    dma = pltpu.SemaphoreType.DMA
    return pl.pallas_call(
        front_kernel,
        out_shape=(
            shape((4, 4, 4, 2, 432, 128), BF),
            shape((4, 9, 4, 4, 2, 16, 128), BF),
            shape((4, 4, 2, 4, 16, 512), BF),
            shape((27, 512, 512), BF),
            shape((512, 512), BF),
            shape((512, 512), BF),
            shape((16, 512), F32),
            shape((4, 512), F32),
            shape((1, 512), jnp.int32),
            shape((1, 512), jnp.int32),
            shape((9, 3, 512), jnp.int32),
        ),
        in_specs=[ANY, VM, ANY] + [VM] * 5,
        out_specs=[ANY] * 4 + [VM] * 7,
        scratch_shapes=[
            pltpu.VMEM((128, 8, 512), BF),
            pltpu.VMEM((128, 8, 512), BF),
            pltpu.VMEM((768, 512), BF),
            pltpu.VMEM((27, 512, 512), BF),
            pltpu.VMEM((512, 512), F32),
            pltpu.VMEM((2, 4, 3, 512, 128), BF),
            pltpu.VMEM((9, 8, 512), F32),
            pltpu.VMEM((4, 9, 4, 128), BF),
            pltpu.VMEM((9, 16, 128), BF),
            pltpu.VMEM((4, 16, 128), BF),
            pltpu.VMEM((16, 128), BF),
            pltpu.VMEM((4, 4, 2, 16, 128), BF),
            dma((n, SLOTS)),
            dma((n, SLOTS)),
            dma((n, 2)),
            dma((2, 4)),
            dma((2, 4)),
            dma((2,)),
            dma((2,)),
            dma((9,)),
            dma((2,)),
            dma,
            dma,
            pltpu.SemaphoreType.REGULAR((3,)),
        ],
        compiler_params=pltpu.CompilerParams(
            collective_id=0, has_side_effects=True, vmem_limit_bytes=48 * 2**20
        ),
        name="front",
    )(conv, m1p, m2, vt, points, inverse, perm, neighbours)


CHAINS = (
    ("cz", "zxycRL", {"R": 112, "L": 128}, "R", 0, "zyx", ((0, 64), (64, 112))),
    ("cx", "zxycRL", {"R": 160, "L": 128}, "R", 112, "xzy", ((0, 80), (80, 160))),
    ("cy", "zxycRL", {"R": 160, "L": 128}, "R", 272, "yxz", ((0, 80), (80, 160))),
    ("m2", "xyczSL", {"S": 16, "L": 512}, "L", 0, "xyz", ((0, 256), (256, 512))),
    ("m1", "zKxycSL", {"K": 9, "S": 16, "L": 128}, "K", 0, "zyx", ((0, 5), (5, 9))),
)
CONV_CHAINS, MORE_CHAINS = (0, 1, 2), (4, 3)


def cut_view(ref, layout, sel, cut=None, span=None, base=0):
    index = []
    for dim in layout:
        if dim in sel:
            index.append(sel[dim])
        elif dim == cut and span is not None:
            index.append(pl.ds(base + span[0], span[1] - span[0]))
        else:
            index.append(slice(None))
    return ref.at[tuple(index)]


def sizes_of(layout, plain):
    return tuple(plain[d] if d in plain else 4 for d in layout)


def landing_shapes(i):
    name, layout, plain, cut, base, order, halves = CHAINS[i]
    left = layout.replace("c", "")
    shapes = []
    for axis in order:
        left = left.replace(axis, "")
        for span in halves:
            shapes.append(sizes_of(left, {**plain, cut: span[1] - span[0]}))
        shapes += [sizes_of(left, plain)] * 2
    return shapes


STEPS = (2, 1, 3, 0)


def back_kernel(
    grad, first_grad, take, send, picks, w, picked, g1, g2, gv,
    points_grad, oc, o1, o2, ov,
    returning, arrived,
    kernel_grad, theirs, spread, p_buf, w_buf, rims, landed, own1, sib1, own2, sib2, *rest,
):
    count = 12 * len(CHAINS)
    landing, rest = rest[:count], rest[count:]
    post, postr, vx, vr, p_sem, w_sem, xy_send, xy_recv, sends, recvs, locs, vsend, vrecv, psend, precv, rim_s, rim_r, deal_s, deal_r, met = rest
    at = place()
    me = ((at["x"] * 4 + at["y"]) * 2 + at["c"]) * 4 + at["z"]
    meet_lines(at)
    tell_line(at, "x", met.at[0])
    other = moved(at, "c", 1)
    pending = []
    tiles = kernel_grad.reshape((4, 4, 4, 2, 432, 128))

    def remote(src, dst, send, recv, device):
        return pltpu.make_async_remote_copy(
            src_ref=src, dst_ref=dst, send_sem=send, recv_sem=recv,
            device_id=device, device_id_type=MESH,
        )

    def push(src, dst, send, recv, to):
        copy = remote(src, dst, send, recv, device_at(to))
        copy.start()
        pending.append(copy)
        return copy

    stores = {
        0: (tiles, "zxycRL", {"c": at["c"]}),
        1: (tiles, "zxycRL", {"c": at["c"]}),
        2: (tiles, "zxycRL", {"c": at["c"]}),
        3: (own2, "xyzSL", {}),
        4: (own1, "zKxySL", {}),
    }

    def view(i, sel, span):
        name, layout, plain, cut, base, order, halves = CHAINS[i]
        ref, inner, fixed = stores[i]
        return cut_view(ref, inner, {**fixed, **sel}, cut, span, base)

    def add(i, sel, srcs, span):
        name, layout, plain, cut, base, order, halves = CHAINS[i]
        ref, inner, fixed = stores[i]
        free = [d for d in inner if d in "xyz" and d not in sel]
        count = 4 ** len(free)

        def one(n, _):
            here = dict(sel)
            for k, d in enumerate(reversed(free)):
                here[d] = lax.rem(lax.div(n, 4**k), 4)
            where = view(i, here, span)
            total = where[...].astype(F32)
            for src, src_layout, src_sel, src_span in srcs:
                full = {**{d: here[d] for d in free}, **src_sel}
                total = total + cut_view(src, src_layout, full, cut, src_span)[...].astype(F32)
            where[...] = total.astype(BF)
            return 0

        if count == 1:
            one(0, 0)
        else:
            lax.fori_loop(0, count, one, 0)

    def load(i, src, own, sib):
        name, layout, plain, cut, base, order, halves = CHAINS[i]
        inner, axis, span = layout.replace("c", ""), order[0], (0, plain[cut])
        copies = []
        for k, step in enumerate(STEPS):
            a = lax.rem(at[axis] + step, 4)
            far = cut_view(src, layout, {"c": other["c"], axis: a}, cut, span)
            near = cut_view(src, layout, {"c": at["c"], axis: a}, cut, span)
            crossing = push(far, cut_view(sib, inner, {axis: a}), sends.at[i, k], recvs.at[i, k], other)
            local = pltpu.make_async_copy(near, cut_view(own, inner, {axis: a}), locs.at[i, k])
            local.start()
            copies.append((crossing, local))
        return copies

    def names(i, phase):
        name, layout, plain, cut, base, order, halves = CHAINS[i]
        inner = layout.replace("c", "")
        axis = order[phase]
        done = {a: at[a] for a in order[:phase]}
        left = "".join(d for d in inner if d not in order[: phase + 1])
        buffers = landing[i * 12 + 4 * phase : i * 12 + 4 * phase + 4]
        slot = lambda k: (sends.at[i, 4 + phase * 6 + k], recvs.at[i, 4 + phase * 6 + k])
        return inner, axis, done, left, buffers, slot, cut, halves, (0, plain[cut])

    def start(i, phase, loaded=None, sib=None):
        inner, axis, done, left, (r0, r1, rp, rm), slot, cut, halves, span = names(i, phase)
        up, down = moved(at, axis, 1), moved(at, axis, 3)
        got = {}
        for k, step in enumerate(STEPS):
            a = lax.rem(at[axis] + step, 4)
            if loaded is not None:
                crossing, local = loaded[k]
                crossing.wait_recv()
                local.wait()
                add(i, {axis: a}, [(sib, inner, {axis: a}, span)], span)
            part = lambda h: view(i, {**done, axis: a}, h)
            if step == 2:
                got["r0"] = push(part(halves[0]), r0, *slot(0), up)
                got["r1"] = push(part(halves[1]), r1, *slot(1), down)
            elif step == 1:
                got["p1"] = push(part(halves[1]), cut_view(rp, left, {}, cut, halves[1]), *slot(2), up)
            elif step == 3:
                got["m0"] = push(part(halves[0]), cut_view(rm, left, {}, cut, halves[0]), *slot(3), down)
        return got

    def middle(i, phase, got):
        inner, axis, done, left, (r0, r1, rp, rm), slot, cut, halves, span = names(i, phase)
        up, down = moved(at, axis, 1), moved(at, axis, 3)
        for key, h, buf, land, to, k in (("r0", 0, r0, rp, up, 4), ("r1", 1, r1, rm, down, 5)):
            half = halves[h]
            got[key].wait_recv()
            sel = {**done, axis: to[axis]}
            add(i, sel, [(buf, left, {}, (0, half[1] - half[0]))], half)
            got[k] = push(view(i, sel, half), cut_view(land, left, {}, cut, half), *slot(k), to)

    def close(i, phase, got):
        inner, axis, done, left, (r0, r1, rp, rm), slot, cut, halves, span = names(i, phase)
        for k in ("p1", "m0", 4, 5):
            got[k].wait_recv()
        add(i, {**done, axis: at[axis]}, [(rp, left, {}, span), (rm, left, {}, span)], span)

    def vector_step(k):
        axis, steps = (("c", (1,)), ("z", (1, 2, 3)), ("y", (1, 2, 3)), ("x", (1, 2, 3)))[k]
        copies = []
        for s in steps:
            to = moved(at, axis, s)
            if axis == "x":
                src, dst = vx.at[3, to["x"]], vr.at[3, s, 0]
            else:
                src, dst = (gv if k == 0 else vx.at[k]), vr.at[k, s]
            copies.append(push(src, dst, vsend.at[k, s], vrecv.at[k, s], to))
        return copies

    def vector_add(k, copies):
        for copy in copies:
            copy.wait_recv()
        if k == 3:
            ov[...] = vx[3, at["x"]] + vr[3, 1, 0] + vr[3, 2, 0] + vr[3, 3, 0]
            return
        sum_now = gv[...] if k == 0 else vx[k]
        for s in (1,) if k == 0 else (1, 2, 3):
            sum_now = sum_now + vr[k, s]
        vx[k + 1] = sum_now

    def p_copy(u):
        slot = lax.rem(u, 2)
        return pltpu.make_async_copy(picked.at[pl.ds(u * 3, 3)], p_buf.at[slot], p_sem.at[slot])

    def w_copy(u):
        slot = lax.rem(u, 2)
        return pltpu.make_async_copy(w.at[:, pl.ds(u * 3, 3)], w_buf.at[slot], w_sem.at[slot])

    def xy_copy(n):
        x, y = lax.div(n, 4), lax.rem(n, 4)
        return remote(
            tiles.at[:, x, y, other["c"]], theirs.at[:, x, y], xy_send.at[n], xy_recv.at[n], device_at(other)
        )

    def weight_unit(u, _):
        @pl.when(u < 8)
        def _():
            p_copy(u + 1).start()

        p_copy(u).wait()
        for j in range(3):
            product = mm_tn(p_buf[lax.rem(u, 2), j], grad[...])
            span = pl.ds(pl.multiple_of(u * 1536 + j * 512, 512), 512)
            for n in range(4):
                kernel_grad[n, span, :] = product[:, 128 * n : 128 * (n + 1)].astype(BF)
        ready, ready_next = lax.div(u * 16, 9), lax.div((u + 1) * 16, 9)
        for j in range(2):
            @pl.when(ready + j < ready_next)
            def _():
                xy_copy(ready + j).start()

        return 0

    def row_unit(u, _):
        @pl.when(u < 8)
        def _():
            w_copy(u + 1).start()

        w_copy(u).wait()
        slot = lax.rem(u, 2)
        g = grad[...]
        back = [
            mm_nt(g, jnp.concatenate([w_buf[slot, n, j] for n in range(4)], axis=1)).astype(BF)
            for j in range(3)
        ]
        for b in range(2):
            hot = jnp.concatenate([spread_rows(picks.at[u], j, b) for j in range(3)], axis=1)
            terms = jnp.concatenate([back[j][256 * b : 256 * (b + 1), :] for j in range(3)], axis=0)
            spread[256 * b : 256 * b + 512, :] += mm(hot, terms)
        return 0

    p_copy(0).start()
    spread[...] = jnp.zeros_like(spread)
    vectors = vector_step(0)
    state = {}
    loaded = {4: load(4, g1, own1, sib1), 3: load(3, g2, own2, sib2)}
    w_copy(0).start()
    lax.fori_loop(0, 3, weight_unit, 0)
    pl.semaphore_wait(met.at[0], 3)
    tell_line(at, "y", met.at[1])
    for i in MORE_CHAINS:
        state[i] = start(i, 0, loaded[i], {4: sib1, 3: sib2}[i])
    vector_add(0, vectors)
    vectors = vector_step(1)
    lax.fori_loop(3, 6, weight_unit, 0)
    pl.semaphore_wait(met.at[1], 3)
    tell_line(at, "c", met.at[2])
    for i in MORE_CHAINS:
        middle(i, 0, state[i])
    lax.fori_loop(6, 9, weight_unit, 0)
    pl.semaphore_wait(met.at[2], 1)
    vector_add(1, vectors)
    vectors = vector_step(2)
    for i in MORE_CHAINS:
        close(i, 0, state[i])
        state[i] = start(i, 1)
    for n in range(16):
        xy_copy(n).wait_recv()

    def join(n, _):
        z, x, y = lax.div(n, 16), lax.rem(lax.div(n, 4), 4), lax.rem(n, 4)
        where = tiles.at[z, x, y, at["c"]]
        where[...] = (where[...].astype(F32) + theirs[z, x, y].astype(F32)).astype(BF)
        return 0

    lax.fori_loop(0, 64, join, 0)
    for i in CONV_CHAINS:
        state[i] = start(i, 0)
    for i in MORE_CHAINS:
        middle(i, 1, state[i])
    lax.fori_loop(0, 3, row_unit, 0)
    vector_add(2, vectors)
    vectors = vector_step(3)
    for i in MORE_CHAINS:
        close(i, 1, state[i])
        state[i] = start(i, 2)
    lax.fori_loop(3, 5, row_unit, 0)
    for i in CONV_CHAINS:
        middle(i, 0, state[i])
    for i in MORE_CHAINS:
        middle(i, 2, state[i])
    lax.fori_loop(5, 9, row_unit, 0)
    rims[0] = spread[0:128, :].astype(BF)
    rims[1] = spread[640:768, :].astype(BF)
    rim_copies = []
    for j, step in ((0, 127), (1, 1)):
        copy = remote(rims.at[j], landed.at[j], rim_s.at[j], rim_r.at[j], line_neighbour(at, step))
        copy.start()
        pending.append(copy)
        rim_copies.append(copy)
    for i in CONV_CHAINS:
        close(i, 0, state[i])
        state[i] = start(i, 1)
    for i in MORE_CHAINS:
        close(i, 2, state[i])
    vector_add(3, vectors)
    o2[...] = own2[at["x"], at["y"], at["z"]].astype(F32)
    wide = own1[at["z"], :, at["x"], at["y"]].astype(F32)
    for n in range(4):
        post[n] = wide[:, 4 * n : 4 * n + 4, :].astype(BF)
    swaps = []
    for s in (1, 2, 3):
        to = moved(at, "z", s)
        swaps.append(push(post.at[to["z"]], postr.at[s], psend.at[s], precv.at[s], to))
    for copy in rim_copies:
        copy.wait_recv()
    spread[512:640, :] += landed[0].astype(F32)
    spread[128:256, :] += landed[1].astype(F32)
    ordered_grad = (first_grad[...] + spread[128:640, :]).astype(BF)
    fold_rows(take[...], ordered_grad, returning)
    deal(returning, arrived, me, deal_s, deal_r)
    for i in CONV_CHAINS:
        middle(i, 1, state[i])
    for i in CONV_CHAINS:
        close(i, 1, state[i])
        state[i] = start(i, 2)
    o1[at["z"]] = post[at["z"]].astype(F32)
    for s in (1, 2, 3):
        swaps[s - 1].wait_recv()
        o1[lax.rem(at["z"] + 4 - s, 4)] = postr[s].astype(F32)
    for i in CONV_CHAINS:
        middle(i, 2, state[i])
    for i in CONV_CHAINS:
        close(i, 2, state[i])
        name, layout, plain, cut, base, order, halves = CHAINS[i]
        oc[pl.ds(base, plain["R"]), :] = tiles[at["z"], at["x"], at["y"], at["c"], pl.ds(base, plain["R"]), :].astype(F32)
    dealt(returning, arrived, me, deal_s, deal_r).wait_recv()
    points_grad[...] = unfold_rows(send[...], arrived)
    for copy in pending:
        copy.wait_send()
    for n in range(16):
        xy_copy(n).wait_send()
    dealt(returning, arrived, me, deal_s, deal_r).wait_send()


def back_scatter(grad, first_grad, take, send, picks, w, picked, g1, g2, gv):
    shape = jax.ShapeDtypeStruct
    n = len(CHAINS)
    dma = pltpu.SemaphoreType.DMA
    own1, own2 = (4, 9, 4, 4, 16, 128), (4, 4, 4, 16, 512)
    landing = [s for i in range(n) for s in landing_shapes(i)]
    return pl.pallas_call(
        back_kernel,
        out_shape=(
            shape((512, 512), BF),
            shape((432, 128), F32),
            shape((4, 9, 4, 128), F32),
            shape((16, 512), F32),
            shape((16, 128), F32),
        ),
        in_specs=[VM, VM, VM, VM, VM, ANY, ANY, ANY, ANY, VM],
        out_specs=[VM] * 5,
        scratch_shapes=[
            pltpu.VMEM((128, 8, 512), BF),
            pltpu.VMEM((128, 8, 512), BF),
            pltpu.VMEM((4, 13824, 128), BF),
            pltpu.VMEM((4, 4, 4, 432, 128), BF),
            pltpu.VMEM((768, 512), F32),
            pltpu.VMEM((2, 3, 512, 512), BF),
            pltpu.VMEM((2, 4, 3, 512, 128), BF),
            pltpu.VMEM((2, 128, 512), BF),
            pltpu.VMEM((2, 128, 512), BF),
            pltpu.VMEM(own1, BF),
            pltpu.VMEM(own1, BF),
            pltpu.VMEM(own2, BF),
            pltpu.VMEM(own2, BF),
        ]
        + [pltpu.VMEM(s, BF) for s in landing]
        + [
            pltpu.VMEM((4, 9, 4, 128), BF),
            pltpu.VMEM((4, 9, 4, 128), BF),
            pltpu.VMEM((4, 4, 16, 128), F32),
            pltpu.VMEM((4, 4, 4, 16, 128), F32),
            dma((2,)),
            dma((2,)),
            dma((16,)),
            dma((16,)),
            dma((n, 22)),
            dma((n, 22)),
            dma((n, 4)),
            dma((4, 4)),
            dma((4, 4)),
            dma((4,)),
            dma((4,)),
            dma((2,)),
            dma((2,)),
            dma,
            dma,
            pltpu.SemaphoreType.REGULAR((3,)),
        ],
        compiler_params=pltpu.CompilerParams(
            collective_id=1, has_side_effects=True, vmem_limit_bytes=62 * 2**20
        ),
        name="back_scatter",
    )(grad, first_grad, take, send, picks, w, picked, g1, g2, gv)


def per_device(
    points,
    perm,
    inverse,
    lengths,
    neighbours,
    conv_weight,
    conv_bias,
    encode_weight,
    encode_bias,
    encode_gain,
    encode_shift,
    before_gain,
    before_shift,
    triple_weight,
    query_bias,
    value_bias,
    output_weight,
    output_bias,
    second_gain,
    second_shift,
    expand_weight,
    expand_bias,
    reduce_weight,
    reduce_bias,
    grad_out,
):
    pts, rep = lax.axis_index("pts"), lax.axis_index("rep")
    lane = lax.rem(pts, 8) * 16 + rep * 4
    wide_piece = jnp.concatenate([encode_weight, triple_weight, output_weight, expand_weight], axis=1)
    wide_piece = wide_piece.reshape(4, 36, 128).transpose(1, 0, 2).reshape(4, 9, 4, 128)
    vector_piece = jnp.concatenate(
        [
            jnp.stack(
                [
                    conv_bias,
                    encode_bias,
                    encode_gain,
                    encode_shift,
                    before_gain,
                    before_shift,
                    query_bias,
                    value_bias,
                    output_bias,
                    second_gain,
                    second_shift,
                    reduce_bias,
                ]
            ),
            expand_bias.reshape(4, 4),
        ],
        axis=0,
    )
    vector_tile = lax.dynamic_update_slice(jnp.zeros((16, 128), BF), vector_piece, (0, lane))
    kernel, wide, tall, picked, conv, ordered, vectors, wide_bias, take, send, picks = front(
        conv_weight,
        wide_piece,
        reduce_weight,
        vector_tile,
        points,
        inverse.reshape(1, 512),
        perm.reshape(1, 512),
        neighbours.reshape(9, 3, 512),
    )
    result, grad_first, grad_conv, grad_wide, grad_tall, vector_grads = block(
        lengths,
        conv,
        ordered,
        grad_out,
        wide.reshape(36, 512, 128),
        tall.reshape(2048, 512),
        vectors,
        wide_bias,
    )
    natural = vector_grads[12:].reshape(128, 4, 4).transpose(1, 0, 2).reshape(4, 512)
    vector_grads = jnp.concatenate([vector_grads[:12], natural], axis=0)
    points_grad, kernel_out, wide_out, tall_out, vector_out = back_scatter(
        grad_conv,
        grad_first,
        take,
        send,
        picks,
        kernel.reshape(4, 27, 512, 128),
        picked,
        grad_wide.reshape(4, 9, 4, 4, 2, 16, 128),
        grad_tall.reshape(4, 4, 2, 4, 16, 512),
        vector_grads.reshape(16, 4, 128).transpose(1, 0, 2),
    )
    wide_out = wide_out.reshape(36, 4, 128).transpose(1, 0, 2).reshape(4, 4608)
    vector_out = lax.dynamic_slice(vector_out, (0, lane), (16, 4))
    reduced = (
        vector_out[V_CONV],
        wide_out[:, :512],
        vector_out[V_ENC],
        vector_out[V_GAIN0],
        vector_out[V_SHIFT0],
        vector_out[V_GAIN1],
        vector_out[V_SHIFT1],
        wide_out[:, 512:2048],
        vector_out[V_QUERY],
        vector_out[V_VALUE],
        wide_out[:, 2048:2560],
        vector_out[V_OUT],
        vector_out[V_GAIN2],
        vector_out[V_SHIFT2],
        wide_out[:, 2560:],
        vector_out[12:].reshape(16),
        tall_out,
        vector_out[V_RED],
    )
    return (result, points_grad, kernel_out) + reduced


def solution(mesh):
    in_specs = (
        P(("pts", "rep"), None),
        P(("pts", "rep")),
        P(("pts", "rep")),
        P(("pts", "rep")),
        P(None, ("pts", "rep")),
        P("pts", "rep"),
        P(("pts", "rep")),
        P(("pts", "rep"), None),
        P(("pts", "rep")),
        P(("pts", "rep")),
        P(("pts", "rep")),
        P(("pts", "rep")),
        P(("pts", "rep")),
        P(("pts", "rep"), None),
        P(("pts", "rep")),
        P(("pts", "rep")),
        P(("pts", "rep"), None),
        P(("pts", "rep")),
        P(("pts", "rep")),
        P(("pts", "rep")),
        P(("pts", "rep"), None),
        P(("pts", "rep")),
        P(("pts", "rep"), None),
        P(("pts", "rep")),
        P(("pts", "rep"), None),
    )
    out_specs = (
        P(("pts", "rep"), None),
        P(("pts", "rep"), None),
        P("pts", "rep"),
        P(("pts", "rep")),
        P(("pts", "rep"), None),
        P(("pts", "rep")),
        P(("pts", "rep")),
        P(("pts", "rep")),
        P(("pts", "rep")),
        P(("pts", "rep")),
        P(("pts", "rep"), None),
        P(("pts", "rep")),
        P(("pts", "rep")),
        P(("pts", "rep"), None),
        P(("pts", "rep")),
        P(("pts", "rep")),
        P(("pts", "rep")),
        P(("pts", "rep"), None),
        P(("pts", "rep")),
        P(("pts", "rep"), None),
        P(("pts", "rep")),
    )
    return jax.shard_map(
        per_device, mesh=mesh, in_specs=in_specs, out_specs=out_specs, check_vma=False
    )
```

```python
import jax
import jax.numpy as jnp
from jax import lax
from jax.experimental import pallas as pl
from jax.experimental.pallas import tpu as pltpu
from jax.sharding import PartitionSpec as P

MESH = pl.DeviceIdType.MESH
BF = jnp.bfloat16
F32 = jnp.float32


def place():
    p = lax.axis_index("pts")
    return {
        "x": lax.div(p, 8),
        "y": lax.rem(lax.div(p, 2), 4),
        "c": lax.rem(p, 2),
        "z": lax.axis_index("rep"),
    }


def device_at(at):
    return ((at["x"] * 4 + at["y"]) * 2 + at["c"], at["z"])


def moved(at, axis, step):
    size = 2 if axis == "c" else 4
    return {**at, axis: lax.rem(at[axis] + step, size)}


def whole(value):
    return slice(None) if value is None else value


def conv_view(ref, sel, h):
    r0, r1 = h
    return ref.at[
        whole(sel.get("z")), whole(sel.get("x")), whole(sel.get("y")), sel["c"], pl.ds(r0, r1 - r0), :
    ]


def wide_view(ref, sel, h):
    k0, k1 = h
    return ref.at[
        whole(sel.get("z")), pl.ds(k0, k1 - k0), whole(sel.get("x")), whole(sel.get("y")), sel["c"]
    ]


def tall_view(ref, sel, h):
    l0, l1 = h
    return ref.at[
        whole(sel.get("x")), whole(sel.get("y")), sel["c"], whole(sel.get("z")), :, pl.ds(l0, l1 - l0)
    ]


def flat_view(ref, sel, h):
    return ref.at[whole(sel.get("x")), whole(sel.get("y")), sel["c"]]


FRONT_STREAMS = (
    ("cz", 0, conv_view, "xyz", ((0, 48), (48, 96))),
    ("cx", 0, conv_view, "yzx", ((96, 176), (176, 256))),
    ("cy", 0, conv_view, "zxy", ((256, 352), (352, 432))),
    ("wide", 1, wide_view, "xyz", ((0, 3), (3, 5))),
    ("vectors", 2, flat_view, "xy", ((0, 16),)),
)
SLOTS = 40


def meet_lines(at):
    barrier = pltpu.get_barrier_semaphore()
    for axis, steps in (("x", (1, 2, 3)), ("y", (1, 2, 3)), ("z", (1, 2, 3)), ("c", (1,))):
        for s in steps:
            pl.semaphore_signal(
                barrier, inc=1, device_id=device_at(moved(at, axis, s)), device_id_type=MESH
            )
    pl.semaphore_wait(barrier, 10)


def tell_line(at, axis, sem):
    for s in (1,) if axis == "c" else (1, 2, 3):
        pl.semaphore_signal(sem, inc=1, device_id=device_at(moved(at, axis, s)), device_id_type=MESH)


def bring(pairs, sem, base=0):
    copies = [pltpu.make_async_copy(src, dst, sem.at[base + n]) for n, (src, dst) in enumerate(pairs)]
    for copy in copies:
        copy.start()
    return copies


def remote_copy(src, dst, send, recv, device):
    return pltpu.make_async_remote_copy(
        src_ref=src, dst_ref=dst, send_sem=send, recv_sem=recv, device_id=device, device_id_type=MESH
    )


def gather_steps(streams, own_view, outs, at, sends, recvs, locs, pending):
    other = moved(at, "c", 1)
    crossing = {i: [] for i in range(len(streams))}
    local_copies, state = {}, {}

    def push(src, dst, i, k, to):
        copy = remote_copy(src, dst, sends.at[i, k], recvs.at[i, k], device_at(to))
        copy.start()
        pending.append(copy)
        return copy

    def cross(ref, i, k):
        crossing[i].append(push(ref, ref, i, k, other))

    def keep_own(i):
        name, op, view, order, halves = streams[i]
        for j, h in enumerate(halves):
            copy = pltpu.make_async_copy(own_view(i, h), view(outs[op], at, h), locs.at[i, j])
            copy.start()
            local_copies[(i, j)] = copy

    def block_sel(order, phase, index=None):
        sel = {"c": at["c"]}
        for a in "xyz":
            if a in order and order.index(a) < phase:
                continue
            sel[a] = at[a]
        if index is not None:
            sel[order[phase]] = index
        return sel

    def begin(i, phase):
        name, op, view, order, halves = streams[i]
        axis = order[phase]
        n = len(halves)
        sel = block_sel(order, phase)
        copies = {}
        if phase == 0:
            keep_own(i)
            span = (halves[0][0], halves[-1][1])
            for d in (1, 3, 2):
                copies[d] = push(own_view(i, span), view(outs[op], sel, span), i, d, moved(at, axis, d))
        else:
            for d, hs in ((1, range(n)), (3, reversed(range(n)))):
                for h in hs:
                    ref = view(outs[op], sel, halves[h])
                    copies[(d, h)] = push(ref, ref, i, phase * 6 + (0 if d == 1 else 2) + h, moved(at, axis, d))
        state[(i, phase)] = copies
        if phase == len(order) - 1:
            for h in range(n):
                cross(view(outs[op], sel, halves[h]), i, 20 + h)

    def relay(i, phase):
        name, op, view, order, halves = streams[i]
        axis = order[phase]
        last = phase == len(order) - 1
        n = len(halves)
        copies = state[(i, phase)]
        for d in (1, 3) if n == 2 else (1,):
            h = 0 if d == 1 else n - 1
            copies[(d, h)].wait_recv()
            ref = view(outs[op], block_sel(order, phase, lax.rem(at[axis] + 4 - d, 4)), halves[h])
            copies[(d, "f")] = push(ref, ref, i, phase * 6 + (4 if d == 1 else 5), moved(at, axis, d))
            if last:
                cross(ref, i, 22 + d)

    def finish(i, phase):
        name, op, view, order, halves = streams[i]
        axis = order[phase]
        last = phase == len(order) - 1
        n = len(halves)
        copies = state[(i, phase)]
        if phase == 0:
            for d in (1, 3, 2):
                copies[d].wait_recv()
            for h in range(n):
                local_copies[(i, h)].wait()
            return
        for d in (1, 3):
            for h in range(n):
                if h == (0 if d == 1 else n - 1) and not (n == 1 and d == 3):
                    continue
                copies[(d, h)].wait_recv()
                if last:
                    sel = block_sel(order, phase, lax.rem(at[axis] + 4 - d, 4))
                    cross(view(outs[op], sel, halves[h]), i, 26 + d)
        for d in (1, 3):
            if (d, "f") not in copies:
                continue
            copies[(d, "f")].wait_recv()
            if last:
                h = 0 if d == 1 else n - 1
                sel = block_sel(order, phase, lax.rem(at[axis] + 2, 4))
                cross(view(outs[op], sel, halves[h]), i, 30 + d)

    def crossed(i):
        for copy in crossing[i]:
            copy.wait_recv()

    return begin, relay, finish, crossed


def cut_view(ref, layout, sel, cut=None, span=None, base=0):
    index = []
    for dim in layout:
        if dim in sel:
            index.append(sel[dim])
        elif dim == cut and span is not None:
            index.append(pl.ds(base + span[0], span[1] - span[0]))
        else:
            index.append(slice(None))
    return ref.at[tuple(index)]


def sizes_of(layout, plain):
    return tuple(plain[d] if d in plain else 4 for d in layout)


def landing_shapes(chain):
    name, layout, plain, cut, base, order, halves = chain
    left = layout.replace("c", "")
    shapes = []
    for axis in order:
        left = left.replace(axis, "")
        for span in halves:
            shapes.append(sizes_of(left, {**plain, cut: span[1] - span[0]}))
        shapes += [sizes_of(left, plain)] * 2
    return shapes


STEPS = (2, 1, 3, 0)


def scatter_steps(chains, stores, landing, at, sends, recvs, pending):
    other = moved(at, "c", 1)

    def push(src, dst, i, k, to):
        copy = remote_copy(src, dst, sends.at[i, k], recvs.at[i, k], device_at(to))
        copy.start()
        pending.append(copy)
        return copy

    def view(i, sel, span):
        name, layout, plain, cut, base, order, halves = chains[i]
        ref, inner, fixed = stores[i]
        return cut_view(ref, inner, {**fixed, **sel}, cut, span, base)

    def add(i, sel, srcs, span):
        name, layout, plain, cut, base, order, halves = chains[i]
        inner = layout.replace("c", "")
        free = [d for d in inner if d in "xyz" and d not in sel]
        tiles = span[1] - span[0]
        for d, size in plain.items():
            tiles = tiles if d == cut else tiles * size
        tiles = max(tiles // 2048, 1)
        while free and tiles * 4 <= 64:
            free.pop()
            tiles *= 4
        count = 4 ** len(free)

        def one(n, _):
            here = dict(sel)
            for k, d in enumerate(reversed(free)):
                here[d] = lax.rem(lax.div(n, 4**k), 4)
            where = view(i, here, span)
            terms = [
                cut_view(src, src_layout, {**{d: here[d] for d in free}, **src_sel}, cut, src_span)
                for src, src_layout, src_sel, src_span in srcs
            ]
            if len(terms) == 1:
                where[...] = where[...] + terms[0][...]
            else:
                where[...] = (
                    where[...].astype(F32) + terms[0][...].astype(F32) + terms[1][...].astype(F32)
                ).astype(BF)
            return 0

        if count == 1:
            one(0, 0)
        else:
            lax.fori_loop(0, count, one, 0)

    def lend(i, sib):
        name, layout, plain, cut, base, order, halves = chains[i]
        ref, inner, fixed = stores[i]
        axis, span = order[0], (0, plain[cut])
        copies = []
        for k, step in enumerate(STEPS):
            a = lax.rem(at[axis] + step, 4)
            far = cut_view(ref, inner, {"c": other["c"], axis: a}, cut, span, base)
            copies.append(push(far, cut_view(sib, layout.replace("c", ""), {axis: a}), i, k, other))
        return copies

    def names(i, phase):
        name, layout, plain, cut, base, order, halves = chains[i]
        inner = layout.replace("c", "")
        axis = order[phase]
        done = {a: at[a] for a in order[:phase]}
        left = "".join(d for d in inner if d not in order[: phase + 1])
        buffers = landing[i * 12 + 4 * phase : i * 12 + 4 * phase + 4]
        return inner, axis, done, left, buffers, 4 + phase * 6, cut, halves, (0, plain[cut])

    def start(i, phase, lent=None, sib=None):
        inner, axis, done, left, (r0, r1, rp, rm), slot, cut, halves, span = names(i, phase)
        up, down = moved(at, axis, 1), moved(at, axis, 3)
        got = {}
        for k, step in enumerate(STEPS):
            a = lax.rem(at[axis] + step, 4)
            if lent is not None:
                lent[k].wait_recv()
                add(i, {axis: a}, [(sib, inner, {axis: a}, span)], span)
            part = lambda h: view(i, {**done, axis: a}, h)
            if step == 2:
                got["r0"] = push(part(halves[0]), r0, i, slot, up)
                got["r1"] = push(part(halves[1]), r1, i, slot + 1, down)
            elif step == 1:
                got["p1"] = push(part(halves[1]), cut_view(rp, left, {}, cut, halves[1]), i, slot + 2, up)
            elif step == 3:
                got["m0"] = push(part(halves[0]), cut_view(rm, left, {}, cut, halves[0]), i, slot + 3, down)
        return got

    def middle(i, phase, got):
        inner, axis, done, left, (r0, r1, rp, rm), slot, cut, halves, span = names(i, phase)
        up, down = moved(at, axis, 1), moved(at, axis, 3)
        for key, h, buf, land, to, k in (("r0", 0, r0, rp, up, 4), ("r1", 1, r1, rm, down, 5)):
            half = halves[h]
            got[key].wait_recv()
            sel = {**done, axis: to[axis]}
            add(i, sel, [(buf, left, {}, (0, half[1] - half[0]))], half)
            got[k] = push(view(i, sel, half), cut_view(land, left, {}, cut, half), i, slot + k, to)

    def close(i, phase, got):
        inner, axis, done, left, (r0, r1, rp, rm), slot, cut, halves, span = names(i, phase)
        for k in ("p1", "m0", 4, 5):
            got[k].wait_recv()
        add(i, {**done, axis: at[axis]}, [(rp, left, {}, span), (rm, left, {}, span)], span)

    return lend, start, middle, close, view


def swap_rows(block, post, postr, at, send, recv, pending):
    for n in range(4):
        post[n] = block[:, 4 * n : 4 * n + 4, :].astype(BF)
    copies = []
    for s in (1, 2, 3):
        to = moved(at, "z", s)
        copy = remote_copy(post.at[to["z"]], postr.at[s], send.at[s], recv.at[s], device_at(to))
        copy.start()
        pending.append(copy)
        copies.append(copy)
    return copies


def swapped_rows(copies, post, postr, at, out):
    out[at["z"]] = post[at["z"]].astype(F32)
    for s in (1, 2, 3):
        copies[s - 1].wait_recv()
        out[lax.rem(at["z"] + 4 - s, 4)] = postr[s].astype(F32)


VM = pl.BlockSpec(memory_space=pltpu.VMEM)
ANY = pl.BlockSpec(memory_space=pl.ANY)
SM = pl.BlockSpec(memory_space=pltpu.SMEM)
epsilon = 1e-05


def mm(a, b):
    return lax.dot_general(a, b, (((1,), (0,)), ((), ())), preferred_element_type=F32)


def mm_nt(a, b):
    return lax.dot_general(a, b, (((1,), (1,)), ((), ())), preferred_element_type=F32)


def mm_tn(a, b):
    return lax.dot_general(a, b, (((0,), (0,)), ((), ())), preferred_element_type=F32)


def wide_block(ref, first, count=4):
    return jnp.concatenate([ref[first + k] for k in range(count)], axis=1)


def put_wide(ref, first, value, count=4):
    for k in range(count):
        ref[first + k] = value[:, 128 * k : 128 * (k + 1)].astype(BF)


V_CONV, V_ENC, V_GAIN0, V_SHIFT0, V_GAIN1, V_SHIFT1, V_QUERY, V_VALUE, V_OUT, V_GAIN2, V_SHIFT2, V_RED = range(12)


def over_rows(body, step=64, rows=512):
    def one(n, _):
        body(pl.ds(pl.multiple_of(n * step, step), step))
        return 0

    lax.fori_loop(0, rows // step, one, 0)


def normalize(v):
    mean = jnp.mean(v, axis=-1, keepdims=True)
    centred = v - mean
    spread = jnp.mean(centred * centred, axis=-1, keepdims=True)
    rstd = lax.rsqrt(spread + epsilon)
    return centred * rstd, rstd


def norm_pull(hat, rstd, gain, grad):
    up = grad * gain
    a = jnp.mean(up, axis=-1, keepdims=True)
    b = jnp.mean(up * hat, axis=-1, keepdims=True)
    return rstd * (up - a - hat * b)


def total(v):
    return jnp.sum(v, axis=0, keepdims=True)


def gelu_both(u):
    cdf = 0.5 * (1.0 + lax.erf(u * 0.7071067811865476))
    pdf = 0.3989422804014327 * jnp.exp(-0.5 * u * u)
    return u * cdf, cdf + u * pdf


def three(v):
    hi = v.astype(BF).astype(F32)
    rest = v - hi
    mid = rest.astype(BF).astype(F32)
    return hi, mid, rest - mid


BLOCK_STREAMS = (
    ("up", 0, wide_view, "xyz", ((0, 2), (2, 4))),
    ("down", 1, tall_view, "zyx", ((0, 256), (256, 512))),
)
BLOCK_CHAINS = (
    ("up", "zKxycSL", {"K": 4, "S": 16, "L": 128}, "K", 0, "zyx", ((0, 2), (2, 4))),
    ("down", "xyczSL", {"S": 16, "L": 512}, "L", 0, "xyz", ((0, 256), (256, 512))),
)


def block_kernel(
    length, conv_in, ordered_in, go_in, w1_in, up_own_in, down_own_in, vec_in, xb_in,
    result_out, first_grad_out, conv_grad_out, g1_out, gv_out, o1, o2,
    conv, ordered, go, w1, up_own, down_own, vec, xb, result, first_grad, conv_grad, g1, gv, gv_tiles,
    big, hat0, rstd0, first, hat1, rstd1, normed, normed_t, q, k, v, k_t, v_t,
    mixed_t, mixed, rows_a, rows_b, kx, xa, ya, hat2, rstd2, n2, n2_t,
    second, act, dh, da, acc, acc2, dn, d_mixed, dq_t, dk, dv, scores,
    up_all, down_all, g_up, g_down, sib_up, sib_down, *rest,
):
    landing = rest[:24]
    post, postr, sends, recvs, locs, back_s, back_r, swap_s, swap_r, in_sem, out_sem = rest[24:]
    at = place()
    fetched = bring(
        (
            (up_own_in, up_own), (down_own_in, down_own), (conv_in, conv), (w1_in, w1), (vec_in, vec),
            (ordered_in, ordered), (go_in, go), (xb_in, xb),
        ),
        in_sem,
    )
    meet_lines(at)
    for copy in fetched[:2]:
        copy.wait()
    pending = []
    own_view = lambda i, h: (
        up_own.at[pl.ds(h[0], h[1] - h[0])] if i == 0 else down_own.at[:, pl.ds(h[0], h[1] - h[0])]
    )
    begin, relay, finish, crossed = gather_steps(
        BLOCK_STREAMS, own_view, (up_all, down_all), at, sends, recvs, locs, pending
    )
    stores = (
        (g_up.reshape((4, 4, 4, 4, 2, 16, 128)), "zKxycSL", {"c": at["c"]}),
        (g_down.reshape((4, 4, 2, 4, 16, 512)), "xyczSL", {"c": at["c"]}),
    )
    lend, start, middle, close, view = scatter_steps(
        BLOCK_CHAINS, stores, landing, at, back_s, back_r, pending
    )
    both = (0, 1)
    up_blocks, down_rows = up_all.reshape((16, 512, 128)), down_all.reshape((2048, 512))
    for i in both:
        begin(i, 0)
    for copy in fetched[2:]:
        copy.wait()
    row = lambda n: vec[n : n + 1, :]
    gv[...] = jnp.zeros_like(gv)

    def gain(n, value):
        gv[n : n + 1, :] += total(value)

    big[...] = mm(conv[...], wide_block(w1, 0))
    for i in both:
        finish(i, 0)
        begin(i, 1)

    def encode(r):
        hat, rstd = normalize(big[r, :] + row(V_ENC))
        hat0[r, :] = hat
        rstd0[r, :] = rstd
        here = ordered[r, :].astype(F32) + hat * row(V_GAIN0) + row(V_SHIFT0)
        first[r, :] = here
        hat, rstd = normalize(here)
        hat1[r, :] = hat
        rstd1[r, :] = rstd
        normed[r, :] = (hat * row(V_GAIN1) + row(V_SHIFT1)).astype(BF)

    over_rows(encode)
    normed_t[...] = normed[...].T
    q[...] = (0.25 * (mm(normed[...], wide_block(w1, 4)) + row(V_QUERY)).astype(BF).astype(F32)).astype(BF)
    k[...] = mm(normed[...], wide_block(w1, 8)).astype(BF)
    v[...] = (mm(normed[...], wide_block(w1, 12)) + row(V_VALUE)).astype(BF)
    k_t[...] = k[...].T
    turned = v[...].T
    one_row = jnp.where(lax.broadcasted_iota(jnp.int32, (16, 512), 0) == 0, 1.0, 0.0).astype(BF)
    for h in range(32):
        v_t[h, 0:16, :] = turned[16 * h : 16 * h + 16, :]
        v_t[h, 16:32, :] = one_row
    for i in both:
        relay(i, 1)

    lane = lax.broadcasted_iota(jnp.int32, (1, 128), 1)
    seat = lax.broadcasted_iota(jnp.int32, (512, 128), 0)
    spot = lax.broadcasted_iota(jnp.int32, (512, 128), 1)
    hidden_key = jnp.where((spot == 96) & (seat >= length[0]), -1e30, 0.0)
    kx[...] = jnp.where(spot < 96, 1.0, hidden_key).astype(BF)
    one_lane = jnp.where(spot == 96, 1.0, 0.0).astype(BF)
    rows_a[...] = jnp.zeros_like(rows_a)
    rows_b[...] = jnp.zeros_like(rows_b)

    def head_places(h):
        group = pl.ds(pl.multiple_of(lax.div(h, 8) * 128, 128), 128)
        mine = jnp.where(lax.div(lane, 16) == lax.rem(h, 8), 1.0, 0.0).astype(BF)
        extra = jnp.where((lax.rem(lane, 32) == h) & (lane < 96) | (lane == 96), 1.0, 0.0).astype(BF)
        return group, mine, extra, pl.ds(pl.multiple_of(h * 16, 16), 16)

    def keys_of(group):
        return jnp.concatenate([k[:, group], kx[...]], axis=1)

    def note(h, value):
        hi, mid, lo = three(value)
        rows_a[pl.ds(h, 1), :] = hi
        rows_a[pl.ds(h + 32, 1), :] = mid
        rows_a[pl.ds(h + 64, 1), :] = lo

    def score_head(h, slot):
        group, mine, extra, channels = head_places(h)
        asks = jnp.concatenate([q[:, group] * mine, one_lane], axis=1)
        scores[slot] = mm_nt(keys_of(group), asks)

    def forward_head(h, slot):
        group, mine, extra, channels = head_places(h)
        peak = jnp.max(scores[slot], axis=0, keepdims=True)
        e = jnp.exp(scores[slot] - peak).astype(BF)
        got = mm(v_t[h], e)
        summed = got[16:17, :]
        mixed_t[channels, :] = got[0:16, :] / summed
        note(h, -(peak + jnp.log(summed)))

    def forward_pair(n, _):
        score_head(n * 2 + 1, 1)
        forward_head(n * 2, 0)
        score_head(lax.rem(n * 2 + 2, 32), 0)
        forward_head(n * 2 + 1, 1)
        return 0

    def two_heads(body):
        def pair(n, _):
            for j in range(2):
                body(n * 2 + j)
            return 0

        return pair

    rows_a[96:97, :] = jnp.ones((1, 512), F32)
    score_head(0, 0)
    lax.fori_loop(0, 4, forward_pair, 0)
    for i in both:
        finish(i, 1)
        begin(i, 2)
    lax.fori_loop(4, 10, forward_pair, 0)
    for i in both:
        relay(i, 2)
    lax.fori_loop(10, 16, forward_pair, 0)
    for i in both:
        finish(i, 2)
    xa[...] = rows_a[...].T.astype(BF)
    mixed[...] = mixed_t[...].T.astype(BF)

    big[...] = mm(mixed[...], wide_block(w1, 16))

    def after(r):
        here = first[r, :] + big[r, :] + row(V_OUT)
        second[r, :] = here
        hat, rstd = normalize(here)
        hat2[r, :] = hat
        rstd2[r, :] = rstd
        n2[r, :] = (hat * row(V_GAIN2) + row(V_SHIFT2)).astype(BF)
        gain(V_RED, go[r, :].astype(F32))

    over_rows(after)
    n2_t[...] = n2[...].T
    acc[...] = jnp.zeros_like(acc)
    acc2[...] = jnp.zeros_like(acc2)
    for i in both:
        crossed(i)

    def chunk(c, _):
        up = jnp.concatenate([up_blocks[4 * c + j] for j in range(4)], axis=1)
        span = pl.ds(pl.multiple_of(c * 512, 512), 512)
        down = down_rows[span, :]
        big[...] = mm(n2[...], up)
        da[...] = mm_nt(go[...], down)

        def gelu_rows(r):
            value, slope = gelu_both(big[r, :] + xb[pl.ds(c, 1), :])
            act[r, :] = value.astype(BF)
            low = (da[r, :] * slope).astype(BF)
            dh[r, :] = low
            gv[pl.ds(12 + c, 1), :] += total(low.astype(F32))

        over_rows(gelu_rows, 32)
        acc[...] += mm(act[...], down)
        acc2[...] += mm_nt(dh[...], up)
        g_down[span, :] = mm_tn(act[...], go[...]).astype(BF)
        grad_up = mm(n2_t[...], dh[...])
        for j in range(4):
            g_up[4 * c + j] = grad_up[:, 128 * j : 128 * (j + 1)].astype(BF)
        return 0

    lax.fori_loop(0, 4, chunk, 0)
    lent = [lend(0, sib_up), lend(1, sib_down)]

    def before_mlp(r):
        result[r, :] = (second[r, :] + acc[r, :] + row(V_RED)).astype(BF)
        grad = acc2[r, :]
        hat = hat2[r, :]
        gain(V_GAIN2, grad * hat)
        gain(V_SHIFT2, grad)
        here = go[r, :].astype(F32) + norm_pull(hat, rstd2[r, :], row(V_GAIN2), grad)
        second[r, :] = here
        low = here.astype(BF)
        dn[r, :] = low
        gain(V_OUT, low.astype(F32))

    over_rows(before_mlp)
    out_copies = bring(((result, result_out),), out_sem)
    put_wide(g1, 16, mm_tn(mixed[...], dn[...]))
    d_mixed[...] = mm_nt(dn[...], wide_block(w1, 16)).astype(BF)
    big[...] = d_mixed[...].astype(F32).T
    state = {0: start(0, 0, lent[0], sib_up), 1: start(1, 0, lent[1], sib_down)}

    def inner(h, _):
        channels = pl.ds(pl.multiple_of(h * 16, 16), 16)
        hi, mid, lo = three(-total(big[channels, :] * mixed_t[channels, :]))
        rows_b[pl.ds(h, 1), :] = hi
        rows_b[pl.ds(h + 32, 1), :] = mid
        rows_b[pl.ds(h + 64, 1), :] = lo
        return 0

    lax.fori_loop(0, 32, inner, 0)
    ya[...] = rows_b[...].T.astype(BF)
    dk[...] = jnp.zeros_like(dk)
    dv[...] = jnp.zeros_like(dv)
    ones = jnp.where(spot < 96, 1.0, 0.0).astype(BF)

    def backward_head(h):
        group, mine, extra, channels = head_places(h)
        q_h = q[:, group] * mine
        m_h = d_mixed[:, group] * mine
        p = jnp.exp(mm_nt(keys_of(group), jnp.concatenate([q_h, xa[...] * extra], axis=1)))
        values = jnp.concatenate([v[:, group], ones], axis=1)
        slope = mm_nt(values, jnp.concatenate([m_h, ya[...] * extra], axis=1))
        ds = (p * slope).astype(BF)
        dv[:, group] += mm(p.astype(BF), m_h)
        dk[:, group] += mm(ds, q_h)
        dq_t[channels, :] = mm(k_t[channels, :], ds)

    backward_heads = two_heads(backward_head)
    lax.fori_loop(0, 4, backward_heads, 0)
    for i in both:
        middle(i, 0, state[i])
    lax.fori_loop(4, 8, backward_heads, 0)
    for i in both:
        close(i, 0, state[i])
        state[i] = start(i, 1)
    lax.fori_loop(8, 11, backward_heads, 0)
    for i in both:
        middle(i, 1, state[i])
    lax.fori_loop(11, 13, backward_heads, 0)
    for i in both:
        close(i, 1, state[i])
        state[i] = start(i, 2)
    lax.fori_loop(13, 16, backward_heads, 0)
    for i in both:
        middle(i, 2, state[i])
    q[...] = (0.25 * dq_t[...].T).astype(BF)
    k[...] = dk[...].astype(BF)
    v[...] = dv[...].astype(BF)
    gain(V_QUERY, q[...].astype(F32))
    gain(V_VALUE, v[...].astype(F32))
    put_wide(g1, 4, mm(normed_t[...], q[...]))
    put_wide(g1, 8, mm(normed_t[...], k[...]))
    put_wide(g1, 12, mm(normed_t[...], v[...]))
    for i in both:
        close(i, 2, state[i])
    o2[...] = g_down.reshape((4, 4, 2, 4, 16, 512))[at["x"], at["y"], at["c"], at["z"]].astype(F32)
    rows_up = g_up.reshape((4, 4, 4, 4, 2, 16, 128))[at["z"], :, at["x"], at["y"], at["c"]].astype(F32)
    swaps = swap_rows(rows_up, post, postr, at, swap_s, swap_r, pending)
    acc2[...] = (
        mm_nt(q[...], wide_block(w1, 4)) + mm_nt(k[...], wide_block(w1, 8)) + mm_nt(v[...], wide_block(w1, 12))
    )

    def before_attention(r):
        grad = acc2[r, :]
        hat = hat1[r, :]
        gain(V_GAIN1, grad * hat)
        gain(V_SHIFT1, grad)
        here = second[r, :] + norm_pull(hat, rstd1[r, :], row(V_GAIN1), grad)
        first_grad[r, :] = here
        hat = hat0[r, :]
        gain(V_GAIN0, here * hat)
        gain(V_SHIFT0, here)
        low = norm_pull(hat, rstd0[r, :], row(V_GAIN0), here).astype(BF)
        dn[r, :] = low
        gain(V_ENC, low.astype(F32))

    over_rows(before_attention)
    put_wide(g1, 0, mm_tn(conv[...], dn[...]))
    out_copies += bring(((g1, g1_out), (first_grad, first_grad_out)), out_sem, 1)
    conv_grad[...] = mm_nt(dn[...], wide_block(w1, 0)).astype(BF)
    out_copies += bring(((conv_grad, conv_grad_out),), out_sem, 3)
    gain(V_CONV, conv_grad[...].astype(F32))
    lane_to = lax.broadcasted_iota(jnp.int32, (128, 512), 1)
    lane_from = lax.broadcasted_iota(jnp.int32, (128, 512), 0)
    shuffle = jnp.where(lane_from == lax.div(lane_to, 16) * 4 + lax.rem(lane_to, 4), 1.0, 0.0).astype(BF)
    which = lax.div(lax.rem(lax.broadcasted_iota(jnp.int32, (16, 512), 1), 16), 4)
    level = lax.broadcasted_iota(jnp.int32, (16, 512), 0) - 12
    for x in range(4):
        chosen = jnp.where(which == level, jnp.broadcast_to(gv[12 + x : 13 + x, :], (16, 512)), 0.0)
        hi, mid, lo = three(chosen)
        dealt_rows = (
            mm_nt(hi.astype(BF), shuffle) + mm_nt(mid.astype(BF), shuffle) + mm_nt(lo.astype(BF), shuffle)
        )
        gv_tiles[x, 0:12, :] = gv[0:12, 128 * x : 128 * (x + 1)]
        gv_tiles[x, 12:16, :] = dealt_rows[12:16, :]
    out_copies += bring(((gv_tiles, gv_out),), out_sem, 4)
    swapped_rows(swaps, post, postr, at, o1)
    for copy in pending:
        copy.wait_send()
    for copy in out_copies:
        copy.wait()


def block(length, conv, ordered, go, w1, up_own, down_own, vec, xb):
    shape = jax.ShapeDtypeStruct
    full = (512, 512)
    f, b, col = pltpu.VMEM(full, F32), pltpu.VMEM(full, BF), pltpu.VMEM((512, 1), F32)
    rows, lanes = pltpu.VMEM((128, 512), F32), pltpu.VMEM((512, 128), BF)
    dma = pltpu.SemaphoreType.DMA
    return pl.pallas_call(
        block_kernel,
        out_shape=(
            shape(full, BF),
            shape(full, F32),
            shape(full, BF),
            shape((20, 512, 128), BF),
            shape((4, 16, 128), F32),
            shape((4, 4, 4, 128), F32),
            shape((16, 512), F32),
        ),
        in_specs=[SM] + [ANY] * 8,
        out_specs=[ANY] * 5 + [VM] * 2,
        scratch_shapes=[
            b, b, b, pltpu.VMEM((20, 512, 128), BF), pltpu.VMEM((4, 16, 128), BF), pltpu.VMEM((16, 512), BF),
            pltpu.VMEM((16, 512), F32), pltpu.VMEM((4, 512), F32),
            b, f, b, pltpu.VMEM((20, 512, 128), BF), pltpu.VMEM((16, 512), F32), pltpu.VMEM((4, 16, 128), F32),
            f, f, col, f, f, col, b, b, b, b, b, b, pltpu.VMEM((32, 32, 512), BF),
            f, b, rows, rows, lanes, lanes, lanes, f, col, b, b,
            f, b, b, f, f, f, b, b, f, f, f, pltpu.VMEM((2, 512, 512), F32),
            pltpu.VMEM((4, 4, 4, 4, 2, 16, 128), BF),
            pltpu.VMEM((4, 4, 2, 4, 16, 512), BF),
            pltpu.VMEM((16, 512, 128), BF),
            pltpu.VMEM((2048, 512), BF),
            pltpu.VMEM((4, 4, 4, 4, 16, 128), BF),
            pltpu.VMEM((4, 4, 4, 16, 512), BF),
        ]
        + [pltpu.VMEM(s, BF) for chain in BLOCK_CHAINS for s in landing_shapes(chain)]
        + [
            pltpu.VMEM((4, 4, 4, 128), BF),
            pltpu.VMEM((4, 4, 4, 128), BF),
            dma((2, SLOTS)),
            dma((2, SLOTS)),
            dma((2, 2)),
            dma((2, 22)),
            dma((2, 22)),
            dma((4,)),
            dma((4,)),
            dma((8,)),
            dma((5,)),
        ],
        compiler_params=pltpu.CompilerParams(
            collective_id=2, has_side_effects=True, vmem_limit_bytes=62 * 2**20
        ),
        name="block",
    )(length, conv, ordered, go, w1, up_own, down_own, vec, xb)


def spread_rows(picks, j, b):
    seat = lax.broadcasted_iota(jnp.int32, (512, 256), 0)
    return jnp.where(seat == picks[j : j + 1, 256 * b : 256 * (b + 1)], 1.0, 0.0).astype(BF)


def line_neighbour(at, step):
    linear = lax.rem(((at["x"] * 4 + at["y"]) * 2 + at["c"]) * 4 + at["z"] + step, 128)
    return (lax.div(linear, 4), lax.rem(linear, 4))


def device_after(me, s):
    linear = lax.rem(me + s, 128)
    return (lax.div(linear, 4), lax.rem(linear, 4))


def deal(rows, landing, me, send, recv):
    def one(s, _):
        pltpu.make_async_remote_copy(
            src_ref=rows.at[lax.rem(me + s, 128)],
            dst_ref=landing.at[me],
            send_sem=send,
            recv_sem=recv,
            device_id=device_after(me, s),
            device_id_type=MESH,
        ).start()
        return 0

    lax.fori_loop(1, 128, one, 0)
    landing[me] = rows[me]


def dealt(rows, landing, me, send, recv):
    return pltpu.make_async_remote_copy(
        src_ref=rows.at[pl.ds(0, 127)],
        dst_ref=landing.at[pl.ds(0, 127)],
        send_sem=send,
        recv_sem=recv,
        device_id=device_after(me, 1),
        device_id_type=MESH,
    )


def fold_rows(index, rows, out):
    for n in range(4):
        seat = lax.broadcasted_iota(jnp.int32, (256, 512), 0) + 256 * n
        hot = jnp.where(seat == index, 1.0, 0.0).astype(BF)
        out[32 * n : 32 * (n + 1)] = mm(hot, rows).reshape(32, 8, 512).astype(BF)


def unfold_rows(index, blocks):
    seat = lax.broadcasted_iota(jnp.int32, (1024, 512), 0)
    hot = jnp.where(seat == index, 1.0, 0.0).astype(BF)
    return mm_tn(hot, blocks[...].astype(F32).reshape(1024, 512).astype(BF)).astype(BF)


def column_of(row):
    return jnp.broadcast_to(row, (128, 512)).T[:, 0:1]


def front_kernel(
    conv, encode_in, triple_in, output_in, expand_in, small_in, points_in, inverse_in, perm_in, neighbours_in,
    gc, g1, up_out, picked, conv_out, ordered_out, vectors_out, natural_out, take_out, send_out, picks_out,
    encode, triple, output, expand, small, points, inverse, perm, neighbours,
    up_own, conv_low, ordered, vectors, natural, take, send, picks,
    outgoing, incoming, m1p, vt,
    extended, all_picks, acc, w_buf, pick_cols, pre, m1b, prev, vb, gv,
    sends, recvs, locs, presend, prerecv, halo_s, halo_r, p_sem, w_sem, deal_s, deal_r, met, in_sem, out_sem,
):
    at = place()
    width = 512
    me = ((at["x"] * 4 + at["y"]) * 2 + at["c"]) * 4 + at["z"]
    fetched = bring(
        (
            (encode_in, encode), (triple_in, triple), (output_in, output), (expand_in, expand), (small_in, small),
            (points_in, points), (inverse_in, inverse), (perm_in, perm), (neighbours_in, neighbours),
        ),
        in_sem,
    )
    for copy in fetched[:5]:
        copy.wait()
    for first_block, per, base, refs in (
        (0, 5, 0, ((encode, 4), (triple, 12), (output, 4))), (0, 4, 5, ((expand, 16),))
    ):
        n = 0
        for ref, blocks in refs:
            for j in range(blocks):
                m1p[n // per, base + n % per] = ref[:, 128 * j : 128 * (j + 1)]
                n += 1
    row64 = lax.broadcasted_iota(jnp.int32, (16, 64), 0)
    lane64 = lax.broadcasted_iota(jnp.int32, (16, 64), 1)
    alone = jnp.where(lax.div(lane64, 4) == row64, jnp.broadcast_to(small[...], (16, 64)), 0.0).astype(BF)
    from64 = lax.broadcasted_iota(jnp.int32, (64, 128), 0)
    to128 = lax.broadcasted_iota(jnp.int32, (64, 128), 1)
    lane0 = lax.rem(at["y"] * 2 + at["c"], 8) * 16 + at["z"] * 4
    vt[...] = mm(alone, jnp.where(to128 == lane0 + lax.rem(from64, 4), 1.0, 0.0).astype(BF)).astype(BF)
    meet_lines(at)
    tell_line(at, "x", met.at[0])
    pending = []

    def own_view(i, h):
        name, op, view, order, halves = FRONT_STREAMS[i]
        if op == 0:
            return conv.at[pl.ds(h[0], h[1] - h[0]), :]
        return m1b.at[pl.ds(h[0], h[1] - h[0])] if op == 1 else vb

    begin, relay, finish, crossed = gather_steps(
        FRONT_STREAMS, own_view, (gc, g1, gv), at, sends, recvs, locs, pending
    )

    def remote(src, dst, send, recv, device):
        copy = remote_copy(src, dst, send, recv, device)
        copy.start()
        pending.append(copy)
        return copy

    pre_copies = []
    for step in (1, 2, 3):
        to = moved(at, "z", step)
        for j, (src, dst) in enumerate(((m1p.at[to["z"]], pre.at[step]), (vt, prev.at[step]))):
            pre_copies.append(remote(src, dst, presend.at[j, step], prerecv.at[j, step], device_at(to)))
    first, more = (0, 1, 2), (3, 4)
    for i in first:
        begin(i, 0)
    for copy in fetched[5:]:
        copy.wait()
    home = lax.div(inverse[...], width)
    row_id = lax.broadcasted_iota(jnp.int32, (width, width), 0)
    lane_id = lax.broadcasted_iota(jnp.int32, (width, width), 1)
    ahead = jnp.where((column_of(home.astype(F32)) == home.astype(F32)) & (row_id < lane_id), 1.0, 0.0)
    send[...] = home * 8 + total(ahead).astype(jnp.int32)
    pl.semaphore_wait(met.at[0], 3)
    tell_line(at, "y", met.at[1])
    fold_rows(send[...], points[...], outgoing)
    pl.semaphore_wait(met.at[1], 3)
    tell_line(at, "c", met.at[2])
    for copy in pre_copies:
        copy.wait_recv()
    pre[0] = m1p[at["z"]]

    def tile(k, _):
        pieces = [pre[lax.rem(at["z"] - s + 4, 4), k].astype(F32) for s in range(4)]
        m1b[k] = jnp.concatenate(pieces, axis=0).astype(BF)
        return 0

    lax.fori_loop(0, 9, tile, 0)
    vb[...] = (
        vt[...].astype(F32) + prev[1].astype(F32) + prev[2].astype(F32) + prev[3].astype(F32)
    ).astype(BF)
    up_own[...] = m1b[5:9]
    for i in more:
        begin(i, 0)
    pl.semaphore_wait(met.at[2], 1)
    deal(outgoing, incoming, me, deal_s, deal_r)
    for i in first + more:
        finish(i, 0)
        begin(i, 1)
    source = lax.div(perm[...], width)
    column = column_of(perm[...].astype(F32))
    source_column = lax.div(column.astype(jnp.int32), width)
    ahead = jnp.where((source_column == source) & (column < perm[...].astype(F32)), 1.0, 0.0)
    take[...] = source * 8 + total(ahead).astype(jnp.int32)
    token = lax.broadcasted_iota(jnp.int32, (1, width), 1)
    shift = me * width - 128 + lax.div(token, 256) * 256

    for u in range(9):
        raw = neighbours[3 * u : 3 * u + 3, :]
        local = jnp.where(raw >= 0, raw - shift, -1)
        picks[u] = local
        pick_cols[u] = jnp.concatenate([local, local, local[0:2]], axis=0).astype(F32)
    out_copies = bring(((up_own, up_out), (take, take_out), (send, send_out), (picks, picks_out)), out_sem)
    for i in first + more:
        relay(i, 1)
    for i in first:
        finish(i, 1)
        begin(i, 2)
    acc[...] = jnp.zeros_like(acc)
    for i in more:
        finish(i, 1)
    dealt(outgoing, incoming, me, deal_s, deal_r).wait_recv()
    mine = unfold_rows(take[...], incoming)
    ordered[...] = mine
    out_copies += bring(((ordered, ordered_out),), out_sem, 4)
    extended[128:640, :] = mine
    halos = []
    for j, (src, dst, step) in enumerate(((128, 640, 127), (512, 0, 1))):
        halos.append(
            remote(
                extended.at[pl.ds(src, 128), :], extended.at[pl.ds(dst, 128), :],
                halo_s.at[j], halo_r.at[j], line_neighbour(at, step),
            )
        )

    def p_copy(u):
        return pltpu.make_async_copy(all_picks.at[pl.ds(u * 3, 3)], picked.at[pl.ds(u * 3, 3)], p_sem.at[u])

    def pick_unit(u, _):
        columns = pick_cols[u].T
        for j in range(3):
            for b in range(2):
                seat = lax.broadcasted_iota(jnp.int32, (256, 512), 1).astype(F32)
                hot = jnp.where(seat == columns[256 * b : 256 * (b + 1), j : j + 1], 1.0, 0.0).astype(BF)
                window = extended[256 * b : 256 * b + 512, :]
                all_picks[u * 3 + j, 256 * b : 256 * (b + 1), :] = mm(hot, window).astype(BF)
        p_copy(u).start()
        return 0

    def w_copy(u):
        slot = lax.rem(u, 2)
        return pltpu.make_async_copy(
            gc.reshape((4, 27, 512, 128)).at[:, pl.ds(u * 3, 3)], w_buf.at[slot], w_sem.at[slot]
        )

    def conv_unit(u, _):
        @pl.when(u < 8)
        def _():
            w_copy(u + 1).start()

        w_copy(u).wait()
        slot = lax.rem(u, 2)
        parts = [
            mm(all_picks[u * 3 + j], jnp.concatenate([w_buf[slot, n, j] for n in range(4)], axis=1))
            for j in range(3)
        ]
        acc[...] += parts[0] + parts[1] + parts[2]
        return 0

    for i in first:
        relay(i, 2)
    for i in (3,):
        begin(i, 2)
    for copy in halos:
        copy.wait_recv()
    lax.fori_loop(0, 5, pick_unit, 0)
    for i in (3,):
        relay(i, 2)
    lax.fori_loop(5, 9, pick_unit, 0)
    for i in first:
        finish(i, 2)
    for i in first:
        crossed(i)
    w_copy(0).start()
    lax.fori_loop(0, 6, conv_unit, 0)
    for i in (3,):
        finish(i, 2)
    lax.fori_loop(6, 9, conv_unit, 0)
    for i in more:
        crossed(i)
    chunks = []
    for x in range(4):
        chunk = jnp.zeros((16, 128), F32)
        for y in range(4):
            for c in range(2):
                chunk = chunk + gv[x, y, c].astype(F32)
        chunks.append(chunk)
    together = jnp.concatenate(chunks, axis=1)
    vectors[...] = together
    lane = lax.broadcasted_iota(jnp.int32, (128, width), 1)
    from_lane = lax.broadcasted_iota(jnp.int32, (128, width), 0)
    shuffle = jnp.where(from_lane == lax.div(lane, 16) * 4 + lax.rem(lane, 4), 1.0, 0.0).astype(BF)
    which = lax.div(lax.rem(lax.broadcasted_iota(jnp.int32, (4, width), 1), 16), 4)
    group = lax.broadcasted_iota(jnp.int32, (4, width), 0)
    for x in range(4):
        spreaded = mm(chunks[x].astype(BF), shuffle)[12:16, :]
        natural[x : x + 1, :] = total(jnp.where(which == group, spreaded, 0.0))
    conv_low[...] = (acc[...] + together[0:1, :]).astype(BF)
    out_copies += bring(((conv_low, conv_out), (vectors, vectors_out), (natural, natural_out)), out_sem, 5)
    for copy in pending:
        copy.wait_send()
    dealt(outgoing, incoming, me, deal_s, deal_r).wait_send()

    def stored(u, _):
        p_copy(u).wait()
        return 0

    lax.fori_loop(0, 9, stored, 0)
    for copy in out_copies:
        copy.wait()


def front(conv, encode, triple, output, expand, small, points, inverse, perm, neighbours):
    shape = jax.ShapeDtypeStruct
    n = len(FRONT_STREAMS)
    dma = pltpu.SemaphoreType.DMA
    i32 = jnp.int32
    kept = (
        ((4, 16, 128), BF),
        ((512, 512), BF),
        ((512, 512), BF),
        ((16, 512), F32),
        ((4, 512), F32),
        ((1, 512), i32),
        ((1, 512), i32),
        ((9, 3, 512), i32),
    )
    return pl.pallas_call(
        front_kernel,
        out_shape=(
            shape((4, 4, 4, 2, 432, 128), BF),
            shape((4, 5, 4, 4, 2, 16, 128), BF),
            shape(*kept[0]),
            shape((27, 512, 512), BF),
        )
        + tuple(shape(*k) for k in kept[1:]),
        in_specs=[ANY] * 10,
        out_specs=[ANY] * 11,
        scratch_shapes=[
            pltpu.VMEM((4, 512), BF),
            pltpu.VMEM((4, 1536), BF),
            pltpu.VMEM((4, 512), BF),
            pltpu.VMEM((4, 2048), BF),
            pltpu.VMEM((1, 64), F32),
            pltpu.VMEM((512, 512), BF),
            pltpu.VMEM((1, 512), i32),
            pltpu.VMEM((1, 512), i32),
            pltpu.VMEM((27, 512), i32),
        ]
        + [pltpu.VMEM(*k) for k in kept]
        + [
            pltpu.VMEM((128, 8, 512), BF),
            pltpu.VMEM((128, 8, 512), BF),
            pltpu.VMEM((4, 9, 4, 128), BF),
            pltpu.VMEM((16, 128), BF),
            pltpu.VMEM((768, 512), BF),
            pltpu.VMEM((27, 512, 512), BF),
            pltpu.VMEM((512, 512), F32),
            pltpu.VMEM((2, 4, 3, 512, 128), BF),
            pltpu.VMEM((9, 8, 512), F32),
            pltpu.VMEM((4, 9, 4, 128), BF),
            pltpu.VMEM((9, 16, 128), BF),
            pltpu.VMEM((4, 16, 128), BF),
            pltpu.VMEM((16, 128), BF),
            pltpu.VMEM((4, 4, 2, 16, 128), BF),
            dma((n, SLOTS)),
            dma((n, SLOTS)),
            dma((n, 2)),
            dma((2, 4)),
            dma((2, 4)),
            dma((2,)),
            dma((2,)),
            dma((9,)),
            dma((2,)),
            dma,
            dma,
            pltpu.SemaphoreType.REGULAR((3,)),
            dma((9,)),
            dma((8,)),
        ],
        compiler_params=pltpu.CompilerParams(
            collective_id=0, has_side_effects=True, vmem_limit_bytes=56 * 2**20
        ),
        name="front",
    )(conv, encode, triple, output, expand, small, points, inverse, perm, neighbours)


BACK_CHAINS = (
    ("cz", "zxycRL", {"R": 96, "L": 128}, "R", 0, "zyx", ((0, 48), (48, 96))),
    ("cx", "zxycRL", {"R": 160, "L": 128}, "R", 96, "xzy", ((0, 80), (80, 160))),
    ("cy", "zxycRL", {"R": 176, "L": 128}, "R", 256, "yxz", ((0, 96), (96, 176))),
    ("wide", "zKxycSL", {"K": 5, "S": 16, "L": 128}, "K", 0, "zyx", ((0, 3), (3, 5))),
)


def back_kernel(
    grad_in, first_grad_in, take_in, send_in, picks_in, w, picked, g1, gv_in,
    points_grad, oc, o1, ov,
    returning, arrived, wide, grad, first_grad, take, send, picks, gv,
    kernel_grad, theirs, spread, p_buf, w_buf, rims, landed, sib, *rest,
):
    count = 12 * len(BACK_CHAINS)
    landing, rest = rest[:count], rest[count:]
    post, postr, vx, vr, p_sem, w_sem, xy_send, xy_recv, sends, recvs, vsend, vrecv, psend, precv, rim_s, rim_r, deal_s, deal_r, met, in_sem = rest
    at = place()
    me = ((at["x"] * 4 + at["y"]) * 2 + at["c"]) * 4 + at["z"]
    fetched = bring(
        (
            (gv_in, gv), (g1, wide), (grad_in, grad), (picks_in, picks), (take_in, take), (send_in, send),
            (first_grad_in, first_grad),
        ),
        in_sem,
    )
    meet_lines(at)
    tell_line(at, "x", met.at[0])
    other = moved(at, "c", 1)
    pending = []
    tiles = kernel_grad.reshape((4, 4, 4, 2, 432, 128))

    def push(src, dst, send, recv, to):
        copy = remote_copy(src, dst, send, recv, device_at(to))
        copy.start()
        pending.append(copy)
        return copy

    mine = (tiles, "zxycRL", {"c": at["c"]})
    stores = (mine, mine, mine, (wide, "zKxycSL", {"c": at["c"]}))
    lend, start, middle, close, view = scatter_steps(
        BACK_CHAINS, stores, landing, at, sends, recvs, pending
    )
    conv_chains = (0, 1, 2)

    def vector_step(k):
        axis, steps = (("c", (1,)), ("z", (1, 2, 3)), ("y", (1, 2, 3)), ("x", (1, 2, 3)))[k]
        copies = []
        for s in steps:
            to = moved(at, axis, s)
            if axis == "x":
                src, dst = vx.at[3, to["x"]], vr.at[3, s, 0]
            else:
                src, dst = (gv if k == 0 else vx.at[k]), vr.at[k, s]
            copies.append(push(src, dst, vsend.at[k, s], vrecv.at[k, s], to))
        return copies

    def vector_add(k, copies):
        for copy in copies:
            copy.wait_recv()
        if k == 3:
            ov[...] = vx[3, at["x"]] + vr[3, 1, 0] + vr[3, 2, 0] + vr[3, 3, 0]
            return
        sum_now = gv[...] if k == 0 else vx[k]
        for s in (1,) if k == 0 else (1, 2, 3):
            sum_now = sum_now + vr[k, s]
        vx[k + 1] = sum_now

    def p_copy(u):
        slot = lax.rem(u, 2)
        return pltpu.make_async_copy(picked.at[pl.ds(u * 3, 3)], p_buf.at[slot], p_sem.at[slot])

    def w_copy(u):
        slot = lax.rem(u, 2)
        return pltpu.make_async_copy(w.at[:, pl.ds(u * 3, 3)], w_buf.at[slot], w_sem.at[slot])

    def xy_copy(n):
        x, y = lax.div(n, 4), lax.rem(n, 4)
        return remote_copy(
            tiles.at[:, x, y, other["c"]], theirs.at[:, x, y], xy_send.at[n], xy_recv.at[n], device_at(other)
        )

    def weight_unit(u, _):
        @pl.when(u < 8)
        def _():
            p_copy(u + 1).start()

        p_copy(u).wait()
        for j in range(3):
            product = mm_tn(p_buf[lax.rem(u, 2), j], grad[...])
            span = pl.ds(pl.multiple_of(u * 1536 + j * 512, 512), 512)
            for n in range(4):
                kernel_grad[n, span, :] = product[:, 128 * n : 128 * (n + 1)].astype(BF)
        ready, ready_next = lax.div(u * 16, 9), lax.div((u + 1) * 16, 9)
        for j in range(2):
            @pl.when(ready + j < ready_next)
            def _():
                xy_copy(ready + j).start()

        return 0

    def row_unit(u, _):
        @pl.when(u < 8)
        def _():
            w_copy(u + 1).start()

        w_copy(u).wait()
        slot = lax.rem(u, 2)
        g = grad[...]
        back = [
            mm_nt(g, jnp.concatenate([w_buf[slot, n, j] for n in range(4)], axis=1)).astype(BF)
            for j in range(3)
        ]
        for b in range(2):
            hot = jnp.concatenate([spread_rows(picks.at[u], j, b) for j in range(3)], axis=1)
            terms = jnp.concatenate([back[j][256 * b : 256 * (b + 1), :] for j in range(3)], axis=0)
            spread[256 * b : 256 * b + 512, :] += mm(hot, terms)
        return 0

    p_copy(0).start()
    spread[...] = jnp.zeros_like(spread)
    fetched[0].wait()
    vectors = vector_step(0)
    state = {}
    fetched[1].wait()
    lent = lend(3, sib)
    w_copy(0).start()
    for copy in fetched[2:]:
        copy.wait()
    lax.fori_loop(0, 3, weight_unit, 0)
    pl.semaphore_wait(met.at[0], 3)
    tell_line(at, "y", met.at[1])
    state[3] = start(3, 0, lent, sib)
    vector_add(0, vectors)
    vectors = vector_step(1)
    lax.fori_loop(3, 6, weight_unit, 0)
    pl.semaphore_wait(met.at[1], 3)
    tell_line(at, "c", met.at[2])
    for i in (3,):
        middle(i, 0, state[i])
    lax.fori_loop(6, 9, weight_unit, 0)
    pl.semaphore_wait(met.at[2], 1)
    vector_add(1, vectors)
    vectors = vector_step(2)
    for i in (3,):
        close(i, 0, state[i])
        state[i] = start(i, 1)
    for n in range(16):
        xy_copy(n).wait_recv()

    def join(n, _):
        z, x, y = lax.div(n, 16), lax.rem(lax.div(n, 4), 4), lax.rem(n, 4)
        where = tiles.at[z, x, y, at["c"]]
        where[...] = (where[...].astype(F32) + theirs[z, x, y].astype(F32)).astype(BF)
        return 0

    lax.fori_loop(0, 64, join, 0)
    for i in conv_chains:
        state[i] = start(i, 0)
    for i in (3,):
        middle(i, 1, state[i])
    lax.fori_loop(0, 3, row_unit, 0)
    vector_add(2, vectors)
    vectors = vector_step(3)
    for i in (3,):
        close(i, 1, state[i])
        state[i] = start(i, 2)
    lax.fori_loop(3, 5, row_unit, 0)
    for i in conv_chains:
        middle(i, 0, state[i])
    for i in (3,):
        middle(i, 2, state[i])
    lax.fori_loop(5, 9, row_unit, 0)
    rims[0] = spread[0:128, :].astype(BF)
    rims[1] = spread[640:768, :].astype(BF)
    rim_copies = []
    for j, step in ((0, 127), (1, 1)):
        copy = remote_copy(rims.at[j], landed.at[j], rim_s.at[j], rim_r.at[j], line_neighbour(at, step))
        copy.start()
        pending.append(copy)
        rim_copies.append(copy)
    for i in conv_chains:
        close(i, 0, state[i])
        state[i] = start(i, 1)
    for i in (3,):
        close(i, 2, state[i])
    vector_add(3, vectors)
    swaps = swap_rows(
        wide[at["z"], :, at["x"], at["y"], at["c"]].astype(F32), post, postr, at, psend, precv, pending
    )
    for copy in rim_copies:
        copy.wait_recv()
    spread[512:640, :] += landed[0].astype(F32)
    spread[128:256, :] += landed[1].astype(F32)
    ordered_grad = (first_grad[...] + spread[128:640, :]).astype(BF)
    fold_rows(take[...], ordered_grad, returning)
    deal(returning, arrived, me, deal_s, deal_r)
    for i in conv_chains:
        middle(i, 1, state[i])
    for i in conv_chains:
        close(i, 1, state[i])
        state[i] = start(i, 2)
    swapped_rows(swaps, post, postr, at, o1)
    for i in conv_chains:
        middle(i, 2, state[i])
    for i in conv_chains:
        close(i, 2, state[i])
        name, layout, plain, cut, base, order, halves = BACK_CHAINS[i]
        oc[pl.ds(base, plain["R"]), :] = tiles[at["z"], at["x"], at["y"], at["c"], pl.ds(base, plain["R"]), :].astype(F32)
    dealt(returning, arrived, me, deal_s, deal_r).wait_recv()
    points_grad[...] = unfold_rows(send[...], arrived)
    for copy in pending:
        copy.wait_send()
    for n in range(16):
        xy_copy(n).wait_send()
    dealt(returning, arrived, me, deal_s, deal_r).wait_send()


def back_scatter(grad, first_grad, take, send, picks, w, picked, g1, gv):
    shape = jax.ShapeDtypeStruct
    n = len(BACK_CHAINS)
    dma = pltpu.SemaphoreType.DMA
    return pl.pallas_call(
        back_kernel,
        out_shape=(
            shape((512, 512), BF),
            shape((432, 128), F32),
            shape((4, 5, 4, 128), F32),
            shape((16, 128), F32),
        ),
        in_specs=[ANY] * 9,
        out_specs=[VM] * 4,
        scratch_shapes=[
            pltpu.VMEM((128, 8, 512), BF),
            pltpu.VMEM((128, 8, 512), BF),
            pltpu.VMEM((4, 5, 4, 4, 2, 16, 128), BF),
            pltpu.VMEM((512, 512), BF),
            pltpu.VMEM((512, 512), F32),
            pltpu.VMEM((1, 512), jnp.int32),
            pltpu.VMEM((1, 512), jnp.int32),
            pltpu.VMEM((9, 3, 512), jnp.int32),
            pltpu.VMEM((4, 16, 128), F32),
            pltpu.VMEM((4, 13824, 128), BF),
            pltpu.VMEM((4, 4, 4, 432, 128), BF),
            pltpu.VMEM((768, 512), F32),
            pltpu.VMEM((2, 3, 512, 512), BF),
            pltpu.VMEM((2, 4, 3, 512, 128), BF),
            pltpu.VMEM((2, 128, 512), BF),
            pltpu.VMEM((2, 128, 512), BF),
            pltpu.VMEM((4, 5, 4, 4, 16, 128), BF),
        ]
        + [pltpu.VMEM(s, BF) for chain in BACK_CHAINS for s in landing_shapes(chain)]
        + [
            pltpu.VMEM((4, 5, 4, 128), BF),
            pltpu.VMEM((4, 5, 4, 128), BF),
            pltpu.VMEM((4, 4, 16, 128), F32),
            pltpu.VMEM((4, 4, 4, 16, 128), F32),
            dma((2,)),
            dma((2,)),
            dma((16,)),
            dma((16,)),
            dma((n, 22)),
            dma((n, 22)),
            dma((4, 4)),
            dma((4, 4)),
            dma((4,)),
            dma((4,)),
            dma((2,)),
            dma((2,)),
            dma,
            dma,
            pltpu.SemaphoreType.REGULAR((3,)),
            dma((7,)),
        ],
        compiler_params=pltpu.CompilerParams(
            collective_id=1, has_side_effects=True, vmem_limit_bytes=62 * 2**20
        ),
        name="back_scatter",
    )(grad, first_grad, take, send, picks, w, picked, g1, gv)


def per_device(
    points,
    perm,
    inverse,
    lengths,
    neighbours,
    conv_weight,
    conv_bias,
    encode_weight,
    encode_bias,
    encode_gain,
    encode_shift,
    before_gain,
    before_shift,
    triple_weight,
    query_bias,
    value_bias,
    output_weight,
    output_bias,
    second_gain,
    second_shift,
    expand_weight,
    expand_bias,
    reduce_weight,
    reduce_bias,
    grad_out,
):
    pts, rep = lax.axis_index("pts"), lax.axis_index("rep")
    lane = lax.rem(pts, 8) * 16 + rep * 4
    small = jnp.concatenate(
        [
            conv_bias,
            encode_bias,
            encode_gain,
            encode_shift,
            before_gain,
            before_shift,
            query_bias,
            value_bias,
            output_bias,
            second_gain,
            second_shift,
            reduce_bias,
            expand_bias,
        ]
    )
    kernel, wide, up_own, picked, conv, ordered, vectors, wide_bias, take, send, picks = front(
        conv_weight,
        encode_weight,
        triple_weight,
        output_weight,
        expand_weight,
        small.astype(F32).reshape(1, 64),
        points,
        inverse.reshape(1, 512),
        perm.reshape(1, 512),
        neighbours,
    )
    result, grad_first, grad_conv, grad_wide, vector_grads, up_out, tall_out = block(
        lengths,
        conv,
        ordered,
        grad_out,
        wide.reshape(20, 512, 128),
        up_own,
        reduce_weight,
        vectors,
        wide_bias,
    )
    points_grad, kernel_out, wide_out, vector_out = back_scatter(
        grad_conv,
        grad_first,
        take,
        send,
        picks,
        kernel.reshape(4, 27, 512, 128),
        picked,
        grad_wide.reshape(4, 5, 4, 4, 2, 16, 128),
        vector_grads,
    )
    wide_out = wide_out.reshape(20, 4, 128).transpose(1, 0, 2).reshape(4, 2560)
    up_out = up_out.reshape(16, 4, 128).transpose(1, 0, 2).reshape(4, 2048)
    vector_out = lax.dynamic_slice(vector_out, (0, lane), (16, 4))
    reduced = (
        vector_out[V_CONV],
        wide_out[:, :512],
        vector_out[V_ENC],
        vector_out[V_GAIN0],
        vector_out[V_SHIFT0],
        vector_out[V_GAIN1],
        vector_out[V_SHIFT1],
        wide_out[:, 512:2048],
        vector_out[V_QUERY],
        vector_out[V_VALUE],
        wide_out[:, 2048:],
        vector_out[V_OUT],
        vector_out[V_GAIN2],
        vector_out[V_SHIFT2],
        up_out,
        vector_out[12:].reshape(16),
        tall_out,
        vector_out[V_RED],
    )
    return (result, points_grad, kernel_out) + reduced


def solution(mesh):
    in_specs = (
        P(("pts", "rep"), None),
        P(("pts", "rep")),
        P(("pts", "rep")),
        P(("pts", "rep")),
        P(None, ("pts", "rep")),
        P("pts", "rep"),
        P(("pts", "rep")),
        P(("pts", "rep"), None),
        P(("pts", "rep")),
        P(("pts", "rep")),
        P(("pts", "rep")),
        P(("pts", "rep")),
        P(("pts", "rep")),
        P(("pts", "rep"), None),
        P(("pts", "rep")),
        P(("pts", "rep")),
        P(("pts", "rep"), None),
        P(("pts", "rep")),
        P(("pts", "rep")),
        P(("pts", "rep")),
        P(("pts", "rep"), None),
        P(("pts", "rep")),
        P(("pts", "rep"), None),
        P(("pts", "rep")),
        P(("pts", "rep"), None),
    )
    out_specs = (
        P(("pts", "rep"), None),
        P(("pts", "rep"), None),
        P("pts", "rep"),
        P(("pts", "rep")),
        P(("pts", "rep"), None),
        P(("pts", "rep")),
        P(("pts", "rep")),
        P(("pts", "rep")),
        P(("pts", "rep")),
        P(("pts", "rep")),
        P(("pts", "rep"), None),
        P(("pts", "rep")),
        P(("pts", "rep")),
        P(("pts", "rep"), None),
        P(("pts", "rep")),
        P(("pts", "rep")),
        P(("pts", "rep")),
        P(("pts", "rep"), None),
        P(("pts", "rep")),
        P(("pts", "rep"), None),
        P(("pts", "rep")),
    )
    return jax.shard_map(
        per_device, mesh=mesh, in_specs=in_specs, out_specs=out_specs, check_vma=False
    )
```

```python
import jax
import jax.numpy as jnp
from jax import lax
from jax.experimental import pallas as pl
from jax.experimental.pallas import tpu as pltpu
from jax.sharding import PartitionSpec as P

MESH = pl.DeviceIdType.MESH
BF = jnp.bfloat16
F32 = jnp.float32


def place():
    p = lax.axis_index("pts")
    return {
        "x": lax.div(p, 8),
        "y": lax.rem(lax.div(p, 2), 4),
        "c": lax.rem(p, 2),
        "z": lax.axis_index("rep"),
    }


def device_at(at):
    return ((at["x"] * 4 + at["y"]) * 2 + at["c"], at["z"])


def moved(at, axis, step):
    size = 2 if axis == "c" else 4
    return {**at, axis: lax.rem(at[axis] + step, size)}


def whole(value):
    return slice(None) if value is None else value


def conv_view(ref, sel, h):
    r0, r1 = h
    return ref.at[
        whole(sel.get("z")), whole(sel.get("x")), whole(sel.get("y")), sel["c"], pl.ds(r0, r1 - r0), :
    ]


def wide_view(ref, sel, h):
    k0, k1 = h
    return ref.at[
        whole(sel.get("z")), pl.ds(k0, k1 - k0), whole(sel.get("x")), whole(sel.get("y")), sel["c"]
    ]


def tall_view(ref, sel, h):
    l0, l1 = h
    return ref.at[
        whole(sel.get("x")), whole(sel.get("y")), sel["c"], whole(sel.get("z")), :, pl.ds(l0, l1 - l0)
    ]


def flat_view(ref, sel, h):
    return ref.at[whole(sel.get("x")), whole(sel.get("y")), sel["c"]]


FRONT_STREAMS = (
    ("cz", 0, conv_view, "xyz", ((0, 48), (48, 96))),
    ("cx", 0, conv_view, "yzx", ((96, 176), (176, 256))),
    ("cy", 0, conv_view, "zxy", ((256, 352), (352, 432))),
    ("wide", 1, wide_view, "xyz", ((0, 3), (3, 5))),
    ("vectors", 2, flat_view, "xy", ((0, 16),)),
)
SLOTS = 40


def greet_lines(at):
    barrier = pltpu.get_barrier_semaphore()
    for axis, steps in (("x", (1, 2, 3)), ("y", (1, 2, 3)), ("z", (1, 2, 3)), ("c", (1,))):
        for s in steps:
            pl.semaphore_signal(
                barrier, inc=1, device_id=device_at(moved(at, axis, s)), device_id_type=MESH
            )


def meet_lines():
    pl.semaphore_wait(pltpu.get_barrier_semaphore(), 10)


def tell_line(at, axis, sem):
    for s in (1,) if axis == "c" else (1, 2, 3):
        pl.semaphore_signal(sem, inc=1, device_id=device_at(moved(at, axis, s)), device_id_type=MESH)


def bring(pairs, sem, base=0):
    copies = [pltpu.make_async_copy(src, dst, sem.at[base + n]) for n, (src, dst) in enumerate(pairs)]
    for copy in copies:
        copy.start()
    return copies


def remote_copy(src, dst, send, recv, device):
    return pltpu.make_async_remote_copy(
        src_ref=src, dst_ref=dst, send_sem=send, recv_sem=recv, device_id=device, device_id_type=MESH
    )


def gather_steps(streams, own_view, outs, at, sends, recvs, locs, pending):
    other = moved(at, "c", 1)
    crossing = {i: [] for i in range(len(streams))}
    local_copies, state = {}, {}

    def push(src, dst, i, k, to):
        copy = remote_copy(src, dst, sends.at[i, k], recvs.at[i, k], device_at(to))
        copy.start()
        pending.append(copy)
        return copy

    def cross(ref, i, k):
        crossing[i].append(push(ref, ref, i, k, other))

    def keep_own(i):
        name, op, view, order, halves = streams[i]
        for j, h in enumerate(halves):
            copy = pltpu.make_async_copy(own_view(i, h), view(outs[op], at, h), locs.at[i, j])
            copy.start()
            local_copies[(i, j)] = copy

    def block_sel(order, phase, index=None):
        sel = {"c": at["c"]}
        for a in "xyz":
            if a in order and order.index(a) < phase:
                continue
            sel[a] = at[a]
        if index is not None:
            sel[order[phase]] = index
        return sel

    def begin(i, phase):
        name, op, view, order, halves = streams[i]
        axis = order[phase]
        n = len(halves)
        sel = block_sel(order, phase)
        copies = {}
        if phase == 0:
            keep_own(i)
            span = (halves[0][0], halves[-1][1])
            for d in (1, 3, 2):
                copies[d] = push(own_view(i, span), view(outs[op], sel, span), i, d, moved(at, axis, d))
        else:
            for d, hs in ((1, range(n)), (3, reversed(range(n)))):
                for h in hs:
                    ref = view(outs[op], sel, halves[h])
                    copies[(d, h)] = push(ref, ref, i, phase * 6 + (0 if d == 1 else 2) + h, moved(at, axis, d))
        state[(i, phase)] = copies
        if phase == len(order) - 1:
            for h in range(n):
                cross(view(outs[op], sel, halves[h]), i, 20 + h)

    def relay(i, phase):
        name, op, view, order, halves = streams[i]
        axis = order[phase]
        last = phase == len(order) - 1
        n = len(halves)
        copies = state[(i, phase)]
        for d in (1, 3) if n == 2 else (1,):
            h = 0 if d == 1 else n - 1
            copies[(d, h)].wait_recv()
            ref = view(outs[op], block_sel(order, phase, lax.rem(at[axis] + 4 - d, 4)), halves[h])
            copies[(d, "f")] = push(ref, ref, i, phase * 6 + (4 if d == 1 else 5), moved(at, axis, d))
            if last:
                cross(ref, i, 22 + d)

    def finish(i, phase):
        name, op, view, order, halves = streams[i]
        axis = order[phase]
        last = phase == len(order) - 1
        n = len(halves)
        copies = state[(i, phase)]
        if phase == 0:
            for d in (1, 3, 2):
                copies[d].wait_recv()
            for h in range(n):
                local_copies[(i, h)].wait()
            return
        for d in (1, 3):
            for h in range(n):
                if h == (0 if d == 1 else n - 1) and not (n == 1 and d == 3):
                    continue
                copies[(d, h)].wait_recv()
                if last:
                    sel = block_sel(order, phase, lax.rem(at[axis] + 4 - d, 4))
                    cross(view(outs[op], sel, halves[h]), i, 26 + d)
        for d in (1, 3):
            if (d, "f") not in copies:
                continue
            copies[(d, "f")].wait_recv()
            if last:
                h = 0 if d == 1 else n - 1
                sel = block_sel(order, phase, lax.rem(at[axis] + 2, 4))
                cross(view(outs[op], sel, halves[h]), i, 30 + d)

    def crossed(i):
        for copy in crossing[i]:
            copy.wait_recv()

    return begin, relay, finish, crossed


def cut_view(ref, layout, sel, cut=None, span=None, base=0):
    index = []
    for dim in layout:
        if dim in sel:
            index.append(sel[dim])
        elif dim == cut and span is not None:
            index.append(pl.ds(base + span[0], span[1] - span[0]))
        else:
            index.append(slice(None))
    return ref.at[tuple(index)]


def sizes_of(layout, plain):
    return tuple(plain[d] if d in plain else 4 for d in layout)


def landing_shapes(chain):
    name, layout, plain, cut, base, order, halves = chain
    left = layout.replace("c", "")
    shapes = []
    for axis in order:
        left = left.replace(axis, "")
        for span in halves:
            shapes.append(sizes_of(left, {**plain, cut: span[1] - span[0]}))
        shapes += [sizes_of(left, plain)] * 2
    return shapes


STEPS = (2, 1, 3, 0)


def scatter_steps(chains, stores, landing, at, sends, recvs, pending):
    other = moved(at, "c", 1)

    def push(src, dst, i, k, to):
        copy = remote_copy(src, dst, sends.at[i, k], recvs.at[i, k], device_at(to))
        copy.start()
        pending.append(copy)
        return copy

    def view(i, sel, span):
        name, layout, plain, cut, base, order, halves = chains[i]
        ref, inner, fixed = stores[i]
        return cut_view(ref, inner, {**fixed, **sel}, cut, span, base)

    def add(i, sel, srcs, span):
        name, layout, plain, cut, base, order, halves = chains[i]
        inner = layout.replace("c", "")
        free = [d for d in inner if d in "xyz" and d not in sel]
        tiles = span[1] - span[0]
        for d, size in plain.items():
            tiles = tiles if d == cut else tiles * size
        tiles = max(tiles // 2048, 1)
        while free and tiles * 4 <= 64:
            free.pop()
            tiles *= 4
        count = 4 ** len(free)

        def one(n, _):
            here = dict(sel)
            for k, d in enumerate(reversed(free)):
                here[d] = lax.rem(lax.div(n, 4**k), 4)
            where = view(i, here, span)
            terms = [
                cut_view(src, src_layout, {**{d: here[d] for d in free}, **src_sel}, cut, src_span)
                for src, src_layout, src_sel, src_span in srcs
            ]
            if len(terms) == 1:
                where[...] = where[...] + terms[0][...]
            else:
                where[...] = (
                    where[...].astype(F32) + terms[0][...].astype(F32) + terms[1][...].astype(F32)
                ).astype(BF)
            return 0

        if count == 1:
            one(0, 0)
        else:
            lax.fori_loop(0, count, one, 0)

    def lend(i, sib):
        name, layout, plain, cut, base, order, halves = chains[i]
        ref, inner, fixed = stores[i]
        axis, span = order[0], (0, plain[cut])
        copies = []
        for k, step in enumerate(STEPS):
            a = lax.rem(at[axis] + step, 4)
            far = cut_view(ref, inner, {"c": other["c"], axis: a}, cut, span, base)
            copies.append(push(far, cut_view(sib, layout.replace("c", ""), {axis: a}), i, k, other))
        return copies

    def names(i, phase):
        name, layout, plain, cut, base, order, halves = chains[i]
        inner = layout.replace("c", "")
        axis = order[phase]
        done = {a: at[a] for a in order[:phase]}
        left = "".join(d for d in inner if d not in order[: phase + 1])
        buffers = landing[i * 12 + 4 * phase : i * 12 + 4 * phase + 4]
        return inner, axis, done, left, buffers, 4 + phase * 6, cut, halves, (0, plain[cut])

    def start(i, phase, lent=None, sib=None):
        inner, axis, done, left, (r0, r1, rp, rm), slot, cut, halves, span = names(i, phase)
        up, down = moved(at, axis, 1), moved(at, axis, 3)
        got = {}
        for k, step in enumerate(STEPS):
            a = lax.rem(at[axis] + step, 4)
            if lent is not None:
                lent[k].wait_recv()
                add(i, {axis: a}, [(sib, inner, {axis: a}, span)], span)
            part = lambda h: view(i, {**done, axis: a}, h)
            if step == 2:
                got["r0"] = push(part(halves[0]), r0, i, slot, up)
                got["r1"] = push(part(halves[1]), r1, i, slot + 1, down)
            elif step == 1:
                got["p1"] = push(part(halves[1]), cut_view(rp, left, {}, cut, halves[1]), i, slot + 2, up)
            elif step == 3:
                got["m0"] = push(part(halves[0]), cut_view(rm, left, {}, cut, halves[0]), i, slot + 3, down)
        return got

    def middle(i, phase, got):
        inner, axis, done, left, (r0, r1, rp, rm), slot, cut, halves, span = names(i, phase)
        up, down = moved(at, axis, 1), moved(at, axis, 3)
        for key, h, buf, land, to, k in (("r0", 0, r0, rp, up, 4), ("r1", 1, r1, rm, down, 5)):
            half = halves[h]
            got[key].wait_recv()
            sel = {**done, axis: to[axis]}
            add(i, sel, [(buf, left, {}, (0, half[1] - half[0]))], half)
            got[k] = push(view(i, sel, half), cut_view(land, left, {}, cut, half), i, slot + k, to)

    def close(i, phase, got):
        inner, axis, done, left, (r0, r1, rp, rm), slot, cut, halves, span = names(i, phase)
        for k in ("p1", "m0", 4, 5):
            got[k].wait_recv()
        add(i, {**done, axis: at[axis]}, [(rp, left, {}, span), (rm, left, {}, span)], span)

    return lend, start, middle, close, view


def swap_rows(block, post, postr, at, send, recv, pending):
    for n in range(4):
        post[n] = block[:, 4 * n : 4 * n + 4, :].astype(BF)
    copies = []
    for s in (1, 2, 3):
        to = moved(at, "z", s)
        copy = remote_copy(post.at[to["z"]], postr.at[s], send.at[s], recv.at[s], device_at(to))
        copy.start()
        pending.append(copy)
        copies.append(copy)
    return copies


def swapped_rows(copies, post, postr, at, out):
    out[at["z"]] = post[at["z"]].astype(F32)
    for s in (1, 2, 3):
        copies[s - 1].wait_recv()
        out[lax.rem(at["z"] + 4 - s, 4)] = postr[s].astype(F32)


VM = pl.BlockSpec(memory_space=pltpu.VMEM)
ANY = pl.BlockSpec(memory_space=pl.ANY)
SM = pl.BlockSpec(memory_space=pltpu.SMEM)
epsilon = 1e-05


def mm(a, b):
    return lax.dot_general(a, b, (((1,), (0,)), ((), ())), preferred_element_type=F32)


def mm_nt(a, b):
    return lax.dot_general(a, b, (((1,), (1,)), ((), ())), preferred_element_type=F32)


def mm_tn(a, b):
    return lax.dot_general(a, b, (((0,), (0,)), ((), ())), preferred_element_type=F32)


def wide_block(ref, first, count=4):
    return jnp.concatenate([ref[first + k] for k in range(count)], axis=1)


def put_wide(ref, first, value, count=4):
    for k in range(count):
        ref[first + k] = value[:, 128 * k : 128 * (k + 1)].astype(BF)


V_CONV, V_ENC, V_GAIN0, V_SHIFT0, V_GAIN1, V_SHIFT1, V_QUERY, V_VALUE, V_OUT, V_GAIN2, V_SHIFT2, V_RED = range(12)


def over_rows(body, step=512, rows=512):
    def one(n, _):
        body(pl.ds(pl.multiple_of(n * step, step), step))
        return 0

    lax.fori_loop(0, rows // step, one, 0)


def normalize(v):
    mean = jnp.mean(v, axis=-1, keepdims=True)
    centred = v - mean
    spread = jnp.mean(centred * centred, axis=-1, keepdims=True)
    rstd = lax.rsqrt(spread + epsilon)
    return centred * rstd, rstd


def norm_pull(hat, rstd, gain, grad):
    up = grad * gain
    a = jnp.mean(up, axis=-1, keepdims=True)
    b = jnp.mean(up * hat, axis=-1, keepdims=True)
    return rstd * (up - a - hat * b)


def total(v):
    return jnp.sum(v, axis=0, keepdims=True)


def gelu_both(u):
    cdf = 0.5 * (1.0 + lax.erf(u * 0.7071067811865476))
    pdf = 0.3989422804014327 * jnp.exp(-0.5 * u * u)
    return u * cdf, cdf + u * pdf


def three(v):
    hi = v.astype(BF).astype(F32)
    rest = v - hi
    mid = rest.astype(BF).astype(F32)
    return hi, mid, rest - mid


BLOCK_STREAMS = (
    ("up", 0, wide_view, "xyz", ((0, 2), (2, 4))),
    ("down", 1, tall_view, "zyx", ((0, 256), (256, 512))),
)
BLOCK_CHAINS = (
    ("up", "zKxycSL", {"K": 4, "S": 16, "L": 128}, "K", 0, "zyx", ((0, 2), (2, 4))),
    ("down", "xyczSL", {"S": 16, "L": 512}, "L", 0, "xyz", ((0, 256), (256, 512))),
)


def block_kernel(
    length, conv_in, ordered_in, go_in, w1_in, up_own_in, down_own_in, vec_in, xb_in,
    result_out, first_grad_out, conv_grad_out, g1_out, gv_out, o1, o2,
    conv, ordered, go, w1, up_own, down_own, vec, xb, result, first_grad, conv_grad, g1, gv, gv_tiles,
    big, hat0, rstd0, first, hat1, rstd1, normed, normed_t, q, k, v, k_t, v_t,
    mixed_t, mixed, rows_a, rows_b, kx, xa, ya, hat2, rstd2, n2, n2_t,
    second, act, dh, da, acc, acc2, dn, d_mixed, dq_t, dk, dv, scores,
    up_all, down_all, g_up, g_down, sib_up, sib_down, *rest,
):
    landing = rest[:24]
    post, postr, sends, recvs, locs, back_s, back_r, swap_s, swap_r, in_sem, out_sem = rest[24:]
    at = place()
    greet_lines(at)
    fetched = bring(
        (
            (up_own_in, up_own), (down_own_in, down_own), (conv_in, conv), (w1_in, w1), (vec_in, vec),
            (ordered_in, ordered), (go_in, go), (xb_in, xb),
        ),
        in_sem,
    )
    meet_lines()
    for copy in fetched[:2]:
        copy.wait()
    pending = []
    own_view = lambda i, h: (
        up_own.at[pl.ds(h[0], h[1] - h[0])] if i == 0 else down_own.at[:, pl.ds(h[0], h[1] - h[0])]
    )
    begin, relay, finish, crossed = gather_steps(
        BLOCK_STREAMS, own_view, (up_all, down_all), at, sends, recvs, locs, pending
    )
    stores = (
        (g_up.reshape((4, 4, 4, 4, 2, 16, 128)), "zKxycSL", {"c": at["c"]}),
        (g_down.reshape((4, 4, 2, 4, 16, 512)), "xyczSL", {"c": at["c"]}),
    )
    lend, start, middle, close, view = scatter_steps(
        BLOCK_CHAINS, stores, landing, at, back_s, back_r, pending
    )
    both = (0, 1)
    up_blocks, down_rows = up_all.reshape((16, 512, 128)), down_all.reshape((2048, 512))
    for i in both:
        begin(i, 0)
    for copy in fetched[2:]:
        copy.wait()
    row = lambda n: vec[n : n + 1, :]
    gv[...] = jnp.zeros_like(gv)

    def gain(n, value):
        gv[n : n + 1, :] += total(value)

    big[...] = mm(conv[...], wide_block(w1, 0))
    for i in both:
        finish(i, 0)
        begin(i, 1)

    def encode(r):
        hat, rstd = normalize(big[r, :] + row(V_ENC))
        hat0[r, :] = hat
        rstd0[r, :] = rstd
        here = ordered[r, :].astype(F32) + hat * row(V_GAIN0) + row(V_SHIFT0)
        first[r, :] = here
        hat, rstd = normalize(here)
        hat1[r, :] = hat
        rstd1[r, :] = rstd
        normed[r, :] = (hat * row(V_GAIN1) + row(V_SHIFT1)).astype(BF)

    over_rows(encode)
    normed_t[...] = normed[...].T
    q[...] = (0.25 * (mm(normed[...], wide_block(w1, 4)) + row(V_QUERY)).astype(BF).astype(F32)).astype(BF)
    k[...] = mm(normed[...], wide_block(w1, 8)).astype(BF)
    v[...] = (mm(normed[...], wide_block(w1, 12)) + row(V_VALUE)).astype(BF)
    k_t[...] = k[...].T
    turned = v[...].T
    one_row = jnp.where(lax.broadcasted_iota(jnp.int32, (16, 512), 0) == 0, 1.0, 0.0).astype(BF)
    for h in range(32):
        v_t[h, 0:16, :] = turned[16 * h : 16 * h + 16, :]
        v_t[h, 16:32, :] = one_row
    for i in both:
        relay(i, 1)

    lane = lax.broadcasted_iota(jnp.int32, (1, 128), 1)
    seat = lax.broadcasted_iota(jnp.int32, (512, 128), 0)
    spot = lax.broadcasted_iota(jnp.int32, (512, 128), 1)
    hidden_key = jnp.where((spot == 96) & (seat >= length[0]), -1e30, 0.0)
    kx[...] = jnp.where(spot < 96, 1.0, hidden_key).astype(BF)
    one_lane = jnp.where(spot == 96, 1.0, 0.0).astype(BF)
    rows_a[...] = jnp.zeros_like(rows_a)
    rows_b[...] = jnp.zeros_like(rows_b)

    def head_places(h):
        group = pl.ds(pl.multiple_of(lax.div(h, 8) * 128, 128), 128)
        mine = jnp.where(lax.div(lane, 16) == lax.rem(h, 8), 1.0, 0.0).astype(BF)
        extra = jnp.where((lax.rem(lane, 32) == h) & (lane < 96) | (lane == 96), 1.0, 0.0).astype(BF)
        return group, mine, extra, pl.ds(pl.multiple_of(h * 16, 16), 16)

    def keys_of(group):
        return jnp.concatenate([k[:, group], kx[...]], axis=1)

    def note(h, value):
        hi, mid, lo = three(value)
        rows_a[pl.ds(h, 1), :] = hi
        rows_a[pl.ds(h + 32, 1), :] = mid
        rows_a[pl.ds(h + 64, 1), :] = lo

    def score_head(h, slot):
        group, mine, extra, channels = head_places(h)
        asks = jnp.concatenate([q[:, group] * mine, one_lane], axis=1)
        scores[slot] = mm_nt(keys_of(group), asks)

    def forward_head(h, slot):
        group, mine, extra, channels = head_places(h)
        peak = jnp.max(scores[slot], axis=0, keepdims=True)
        e = jnp.exp(scores[slot] - peak).astype(BF)
        got = mm(v_t[h], e)
        summed = got[16:17, :]
        mixed_t[channels, :] = got[0:16, :] / summed
        note(h, -(peak + jnp.log(summed)))

    def forward_pair(n, _):
        score_head(n * 2 + 1, 1)
        forward_head(n * 2, 0)
        score_head(lax.rem(n * 2 + 2, 32), 0)
        forward_head(n * 2 + 1, 1)
        return 0

    def two_heads(body):
        def pair(n, _):
            for j in range(2):
                body(n * 2 + j)
            return 0

        return pair

    rows_a[96:97, :] = jnp.ones((1, 512), F32)
    score_head(0, 0)
    lax.fori_loop(0, 4, forward_pair, 0)
    for i in both:
        finish(i, 1)
        begin(i, 2)
    lax.fori_loop(4, 10, forward_pair, 0)
    for i in both:
        relay(i, 2)
    lax.fori_loop(10, 16, forward_pair, 0)
    for i in both:
        finish(i, 2)
    xa[...] = rows_a[...].T.astype(BF)
    mixed[...] = mixed_t[...].T.astype(BF)

    big[...] = mm(mixed[...], wide_block(w1, 16))

    def after(r):
        here = first[r, :] + big[r, :] + row(V_OUT)
        second[r, :] = here
        hat, rstd = normalize(here)
        hat2[r, :] = hat
        rstd2[r, :] = rstd
        n2[r, :] = (hat * row(V_GAIN2) + row(V_SHIFT2)).astype(BF)
        gain(V_RED, go[r, :].astype(F32))

    over_rows(after)
    n2_t[...] = n2[...].T
    acc[...] = jnp.zeros_like(acc)
    acc2[...] = jnp.zeros_like(acc2)
    for i in both:
        crossed(i)

    def chunk(c, _):
        up = jnp.concatenate([up_blocks[4 * c + j] for j in range(4)], axis=1)
        span = pl.ds(pl.multiple_of(c * 512, 512), 512)
        down = down_rows[span, :]
        big[...] = mm(n2[...], up)
        da[...] = mm_nt(go[...], down)

        def gelu_rows(r):
            value, slope = gelu_both(big[r, :] + xb[pl.ds(c, 1), :])
            act[r, :] = value.astype(BF)
            low = (da[r, :] * slope).astype(BF)
            dh[r, :] = low
            gv[pl.ds(12 + c, 1), :] += total(low.astype(F32))

        over_rows(gelu_rows, 128)
        acc[...] += mm(act[...], down)
        acc2[...] += mm_nt(dh[...], up)
        g_down[span, :] = mm_tn(act[...], go[...]).astype(BF)
        grad_up = mm(n2_t[...], dh[...])
        for j in range(4):
            g_up[4 * c + j] = grad_up[:, 128 * j : 128 * (j + 1)].astype(BF)
        return 0

    lax.fori_loop(0, 4, chunk, 0)
    lent = [lend(0, sib_up), lend(1, sib_down)]

    def before_mlp(r):
        result[r, :] = (second[r, :] + acc[r, :] + row(V_RED)).astype(BF)
        grad = acc2[r, :]
        hat = hat2[r, :]
        gain(V_GAIN2, grad * hat)
        gain(V_SHIFT2, grad)
        here = go[r, :].astype(F32) + norm_pull(hat, rstd2[r, :], row(V_GAIN2), grad)
        second[r, :] = here
        low = here.astype(BF)
        dn[r, :] = low
        gain(V_OUT, low.astype(F32))

    over_rows(before_mlp)
    out_copies = bring(((result, result_out),), out_sem)
    put_wide(g1, 16, mm_tn(mixed[...], dn[...]))
    d_mixed[...] = mm_nt(dn[...], wide_block(w1, 16)).astype(BF)
    big[...] = d_mixed[...].astype(F32).T
    state = {0: start(0, 0, lent[0], sib_up), 1: start(1, 0, lent[1], sib_down)}

    def inner(h, _):
        channels = pl.ds(pl.multiple_of(h * 16, 16), 16)
        hi, mid, lo = three(-total(big[channels, :] * mixed_t[channels, :]))
        rows_b[pl.ds(h, 1), :] = hi
        rows_b[pl.ds(h + 32, 1), :] = mid
        rows_b[pl.ds(h + 64, 1), :] = lo
        return 0

    lax.fori_loop(0, 32, inner, 0)
    ya[...] = rows_b[...].T.astype(BF)
    dk[...] = jnp.zeros_like(dk)
    dv[...] = jnp.zeros_like(dv)
    ones = jnp.where(spot < 96, 1.0, 0.0).astype(BF)

    def backward_head(h):
        group, mine, extra, channels = head_places(h)
        q_h = q[:, group] * mine
        m_h = d_mixed[:, group] * mine
        p = jnp.exp(mm_nt(keys_of(group), jnp.concatenate([q_h, xa[...] * extra], axis=1)))
        values = jnp.concatenate([v[:, group], ones], axis=1)
        slope = mm_nt(values, jnp.concatenate([m_h, ya[...] * extra], axis=1))
        ds = (p * slope).astype(BF)
        dv[:, group] += mm(p.astype(BF), m_h)
        dk[:, group] += mm(ds, q_h)
        dq_t[channels, :] = mm(k_t[channels, :], ds)

    backward_heads = two_heads(backward_head)
    lax.fori_loop(0, 4, backward_heads, 0)
    for i in both:
        middle(i, 0, state[i])
    lax.fori_loop(4, 8, backward_heads, 0)
    for i in both:
        close(i, 0, state[i])
        state[i] = start(i, 1)
    lax.fori_loop(8, 11, backward_heads, 0)
    for i in both:
        middle(i, 1, state[i])
    lax.fori_loop(11, 13, backward_heads, 0)
    for i in both:
        close(i, 1, state[i])
        state[i] = start(i, 2)
    lax.fori_loop(13, 16, backward_heads, 0)
    for i in both:
        middle(i, 2, state[i])
    q[...] = (0.25 * dq_t[...].T).astype(BF)
    k[...] = dk[...].astype(BF)
    v[...] = dv[...].astype(BF)
    gain(V_QUERY, q[...].astype(F32))
    gain(V_VALUE, v[...].astype(F32))
    put_wide(g1, 4, mm(normed_t[...], q[...]))
    put_wide(g1, 8, mm(normed_t[...], k[...]))
    put_wide(g1, 12, mm(normed_t[...], v[...]))
    for i in both:
        close(i, 2, state[i])
    o2[...] = g_down.reshape((4, 4, 2, 4, 16, 512))[at["x"], at["y"], at["c"], at["z"]].astype(F32)
    rows_up = g_up.reshape((4, 4, 4, 4, 2, 16, 128))[at["z"], :, at["x"], at["y"], at["c"]].astype(F32)
    swaps = swap_rows(rows_up, post, postr, at, swap_s, swap_r, pending)
    acc2[...] = (
        mm_nt(q[...], wide_block(w1, 4)) + mm_nt(k[...], wide_block(w1, 8)) + mm_nt(v[...], wide_block(w1, 12))
    )

    def before_attention(r):
        grad = acc2[r, :]
        hat = hat1[r, :]
        gain(V_GAIN1, grad * hat)
        gain(V_SHIFT1, grad)
        here = second[r, :] + norm_pull(hat, rstd1[r, :], row(V_GAIN1), grad)
        first_grad[r, :] = here
        hat = hat0[r, :]
        gain(V_GAIN0, here * hat)
        gain(V_SHIFT0, here)
        low = norm_pull(hat, rstd0[r, :], row(V_GAIN0), here).astype(BF)
        dn[r, :] = low
        gain(V_ENC, low.astype(F32))

    over_rows(before_attention)
    put_wide(g1, 0, mm_tn(conv[...], dn[...]))
    out_copies += bring(((g1, g1_out), (first_grad, first_grad_out)), out_sem, 1)
    conv_grad[...] = mm_nt(dn[...], wide_block(w1, 0)).astype(BF)
    out_copies += bring(((conv_grad, conv_grad_out),), out_sem, 3)
    gain(V_CONV, conv_grad[...].astype(F32))
    lane_to = lax.broadcasted_iota(jnp.int32, (128, 512), 1)
    lane_from = lax.broadcasted_iota(jnp.int32, (128, 512), 0)
    shuffle = jnp.where(lane_from == lax.div(lane_to, 16) * 4 + lax.rem(lane_to, 4), 1.0, 0.0).astype(BF)
    which = lax.div(lax.rem(lax.broadcasted_iota(jnp.int32, (16, 512), 1), 16), 4)
    level = lax.broadcasted_iota(jnp.int32, (16, 512), 0) - 12
    for x in range(4):
        chosen = jnp.where(which == level, jnp.broadcast_to(gv[12 + x : 13 + x, :], (16, 512)), 0.0)
        hi, mid, lo = three(chosen)
        dealt_rows = (
            mm_nt(hi.astype(BF), shuffle) + mm_nt(mid.astype(BF), shuffle) + mm_nt(lo.astype(BF), shuffle)
        )
        gv_tiles[x, 0:12, :] = gv[0:12, 128 * x : 128 * (x + 1)]
        gv_tiles[x, 12:16, :] = dealt_rows[12:16, :]
    out_copies += bring(((gv_tiles, gv_out),), out_sem, 4)
    swapped_rows(swaps, post, postr, at, o1)
    for copy in pending:
        copy.wait_send()
    for copy in out_copies:
        copy.wait()


def block(length, conv, ordered, go, w1, up_own, down_own, vec, xb):
    shape = jax.ShapeDtypeStruct
    full = (512, 512)
    f, b, col = pltpu.VMEM(full, F32), pltpu.VMEM(full, BF), pltpu.VMEM((512, 1), F32)
    rows, lanes = pltpu.VMEM((128, 512), F32), pltpu.VMEM((512, 128), BF)
    dma = pltpu.SemaphoreType.DMA
    return pl.pallas_call(
        block_kernel,
        out_shape=(
            shape(full, BF),
            shape(full, F32),
            shape(full, BF),
            shape((20, 512, 128), BF),
            shape((4, 16, 128), F32),
            shape((4, 4, 4, 128), F32),
            shape((16, 512), F32),
        ),
        in_specs=[SM] + [ANY] * 8,
        out_specs=[ANY] * 5 + [VM] * 2,
        scratch_shapes=[
            b, b, b, pltpu.VMEM((20, 512, 128), BF), pltpu.VMEM((4, 16, 128), BF), pltpu.VMEM((16, 512), BF),
            pltpu.VMEM((16, 512), F32), pltpu.VMEM((4, 512), F32),
            b, f, b, pltpu.VMEM((20, 512, 128), BF), pltpu.VMEM((16, 512), F32), pltpu.VMEM((4, 16, 128), F32),
            f, f, col, f, f, col, b, b, b, b, b, b, pltpu.VMEM((32, 32, 512), BF),
            f, b, rows, rows, lanes, lanes, lanes, f, col, b, b,
            f, b, b, f, f, f, b, b, f, f, f, pltpu.VMEM((2, 512, 512), F32),
            pltpu.VMEM((4, 4, 4, 4, 2, 16, 128), BF),
            pltpu.VMEM((4, 4, 2, 4, 16, 512), BF),
            pltpu.VMEM((16, 512, 128), BF),
            pltpu.VMEM((2048, 512), BF),
            pltpu.VMEM((4, 4, 4, 4, 16, 128), BF),
            pltpu.VMEM((4, 4, 4, 16, 512), BF),
        ]
        + [pltpu.VMEM(s, BF) for chain in BLOCK_CHAINS for s in landing_shapes(chain)]
        + [
            pltpu.VMEM((4, 4, 4, 128), BF),
            pltpu.VMEM((4, 4, 4, 128), BF),
            dma((2, SLOTS)),
            dma((2, SLOTS)),
            dma((2, 2)),
            dma((2, 22)),
            dma((2, 22)),
            dma((4,)),
            dma((4,)),
            dma((8,)),
            dma((5,)),
        ],
        compiler_params=pltpu.CompilerParams(
            collective_id=2, has_side_effects=True, vmem_limit_bytes=62 * 2**20
        ),
        name="block",
    )(length, conv, ordered, go, w1, up_own, down_own, vec, xb)


def spread_rows(picks, j, b):
    seat = lax.broadcasted_iota(jnp.int32, (512, 256), 0)
    return jnp.where(seat == picks[j : j + 1, 256 * b : 256 * (b + 1)], 1.0, 0.0).astype(BF)


def line_neighbour(at, step):
    linear = lax.rem(((at["x"] * 4 + at["y"]) * 2 + at["c"]) * 4 + at["z"] + step, 128)
    return (lax.div(linear, 4), lax.rem(linear, 4))


def device_after(me, s):
    linear = lax.rem(me + s, 128)
    return (lax.div(linear, 4), lax.rem(linear, 4))


def deal(rows, landing, me, send, recv):
    def one(s, _):
        pltpu.make_async_remote_copy(
            src_ref=rows.at[lax.rem(me + s, 128)],
            dst_ref=landing.at[me],
            send_sem=send,
            recv_sem=recv,
            device_id=device_after(me, s),
            device_id_type=MESH,
        ).start()
        return 0

    lax.fori_loop(1, 128, one, 0)
    landing[me] = rows[me]


def dealt(rows, landing, me, send, recv):
    return pltpu.make_async_remote_copy(
        src_ref=rows.at[pl.ds(0, 127)],
        dst_ref=landing.at[pl.ds(0, 127)],
        send_sem=send,
        recv_sem=recv,
        device_id=device_after(me, 1),
        device_id_type=MESH,
    )


def fold_rows(index, rows, out):
    for n in range(4):
        seat = lax.broadcasted_iota(jnp.int32, (256, 512), 0) + 256 * n
        hot = jnp.where(seat == index, 1.0, 0.0).astype(BF)
        out[32 * n : 32 * (n + 1)] = mm(hot, rows).reshape(32, 8, 512).astype(BF)


def unfold_rows(index, blocks):
    seat = lax.broadcasted_iota(jnp.int32, (1024, 512), 0)
    hot = jnp.where(seat == index, 1.0, 0.0).astype(BF)
    return mm_tn(hot, blocks[...].astype(F32).reshape(1024, 512).astype(BF)).astype(BF)


def column_of(row):
    return jnp.broadcast_to(row, (128, 512)).T[:, 0:1]


def front_kernel(
    conv_in, encode_in, triple_in, output_in, expand_in, small_in, points_in, inverse_in, perm_in, neighbours_in,
    gc, g1, up_out, picked, conv_out, ordered_out, vectors_out, natural_out, take_out, send_out, picks_out,
    encode, triple, output, expand, small, points, inverse, perm, neighbours, conv,
    up_own, conv_low, ordered, vectors, natural, take, send, picks,
    outgoing, incoming, m1p, vt,
    extended, all_picks, acc, w_buf, pick_cols, pre, m1b, prev, vb, gv,
    sends, recvs, locs, presend, prerecv, halo_s, halo_r, p_sem, w_sem, deal_s, deal_r, met, in_sem, out_sem,
):
    at = place()
    width = 512
    me = ((at["x"] * 4 + at["y"]) * 2 + at["c"]) * 4 + at["z"]
    greet_lines(at)
    fetched = bring(
        (
            (encode_in, encode), (triple_in, triple), (output_in, output), (expand_in, expand), (small_in, small),
            (conv_in, conv), (points_in, points), (inverse_in, inverse), (perm_in, perm), (neighbours_in, neighbours),
        ),
        in_sem,
    )
    for copy in fetched[:6]:
        copy.wait()
    for first_block, per, base, refs in (
        (0, 5, 0, ((encode, 4), (triple, 12), (output, 4))), (0, 4, 5, ((expand, 16),))
    ):
        n = 0
        for ref, blocks in refs:
            for j in range(blocks):
                m1p[n // per, base + n % per] = ref[:, 128 * j : 128 * (j + 1)]
                n += 1
    row64 = lax.broadcasted_iota(jnp.int32, (16, 64), 0)
    lane64 = lax.broadcasted_iota(jnp.int32, (16, 64), 1)
    alone = jnp.where(lax.div(lane64, 4) == row64, jnp.broadcast_to(small[...], (16, 64)), 0.0).astype(BF)
    from64 = lax.broadcasted_iota(jnp.int32, (64, 128), 0)
    to128 = lax.broadcasted_iota(jnp.int32, (64, 128), 1)
    lane0 = lax.rem(at["y"] * 2 + at["c"], 8) * 16 + at["z"] * 4
    vt[...] = mm(alone, jnp.where(to128 == lane0 + lax.rem(from64, 4), 1.0, 0.0).astype(BF)).astype(BF)
    meet_lines()
    tell_line(at, "x", met.at[0])
    pending = []

    def own_view(i, h):
        name, op, view, order, halves = FRONT_STREAMS[i]
        if op == 0:
            return conv.at[pl.ds(h[0], h[1] - h[0]), :]
        return m1b.at[pl.ds(h[0], h[1] - h[0])] if op == 1 else vb

    begin, relay, finish, crossed = gather_steps(
        FRONT_STREAMS, own_view, (gc, g1, gv), at, sends, recvs, locs, pending
    )

    def remote(src, dst, send, recv, device):
        copy = remote_copy(src, dst, send, recv, device)
        copy.start()
        pending.append(copy)
        return copy

    pre_copies = []
    for step in (1, 2, 3):
        to = moved(at, "z", step)
        for j, (src, dst) in enumerate(((m1p.at[to["z"]], pre.at[step]), (vt, prev.at[step]))):
            pre_copies.append(remote(src, dst, presend.at[j, step], prerecv.at[j, step], device_at(to)))
    first, more = (0, 1, 2), (3, 4)
    for i in first:
        begin(i, 0)
    for copy in fetched[6:]:
        copy.wait()
    home = lax.div(inverse[...], width)
    row_id = lax.broadcasted_iota(jnp.int32, (width, width), 0)
    lane_id = lax.broadcasted_iota(jnp.int32, (width, width), 1)
    ahead = jnp.where((column_of(home.astype(F32)) == home.astype(F32)) & (row_id < lane_id), 1.0, 0.0)
    send[...] = home * 8 + total(ahead).astype(jnp.int32)
    pl.semaphore_wait(met.at[0], 3)
    tell_line(at, "y", met.at[1])
    fold_rows(send[...], points[...], outgoing)
    pl.semaphore_wait(met.at[1], 3)
    tell_line(at, "c", met.at[2])
    for copy in pre_copies:
        copy.wait_recv()
    pre[0] = m1p[at["z"]]

    def tile(k, _):
        pieces = [pre[lax.rem(at["z"] - s + 4, 4), k].astype(F32) for s in range(4)]
        m1b[k] = jnp.concatenate(pieces, axis=0).astype(BF)
        return 0

    lax.fori_loop(0, 9, tile, 0)
    vb[...] = (
        vt[...].astype(F32) + prev[1].astype(F32) + prev[2].astype(F32) + prev[3].astype(F32)
    ).astype(BF)
    up_own[...] = m1b[5:9]
    for i in more:
        begin(i, 0)
    pl.semaphore_wait(met.at[2], 1)
    deal(outgoing, incoming, me, deal_s, deal_r)
    for i in first + more:
        finish(i, 0)
        begin(i, 1)
    source = lax.div(perm[...], width)
    column = column_of(perm[...].astype(F32))
    source_column = lax.div(column.astype(jnp.int32), width)
    ahead = jnp.where((source_column == source) & (column < perm[...].astype(F32)), 1.0, 0.0)
    take[...] = source * 8 + total(ahead).astype(jnp.int32)
    token = lax.broadcasted_iota(jnp.int32, (1, width), 1)
    shift = me * width - 128 + lax.div(token, 256) * 256

    for u in range(9):
        raw = neighbours[3 * u : 3 * u + 3, :]
        local = jnp.where(raw >= 0, raw - shift, -1)
        picks[u] = local
        pick_cols[u] = jnp.concatenate([local, local, local[0:2]], axis=0).astype(F32)
    out_copies = bring(((up_own, up_out), (take, take_out), (send, send_out), (picks, picks_out)), out_sem)
    for i in first + more:
        relay(i, 1)
    for i in first:
        finish(i, 1)
        begin(i, 2)
    acc[...] = jnp.zeros_like(acc)
    for i in more:
        finish(i, 1)
    dealt(outgoing, incoming, me, deal_s, deal_r).wait_recv()
    mine = unfold_rows(take[...], incoming)
    ordered[...] = mine
    out_copies += bring(((ordered, ordered_out),), out_sem, 4)
    extended[128:640, :] = mine
    halos = []
    for j, (src, dst, step) in enumerate(((128, 640, 127), (512, 0, 1))):
        halos.append(
            remote(
                extended.at[pl.ds(src, 128), :], extended.at[pl.ds(dst, 128), :],
                halo_s.at[j], halo_r.at[j], line_neighbour(at, step),
            )
        )

    def p_copy(u):
        return pltpu.make_async_copy(all_picks.at[pl.ds(u * 3, 3)], picked.at[pl.ds(u * 3, 3)], p_sem.at[u])

    def pick_unit(u, _):
        columns = pick_cols[u].T
        for j in range(3):
            for b in range(2):
                seat = lax.broadcasted_iota(jnp.int32, (256, 512), 1).astype(F32)
                hot = jnp.where(seat == columns[256 * b : 256 * (b + 1), j : j + 1], 1.0, 0.0).astype(BF)
                window = extended[256 * b : 256 * b + 512, :]
                all_picks[u * 3 + j, 256 * b : 256 * (b + 1), :] = mm(hot, window).astype(BF)
        p_copy(u).start()
        return 0

    def w_copy(u):
        slot = lax.rem(u, 2)
        return pltpu.make_async_copy(
            gc.reshape((4, 27, 512, 128)).at[:, pl.ds(u * 3, 3)], w_buf.at[slot], w_sem.at[slot]
        )

    def conv_unit(u, _):
        @pl.when(u < 8)
        def _():
            w_copy(u + 1).start()

        w_copy(u).wait()
        slot = lax.rem(u, 2)
        parts = [
            mm(all_picks[u * 3 + j], jnp.concatenate([w_buf[slot, n, j] for n in range(4)], axis=1))
            for j in range(3)
        ]
        acc[...] += parts[0] + parts[1] + parts[2]
        return 0

    for i in first:
        relay(i, 2)
    for i in (3,):
        begin(i, 2)
    for copy in halos:
        copy.wait_recv()
    lax.fori_loop(0, 5, pick_unit, 0)
    for i in (3,):
        relay(i, 2)
    lax.fori_loop(5, 9, pick_unit, 0)
    for i in first:
        finish(i, 2)
    for i in first:
        crossed(i)
    w_copy(0).start()
    lax.fori_loop(0, 6, conv_unit, 0)
    for i in (3,):
        finish(i, 2)
    lax.fori_loop(6, 9, conv_unit, 0)
    for i in more:
        crossed(i)
    chunks = []
    for x in range(4):
        chunk = jnp.zeros((16, 128), F32)
        for y in range(4):
            for c in range(2):
                chunk = chunk + gv[x, y, c].astype(F32)
        chunks.append(chunk)
    together = jnp.concatenate(chunks, axis=1)
    vectors[...] = together
    lane = lax.broadcasted_iota(jnp.int32, (128, width), 1)
    from_lane = lax.broadcasted_iota(jnp.int32, (128, width), 0)
    shuffle = jnp.where(from_lane == lax.div(lane, 16) * 4 + lax.rem(lane, 4), 1.0, 0.0).astype(BF)
    which = lax.div(lax.rem(lax.broadcasted_iota(jnp.int32, (4, width), 1), 16), 4)
    group = lax.broadcasted_iota(jnp.int32, (4, width), 0)
    for x in range(4):
        spreaded = mm(chunks[x].astype(BF), shuffle)[12:16, :]
        natural[x : x + 1, :] = total(jnp.where(which == group, spreaded, 0.0))
    conv_low[...] = (acc[...] + together[0:1, :]).astype(BF)
    out_copies += bring(((conv_low, conv_out), (vectors, vectors_out), (natural, natural_out)), out_sem, 5)
    for copy in pending:
        copy.wait_send()
    dealt(outgoing, incoming, me, deal_s, deal_r).wait_send()

    def stored(u, _):
        p_copy(u).wait()
        return 0

    lax.fori_loop(0, 9, stored, 0)
    for copy in out_copies:
        copy.wait()


def front(conv, encode, triple, output, expand, small, points, inverse, perm, neighbours):
    shape = jax.ShapeDtypeStruct
    n = len(FRONT_STREAMS)
    dma = pltpu.SemaphoreType.DMA
    i32 = jnp.int32
    kept = (
        ((4, 16, 128), BF),
        ((512, 512), BF),
        ((512, 512), BF),
        ((16, 512), F32),
        ((4, 512), F32),
        ((1, 512), i32),
        ((1, 512), i32),
        ((9, 3, 512), i32),
    )
    return pl.pallas_call(
        front_kernel,
        out_shape=(
            shape((4, 4, 4, 2, 432, 128), BF),
            shape((4, 5, 4, 4, 2, 16, 128), BF),
            shape(*kept[0]),
            shape((27, 512, 512), BF),
        )
        + tuple(shape(*k) for k in kept[1:]),
        in_specs=[ANY] * 10,
        out_specs=[ANY] * 11,
        scratch_shapes=[
            pltpu.VMEM((4, 512), BF),
            pltpu.VMEM((4, 1536), BF),
            pltpu.VMEM((4, 512), BF),
            pltpu.VMEM((4, 2048), BF),
            pltpu.VMEM((1, 64), F32),
            pltpu.VMEM((512, 512), BF),
            pltpu.VMEM((1, 512), i32),
            pltpu.VMEM((1, 512), i32),
            pltpu.VMEM((27, 512), i32),
            pltpu.VMEM((432, 128), BF),
        ]
        + [pltpu.VMEM(*k) for k in kept]
        + [
            pltpu.VMEM((128, 8, 512), BF),
            pltpu.VMEM((128, 8, 512), BF),
            pltpu.VMEM((4, 9, 4, 128), BF),
            pltpu.VMEM((16, 128), BF),
            pltpu.VMEM((768, 512), BF),
            pltpu.VMEM((27, 512, 512), BF),
            pltpu.VMEM((512, 512), F32),
            pltpu.VMEM((2, 4, 3, 512, 128), BF),
            pltpu.VMEM((9, 8, 512), F32),
            pltpu.VMEM((4, 9, 4, 128), BF),
            pltpu.VMEM((9, 16, 128), BF),
            pltpu.VMEM((4, 16, 128), BF),
            pltpu.VMEM((16, 128), BF),
            pltpu.VMEM((4, 4, 2, 16, 128), BF),
            dma((n, SLOTS)),
            dma((n, SLOTS)),
            dma((n, 2)),
            dma((2, 4)),
            dma((2, 4)),
            dma((2,)),
            dma((2,)),
            dma((9,)),
            dma((2,)),
            dma,
            dma,
            pltpu.SemaphoreType.REGULAR((3,)),
            dma((10,)),
            dma((8,)),
        ],
        compiler_params=pltpu.CompilerParams(
            collective_id=0, has_side_effects=True, vmem_limit_bytes=56 * 2**20
        ),
        name="front",
    )(conv, encode, triple, output, expand, small, points, inverse, perm, neighbours)


BACK_CHAINS = (
    ("cz", "zxycRL", {"R": 96, "L": 128}, "R", 0, "zyx", ((0, 48), (48, 96))),
    ("cx", "zxycRL", {"R": 160, "L": 128}, "R", 96, "xzy", ((0, 80), (80, 160))),
    ("cy", "zxycRL", {"R": 176, "L": 128}, "R", 256, "yxz", ((0, 96), (96, 176))),
    ("wide", "zKxycSL", {"K": 5, "S": 16, "L": 128}, "K", 0, "zyx", ((0, 3), (3, 5))),
)


def back_kernel(
    grad_in, first_grad_in, take_in, picks_in, w, picked, g1, gv_in,
    arrived_out, oc, o1, ov,
    returning, arrived, wide, grad, first_grad, take, picks, gv,
    kernel_grad, theirs, spread, p_buf, w_buf, rims, landed, sib, *rest,
):
    count = 12 * len(BACK_CHAINS)
    landing, rest = rest[:count], rest[count:]
    post, postr, vx, vr, p_sem, w_sem, xy_send, xy_recv, sends, recvs, vsend, vrecv, psend, precv, rim_s, rim_r, deal_s, deal_r, met, in_sem = rest
    at = place()
    me = ((at["x"] * 4 + at["y"]) * 2 + at["c"]) * 4 + at["z"]
    greet_lines(at)
    fetched = bring(
        (
            (gv_in, gv), (g1, wide), (grad_in, grad), (picks_in, picks), (take_in, take),
            (first_grad_in, first_grad),
        ),
        in_sem,
    )
    meet_lines()
    tell_line(at, "x", met.at[0])
    other = moved(at, "c", 1)
    pending = []
    tiles = kernel_grad.reshape((4, 4, 4, 2, 432, 128))

    def push(src, dst, send, recv, to):
        copy = remote_copy(src, dst, send, recv, device_at(to))
        copy.start()
        pending.append(copy)
        return copy

    mine = (tiles, "zxycRL", {"c": at["c"]})
    stores = (mine, mine, mine, (wide, "zKxycSL", {"c": at["c"]}))
    lend, start, middle, close, view = scatter_steps(
        BACK_CHAINS, stores, landing, at, sends, recvs, pending
    )
    conv_chains = (0, 1, 2)

    def vector_step(k):
        axis, steps = (("c", (1,)), ("z", (1, 2, 3)), ("y", (1, 2, 3)), ("x", (1, 2, 3)))[k]
        copies = []
        for s in steps:
            to = moved(at, axis, s)
            if axis == "x":
                src, dst = vx.at[3, to["x"]], vr.at[3, s, 0]
            else:
                src, dst = (gv if k == 0 else vx.at[k]), vr.at[k, s]
            copies.append(push(src, dst, vsend.at[k, s], vrecv.at[k, s], to))
        return copies

    def vector_add(k, copies):
        for copy in copies:
            copy.wait_recv()
        if k == 3:
            ov[...] = vx[3, at["x"]] + vr[3, 1, 0] + vr[3, 2, 0] + vr[3, 3, 0]
            return
        sum_now = gv[...] if k == 0 else vx[k]
        for s in (1,) if k == 0 else (1, 2, 3):
            sum_now = sum_now + vr[k, s]
        vx[k + 1] = sum_now

    def p_copy(u):
        slot = lax.rem(u, 2)
        return pltpu.make_async_copy(picked.at[pl.ds(u * 3, 3)], p_buf.at[slot], p_sem.at[slot])

    def w_copy(u):
        slot = lax.rem(u, 2)
        return pltpu.make_async_copy(w.at[:, pl.ds(u * 3, 3)], w_buf.at[slot], w_sem.at[slot])

    def xy_copy(n):
        x, y = lax.div(n, 4), lax.rem(n, 4)
        return remote_copy(
            tiles.at[:, x, y, other["c"]], theirs.at[:, x, y], xy_send.at[n], xy_recv.at[n], device_at(other)
        )

    def join(n):
        x, y = lax.div(n, 4), lax.rem(n, 4)
        xy_copy(n).wait_recv()
        where = tiles.at[:, x, y, at["c"]]
        where[...] = where[...] + theirs[:, x, y]

    def weight_unit(u, _):
        @pl.when(u < 8)
        def _():
            p_copy(u + 1).start()

        p_copy(u).wait()
        for j in range(3):
            product = mm_tn(p_buf[lax.rem(u, 2), j], grad[...])
            span = pl.ds(pl.multiple_of(u * 1536 + j * 512, 512), 512)
            for n in range(4):
                kernel_grad[n, span, :] = product[:, 128 * n : 128 * (n + 1)].astype(BF)
        ready, ready_next = lax.div(u * 16, 9), lax.div((u + 1) * 16, 9)
        for j in range(2):
            @pl.when(ready + j < ready_next)
            def _():
                xy_copy(ready + j).start()

        for j in range(2):
            n = lax.div((u - 2) * 16, 9) + j

            @pl.when((u >= 2) & (n < lax.div((u - 1) * 16, 9)))
            def _():
                join(n)

        return 0

    def row_unit(u, _):
        @pl.when(u < 8)
        def _():
            w_copy(u + 1).start()

        w_copy(u).wait()
        slot = lax.rem(u, 2)
        g = grad[...]
        back = [
            mm_nt(g, jnp.concatenate([w_buf[slot, n, j] for n in range(4)], axis=1)).astype(BF)
            for j in range(3)
        ]
        for b in range(2):
            hot = jnp.concatenate([spread_rows(picks.at[u], j, b) for j in range(3)], axis=1)
            terms = jnp.concatenate([back[j][256 * b : 256 * (b + 1), :] for j in range(3)], axis=0)
            spread[256 * b : 256 * b + 512, :] += mm(hot, terms)
        return 0

    p_copy(0).start()
    spread[...] = jnp.zeros_like(spread)
    fetched[0].wait()
    vectors = vector_step(0)
    state = {}
    fetched[1].wait()
    lent = lend(3, sib)
    w_copy(0).start()
    for copy in fetched[2:]:
        copy.wait()
    lax.fori_loop(0, 3, weight_unit, 0)
    pl.semaphore_wait(met.at[0], 3)
    tell_line(at, "y", met.at[1])
    state[3] = start(3, 0, lent, sib)
    vector_add(0, vectors)
    vectors = vector_step(1)
    lax.fori_loop(3, 6, weight_unit, 0)
    pl.semaphore_wait(met.at[1], 3)
    tell_line(at, "c", met.at[2])
    for i in (3,):
        middle(i, 0, state[i])
    lax.fori_loop(6, 9, weight_unit, 0)
    pl.semaphore_wait(met.at[2], 1)
    vector_add(1, vectors)
    vectors = vector_step(2)
    for i in (3,):
        close(i, 0, state[i])
        state[i] = start(i, 1)
    lax.fori_loop(0, 2, row_unit, 0)
    for n in range(12, 16):
        join(n)
    for i in conv_chains:
        state[i] = start(i, 0)
    for i in (3,):
        middle(i, 1, state[i])
    lax.fori_loop(2, 4, row_unit, 0)
    vector_add(2, vectors)
    vectors = vector_step(3)
    for i in (3,):
        close(i, 1, state[i])
        state[i] = start(i, 2)
    lax.fori_loop(4, 6, row_unit, 0)
    for i in conv_chains:
        middle(i, 0, state[i])
    for i in (3,):
        middle(i, 2, state[i])
    lax.fori_loop(6, 9, row_unit, 0)
    rims[0] = spread[0:128, :].astype(BF)
    rims[1] = spread[640:768, :].astype(BF)
    rim_copies = []
    for j, step in ((0, 127), (1, 1)):
        copy = remote_copy(rims.at[j], landed.at[j], rim_s.at[j], rim_r.at[j], line_neighbour(at, step))
        copy.start()
        pending.append(copy)
        rim_copies.append(copy)
    for i in conv_chains:
        close(i, 0, state[i])
        state[i] = start(i, 1)
    for i in (3,):
        close(i, 2, state[i])
    vector_add(3, vectors)
    swaps = swap_rows(
        wide[at["z"], :, at["x"], at["y"], at["c"]].astype(F32), post, postr, at, psend, precv, pending
    )
    for copy in rim_copies:
        copy.wait_recv()
    spread[512:640, :] += landed[0].astype(F32)
    spread[128:256, :] += landed[1].astype(F32)
    ordered_grad = (first_grad[...] + spread[128:640, :]).astype(BF)
    fold_rows(take[...], ordered_grad, returning)
    deal(returning, arrived, me, deal_s, deal_r)
    for i in conv_chains:
        middle(i, 1, state[i])
    for i in conv_chains:
        close(i, 1, state[i])
        state[i] = start(i, 2)
    swapped_rows(swaps, post, postr, at, o1)
    for i in conv_chains:
        middle(i, 2, state[i])
    for i in conv_chains:
        close(i, 2, state[i])
        name, layout, plain, cut, base, order, halves = BACK_CHAINS[i]
        oc[pl.ds(base, plain["R"]), :] = tiles[at["z"], at["x"], at["y"], at["c"], pl.ds(base, plain["R"]), :].astype(F32)
    dealt(returning, arrived, me, deal_s, deal_r).wait_recv()
    last = pltpu.make_async_copy(arrived, arrived_out, in_sem.at[6])
    last.start()
    for copy in pending:
        copy.wait_send()
    for n in range(16):
        xy_copy(n).wait_send()
    dealt(returning, arrived, me, deal_s, deal_r).wait_send()
    last.wait()


def back_scatter(grad, first_grad, take, picks, w, picked, g1, gv):
    shape = jax.ShapeDtypeStruct
    n = len(BACK_CHAINS)
    dma = pltpu.SemaphoreType.DMA
    return pl.pallas_call(
        back_kernel,
        out_shape=(
            shape((128, 8, 512), BF),
            shape((432, 128), F32),
            shape((4, 5, 4, 128), F32),
            shape((16, 128), F32),
        ),
        in_specs=[ANY] * 8,
        out_specs=[ANY] + [VM] * 3,
        scratch_shapes=[
            pltpu.VMEM((128, 8, 512), BF),
            pltpu.VMEM((128, 8, 512), BF),
            pltpu.VMEM((4, 5, 4, 4, 2, 16, 128), BF),
            pltpu.VMEM((512, 512), BF),
            pltpu.VMEM((512, 512), F32),
            pltpu.VMEM((1, 512), jnp.int32),
            pltpu.VMEM((9, 3, 512), jnp.int32),
            pltpu.VMEM((4, 16, 128), F32),
            pltpu.VMEM((4, 13824, 128), BF),
            pltpu.VMEM((4, 4, 4, 432, 128), BF),
            pltpu.VMEM((768, 512), F32),
            pltpu.VMEM((2, 3, 512, 512), BF),
            pltpu.VMEM((2, 4, 3, 512, 128), BF),
            pltpu.VMEM((2, 128, 512), BF),
            pltpu.VMEM((2, 128, 512), BF),
            pltpu.VMEM((4, 5, 4, 4, 16, 128), BF),
        ]
        + [pltpu.VMEM(s, BF) for chain in BACK_CHAINS for s in landing_shapes(chain)]
        + [
            pltpu.VMEM((4, 5, 4, 128), BF),
            pltpu.VMEM((4, 5, 4, 128), BF),
            pltpu.VMEM((4, 4, 16, 128), F32),
            pltpu.VMEM((4, 4, 4, 16, 128), F32),
            dma((2,)),
            dma((2,)),
            dma((16,)),
            dma((16,)),
            dma((n, 22)),
            dma((n, 22)),
            dma((4, 4)),
            dma((4, 4)),
            dma((4,)),
            dma((4,)),
            dma((2,)),
            dma((2,)),
            dma,
            dma,
            pltpu.SemaphoreType.REGULAR((3,)),
            dma((7,)),
        ],
        compiler_params=pltpu.CompilerParams(
            collective_id=1, has_side_effects=True, vmem_limit_bytes=62 * 2**20
        ),
        name="back_scatter",
    )(grad, first_grad, take, picks, w, picked, g1, gv)


def last_kernel(
    arrived_in, send_in, result_in, oc_in, wide_in, up_in, tall_in, ov_in,
    result, points_grad, oc, tall, encode, triple, output, expand, small,
    arrived, send, wide, up, ov, rows, encode_v, triple_v, output_v, expand_v, small_v, result_v, oc_v, tall_v, in_sem, out_sem,
):
    through = bring(((result_in, result_v), (oc_in, oc_v), (tall_in, tall_v)), in_sem)
    fetched = bring(
        ((wide_in, wide), (up_in, up), (ov_in, ov), (send_in, send), (arrived_in, arrived)), in_sem, 3
    )
    at = place()
    fetched[0].wait()
    n = 0
    for ref, blocks in ((encode_v, 4), (triple_v, 12), (output_v, 4)):
        for j in range(blocks):
            ref[:, 128 * j : 128 * (j + 1)] = wide[n // 5, n % 5]
            n += 1
    out = bring(((encode_v, encode), (triple_v, triple), (output_v, output)), out_sem)
    fetched[1].wait()
    for j in range(16):
        expand_v[:, 128 * j : 128 * (j + 1)] = up[j // 4, j % 4]
    out += bring(((expand_v, expand),), out_sem, 3)
    fetched[2].wait()
    lane0 = lax.rem(at["y"] * 2 + at["c"], 8) * 16 + at["z"] * 4
    lane = lax.broadcasted_iota(jnp.int32, (128, 128), 0)
    to = lax.broadcasted_iota(jnp.int32, (128, 128), 1)
    pick = jnp.where((lane == lane0 + to) & (to < 4), 1.0, 0.0).astype(BF)
    hi, mid, lo = three(ov[...])
    small_v[...] = mm(hi.astype(BF), pick) + mm(mid.astype(BF), pick) + mm(lo.astype(BF), pick)
    out += bring(((small_v, small),), out_sem, 4)
    for copy in through:
        copy.wait()
    out += bring(((result_v, result), (oc_v, oc), (tall_v, tall)), out_sem, 6)
    fetched[3].wait()
    fetched[4].wait()
    rows[...] = unfold_rows(send[...], arrived)
    out += bring(((rows, points_grad),), out_sem, 5)
    for copy in out:
        copy.wait()


def last(arrived, send, result, oc, wide, up, tall, ov):
    shape = jax.ShapeDtypeStruct
    widths = (512, 1536, 512, 2048)
    return pl.pallas_call(
        last_kernel,
        out_shape=(
            shape((512, 512), BF),
            shape((512, 512), BF),
            shape((432, 128), F32),
            shape((16, 512), F32),
        )
        + tuple(shape((4, w), F32) for w in widths)
        + (shape((16, 128), F32),),
        in_specs=[ANY] * 8,
        out_specs=[ANY] * 9,
        scratch_shapes=[
            pltpu.VMEM((128, 8, 512), BF),
            pltpu.VMEM((1, 512), jnp.int32),
            pltpu.VMEM((4, 5, 4, 128), F32),
            pltpu.VMEM((4, 4, 4, 128), F32),
            pltpu.VMEM((16, 128), F32),
            pltpu.VMEM((512, 512), BF),
        ]
        + [pltpu.VMEM((4, w), F32) for w in widths]
        + [
            pltpu.VMEM((16, 128), F32),
            pltpu.VMEM((512, 512), BF),
            pltpu.VMEM((432, 128), F32),
            pltpu.VMEM((16, 512), F32),
            pltpu.SemaphoreType.DMA((8,)),
            pltpu.SemaphoreType.DMA((9,)),
        ],
        compiler_params=pltpu.CompilerParams(vmem_limit_bytes=60 * 2**20),
        name="last",
    )(arrived, send, result, oc, wide, up, tall, ov)


def per_device(
    points,
    perm,
    inverse,
    lengths,
    neighbours,
    conv_weight,
    conv_bias,
    encode_weight,
    encode_bias,
    encode_gain,
    encode_shift,
    before_gain,
    before_shift,
    triple_weight,
    query_bias,
    value_bias,
    output_weight,
    output_bias,
    second_gain,
    second_shift,
    expand_weight,
    expand_bias,
    reduce_weight,
    reduce_bias,
    grad_out,
):
    small = jnp.concatenate(
        [
            conv_bias,
            encode_bias,
            encode_gain,
            encode_shift,
            before_gain,
            before_shift,
            query_bias,
            value_bias,
            output_bias,
            second_gain,
            second_shift,
            reduce_bias,
            expand_bias,
        ]
    )
    kernel, wide, up_own, picked, conv, ordered, vectors, wide_bias, take, send, picks = front(
        conv_weight,
        encode_weight,
        triple_weight,
        output_weight,
        expand_weight,
        small.astype(F32).reshape(1, 64),
        points,
        inverse.reshape(1, 512),
        perm.reshape(1, 512),
        neighbours,
    )
    result, grad_first, grad_conv, grad_wide, vector_grads, up_out, tall_out = block(
        lengths,
        conv,
        ordered,
        grad_out,
        wide.reshape(20, 512, 128),
        up_own,
        reduce_weight,
        vectors,
        wide_bias,
    )
    arrived, kernel_out, wide_out, vector_out = back_scatter(
        grad_conv,
        grad_first,
        take,
        picks,
        kernel.reshape(4, 27, 512, 128),
        picked,
        grad_wide.reshape(4, 5, 4, 4, 2, 16, 128),
        vector_grads,
    )
    result, points_grad, kernel_out, tall_out, encode_out, triple_out, output_out, up_out, vector_out = last(
        arrived, send, result, kernel_out, wide_out, up_out, tall_out, vector_out
    )
    vector_out = vector_out[:, :4]
    reduced = (
        vector_out[V_CONV],
        encode_out,
        vector_out[V_ENC],
        vector_out[V_GAIN0],
        vector_out[V_SHIFT0],
        vector_out[V_GAIN1],
        vector_out[V_SHIFT1],
        triple_out,
        vector_out[V_QUERY],
        vector_out[V_VALUE],
        output_out,
        vector_out[V_OUT],
        vector_out[V_GAIN2],
        vector_out[V_SHIFT2],
        up_out,
        vector_out[12:].reshape(16),
        tall_out,
        vector_out[V_RED],
    )
    return (result, points_grad, kernel_out) + reduced


def solution(mesh):
    in_specs = (
        P(("pts", "rep"), None),
        P(("pts", "rep")),
        P(("pts", "rep")),
        P(("pts", "rep")),
        P(None, ("pts", "rep")),
        P("pts", "rep"),
        P(("pts", "rep")),
        P(("pts", "rep"), None),
        P(("pts", "rep")),
        P(("pts", "rep")),
        P(("pts", "rep")),
        P(("pts", "rep")),
        P(("pts", "rep")),
        P(("pts", "rep"), None),
        P(("pts", "rep")),
        P(("pts", "rep")),
        P(("pts", "rep"), None),
        P(("pts", "rep")),
        P(("pts", "rep")),
        P(("pts", "rep")),
        P(("pts", "rep"), None),
        P(("pts", "rep")),
        P(("pts", "rep"), None),
        P(("pts", "rep")),
        P(("pts", "rep"), None),
    )
    out_specs = (
        P(("pts", "rep"), None),
        P(("pts", "rep"), None),
        P("pts", "rep"),
        P(("pts", "rep")),
        P(("pts", "rep"), None),
        P(("pts", "rep")),
        P(("pts", "rep")),
        P(("pts", "rep")),
        P(("pts", "rep")),
        P(("pts", "rep")),
        P(("pts", "rep"), None),
        P(("pts", "rep")),
        P(("pts", "rep")),
        P(("pts", "rep"), None),
        P(("pts", "rep")),
        P(("pts", "rep")),
        P(("pts", "rep")),
        P(("pts", "rep"), None),
        P(("pts", "rep")),
        P(("pts", "rep"), None),
        P(("pts", "rep")),
    )
    return jax.shard_map(
        per_device, mesh=mesh, in_specs=in_specs, out_specs=out_specs, check_vma=False
    )
```

```python
import jax
import jax.numpy as jnp
from jax import lax
from jax.experimental import pallas as pl
from jax.experimental.pallas import tpu as pltpu
from jax.sharding import PartitionSpec as P

MESH = pl.DeviceIdType.MESH
BF = jnp.bfloat16
F32 = jnp.float32


def place():
    p = lax.axis_index("pts")
    return {
        "x": lax.div(p, 8),
        "y": lax.rem(lax.div(p, 2), 4),
        "c": lax.rem(p, 2),
        "z": lax.axis_index("rep"),
    }


def device_at(at):
    return ((at["x"] * 4 + at["y"]) * 2 + at["c"], at["z"])


def moved(at, axis, step):
    size = 2 if axis == "c" else 4
    return {**at, axis: lax.rem(at[axis] + step, size)}


def whole(value):
    return slice(None) if value is None else value


def conv_view(ref, sel, h):
    r0, r1 = h
    return ref.at[
        whole(sel.get("z")), whole(sel.get("x")), whole(sel.get("y")), sel["c"], pl.ds(r0, r1 - r0), :
    ]


def wide_view(ref, sel, h):
    k0, k1 = h
    return ref.at[
        whole(sel.get("z")), pl.ds(k0, k1 - k0), whole(sel.get("x")), whole(sel.get("y")), sel["c"]
    ]


def tall_view(ref, sel, h):
    l0, l1 = h
    return ref.at[
        whole(sel.get("x")), whole(sel.get("y")), sel["c"], whole(sel.get("z")), :, pl.ds(l0, l1 - l0)
    ]


def flat_view(ref, sel, h):
    return ref.at[whole(sel.get("x")), whole(sel.get("y")), sel["c"]]


FRONT_STREAMS = (
    ("cz", 0, conv_view, "xyz", ((0, 48), (48, 96))),
    ("cx", 0, conv_view, "yzx", ((96, 176), (176, 256))),
    ("cy", 0, conv_view, "zxy", ((256, 352), (352, 432))),
    ("wide", 1, wide_view, "xyz", ((0, 3), (3, 5))),
    ("vectors", 2, flat_view, "xy", ((0, 16),)),
)
SLOTS = 40


def greet_lines(at):
    barrier = pltpu.get_barrier_semaphore()
    for axis, steps in (("x", (1, 2, 3)), ("y", (1, 2, 3)), ("z", (1, 2, 3)), ("c", (1,))):
        for s in steps:
            pl.semaphore_signal(
                barrier, inc=1, device_id=device_at(moved(at, axis, s)), device_id_type=MESH
            )


def meet_lines():
    pl.semaphore_wait(pltpu.get_barrier_semaphore(), 10)


def tell_line(at, axis, sem):
    for s in (1,) if axis == "c" else (1, 2, 3):
        pl.semaphore_signal(sem, inc=1, device_id=device_at(moved(at, axis, s)), device_id_type=MESH)


def bring(pairs, sem, base=0):
    copies = [pltpu.make_async_copy(src, dst, sem.at[base + n]) for n, (src, dst) in enumerate(pairs)]
    for copy in copies:
        copy.start()
    return copies


def remote_copy(src, dst, send, recv, device):
    return pltpu.make_async_remote_copy(
        src_ref=src, dst_ref=dst, send_sem=send, recv_sem=recv, device_id=device, device_id_type=MESH
    )


def gather_steps(streams, own_view, outs, at, sends, recvs, locs, pending):
    other = moved(at, "c", 1)
    crossing = {i: [] for i in range(len(streams))}
    local_copies, state = {}, {}

    def push(src, dst, i, k, to):
        copy = remote_copy(src, dst, sends.at[i, k], recvs.at[i, k], device_at(to))
        copy.start()
        pending.append(copy)
        return copy

    def cross(ref, i, k):
        crossing[i].append(push(ref, ref, i, k, other))

    def keep_own(i):
        name, op, view, order, halves = streams[i]
        for j, h in enumerate(halves):
            copy = pltpu.make_async_copy(own_view(i, h), view(outs[op], at, h), locs.at[i, j])
            copy.start()
            local_copies[(i, j)] = copy

    def block_sel(order, phase, index=None):
        sel = {"c": at["c"]}
        for a in "xyz":
            if a in order and order.index(a) < phase:
                continue
            sel[a] = at[a]
        if index is not None:
            sel[order[phase]] = index
        return sel

    def begin(i, phase):
        name, op, view, order, halves = streams[i]
        axis = order[phase]
        n = len(halves)
        sel = block_sel(order, phase)
        copies = {}
        if phase == 0:
            keep_own(i)
            span = (halves[0][0], halves[-1][1])
            for d in (1, 3, 2):
                copies[d] = push(own_view(i, span), view(outs[op], sel, span), i, d, moved(at, axis, d))
        else:
            for d, hs in ((1, range(n)), (3, reversed(range(n)))):
                for h in hs:
                    ref = view(outs[op], sel, halves[h])
                    copies[(d, h)] = push(ref, ref, i, phase * 6 + (0 if d == 1 else 2) + h, moved(at, axis, d))
        state[(i, phase)] = copies
        if phase == len(order) - 1:
            for h in range(n):
                cross(view(outs[op], sel, halves[h]), i, 20 + h)

    def relay(i, phase):
        name, op, view, order, halves = streams[i]
        axis = order[phase]
        last = phase == len(order) - 1
        n = len(halves)
        copies = state[(i, phase)]
        for d in (1, 3) if n == 2 else (1,):
            h = 0 if d == 1 else n - 1
            copies[(d, h)].wait_recv()
            ref = view(outs[op], block_sel(order, phase, lax.rem(at[axis] + 4 - d, 4)), halves[h])
            copies[(d, "f")] = push(ref, ref, i, phase * 6 + (4 if d == 1 else 5), moved(at, axis, d))
            if last:
                cross(ref, i, 22 + d)

    def finish(i, phase):
        name, op, view, order, halves = streams[i]
        axis = order[phase]
        last = phase == len(order) - 1
        n = len(halves)
        copies = state[(i, phase)]
        if phase == 0:
            for d in (1, 3, 2):
                copies[d].wait_recv()
            for h in range(n):
                local_copies[(i, h)].wait()
            return
        for d in (1, 3):
            for h in range(n):
                if h == (0 if d == 1 else n - 1) and not (n == 1 and d == 3):
                    continue
                copies[(d, h)].wait_recv()
                if last:
                    sel = block_sel(order, phase, lax.rem(at[axis] + 4 - d, 4))
                    cross(view(outs[op], sel, halves[h]), i, 26 + d)
        for d in (1, 3):
            if (d, "f") not in copies:
                continue
            copies[(d, "f")].wait_recv()
            if last:
                h = 0 if d == 1 else n - 1
                sel = block_sel(order, phase, lax.rem(at[axis] + 2, 4))
                cross(view(outs[op], sel, halves[h]), i, 30 + d)

    def crossed(i):
        for copy in crossing[i]:
            copy.wait_recv()

    return begin, relay, finish, crossed


def cut_view(ref, layout, sel, cut=None, span=None, base=0):
    index = []
    for dim in layout:
        if dim in sel:
            index.append(sel[dim])
        elif dim == cut and span is not None:
            index.append(pl.ds(base + span[0], span[1] - span[0]))
        else:
            index.append(slice(None))
    return ref.at[tuple(index)]


def sizes_of(layout, plain):
    return tuple(plain[d] if d in plain else 4 for d in layout)


def landing_shapes(chain):
    name, layout, plain, cut, base, order, halves = chain
    left = layout.replace("c", "")
    shapes = []
    for axis in order:
        left = left.replace(axis, "")
        for span in halves:
            shapes.append(sizes_of(left, {**plain, cut: span[1] - span[0]}))
        shapes += [sizes_of(left, plain)] * 2
    return shapes


STEPS = (2, 1, 3, 0)


def scatter_steps(chains, stores, landing, at, sends, recvs, pending):
    other = moved(at, "c", 1)

    def push(src, dst, i, k, to):
        copy = remote_copy(src, dst, sends.at[i, k], recvs.at[i, k], device_at(to))
        copy.start()
        pending.append(copy)
        return copy

    def view(i, sel, span):
        name, layout, plain, cut, base, order, halves = chains[i]
        ref, inner, fixed = stores[i]
        return cut_view(ref, inner, {**fixed, **sel}, cut, span, base)

    def add(i, sel, srcs, span):
        name, layout, plain, cut, base, order, halves = chains[i]
        inner = layout.replace("c", "")
        free = [d for d in inner if d in "xyz" and d not in sel]
        tiles = span[1] - span[0]
        for d, size in plain.items():
            tiles = tiles if d == cut else tiles * size
        tiles = max(tiles // 2048, 1)
        while free and tiles * 4 <= 64:
            free.pop()
            tiles *= 4
        count = 4 ** len(free)

        def one(n, _):
            here = dict(sel)
            for k, d in enumerate(reversed(free)):
                here[d] = lax.rem(lax.div(n, 4**k), 4)
            where = view(i, here, span)
            terms = [
                cut_view(src, src_layout, {**{d: here[d] for d in free}, **src_sel}, cut, src_span)
                for src, src_layout, src_sel, src_span in srcs
            ]
            if len(terms) == 1:
                where[...] = where[...] + terms[0][...]
            else:
                where[...] = (
                    where[...].astype(F32) + terms[0][...].astype(F32) + terms[1][...].astype(F32)
                ).astype(BF)
            return 0

        if count == 1:
            one(0, 0)
        else:
            lax.fori_loop(0, count, one, 0)

    def lend(i, sib):
        name, layout, plain, cut, base, order, halves = chains[i]
        ref, inner, fixed = stores[i]
        axis, span = order[0], (0, plain[cut])
        copies = []
        for k, step in enumerate(STEPS):
            a = lax.rem(at[axis] + step, 4)
            far = cut_view(ref, inner, {"c": other["c"], axis: a}, cut, span, base)
            copies.append(push(far, cut_view(sib, layout.replace("c", ""), {axis: a}), i, k, other))
        return copies

    def names(i, phase):
        name, layout, plain, cut, base, order, halves = chains[i]
        inner = layout.replace("c", "")
        axis = order[phase]
        done = {a: at[a] for a in order[:phase]}
        left = "".join(d for d in inner if d not in order[: phase + 1])
        buffers = landing[i * 12 + 4 * phase : i * 12 + 4 * phase + 4]
        return inner, axis, done, left, buffers, 4 + phase * 6, cut, halves, (0, plain[cut])

    def start(i, phase, lent=None, sib=None):
        inner, axis, done, left, (r0, r1, rp, rm), slot, cut, halves, span = names(i, phase)
        up, down = moved(at, axis, 1), moved(at, axis, 3)
        got = {}
        for k, step in enumerate(STEPS):
            a = lax.rem(at[axis] + step, 4)
            if lent is not None:
                lent[k].wait_recv()
                add(i, {axis: a}, [(sib, inner, {axis: a}, span)], span)
            part = lambda h: view(i, {**done, axis: a}, h)
            if step == 2:
                got["r0"] = push(part(halves[0]), r0, i, slot, up)
                got["r1"] = push(part(halves[1]), r1, i, slot + 1, down)
            elif step == 1:
                got["p1"] = push(part(halves[1]), cut_view(rp, left, {}, cut, halves[1]), i, slot + 2, up)
            elif step == 3:
                got["m0"] = push(part(halves[0]), cut_view(rm, left, {}, cut, halves[0]), i, slot + 3, down)
        return got

    def middle(i, phase, got):
        inner, axis, done, left, (r0, r1, rp, rm), slot, cut, halves, span = names(i, phase)
        up, down = moved(at, axis, 1), moved(at, axis, 3)
        for key, h, buf, land, to, k in (("r0", 0, r0, rp, up, 4), ("r1", 1, r1, rm, down, 5)):
            half = halves[h]
            got[key].wait_recv()
            sel = {**done, axis: to[axis]}
            add(i, sel, [(buf, left, {}, (0, half[1] - half[0]))], half)
            got[k] = push(view(i, sel, half), cut_view(land, left, {}, cut, half), i, slot + k, to)

    def close(i, phase, got):
        inner, axis, done, left, (r0, r1, rp, rm), slot, cut, halves, span = names(i, phase)
        for k in ("p1", "m0", 4, 5):
            got[k].wait_recv()
        add(i, {**done, axis: at[axis]}, [(rp, left, {}, span), (rm, left, {}, span)], span)

    return lend, start, middle, close, view


def swap_rows(block, post, postr, at, send, recv, pending):
    for n in range(4):
        post[n] = block[:, 4 * n : 4 * n + 4, :].astype(BF)
    copies = []
    for s in (1, 2, 3):
        to = moved(at, "z", s)
        copy = remote_copy(post.at[to["z"]], postr.at[s], send.at[s], recv.at[s], device_at(to))
        copy.start()
        pending.append(copy)
        copies.append(copy)
    return copies


def swapped_rows(copies, post, postr, at, out):
    out[at["z"]] = post[at["z"]].astype(F32)
    for s in (1, 2, 3):
        copies[s - 1].wait_recv()
        out[lax.rem(at["z"] + 4 - s, 4)] = postr[s].astype(F32)


VM = pl.BlockSpec(memory_space=pltpu.VMEM)
ANY = pl.BlockSpec(memory_space=pl.ANY)
SM = pl.BlockSpec(memory_space=pltpu.SMEM)
epsilon = 1e-05


def mm(a, b):
    return lax.dot_general(a, b, (((1,), (0,)), ((), ())), preferred_element_type=F32)


def mm_nt(a, b):
    return lax.dot_general(a, b, (((1,), (1,)), ((), ())), preferred_element_type=F32)


def mm_tn(a, b):
    return lax.dot_general(a, b, (((0,), (0,)), ((), ())), preferred_element_type=F32)


def wide_block(ref, first, count=4):
    return jnp.concatenate([ref[first + k] for k in range(count)], axis=1)


def put_wide(ref, first, value, count=4):
    for k in range(count):
        ref[first + k] = value[:, 128 * k : 128 * (k + 1)].astype(BF)


V_CONV, V_ENC, V_GAIN0, V_SHIFT0, V_GAIN1, V_SHIFT1, V_QUERY, V_VALUE, V_OUT, V_GAIN2, V_SHIFT2, V_RED = range(12)


def over_rows(body, step=512, rows=512):
    def one(n, _):
        body(pl.ds(pl.multiple_of(n * step, step), step))
        return 0

    lax.fori_loop(0, rows // step, one, 0)


def normalize(v):
    mean = jnp.mean(v, axis=-1, keepdims=True)
    centred = v - mean
    spread = jnp.mean(centred * centred, axis=-1, keepdims=True)
    rstd = lax.rsqrt(spread + epsilon)
    return centred * rstd, rstd


def norm_pull(hat, rstd, gain, grad):
    up = grad * gain
    a = jnp.mean(up, axis=-1, keepdims=True)
    b = jnp.mean(up * hat, axis=-1, keepdims=True)
    return rstd * (up - a - hat * b)


def total(v):
    return jnp.sum(v, axis=0, keepdims=True)


def gelu_both(u):
    cdf = 0.5 * (1.0 + lax.erf(u * 0.7071067811865476))
    pdf = 0.3989422804014327 * jnp.exp(-0.5 * u * u)
    return u * cdf, cdf + u * pdf


def three(v):
    hi = v.astype(BF).astype(F32)
    rest = v - hi
    mid = rest.astype(BF).astype(F32)
    return hi, mid, rest - mid


BLOCK_STREAMS = (
    ("up", 0, wide_view, "xyz", ((0, 2), (2, 4))),
    ("down", 1, tall_view, "zyx", ((0, 256), (256, 512))),
)
BLOCK_CHAINS = (
    ("up", "zKxycSL", {"K": 4, "S": 16, "L": 128}, "K", 0, "zyx", ((0, 2), (2, 4))),
    ("down", "xyczSL", {"S": 16, "L": 512}, "L", 0, "xyz", ((0, 256), (256, 512))),
)


def block_kernel(
    length, conv_in, ordered_in, go_in, w1_in, up_own_in, down_own_in, vec_in, xb_in,
    result_out, first_grad_out, conv_grad_out, g1_out, gv_out, o1, o2,
    conv, ordered, go, w1, up_own, down_own, vec, xb, result, first_grad, conv_grad, g1, gv, gv_tiles,
    big, hat0, rstd0, first, hat1, rstd1, normed, normed_t, q, k, v, k_t, v_t,
    mixed_t, mixed, rows_a, rows_b, kx, xa, ya, hat2, rstd2, n2, n2_t,
    second, act, dh, da, acc, acc2, dn, d_mixed, dq_t, dk, dv, scores,
    up_all, down_all, g_up, g_down, sib_up, sib_down, *rest,
):
    landing = rest[:24]
    post, postr, sends, recvs, locs, back_s, back_r, swap_s, swap_r, in_sem, out_sem = rest[24:]
    at = place()
    greet_lines(at)
    fetched = bring(
        (
            (up_own_in, up_own), (down_own_in, down_own), (conv_in, conv), (w1_in, w1), (vec_in, vec),
            (ordered_in, ordered), (go_in, go), (xb_in, xb),
        ),
        in_sem,
    )
    meet_lines()
    for copy in fetched[:2]:
        copy.wait()
    pending = []
    own_view = lambda i, h: (
        up_own.at[pl.ds(h[0], h[1] - h[0])] if i == 0 else down_own.at[:, pl.ds(h[0], h[1] - h[0])]
    )
    begin, relay, finish, crossed = gather_steps(
        BLOCK_STREAMS, own_view, (up_all, down_all), at, sends, recvs, locs, pending
    )
    stores = (
        (g_up.reshape((4, 4, 4, 4, 2, 16, 128)), "zKxycSL", {"c": at["c"]}),
        (g_down.reshape((4, 4, 2, 4, 16, 512)), "xyczSL", {"c": at["c"]}),
    )
    lend, start, middle, close, view = scatter_steps(
        BLOCK_CHAINS, stores, landing, at, back_s, back_r, pending
    )
    both = (0, 1)
    up_blocks, down_rows = up_all.reshape((16, 512, 128)), down_all.reshape((2048, 512))
    for i in both:
        begin(i, 0)
    for copy in fetched[2:]:
        copy.wait()
    row = lambda n: vec[n : n + 1, :]
    gv[...] = jnp.zeros_like(gv)

    def gain(n, value):
        gv[n : n + 1, :] += total(value)

    big[...] = mm(conv[...], wide_block(w1, 0))
    for i in both:
        finish(i, 0)
        begin(i, 1)

    def encode(r):
        hat, rstd = normalize(big[r, :] + row(V_ENC))
        hat0[r, :] = hat
        rstd0[r, :] = rstd
        here = ordered[r, :].astype(F32) + hat * row(V_GAIN0) + row(V_SHIFT0)
        first[r, :] = here
        hat, rstd = normalize(here)
        hat1[r, :] = hat
        rstd1[r, :] = rstd
        normed[r, :] = (hat * row(V_GAIN1) + row(V_SHIFT1)).astype(BF)

    over_rows(encode)
    normed_t[...] = normed[...].T
    q[...] = (0.25 * (mm(normed[...], wide_block(w1, 4)) + row(V_QUERY)).astype(BF).astype(F32)).astype(BF)
    k[...] = mm(normed[...], wide_block(w1, 8)).astype(BF)
    v[...] = (mm(normed[...], wide_block(w1, 12)) + row(V_VALUE)).astype(BF)
    k_t[...] = k[...].T
    turned = v[...].T
    one_row = jnp.where(lax.broadcasted_iota(jnp.int32, (16, 512), 0) == 0, 1.0, 0.0).astype(BF)
    for h in range(32):
        v_t[h, 0:16, :] = turned[16 * h : 16 * h + 16, :]
        v_t[h, 16:32, :] = one_row
    for i in both:
        relay(i, 1)

    lane = lax.broadcasted_iota(jnp.int32, (1, 128), 1)
    seat = lax.broadcasted_iota(jnp.int32, (512, 128), 0)
    spot = lax.broadcasted_iota(jnp.int32, (512, 128), 1)
    hidden_key = jnp.where((spot == 96) & (seat >= length[0]), -1e30, 0.0)
    kx[...] = jnp.where(spot < 96, 1.0, hidden_key).astype(BF)
    one_lane = jnp.where(spot == 96, 1.0, 0.0).astype(BF)
    rows_a[...] = jnp.zeros_like(rows_a)
    rows_b[...] = jnp.zeros_like(rows_b)

    def head_places(h):
        group = pl.ds(pl.multiple_of(lax.div(h, 8) * 128, 128), 128)
        mine = jnp.where(lax.div(lane, 16) == lax.rem(h, 8), 1.0, 0.0).astype(BF)
        extra = jnp.where((lax.rem(lane, 32) == h) & (lane < 96) | (lane == 96), 1.0, 0.0).astype(BF)
        return group, mine, extra, pl.ds(pl.multiple_of(h * 16, 16), 16)

    def keys_of(group):
        return jnp.concatenate([k[:, group], kx[...]], axis=1)

    def note(h, value):
        hi, mid, lo = three(value)
        rows_a[pl.ds(h, 1), :] = hi
        rows_a[pl.ds(h + 32, 1), :] = mid
        rows_a[pl.ds(h + 64, 1), :] = lo

    def score_head(h, slot):
        group, mine, extra, channels = head_places(h)
        asks = jnp.concatenate([q[:, group] * mine, one_lane], axis=1)
        scores[slot] = mm_nt(keys_of(group), asks)

    def forward_head(h, slot):
        group, mine, extra, channels = head_places(h)
        peak = jnp.max(scores[slot], axis=0, keepdims=True)
        e = jnp.exp(scores[slot] - peak).astype(BF)
        got = mm(v_t[h], e)
        summed = got[16:17, :]
        mixed_t[channels, :] = got[0:16, :] / summed
        note(h, -(peak + jnp.log(summed)))

    def forward_pair(n, _):
        score_head(n * 2 + 1, 1)
        forward_head(n * 2, 0)
        score_head(lax.rem(n * 2 + 2, 32), 0)
        forward_head(n * 2 + 1, 1)
        return 0

    def two_heads(body):
        def pair(n, _):
            for j in range(2):
                body(n * 2 + j)
            return 0

        return pair

    rows_a[96:97, :] = jnp.ones((1, 512), F32)
    score_head(0, 0)
    lax.fori_loop(0, 4, forward_pair, 0)
    for i in both:
        finish(i, 1)
        begin(i, 2)
    lax.fori_loop(4, 10, forward_pair, 0)
    for i in both:
        relay(i, 2)
    lax.fori_loop(10, 16, forward_pair, 0)
    for i in both:
        finish(i, 2)
    xa[...] = rows_a[...].T.astype(BF)
    mixed[...] = mixed_t[...].T.astype(BF)

    big[...] = mm(mixed[...], wide_block(w1, 16))

    def after(r):
        here = first[r, :] + big[r, :] + row(V_OUT)
        second[r, :] = here
        hat, rstd = normalize(here)
        hat2[r, :] = hat
        rstd2[r, :] = rstd
        n2[r, :] = (hat * row(V_GAIN2) + row(V_SHIFT2)).astype(BF)
        gain(V_RED, go[r, :].astype(F32))

    over_rows(after)
    n2_t[...] = n2[...].T
    acc[...] = jnp.zeros_like(acc)
    acc2[...] = jnp.zeros_like(acc2)
    for i in both:
        crossed(i)

    def chunk(c, _):
        up = jnp.concatenate([up_blocks[4 * c + j] for j in range(4)], axis=1)
        span = pl.ds(pl.multiple_of(c * 512, 512), 512)
        down = down_rows[span, :]
        big[...] = mm(n2[...], up)
        da[...] = mm_nt(go[...], down)

        def gelu_rows(r):
            value, slope = gelu_both(big[r, :] + xb[pl.ds(c, 1), :])
            act[r, :] = value.astype(BF)
            low = (da[r, :] * slope).astype(BF)
            dh[r, :] = low
            gv[pl.ds(12 + c, 1), :] += total(low.astype(F32))

        over_rows(gelu_rows, 128)
        acc[...] += mm(act[...], down)
        acc2[...] += mm_nt(dh[...], up)
        g_down[span, :] = mm_tn(act[...], go[...]).astype(BF)
        grad_up = mm(n2_t[...], dh[...])
        for j in range(4):
            g_up[4 * c + j] = grad_up[:, 128 * j : 128 * (j + 1)].astype(BF)
        return 0

    lax.fori_loop(0, 4, chunk, 0)
    lent = [lend(0, sib_up), lend(1, sib_down)]

    def before_mlp(r):
        result[r, :] = (second[r, :] + acc[r, :] + row(V_RED)).astype(BF)
        grad = acc2[r, :]
        hat = hat2[r, :]
        gain(V_GAIN2, grad * hat)
        gain(V_SHIFT2, grad)
        here = go[r, :].astype(F32) + norm_pull(hat, rstd2[r, :], row(V_GAIN2), grad)
        second[r, :] = here
        low = here.astype(BF)
        dn[r, :] = low
        gain(V_OUT, low.astype(F32))

    over_rows(before_mlp)
    out_copies = bring(((result, result_out),), out_sem)
    put_wide(g1, 16, mm_tn(mixed[...], dn[...]))
    d_mixed[...] = mm_nt(dn[...], wide_block(w1, 16)).astype(BF)
    big[...] = d_mixed[...].astype(F32).T
    state = {0: start(0, 0, lent[0], sib_up), 1: start(1, 0, lent[1], sib_down)}

    def inner(h, _):
        channels = pl.ds(pl.multiple_of(h * 16, 16), 16)
        hi, mid, lo = three(-total(big[channels, :] * mixed_t[channels, :]))
        rows_b[pl.ds(h, 1), :] = hi
        rows_b[pl.ds(h + 32, 1), :] = mid
        rows_b[pl.ds(h + 64, 1), :] = lo
        return 0

    lax.fori_loop(0, 32, inner, 0)
    ya[...] = rows_b[...].T.astype(BF)
    dk[...] = jnp.zeros_like(dk)
    dv[...] = jnp.zeros_like(dv)
    ones = jnp.where(spot < 96, 1.0, 0.0).astype(BF)

    def backward_head(h):
        group, mine, extra, channels = head_places(h)
        q_h = q[:, group] * mine
        m_h = d_mixed[:, group] * mine
        p = jnp.exp(mm_nt(keys_of(group), jnp.concatenate([q_h, xa[...] * extra], axis=1)))
        values = jnp.concatenate([v[:, group], ones], axis=1)
        slope = mm_nt(values, jnp.concatenate([m_h, ya[...] * extra], axis=1))
        ds = (p * slope).astype(BF)
        dv[:, group] += mm(p.astype(BF), m_h)
        dk[:, group] += mm(ds, q_h)
        dq_t[channels, :] = mm(k_t[channels, :], ds)

    backward_heads = two_heads(backward_head)
    lax.fori_loop(0, 4, backward_heads, 0)
    for i in both:
        middle(i, 0, state[i])
    lax.fori_loop(4, 8, backward_heads, 0)
    for i in both:
        close(i, 0, state[i])
        state[i] = start(i, 1)
    lax.fori_loop(8, 11, backward_heads, 0)
    for i in both:
        middle(i, 1, state[i])
    lax.fori_loop(11, 13, backward_heads, 0)
    for i in both:
        close(i, 1, state[i])
        state[i] = start(i, 2)
    lax.fori_loop(13, 16, backward_heads, 0)
    for i in both:
        middle(i, 2, state[i])
    q[...] = (0.25 * dq_t[...].T).astype(BF)
    k[...] = dk[...].astype(BF)
    v[...] = dv[...].astype(BF)
    gain(V_QUERY, q[...].astype(F32))
    gain(V_VALUE, v[...].astype(F32))
    put_wide(g1, 4, mm(normed_t[...], q[...]))
    put_wide(g1, 8, mm(normed_t[...], k[...]))
    put_wide(g1, 12, mm(normed_t[...], v[...]))
    for i in both:
        close(i, 2, state[i])
    o2[...] = g_down.reshape((4, 4, 2, 4, 16, 512))[at["x"], at["y"], at["c"], at["z"]].astype(F32)
    rows_up = g_up.reshape((4, 4, 4, 4, 2, 16, 128))[at["z"], :, at["x"], at["y"], at["c"]].astype(F32)
    swaps = swap_rows(rows_up, post, postr, at, swap_s, swap_r, pending)
    acc2[...] = (
        mm_nt(q[...], wide_block(w1, 4)) + mm_nt(k[...], wide_block(w1, 8)) + mm_nt(v[...], wide_block(w1, 12))
    )

    def before_attention(r):
        grad = acc2[r, :]
        hat = hat1[r, :]
        gain(V_GAIN1, grad * hat)
        gain(V_SHIFT1, grad)
        here = second[r, :] + norm_pull(hat, rstd1[r, :], row(V_GAIN1), grad)
        first_grad[r, :] = here
        hat = hat0[r, :]
        gain(V_GAIN0, here * hat)
        gain(V_SHIFT0, here)
        low = norm_pull(hat, rstd0[r, :], row(V_GAIN0), here).astype(BF)
        dn[r, :] = low
        gain(V_ENC, low.astype(F32))

    over_rows(before_attention)
    put_wide(g1, 0, mm_tn(conv[...], dn[...]))
    out_copies += bring(((g1, g1_out), (first_grad, first_grad_out)), out_sem, 1)
    conv_grad[...] = mm_nt(dn[...], wide_block(w1, 0)).astype(BF)
    out_copies += bring(((conv_grad, conv_grad_out),), out_sem, 3)
    gain(V_CONV, conv_grad[...].astype(F32))
    lane_to = lax.broadcasted_iota(jnp.int32, (128, 512), 1)
    lane_from = lax.broadcasted_iota(jnp.int32, (128, 512), 0)
    shuffle = jnp.where(lane_from == lax.div(lane_to, 16) * 4 + lax.rem(lane_to, 4), 1.0, 0.0).astype(BF)
    which = lax.div(lax.rem(lax.broadcasted_iota(jnp.int32, (16, 512), 1), 16), 4)
    level = lax.broadcasted_iota(jnp.int32, (16, 512), 0) - 12
    for x in range(4):
        chosen = jnp.where(which == level, jnp.broadcast_to(gv[12 + x : 13 + x, :], (16, 512)), 0.0)
        hi, mid, lo = three(chosen)
        dealt_rows = (
            mm_nt(hi.astype(BF), shuffle) + mm_nt(mid.astype(BF), shuffle) + mm_nt(lo.astype(BF), shuffle)
        )
        gv_tiles[x, 0:12, :] = gv[0:12, 128 * x : 128 * (x + 1)]
        gv_tiles[x, 12:16, :] = dealt_rows[12:16, :]
    out_copies += bring(((gv_tiles, gv_out),), out_sem, 4)
    swapped_rows(swaps, post, postr, at, o1)
    for copy in pending:
        copy.wait_send()
    for copy in out_copies:
        copy.wait()


def block(length, conv, ordered, go, w1, up_own, down_own, vec, xb):
    shape = jax.ShapeDtypeStruct
    full = (512, 512)
    f, b, col = pltpu.VMEM(full, F32), pltpu.VMEM(full, BF), pltpu.VMEM((512, 1), F32)
    rows, lanes = pltpu.VMEM((128, 512), F32), pltpu.VMEM((512, 128), BF)
    dma = pltpu.SemaphoreType.DMA
    return pl.pallas_call(
        block_kernel,
        out_shape=(
            shape(full, BF),
            shape(full, F32),
            shape(full, BF),
            shape((20, 512, 128), BF),
            shape((4, 16, 128), F32),
            shape((4, 4, 4, 128), F32),
            shape((16, 512), F32),
        ),
        in_specs=[SM] + [ANY] * 8,
        out_specs=[ANY] * 5 + [VM] * 2,
        scratch_shapes=[
            b, b, b, pltpu.VMEM((20, 512, 128), BF), pltpu.VMEM((4, 16, 128), BF), pltpu.VMEM((16, 512), BF),
            pltpu.VMEM((16, 512), F32), pltpu.VMEM((4, 512), F32),
            b, f, b, pltpu.VMEM((20, 512, 128), BF), pltpu.VMEM((16, 512), F32), pltpu.VMEM((4, 16, 128), F32),
            f, f, col, f, f, col, b, b, b, b, b, b, pltpu.VMEM((32, 32, 512), BF),
            f, b, rows, rows, lanes, lanes, lanes, f, col, b, b,
            f, b, b, f, f, f, b, b, f, f, f, pltpu.VMEM((2, 512, 512), F32),
            pltpu.VMEM((4, 4, 4, 4, 2, 16, 128), BF),
            pltpu.VMEM((4, 4, 2, 4, 16, 512), BF),
            pltpu.VMEM((16, 512, 128), BF),
            pltpu.VMEM((2048, 512), BF),
            pltpu.VMEM((4, 4, 4, 4, 16, 128), BF),
            pltpu.VMEM((4, 4, 4, 16, 512), BF),
        ]
        + [pltpu.VMEM(s, BF) for chain in BLOCK_CHAINS for s in landing_shapes(chain)]
        + [
            pltpu.VMEM((4, 4, 4, 128), BF),
            pltpu.VMEM((4, 4, 4, 128), BF),
            dma((2, SLOTS)),
            dma((2, SLOTS)),
            dma((2, 2)),
            dma((2, 22)),
            dma((2, 22)),
            dma((4,)),
            dma((4,)),
            dma((8,)),
            dma((5,)),
        ],
        compiler_params=pltpu.CompilerParams(
            collective_id=2, has_side_effects=True, vmem_limit_bytes=62 * 2**20
        ),
        name="block",
    )(length, conv, ordered, go, w1, up_own, down_own, vec, xb)


def spread_rows(picks, j, b):
    seat = lax.broadcasted_iota(jnp.int32, (512, 256), 0)
    return jnp.where(seat == picks[j : j + 1, 256 * b : 256 * (b + 1)], 1.0, 0.0).astype(BF)


def line_neighbour(at, step):
    linear = lax.rem(((at["x"] * 4 + at["y"]) * 2 + at["c"]) * 4 + at["z"] + step, 128)
    return (lax.div(linear, 4), lax.rem(linear, 4))


def device_after(me, s):
    linear = lax.rem(me + s, 128)
    return (lax.div(linear, 4), lax.rem(linear, 4))


def deal(rows, landing, me, send, recv):
    def one(s, _):
        pltpu.make_async_remote_copy(
            src_ref=rows.at[lax.rem(me + s, 128)],
            dst_ref=landing.at[me],
            send_sem=send,
            recv_sem=recv,
            device_id=device_after(me, s),
            device_id_type=MESH,
        ).start()
        return 0

    lax.fori_loop(1, 128, one, 0)
    landing[me] = rows[me]


def dealt(rows, landing, me, send, recv):
    return pltpu.make_async_remote_copy(
        src_ref=rows.at[pl.ds(0, 127)],
        dst_ref=landing.at[pl.ds(0, 127)],
        send_sem=send,
        recv_sem=recv,
        device_id=device_after(me, 1),
        device_id_type=MESH,
    )


def fold_rows(index, rows, out):
    for n in range(4):
        seat = lax.broadcasted_iota(jnp.int32, (256, 512), 0) + 256 * n
        hot = jnp.where(seat == index, 1.0, 0.0).astype(BF)
        out[32 * n : 32 * (n + 1)] = mm(hot, rows).reshape(32, 8, 512).astype(BF)


def unfold_rows(index, blocks):
    seat = lax.broadcasted_iota(jnp.int32, (1024, 512), 0)
    hot = jnp.where(seat == index, 1.0, 0.0).astype(BF)
    return mm_tn(hot, blocks[...].astype(F32).reshape(1024, 512).astype(BF)).astype(BF)


def column_of(row):
    return jnp.broadcast_to(row, (128, 512)).T[:, 0:1]


def front_kernel(
    conv_in, encode_in, triple_in, output_in, expand_in, small_in, points_in, inverse_in, perm_in, neighbours_in,
    gc, g1, up_out, picked, conv_out, ordered_out, vectors_out, natural_out, take_out, send_out, picks_out,
    encode, triple, output, expand, small, points, inverse, perm, neighbours, conv,
    up_own, conv_low, ordered, vectors, natural, take, send, picks,
    outgoing, incoming, m1p, vt,
    extended, all_picks, acc, w_buf, pick_cols, pre, m1b, prev, vb, gv,
    sends, recvs, locs, presend, prerecv, halo_s, halo_r, p_sem, w_sem, deal_s, deal_r, met, in_sem, out_sem,
):
    at = place()
    width = 512
    me = ((at["x"] * 4 + at["y"]) * 2 + at["c"]) * 4 + at["z"]
    greet_lines(at)
    fetched = bring(
        (
            (encode_in, encode), (triple_in, triple), (output_in, output), (expand_in, expand), (small_in, small),
            (conv_in, conv), (points_in, points), (inverse_in, inverse), (perm_in, perm), (neighbours_in, neighbours),
        ),
        in_sem,
    )
    for copy in fetched[:6]:
        copy.wait()
    for first_block, per, base, refs in (
        (0, 5, 0, ((encode, 4), (triple, 12), (output, 4))), (0, 4, 5, ((expand, 16),))
    ):
        n = 0
        for ref, blocks in refs:
            for j in range(blocks):
                m1p[n // per, base + n % per] = ref[:, 128 * j : 128 * (j + 1)]
                n += 1
    row64 = lax.broadcasted_iota(jnp.int32, (16, 64), 0)
    lane64 = lax.broadcasted_iota(jnp.int32, (16, 64), 1)
    alone = jnp.where(lax.div(lane64, 4) == row64, jnp.broadcast_to(small[...], (16, 64)), 0.0).astype(BF)
    from64 = lax.broadcasted_iota(jnp.int32, (64, 128), 0)
    to128 = lax.broadcasted_iota(jnp.int32, (64, 128), 1)
    lane0 = lax.rem(at["y"] * 2 + at["c"], 8) * 16 + at["z"] * 4
    vt[...] = mm(alone, jnp.where(to128 == lane0 + lax.rem(from64, 4), 1.0, 0.0).astype(BF)).astype(BF)
    meet_lines()
    tell_line(at, "x", met.at[0])
    pending = []

    def own_view(i, h):
        name, op, view, order, halves = FRONT_STREAMS[i]
        if op == 0:
            return conv.at[pl.ds(h[0], h[1] - h[0]), :]
        return m1b.at[pl.ds(h[0], h[1] - h[0])] if op == 1 else vb

    begin, relay, finish, crossed = gather_steps(
        FRONT_STREAMS, own_view, (gc, g1, gv), at, sends, recvs, locs, pending
    )

    def remote(src, dst, send, recv, device):
        copy = remote_copy(src, dst, send, recv, device)
        copy.start()
        pending.append(copy)
        return copy

    pre_copies = []
    for step in (1, 2, 3):
        to = moved(at, "z", step)
        for j, (src, dst) in enumerate(((m1p.at[to["z"]], pre.at[step]), (vt, prev.at[step]))):
            pre_copies.append(remote(src, dst, presend.at[j, step], prerecv.at[j, step], device_at(to)))
    first, more = (0, 1, 2), (3, 4)
    for i in first:
        begin(i, 0)
    for copy in fetched[6:]:
        copy.wait()
    home = lax.div(inverse[...], width)
    row_id = lax.broadcasted_iota(jnp.int32, (width, width), 0)
    lane_id = lax.broadcasted_iota(jnp.int32, (width, width), 1)
    ahead = jnp.where((column_of(home.astype(F32)) == home.astype(F32)) & (row_id < lane_id), 1.0, 0.0)
    send[...] = home * 8 + total(ahead).astype(jnp.int32)
    pl.semaphore_wait(met.at[0], 3)
    tell_line(at, "y", met.at[1])
    fold_rows(send[...], points[...], outgoing)
    pl.semaphore_wait(met.at[1], 3)
    tell_line(at, "c", met.at[2])
    for copy in pre_copies:
        copy.wait_recv()
    pre[0] = m1p[at["z"]]

    def tile(k, _):
        pieces = [pre[lax.rem(at["z"] - s + 4, 4), k].astype(F32) for s in range(4)]
        m1b[k] = jnp.concatenate(pieces, axis=0).astype(BF)
        return 0

    lax.fori_loop(0, 9, tile, 0)
    vb[...] = (
        vt[...].astype(F32) + prev[1].astype(F32) + prev[2].astype(F32) + prev[3].astype(F32)
    ).astype(BF)
    up_own[...] = m1b[5:9]
    for i in more:
        begin(i, 0)
    pl.semaphore_wait(met.at[2], 1)
    deal(outgoing, incoming, me, deal_s, deal_r)
    for i in first + more:
        finish(i, 0)
        begin(i, 1)
    source = lax.div(perm[...], width)
    column = column_of(perm[...].astype(F32))
    source_column = lax.div(column.astype(jnp.int32), width)
    ahead = jnp.where((source_column == source) & (column < perm[...].astype(F32)), 1.0, 0.0)
    take[...] = source * 8 + total(ahead).astype(jnp.int32)
    token = lax.broadcasted_iota(jnp.int32, (1, width), 1)
    shift = me * width - 128 + lax.div(token, 256) * 256

    for u in range(9):
        raw = neighbours[3 * u : 3 * u + 3, :]
        local = jnp.where(raw >= 0, raw - shift, -1)
        picks[u] = local
        pick_cols[u] = jnp.concatenate([local, local, local[0:2]], axis=0).astype(F32)
    out_copies = bring(((up_own, up_out), (take, take_out), (send, send_out), (picks, picks_out)), out_sem)
    for i in first + more:
        relay(i, 1)
    for i in first:
        finish(i, 1)
        begin(i, 2)
    acc[...] = jnp.zeros_like(acc)
    for i in more:
        finish(i, 1)
    dealt(outgoing, incoming, me, deal_s, deal_r).wait_recv()
    mine = unfold_rows(take[...], incoming)
    ordered[...] = mine
    out_copies += bring(((ordered, ordered_out),), out_sem, 4)
    extended[128:640, :] = mine
    halos = []
    for j, (src, dst, step) in enumerate(((128, 640, 127), (512, 0, 1))):
        halos.append(
            remote(
                extended.at[pl.ds(src, 128), :], extended.at[pl.ds(dst, 128), :],
                halo_s.at[j], halo_r.at[j], line_neighbour(at, step),
            )
        )

    def p_copy(u):
        return pltpu.make_async_copy(all_picks.at[pl.ds(u * 3, 3)], picked.at[pl.ds(u * 3, 3)], p_sem.at[u])

    def pick_unit(u, _):
        columns = pick_cols[u].T
        for j in range(3):
            for b in range(2):
                seat = lax.broadcasted_iota(jnp.int32, (256, 512), 1).astype(F32)
                hot = jnp.where(seat == columns[256 * b : 256 * (b + 1), j : j + 1], 1.0, 0.0).astype(BF)
                window = extended[256 * b : 256 * b + 512, :]
                all_picks[u * 3 + j, 256 * b : 256 * (b + 1), :] = mm(hot, window).astype(BF)
        p_copy(u).start()
        return 0

    def w_copy(u):
        slot = lax.rem(u, 2)
        return pltpu.make_async_copy(
            gc.reshape((4, 27, 512, 128)).at[:, pl.ds(u * 3, 3)], w_buf.at[slot], w_sem.at[slot]
        )

    def conv_unit(u, _):
        @pl.when(u < 8)
        def _():
            w_copy(u + 1).start()

        w_copy(u).wait()
        slot = lax.rem(u, 2)
        parts = [
            mm(all_picks[u * 3 + j], jnp.concatenate([w_buf[slot, n, j] for n in range(4)], axis=1))
            for j in range(3)
        ]
        acc[...] += parts[0] + parts[1] + parts[2]
        return 0

    for i in first:
        relay(i, 2)
    for i in (3,):
        begin(i, 2)
    for copy in halos:
        copy.wait_recv()
    lax.fori_loop(0, 5, pick_unit, 0)
    for i in (3,):
        relay(i, 2)
    lax.fori_loop(5, 9, pick_unit, 0)
    for i in first:
        finish(i, 2)
    for i in first:
        crossed(i)
    w_copy(0).start()
    lax.fori_loop(0, 6, conv_unit, 0)
    for i in (3,):
        finish(i, 2)
    lax.fori_loop(6, 9, conv_unit, 0)
    for i in more:
        crossed(i)
    chunks = []
    for x in range(4):
        chunk = jnp.zeros((16, 128), F32)
        for y in range(4):
            for c in range(2):
                chunk = chunk + gv[x, y, c].astype(F32)
        chunks.append(chunk)
    together = jnp.concatenate(chunks, axis=1)
    vectors[...] = together
    lane = lax.broadcasted_iota(jnp.int32, (128, width), 1)
    from_lane = lax.broadcasted_iota(jnp.int32, (128, width), 0)
    shuffle = jnp.where(from_lane == lax.div(lane, 16) * 4 + lax.rem(lane, 4), 1.0, 0.0).astype(BF)
    which = lax.div(lax.rem(lax.broadcasted_iota(jnp.int32, (4, width), 1), 16), 4)
    group = lax.broadcasted_iota(jnp.int32, (4, width), 0)
    for x in range(4):
        spreaded = mm(chunks[x].astype(BF), shuffle)[12:16, :]
        natural[x : x + 1, :] = total(jnp.where(which == group, spreaded, 0.0))
    conv_low[...] = (acc[...] + together[0:1, :]).astype(BF)
    out_copies += bring(((conv_low, conv_out), (vectors, vectors_out), (natural, natural_out)), out_sem, 5)
    for copy in pending:
        copy.wait_send()
    dealt(outgoing, incoming, me, deal_s, deal_r).wait_send()

    def stored(u, _):
        p_copy(u).wait()
        return 0

    lax.fori_loop(0, 9, stored, 0)
    for copy in out_copies:
        copy.wait()


def front(conv, encode, triple, output, expand, small, points, inverse, perm, neighbours):
    shape = jax.ShapeDtypeStruct
    n = len(FRONT_STREAMS)
    dma = pltpu.SemaphoreType.DMA
    i32 = jnp.int32
    kept = (
        ((4, 16, 128), BF),
        ((512, 512), BF),
        ((512, 512), BF),
        ((16, 512), F32),
        ((4, 512), F32),
        ((1, 512), i32),
        ((1, 512), i32),
        ((9, 3, 512), i32),
    )
    return pl.pallas_call(
        front_kernel,
        out_shape=(
            shape((4, 4, 4, 2, 432, 128), BF),
            shape((4, 5, 4, 4, 2, 16, 128), BF),
            shape(*kept[0]),
            shape((27, 512, 512), BF),
        )
        + tuple(shape(*k) for k in kept[1:]),
        in_specs=[ANY] * 10,
        out_specs=[ANY] * 11,
        scratch_shapes=[
            pltpu.VMEM((4, 512), BF),
            pltpu.VMEM((4, 1536), BF),
            pltpu.VMEM((4, 512), BF),
            pltpu.VMEM((4, 2048), BF),
            pltpu.VMEM((1, 64), F32),
            pltpu.VMEM((512, 512), BF),
            pltpu.VMEM((1, 512), i32),
            pltpu.VMEM((1, 512), i32),
            pltpu.VMEM((27, 512), i32),
            pltpu.VMEM((432, 128), BF),
        ]
        + [pltpu.VMEM(*k) for k in kept]
        + [
            pltpu.VMEM((128, 8, 512), BF),
            pltpu.VMEM((128, 8, 512), BF),
            pltpu.VMEM((4, 9, 4, 128), BF),
            pltpu.VMEM((16, 128), BF),
            pltpu.VMEM((768, 512), BF),
            pltpu.VMEM((27, 512, 512), BF),
            pltpu.VMEM((512, 512), F32),
            pltpu.VMEM((2, 4, 3, 512, 128), BF),
            pltpu.VMEM((9, 8, 512), F32),
            pltpu.VMEM((4, 9, 4, 128), BF),
            pltpu.VMEM((9, 16, 128), BF),
            pltpu.VMEM((4, 16, 128), BF),
            pltpu.VMEM((16, 128), BF),
            pltpu.VMEM((4, 4, 2, 16, 128), BF),
            dma((n, SLOTS)),
            dma((n, SLOTS)),
            dma((n, 2)),
            dma((2, 4)),
            dma((2, 4)),
            dma((2,)),
            dma((2,)),
            dma((9,)),
            dma((2,)),
            dma,
            dma,
            pltpu.SemaphoreType.REGULAR((3,)),
            dma((10,)),
            dma((8,)),
        ],
        compiler_params=pltpu.CompilerParams(
            collective_id=0, has_side_effects=True, vmem_limit_bytes=56 * 2**20
        ),
        name="front",
    )(conv, encode, triple, output, expand, small, points, inverse, perm, neighbours)


BACK_CHAINS = (
    ("cz", "zxycRL", {"R": 96, "L": 128}, "R", 0, "zyx", ((0, 48), (48, 96))),
    ("cx", "zxycRL", {"R": 160, "L": 128}, "R", 96, "xzy", ((0, 80), (80, 160))),
    ("cy", "zxycRL", {"R": 176, "L": 128}, "R", 256, "yxz", ((0, 96), (96, 176))),
    ("wide", "zKxycSL", {"K": 5, "S": 16, "L": 128}, "K", 0, "zyx", ((0, 3), (3, 5))),
)


def back_kernel(
    grad_in, first_grad_in, take_in, picks_in, w, picked, g1, gv_in,
    arrived_out, oc, o1, ov,
    returning, arrived, wide, grad, first_grad, take, picks, gv,
    kernel_grad, theirs, spread, p_buf, w_buf, rims, landed, sib, *rest,
):
    count = 12 * len(BACK_CHAINS)
    landing, rest = rest[:count], rest[count:]
    post, postr, vx, vr, p_sem, w_sem, xy_send, xy_recv, sends, recvs, vsend, vrecv, psend, precv, rim_s, rim_r, deal_s, deal_r, met, in_sem = rest
    at = place()
    me = ((at["x"] * 4 + at["y"]) * 2 + at["c"]) * 4 + at["z"]
    greet_lines(at)
    fetched = bring(
        (
            (gv_in, gv), (g1, wide), (grad_in, grad), (picks_in, picks), (take_in, take),
            (first_grad_in, first_grad),
        ),
        in_sem,
    )
    meet_lines()
    tell_line(at, "x", met.at[0])
    other = moved(at, "c", 1)
    pending = []
    tiles = kernel_grad.reshape((4, 4, 4, 2, 432, 128))

    def push(src, dst, send, recv, to):
        copy = remote_copy(src, dst, send, recv, device_at(to))
        copy.start()
        pending.append(copy)
        return copy

    mine = (tiles, "zxycRL", {"c": at["c"]})
    stores = (mine, mine, mine, (wide, "zKxycSL", {"c": at["c"]}))
    lend, start, middle, close, view = scatter_steps(
        BACK_CHAINS, stores, landing, at, sends, recvs, pending
    )
    conv_chains = (0, 1, 2)

    def vector_step(k):
        axis, steps = (("c", (1,)), ("z", (1, 2, 3)), ("y", (1, 2, 3)), ("x", (1, 2, 3)))[k]
        copies = []
        for s in steps:
            to = moved(at, axis, s)
            if axis == "x":
                src, dst = vx.at[3, to["x"]], vr.at[3, s, 0]
            else:
                src, dst = (gv if k == 0 else vx.at[k]), vr.at[k, s]
            copies.append(push(src, dst, vsend.at[k, s], vrecv.at[k, s], to))
        return copies

    def vector_add(k, copies):
        for copy in copies:
            copy.wait_recv()
        if k == 3:
            ov[...] = vx[3, at["x"]] + vr[3, 1, 0] + vr[3, 2, 0] + vr[3, 3, 0]
            return
        sum_now = gv[...] if k == 0 else vx[k]
        for s in (1,) if k == 0 else (1, 2, 3):
            sum_now = sum_now + vr[k, s]
        vx[k + 1] = sum_now

    def p_copy(u):
        slot = lax.rem(u, 2)
        return pltpu.make_async_copy(picked.at[pl.ds(u * 3, 3)], p_buf.at[slot], p_sem.at[slot])

    def w_copy(u):
        slot = lax.rem(u, 2)
        return pltpu.make_async_copy(w.at[:, pl.ds(u * 3, 3)], w_buf.at[slot], w_sem.at[slot])

    def xy_copy(n):
        x, y = lax.div(n, 4), lax.rem(n, 4)
        return remote_copy(
            tiles.at[:, x, y, other["c"]], theirs.at[:, x, y], xy_send.at[n], xy_recv.at[n], device_at(other)
        )

    def join(n):
        x, y = lax.div(n, 4), lax.rem(n, 4)
        xy_copy(n).wait_recv()
        where = tiles.at[:, x, y, at["c"]]
        where[...] = where[...] + theirs[:, x, y]

    def weight_unit(u, _):
        @pl.when(u < 8)
        def _():
            p_copy(u + 1).start()

        p_copy(u).wait()
        for j in range(3):
            product = mm_tn(p_buf[lax.rem(u, 2), j], grad[...])
            span = pl.ds(pl.multiple_of(u * 1536 + j * 512, 512), 512)
            for n in range(4):
                kernel_grad[n, span, :] = product[:, 128 * n : 128 * (n + 1)].astype(BF)
        ready, ready_next = lax.div(u * 16, 9), lax.div((u + 1) * 16, 9)
        for j in range(2):
            @pl.when(ready + j < ready_next)
            def _():
                xy_copy(ready + j).start()

        for j in range(2):
            n = lax.div((u - 2) * 16, 9) + j

            @pl.when((u >= 2) & (n < lax.div((u - 1) * 16, 9)))
            def _():
                join(n)

        return 0

    def row_unit(u, _):
        @pl.when(u < 8)
        def _():
            w_copy(u + 1).start()

        w_copy(u).wait()
        slot = lax.rem(u, 2)
        g = grad[...]
        back = [
            mm_nt(g, jnp.concatenate([w_buf[slot, n, j] for n in range(4)], axis=1)).astype(BF)
            for j in range(3)
        ]
        for b in range(2):
            hot = jnp.concatenate([spread_rows(picks.at[u], j, b) for j in range(3)], axis=1)
            terms = jnp.concatenate([back[j][256 * b : 256 * (b + 1), :] for j in range(3)], axis=0)
            spread[256 * b : 256 * b + 512, :] += mm(hot, terms)
        return 0

    p_copy(0).start()
    spread[...] = jnp.zeros_like(spread)
    fetched[0].wait()
    vectors = vector_step(0)
    state = {}
    fetched[1].wait()
    lent = lend(3, sib)
    w_copy(0).start()
    for copy in fetched[2:]:
        copy.wait()
    lax.fori_loop(0, 3, weight_unit, 0)
    pl.semaphore_wait(met.at[0], 3)
    tell_line(at, "y", met.at[1])
    state[3] = start(3, 0, lent, sib)
    vector_add(0, vectors)
    vectors = vector_step(1)
    lax.fori_loop(3, 6, weight_unit, 0)
    pl.semaphore_wait(met.at[1], 3)
    tell_line(at, "c", met.at[2])
    for i in (3,):
        middle(i, 0, state[i])
    lax.fori_loop(6, 9, weight_unit, 0)
    pl.semaphore_wait(met.at[2], 1)
    vector_add(1, vectors)
    vectors = vector_step(2)
    for i in (3,):
        close(i, 0, state[i])
        state[i] = start(i, 1)
    for n in range(12, 16):
        join(n)
    for i in conv_chains:
        state[i] = start(i, 0)
    for i in (3,):
        middle(i, 1, state[i])
    lax.fori_loop(0, 3, row_unit, 0)
    vector_add(2, vectors)
    vectors = vector_step(3)
    for i in (3,):
        close(i, 1, state[i])
        state[i] = start(i, 2)
    lax.fori_loop(3, 5, row_unit, 0)
    for i in conv_chains:
        middle(i, 0, state[i])
    for i in (3,):
        middle(i, 2, state[i])
    lax.fori_loop(5, 9, row_unit, 0)
    rims[0] = spread[0:128, :].astype(BF)
    rims[1] = spread[640:768, :].astype(BF)
    rim_copies = []
    for j, step in ((0, 127), (1, 1)):
        copy = remote_copy(rims.at[j], landed.at[j], rim_s.at[j], rim_r.at[j], line_neighbour(at, step))
        copy.start()
        pending.append(copy)
        rim_copies.append(copy)
    for i in conv_chains:
        close(i, 0, state[i])
        state[i] = start(i, 1)
    for i in (3,):
        close(i, 2, state[i])
    vector_add(3, vectors)
    swaps = swap_rows(
        wide[at["z"], :, at["x"], at["y"], at["c"]].astype(F32), post, postr, at, psend, precv, pending
    )
    for copy in rim_copies:
        copy.wait_recv()
    spread[512:640, :] += landed[0].astype(F32)
    spread[128:256, :] += landed[1].astype(F32)
    ordered_grad = (first_grad[...] + spread[128:640, :]).astype(BF)
    fold_rows(take[...], ordered_grad, returning)
    deal(returning, arrived, me, deal_s, deal_r)
    for i in conv_chains:
        middle(i, 1, state[i])
    for i in conv_chains:
        close(i, 1, state[i])
        state[i] = start(i, 2)
    swapped_rows(swaps, post, postr, at, o1)
    for i in conv_chains:
        middle(i, 2, state[i])
    for i in conv_chains:
        close(i, 2, state[i])
        name, layout, plain, cut, base, order, halves = BACK_CHAINS[i]
        oc[pl.ds(base, plain["R"]), :] = tiles[at["z"], at["x"], at["y"], at["c"], pl.ds(base, plain["R"]), :].astype(F32)
    dealt(returning, arrived, me, deal_s, deal_r).wait_recv()
    last = pltpu.make_async_copy(arrived, arrived_out, in_sem.at[6])
    last.start()
    for copy in pending:
        copy.wait_send()
    for n in range(16):
        xy_copy(n).wait_send()
    dealt(returning, arrived, me, deal_s, deal_r).wait_send()
    last.wait()


def back_scatter(grad, first_grad, take, picks, w, picked, g1, gv):
    shape = jax.ShapeDtypeStruct
    n = len(BACK_CHAINS)
    dma = pltpu.SemaphoreType.DMA
    return pl.pallas_call(
        back_kernel,
        out_shape=(
            shape((128, 8, 512), BF),
            shape((432, 128), F32),
            shape((4, 5, 4, 128), F32),
            shape((16, 128), F32),
        ),
        in_specs=[ANY] * 8,
        out_specs=[ANY] + [VM] * 3,
        scratch_shapes=[
            pltpu.VMEM((128, 8, 512), BF),
            pltpu.VMEM((128, 8, 512), BF),
            pltpu.VMEM((4, 5, 4, 4, 2, 16, 128), BF),
            pltpu.VMEM((512, 512), BF),
            pltpu.VMEM((512, 512), F32),
            pltpu.VMEM((1, 512), jnp.int32),
            pltpu.VMEM((9, 3, 512), jnp.int32),
            pltpu.VMEM((4, 16, 128), F32),
            pltpu.VMEM((4, 13824, 128), BF),
            pltpu.VMEM((4, 4, 4, 432, 128), BF),
            pltpu.VMEM((768, 512), F32),
            pltpu.VMEM((2, 3, 512, 512), BF),
            pltpu.VMEM((2, 4, 3, 512, 128), BF),
            pltpu.VMEM((2, 128, 512), BF),
            pltpu.VMEM((2, 128, 512), BF),
            pltpu.VMEM((4, 5, 4, 4, 16, 128), BF),
        ]
        + [pltpu.VMEM(s, BF) for chain in BACK_CHAINS for s in landing_shapes(chain)]
        + [
            pltpu.VMEM((4, 5, 4, 128), BF),
            pltpu.VMEM((4, 5, 4, 128), BF),
            pltpu.VMEM((4, 4, 16, 128), F32),
            pltpu.VMEM((4, 4, 4, 16, 128), F32),
            dma((2,)),
            dma((2,)),
            dma((16,)),
            dma((16,)),
            dma((n, 22)),
            dma((n, 22)),
            dma((4, 4)),
            dma((4, 4)),
            dma((4,)),
            dma((4,)),
            dma((2,)),
            dma((2,)),
            dma,
            dma,
            pltpu.SemaphoreType.REGULAR((3,)),
            dma((7,)),
        ],
        compiler_params=pltpu.CompilerParams(
            collective_id=1, has_side_effects=True, vmem_limit_bytes=62 * 2**20
        ),
        name="back_scatter",
    )(grad, first_grad, take, picks, w, picked, g1, gv)


def last_kernel(
    arrived_in, send_in, result_in, oc_in, wide_in, up_in, tall_in, ov_in,
    result, points_grad, oc, tall, encode, triple, output, expand, small,
    arrived, send, wide, up, ov, rows, encode_v, triple_v, output_v, expand_v, small_v, result_v, oc_v, tall_v, in_sem, out_sem,
):
    through = bring(((result_in, result_v), (oc_in, oc_v), (tall_in, tall_v)), in_sem)
    fetched = bring(
        ((wide_in, wide), (up_in, up), (ov_in, ov), (send_in, send), (arrived_in, arrived)), in_sem, 3
    )
    at = place()
    fetched[0].wait()
    n = 0
    for ref, blocks in ((encode_v, 4), (triple_v, 12), (output_v, 4)):
        for j in range(blocks):
            ref[:, 128 * j : 128 * (j + 1)] = wide[n // 5, n % 5]
            n += 1
    out = bring(((encode_v, encode), (triple_v, triple), (output_v, output)), out_sem)
    fetched[1].wait()
    for j in range(16):
        expand_v[:, 128 * j : 128 * (j + 1)] = up[j // 4, j % 4]
    out += bring(((expand_v, expand),), out_sem, 3)
    fetched[2].wait()
    lane0 = lax.rem(at["y"] * 2 + at["c"], 8) * 16 + at["z"] * 4
    lane = lax.broadcasted_iota(jnp.int32, (128, 128), 0)
    to = lax.broadcasted_iota(jnp.int32, (128, 128), 1)
    pick = jnp.where((lane == lane0 + to) & (to < 4), 1.0, 0.0).astype(BF)
    hi, mid, lo = three(ov[...])
    small_v[...] = mm(hi.astype(BF), pick) + mm(mid.astype(BF), pick) + mm(lo.astype(BF), pick)
    out += bring(((small_v, small),), out_sem, 4)
    for copy in through:
        copy.wait()
    out += bring(((result_v, result), (oc_v, oc), (tall_v, tall)), out_sem, 6)
    fetched[3].wait()
    fetched[4].wait()
    rows[...] = unfold_rows(send[...], arrived)
    out += bring(((rows, points_grad),), out_sem, 5)
    for copy in out:
        copy.wait()


def last(arrived, send, result, oc, wide, up, tall, ov):
    shape = jax.ShapeDtypeStruct
    widths = (512, 1536, 512, 2048)
    return pl.pallas_call(
        last_kernel,
        out_shape=(
            shape((512, 512), BF),
            shape((512, 512), BF),
            shape((432, 128), F32),
            shape((16, 512), F32),
        )
        + tuple(shape((4, w), F32) for w in widths)
        + (shape((16, 128), F32),),
        in_specs=[ANY] * 8,
        out_specs=[ANY] * 9,
        scratch_shapes=[
            pltpu.VMEM((128, 8, 512), BF),
            pltpu.VMEM((1, 512), jnp.int32),
            pltpu.VMEM((4, 5, 4, 128), F32),
            pltpu.VMEM((4, 4, 4, 128), F32),
            pltpu.VMEM((16, 128), F32),
            pltpu.VMEM((512, 512), BF),
        ]
        + [pltpu.VMEM((4, w), F32) for w in widths]
        + [
            pltpu.VMEM((16, 128), F32),
            pltpu.VMEM((512, 512), BF),
            pltpu.VMEM((432, 128), F32),
            pltpu.VMEM((16, 512), F32),
            pltpu.SemaphoreType.DMA((8,)),
            pltpu.SemaphoreType.DMA((9,)),
        ],
        compiler_params=pltpu.CompilerParams(vmem_limit_bytes=60 * 2**20),
        name="last",
    )(arrived, send, result, oc, wide, up, tall, ov)


def per_device(
    points,
    perm,
    inverse,
    lengths,
    neighbours,
    conv_weight,
    conv_bias,
    encode_weight,
    encode_bias,
    encode_gain,
    encode_shift,
    before_gain,
    before_shift,
    triple_weight,
    query_bias,
    value_bias,
    output_weight,
    output_bias,
    second_gain,
    second_shift,
    expand_weight,
    expand_bias,
    reduce_weight,
    reduce_bias,
    grad_out,
):
    small = jnp.concatenate(
        [
            conv_bias,
            encode_bias,
            encode_gain,
            encode_shift,
            before_gain,
            before_shift,
            query_bias,
            value_bias,
            output_bias,
            second_gain,
            second_shift,
            reduce_bias,
            expand_bias,
        ]
    )
    kernel, wide, up_own, picked, conv, ordered, vectors, wide_bias, take, send, picks = front(
        conv_weight,
        encode_weight,
        triple_weight,
        output_weight,
        expand_weight,
        small.astype(F32).reshape(1, 64),
        points,
        inverse.reshape(1, 512),
        perm.reshape(1, 512),
        neighbours,
    )
    result, grad_first, grad_conv, grad_wide, vector_grads, up_out, tall_out = block(
        lengths,
        conv,
        ordered,
        grad_out,
        wide.reshape(20, 512, 128),
        up_own,
        reduce_weight,
        vectors,
        wide_bias,
    )
    arrived, kernel_out, wide_out, vector_out = back_scatter(
        grad_conv,
        grad_first,
        take,
        picks,
        kernel.reshape(4, 27, 512, 128),
        picked,
        grad_wide.reshape(4, 5, 4, 4, 2, 16, 128),
        vector_grads,
    )
    result, points_grad, kernel_out, tall_out, encode_out, triple_out, output_out, up_out, vector_out = last(
        arrived, send, result, kernel_out, wide_out, up_out, tall_out, vector_out
    )
    vector_out = vector_out[:, :4]
    reduced = (
        vector_out[V_CONV],
        encode_out,
        vector_out[V_ENC],
        vector_out[V_GAIN0],
        vector_out[V_SHIFT0],
        vector_out[V_GAIN1],
        vector_out[V_SHIFT1],
        triple_out,
        vector_out[V_QUERY],
        vector_out[V_VALUE],
        output_out,
        vector_out[V_OUT],
        vector_out[V_GAIN2],
        vector_out[V_SHIFT2],
        up_out,
        vector_out[12:].reshape(16),
        tall_out,
        vector_out[V_RED],
    )
    return (result, points_grad, kernel_out) + reduced


def solution(mesh):
    in_specs = (
        P(("pts", "rep"), None),
        P(("pts", "rep")),
        P(("pts", "rep")),
        P(("pts", "rep")),
        P(None, ("pts", "rep")),
        P("pts", "rep"),
        P(("pts", "rep")),
        P(("pts", "rep"), None),
        P(("pts", "rep")),
        P(("pts", "rep")),
        P(("pts", "rep")),
        P(("pts", "rep")),
        P(("pts", "rep")),
        P(("pts", "rep"), None),
        P(("pts", "rep")),
        P(("pts", "rep")),
        P(("pts", "rep"), None),
        P(("pts", "rep")),
        P(("pts", "rep")),
        P(("pts", "rep")),
        P(("pts", "rep"), None),
        P(("pts", "rep")),
        P(("pts", "rep"), None),
        P(("pts", "rep")),
        P(("pts", "rep"), None),
    )
    out_specs = (
        P(("pts", "rep"), None),
        P(("pts", "rep"), None),
        P("pts", "rep"),
        P(("pts", "rep")),
        P(("pts", "rep"), None),
        P(("pts", "rep")),
        P(("pts", "rep")),
        P(("pts", "rep")),
        P(("pts", "rep")),
        P(("pts", "rep")),
        P(("pts", "rep"), None),
        P(("pts", "rep")),
        P(("pts", "rep")),
        P(("pts", "rep"), None),
        P(("pts", "rep")),
        P(("pts", "rep")),
        P(("pts", "rep")),
        P(("pts", "rep"), None),
        P(("pts", "rep")),
        P(("pts", "rep"), None),
        P(("pts", "rep")),
    )
    return jax.shard_map(
        per_device, mesh=mesh, in_specs=in_specs, out_specs=out_specs, check_vma=False
    )
```

```python
import jax
import jax.numpy as jnp
from jax import lax
from jax.experimental import pallas as pl
from jax.experimental.pallas import tpu as pltpu
from jax.sharding import PartitionSpec as P

MESH = pl.DeviceIdType.MESH
BF = jnp.bfloat16
F32 = jnp.float32


def place():
    p = lax.axis_index("pts")
    return {
        "x": lax.div(p, 8),
        "y": lax.rem(lax.div(p, 2), 4),
        "c": lax.rem(p, 2),
        "z": lax.axis_index("rep"),
    }


def device_at(at):
    return ((at["x"] * 4 + at["y"]) * 2 + at["c"], at["z"])


def moved(at, axis, step):
    size = 2 if axis == "c" else 4
    return {**at, axis: lax.rem(at[axis] + step, size)}


def whole(value):
    return slice(None) if value is None else value


def conv_view(ref, sel, h):
    r0, r1 = h
    return ref.at[
        whole(sel.get("z")), whole(sel.get("x")), whole(sel.get("y")), sel["c"], pl.ds(r0, r1 - r0), :
    ]


def wide_view(ref, sel, h):
    k0, k1 = h
    return ref.at[
        whole(sel.get("z")), pl.ds(k0, k1 - k0), whole(sel.get("x")), whole(sel.get("y")), sel["c"]
    ]


def tall_view(ref, sel, h):
    l0, l1 = h
    return ref.at[
        whole(sel.get("x")), whole(sel.get("y")), sel["c"], whole(sel.get("z")), :, pl.ds(l0, l1 - l0)
    ]


def flat_view(ref, sel, h):
    return ref.at[whole(sel.get("x")), whole(sel.get("y")), sel["c"]]


FRONT_STREAMS = (
    ("cz", 0, conv_view, "xyz", ((0, 48), (48, 96))),
    ("cx", 0, conv_view, "yzx", ((96, 176), (176, 256))),
    ("cy", 0, conv_view, "zxy", ((256, 352), (352, 432))),
    ("wide", 1, wide_view, "xyz", ((0, 3), (3, 5))),
    ("vectors", 2, flat_view, "xy", ((0, 16),)),
)
SLOTS = 40


def greet_lines(at):
    barrier = pltpu.get_barrier_semaphore()
    for axis, steps in (("x", (1, 2, 3)), ("y", (1, 2, 3)), ("z", (1, 2, 3)), ("c", (1,))):
        for s in steps:
            pl.semaphore_signal(
                barrier, inc=1, device_id=device_at(moved(at, axis, s)), device_id_type=MESH
            )


def meet_lines():
    pl.semaphore_wait(pltpu.get_barrier_semaphore(), 10)


def tell_line(at, axis, sem):
    for s in (1,) if axis == "c" else (1, 2, 3):
        pl.semaphore_signal(sem, inc=1, device_id=device_at(moved(at, axis, s)), device_id_type=MESH)


def bring(pairs, sem, base=0):
    copies = [pltpu.make_async_copy(src, dst, sem.at[base + n]) for n, (src, dst) in enumerate(pairs)]
    for copy in copies:
        copy.start()
    return copies


def remote_copy(src, dst, send, recv, device):
    return pltpu.make_async_remote_copy(
        src_ref=src, dst_ref=dst, send_sem=send, recv_sem=recv, device_id=device, device_id_type=MESH
    )


def gather_steps(streams, own_view, outs, at, sends, recvs, locs, pending):
    other = moved(at, "c", 1)
    crossing = {i: [] for i in range(len(streams))}
    local_copies, state = {}, {}

    def push(src, dst, i, k, to):
        copy = remote_copy(src, dst, sends.at[i, k], recvs.at[i, k], device_at(to))
        copy.start()
        pending.append(copy)
        return copy

    def cross(ref, i, k):
        crossing[i].append(push(ref, ref, i, k, other))

    def keep_own(i):
        name, op, view, order, halves = streams[i]
        for j, h in enumerate(halves):
            copy = pltpu.make_async_copy(own_view(i, h), view(outs[op], at, h), locs.at[i, j])
            copy.start()
            local_copies[(i, j)] = copy

    def block_sel(order, phase, index=None):
        sel = {"c": at["c"]}
        for a in "xyz":
            if a in order and order.index(a) < phase:
                continue
            sel[a] = at[a]
        if index is not None:
            sel[order[phase]] = index
        return sel

    def begin(i, phase):
        name, op, view, order, halves = streams[i]
        axis = order[phase]
        n = len(halves)
        sel = block_sel(order, phase)
        copies = {}
        if phase == 0:
            keep_own(i)
            span = (halves[0][0], halves[-1][1])
            for d in (1, 3, 2):
                copies[d] = push(own_view(i, span), view(outs[op], sel, span), i, d, moved(at, axis, d))
        else:
            for d, hs in ((1, range(n)), (3, reversed(range(n)))):
                for h in hs:
                    ref = view(outs[op], sel, halves[h])
                    copies[(d, h)] = push(ref, ref, i, phase * 6 + (0 if d == 1 else 2) + h, moved(at, axis, d))
        state[(i, phase)] = copies
        if phase == len(order) - 1:
            for h in range(n):
                cross(view(outs[op], sel, halves[h]), i, 20 + h)

    def relay(i, phase):
        name, op, view, order, halves = streams[i]
        axis = order[phase]
        last = phase == len(order) - 1
        n = len(halves)
        copies = state[(i, phase)]
        for d in (1, 3) if n == 2 else (1,):
            h = 0 if d == 1 else n - 1
            copies[(d, h)].wait_recv()
            ref = view(outs[op], block_sel(order, phase, lax.rem(at[axis] + 4 - d, 4)), halves[h])
            copies[(d, "f")] = push(ref, ref, i, phase * 6 + (4 if d == 1 else 5), moved(at, axis, d))
            if last:
                cross(ref, i, 22 + d)

    def finish(i, phase):
        name, op, view, order, halves = streams[i]
        axis = order[phase]
        last = phase == len(order) - 1
        n = len(halves)
        copies = state[(i, phase)]
        if phase == 0:
            for d in (1, 3, 2):
                copies[d].wait_recv()
            for h in range(n):
                local_copies[(i, h)].wait()
            return
        for d in (1, 3):
            for h in range(n):
                if h == (0 if d == 1 else n - 1) and not (n == 1 and d == 3):
                    continue
                copies[(d, h)].wait_recv()
                if last:
                    sel = block_sel(order, phase, lax.rem(at[axis] + 4 - d, 4))
                    cross(view(outs[op], sel, halves[h]), i, 26 + d)
        for d in (1, 3):
            if (d, "f") not in copies:
                continue
            copies[(d, "f")].wait_recv()
            if last:
                h = 0 if d == 1 else n - 1
                sel = block_sel(order, phase, lax.rem(at[axis] + 2, 4))
                cross(view(outs[op], sel, halves[h]), i, 30 + d)

    def crossed(i):
        for copy in crossing[i]:
            copy.wait_recv()

    return begin, relay, finish, crossed


def cut_view(ref, layout, sel, cut=None, span=None, base=0):
    index = []
    for dim in layout:
        if dim in sel:
            index.append(sel[dim])
        elif dim == cut and span is not None:
            index.append(pl.ds(base + span[0], span[1] - span[0]))
        else:
            index.append(slice(None))
    return ref.at[tuple(index)]


def sizes_of(layout, plain):
    return tuple(plain[d] if d in plain else 4 for d in layout)


def landing_shapes(chain):
    name, layout, plain, cut, base, order, halves = chain
    left = layout.replace("c", "")
    shapes = []
    for axis in order:
        left = left.replace(axis, "")
        for span in halves:
            shapes.append(sizes_of(left, {**plain, cut: span[1] - span[0]}))
        shapes += [sizes_of(left, plain)] * 2
    return shapes


STEPS = (2, 1, 3, 0)


def scatter_steps(chains, stores, landing, at, sends, recvs, pending):
    other = moved(at, "c", 1)

    def push(src, dst, i, k, to):
        copy = remote_copy(src, dst, sends.at[i, k], recvs.at[i, k], device_at(to))
        copy.start()
        pending.append(copy)
        return copy

    def view(i, sel, span):
        name, layout, plain, cut, base, order, halves = chains[i]
        ref, inner, fixed = stores[i]
        return cut_view(ref, inner, {**fixed, **sel}, cut, span, base)

    def add(i, sel, srcs, span):
        name, layout, plain, cut, base, order, halves = chains[i]
        inner = layout.replace("c", "")
        free = [d for d in inner if d in "xyz" and d not in sel]
        tiles = span[1] - span[0]
        for d, size in plain.items():
            tiles = tiles if d == cut else tiles * size
        tiles = max(tiles // 2048, 1)
        while free and tiles * 4 <= 64:
            free.pop()
            tiles *= 4
        count = 4 ** len(free)

        def one(n, _):
            here = dict(sel)
            for k, d in enumerate(reversed(free)):
                here[d] = lax.rem(lax.div(n, 4**k), 4)
            where = view(i, here, span)
            terms = [
                cut_view(src, src_layout, {**{d: here[d] for d in free}, **src_sel}, cut, src_span)
                for src, src_layout, src_sel, src_span in srcs
            ]
            if len(terms) == 1:
                where[...] = where[...] + terms[0][...]
            else:
                where[...] = (
                    where[...].astype(F32) + terms[0][...].astype(F32) + terms[1][...].astype(F32)
                ).astype(BF)
            return 0

        if count == 1:
            one(0, 0)
        else:
            lax.fori_loop(0, count, one, 0)

    def lend(i, sib):
        name, layout, plain, cut, base, order, halves = chains[i]
        ref, inner, fixed = stores[i]
        axis, span = order[0], (0, plain[cut])
        copies = []
        for k, step in enumerate(STEPS):
            a = lax.rem(at[axis] + step, 4)
            far = cut_view(ref, inner, {"c": other["c"], axis: a}, cut, span, base)
            copies.append(push(far, cut_view(sib, layout.replace("c", ""), {axis: a}), i, k, other))
        return copies

    def names(i, phase):
        name, layout, plain, cut, base, order, halves = chains[i]
        inner = layout.replace("c", "")
        axis = order[phase]
        done = {a: at[a] for a in order[:phase]}
        left = "".join(d for d in inner if d not in order[: phase + 1])
        buffers = landing[i * 12 + 4 * phase : i * 12 + 4 * phase + 4]
        return inner, axis, done, left, buffers, 4 + phase * 6, cut, halves, (0, plain[cut])

    def start(i, phase, lent=None, sib=None):
        inner, axis, done, left, (r0, r1, rp, rm), slot, cut, halves, span = names(i, phase)
        up, down = moved(at, axis, 1), moved(at, axis, 3)
        got = {}
        for k, step in enumerate(STEPS):
            a = lax.rem(at[axis] + step, 4)
            if lent is not None:
                lent[k].wait_recv()
                add(i, {axis: a}, [(sib, inner, {axis: a}, span)], span)
            part = lambda h: view(i, {**done, axis: a}, h)
            if step == 2:
                got["r0"] = push(part(halves[0]), r0, i, slot, up)
                got["r1"] = push(part(halves[1]), r1, i, slot + 1, down)
            elif step == 1:
                got["p1"] = push(part(halves[1]), cut_view(rp, left, {}, cut, halves[1]), i, slot + 2, up)
            elif step == 3:
                got["m0"] = push(part(halves[0]), cut_view(rm, left, {}, cut, halves[0]), i, slot + 3, down)
        return got

    def middle(i, phase, got):
        inner, axis, done, left, (r0, r1, rp, rm), slot, cut, halves, span = names(i, phase)
        up, down = moved(at, axis, 1), moved(at, axis, 3)
        for key, h, buf, land, to, k in (("r0", 0, r0, rp, up, 4), ("r1", 1, r1, rm, down, 5)):
            half = halves[h]
            got[key].wait_recv()
            sel = {**done, axis: to[axis]}
            add(i, sel, [(buf, left, {}, (0, half[1] - half[0]))], half)
            got[k] = push(view(i, sel, half), cut_view(land, left, {}, cut, half), i, slot + k, to)

    def close(i, phase, got):
        inner, axis, done, left, (r0, r1, rp, rm), slot, cut, halves, span = names(i, phase)
        for k in ("p1", "m0", 4, 5):
            got[k].wait_recv()
        add(i, {**done, axis: at[axis]}, [(rp, left, {}, span), (rm, left, {}, span)], span)

    return lend, start, middle, close, view


def swap_rows(block, post, postr, at, send, recv, pending):
    for n in range(4):
        post[n] = block[:, 4 * n : 4 * n + 4, :].astype(BF)
    copies = []
    for s in (1, 2, 3):
        to = moved(at, "z", s)
        copy = remote_copy(post.at[to["z"]], postr.at[s], send.at[s], recv.at[s], device_at(to))
        copy.start()
        pending.append(copy)
        copies.append(copy)
    return copies


def swapped_rows(copies, post, postr, at, out):
    out[at["z"]] = post[at["z"]].astype(F32)
    for s in (1, 2, 3):
        copies[s - 1].wait_recv()
        out[lax.rem(at["z"] + 4 - s, 4)] = postr[s].astype(F32)


VM = pl.BlockSpec(memory_space=pltpu.VMEM)
ANY = pl.BlockSpec(memory_space=pl.ANY)
SM = pl.BlockSpec(memory_space=pltpu.SMEM)
epsilon = 1e-05


def mm(a, b):
    return lax.dot_general(a, b, (((1,), (0,)), ((), ())), preferred_element_type=F32)


def mm_nt(a, b):
    return lax.dot_general(a, b, (((1,), (1,)), ((), ())), preferred_element_type=F32)


def mm_tn(a, b):
    return lax.dot_general(a, b, (((0,), (0,)), ((), ())), preferred_element_type=F32)


def wide_block(ref, first, count=4):
    return jnp.concatenate([ref[first + k] for k in range(count)], axis=1)


def put_wide(ref, first, value, count=4):
    for k in range(count):
        ref[first + k] = value[:, 128 * k : 128 * (k + 1)].astype(BF)


V_CONV, V_ENC, V_GAIN0, V_SHIFT0, V_GAIN1, V_SHIFT1, V_QUERY, V_VALUE, V_OUT, V_GAIN2, V_SHIFT2, V_RED = range(12)


def over_rows(body, step=512, rows=512):
    def one(n, _):
        body(pl.ds(pl.multiple_of(n * step, step), step))
        return 0

    lax.fori_loop(0, rows // step, one, 0)


def normalize(v):
    mean = jnp.mean(v, axis=-1, keepdims=True)
    centred = v - mean
    spread = jnp.mean(centred * centred, axis=-1, keepdims=True)
    rstd = lax.rsqrt(spread + epsilon)
    return centred * rstd, rstd


def norm_pull(hat, rstd, gain, grad):
    up = grad * gain
    a = jnp.mean(up, axis=-1, keepdims=True)
    b = jnp.mean(up * hat, axis=-1, keepdims=True)
    return rstd * (up - a - hat * b)


def total(v):
    return jnp.sum(v, axis=0, keepdims=True)


def gelu_both(u):
    cdf = 0.5 * (1.0 + lax.erf(u * 0.7071067811865476))
    pdf = 0.3989422804014327 * jnp.exp(-0.5 * u * u)
    return u * cdf, cdf + u * pdf


def three(v):
    hi = v.astype(BF).astype(F32)
    rest = v - hi
    mid = rest.astype(BF).astype(F32)
    return hi, mid, rest - mid


BLOCK_STREAMS = (
    ("up", 0, wide_view, "xyz", ((0, 2), (2, 4))),
    ("down", 1, tall_view, "zyx", ((0, 256), (256, 512))),
)
BLOCK_CHAINS = (
    ("up", "zKxycSL", {"K": 4, "S": 16, "L": 128}, "K", 0, "zyx", ((0, 2), (2, 4))),
    ("down", "xyczSL", {"S": 16, "L": 512}, "L", 0, "xyz", ((0, 256), (256, 512))),
)


def block_kernel(
    length, conv_in, ordered_in, go_in, w1_in, up_own_in, down_own_in, vec_in, xb_in,
    result_out, first_grad_out, conv_grad_out, g1_out, gv_out, o1, o2,
    conv, ordered, go, w1, up_own, down_own, vec, xb, result, first_grad, conv_grad, g1, gv, gv_tiles,
    big, hat0, rstd0, first, hat1, rstd1, normed, normed_t, q, k, v, k_t, v_t,
    mixed_t, mixed, rows_a, rows_b, kx, xa, ya, hat2, rstd2, n2, n2_t,
    second, act, dh, da, acc, acc2, dn, d_mixed, dq_t, dk, dv, scores,
    up_all, down_all, g_up, g_down, sib_up, sib_down, *rest,
):
    landing = rest[:24]
    post, postr, sends, recvs, locs, back_s, back_r, swap_s, swap_r, in_sem, out_sem = rest[24:]
    at = place()
    greet_lines(at)
    fetched = bring(
        (
            (up_own_in, up_own), (down_own_in, down_own), (conv_in, conv), (w1_in, w1), (vec_in, vec),
            (ordered_in, ordered), (go_in, go), (xb_in, xb),
        ),
        in_sem,
    )
    meet_lines()
    for copy in fetched[:2]:
        copy.wait()
    pending = []
    own_view = lambda i, h: (
        up_own.at[pl.ds(h[0], h[1] - h[0])] if i == 0 else down_own.at[:, pl.ds(h[0], h[1] - h[0])]
    )
    begin, relay, finish, crossed = gather_steps(
        BLOCK_STREAMS, own_view, (up_all, down_all), at, sends, recvs, locs, pending
    )
    stores = (
        (g_up.reshape((4, 4, 4, 4, 2, 16, 128)), "zKxycSL", {"c": at["c"]}),
        (g_down.reshape((4, 4, 2, 4, 16, 512)), "xyczSL", {"c": at["c"]}),
    )
    lend, start, middle, close, view = scatter_steps(
        BLOCK_CHAINS, stores, landing, at, back_s, back_r, pending
    )
    both = (0, 1)
    up_blocks, down_rows = up_all.reshape((16, 512, 128)), down_all.reshape((2048, 512))
    for i in both:
        begin(i, 0)
    for copy in fetched[2:]:
        copy.wait()
    row = lambda n: vec[n : n + 1, :]
    gv[...] = jnp.zeros_like(gv)

    def gain(n, value):
        gv[n : n + 1, :] += total(value)

    big[...] = mm(conv[...], wide_block(w1, 0))
    for i in both:
        finish(i, 0)
        begin(i, 1)

    def encode(r):
        hat, rstd = normalize(big[r, :] + row(V_ENC))
        hat0[r, :] = hat
        rstd0[r, :] = rstd
        here = ordered[r, :].astype(F32) + hat * row(V_GAIN0) + row(V_SHIFT0)
        first[r, :] = here
        hat, rstd = normalize(here)
        hat1[r, :] = hat
        rstd1[r, :] = rstd
        normed[r, :] = (hat * row(V_GAIN1) + row(V_SHIFT1)).astype(BF)

    over_rows(encode)
    normed_t[...] = normed[...].T
    q[...] = (0.25 * (mm(normed[...], wide_block(w1, 4)) + row(V_QUERY)).astype(BF).astype(F32)).astype(BF)
    k[...] = mm(normed[...], wide_block(w1, 8)).astype(BF)
    v[...] = (mm(normed[...], wide_block(w1, 12)) + row(V_VALUE)).astype(BF)
    k_t[...] = k[...].T
    turned = v[...].T
    one_row = jnp.where(lax.broadcasted_iota(jnp.int32, (16, 512), 0) == 0, 1.0, 0.0).astype(BF)
    for h in range(32):
        v_t[h, 0:16, :] = turned[16 * h : 16 * h + 16, :]
        v_t[h, 16:32, :] = one_row
    for i in both:
        relay(i, 1)

    lane = lax.broadcasted_iota(jnp.int32, (1, 128), 1)
    seat = lax.broadcasted_iota(jnp.int32, (512, 128), 0)
    spot = lax.broadcasted_iota(jnp.int32, (512, 128), 1)
    hidden_key = jnp.where((spot == 96) & (seat >= length[0]), -1e30, 0.0)
    kx[...] = jnp.where(spot < 96, 1.0, hidden_key).astype(BF)
    one_lane = jnp.where(spot == 96, 1.0, 0.0).astype(BF)
    rows_a[...] = jnp.zeros_like(rows_a)
    rows_b[...] = jnp.zeros_like(rows_b)

    def head_places(h):
        group = pl.ds(pl.multiple_of(lax.div(h, 8) * 128, 128), 128)
        mine = jnp.where(lax.div(lane, 16) == lax.rem(h, 8), 1.0, 0.0).astype(BF)
        extra = jnp.where((lax.rem(lane, 32) == h) & (lane < 96) | (lane == 96), 1.0, 0.0).astype(BF)
        return group, mine, extra, pl.ds(pl.multiple_of(h * 16, 16), 16)

    def keys_of(group):
        return jnp.concatenate([k[:, group], kx[...]], axis=1)

    def note(h, value):
        hi, mid, lo = three(value)
        rows_a[pl.ds(h, 1), :] = hi
        rows_a[pl.ds(h + 32, 1), :] = mid
        rows_a[pl.ds(h + 64, 1), :] = lo

    def score_head(h, slot):
        group, mine, extra, channels = head_places(h)
        asks = jnp.concatenate([q[:, group] * mine, one_lane], axis=1)
        scores[slot] = mm_nt(keys_of(group), asks)

    def forward_head(h, slot):
        group, mine, extra, channels = head_places(h)
        peak = jnp.max(scores[slot], axis=0, keepdims=True)
        e = jnp.exp(scores[slot] - peak).astype(BF)
        got = mm(v_t[h], e)
        summed = got[16:17, :]
        mixed_t[channels, :] = got[0:16, :] / summed
        note(h, -(peak + jnp.log(summed)))

    def forward_pair(n, _):
        score_head(n * 2 + 1, 1)
        forward_head(n * 2, 0)
        score_head(lax.rem(n * 2 + 2, 32), 0)
        forward_head(n * 2 + 1, 1)
        return 0

    def two_heads(body):
        def pair(n, _):
            for j in range(2):
                body(n * 2 + j)
            return 0

        return pair

    rows_a[96:97, :] = jnp.ones((1, 512), F32)
    score_head(0, 0)
    lax.fori_loop(0, 4, forward_pair, 0)
    for i in both:
        finish(i, 1)
        begin(i, 2)
    lax.fori_loop(4, 10, forward_pair, 0)
    for i in both:
        relay(i, 2)
    lax.fori_loop(10, 16, forward_pair, 0)
    for i in both:
        finish(i, 2)
    xa[...] = rows_a[...].T.astype(BF)
    mixed[...] = mixed_t[...].T.astype(BF)

    big[...] = mm(mixed[...], wide_block(w1, 16))

    def after(r):
        here = first[r, :] + big[r, :] + row(V_OUT)
        second[r, :] = here
        hat, rstd = normalize(here)
        hat2[r, :] = hat
        rstd2[r, :] = rstd
        n2[r, :] = (hat * row(V_GAIN2) + row(V_SHIFT2)).astype(BF)
        gain(V_RED, go[r, :].astype(F32))

    over_rows(after)
    n2_t[...] = n2[...].T
    acc[...] = jnp.zeros_like(acc)
    acc2[...] = jnp.zeros_like(acc2)
    for i in both:
        crossed(i)

    def chunk(c, _):
        up = jnp.concatenate([up_blocks[4 * c + j] for j in range(4)], axis=1)
        span = pl.ds(pl.multiple_of(c * 512, 512), 512)
        down = down_rows[span, :]
        big[...] = mm(n2[...], up)
        da[...] = mm_nt(go[...], down)

        def gelu_rows(r):
            value, slope = gelu_both(big[r, :] + xb[pl.ds(c, 1), :])
            act[r, :] = value.astype(BF)
            low = (da[r, :] * slope).astype(BF)
            dh[r, :] = low
            gv[pl.ds(12 + c, 1), :] += total(low.astype(F32))

        over_rows(gelu_rows, 128)
        acc[...] += mm(act[...], down)
        acc2[...] += mm_nt(dh[...], up)
        g_down[span, :] = mm_tn(act[...], go[...]).astype(BF)
        grad_up = mm(n2_t[...], dh[...])
        for j in range(4):
            g_up[4 * c + j] = grad_up[:, 128 * j : 128 * (j + 1)].astype(BF)
        return 0

    lax.fori_loop(0, 4, chunk, 0)
    lent = [lend(0, sib_up), lend(1, sib_down)]

    def before_mlp(r):
        result[r, :] = (second[r, :] + acc[r, :] + row(V_RED)).astype(BF)
        grad = acc2[r, :]
        hat = hat2[r, :]
        gain(V_GAIN2, grad * hat)
        gain(V_SHIFT2, grad)
        here = go[r, :].astype(F32) + norm_pull(hat, rstd2[r, :], row(V_GAIN2), grad)
        second[r, :] = here
        low = here.astype(BF)
        dn[r, :] = low
        gain(V_OUT, low.astype(F32))

    over_rows(before_mlp)
    out_copies = bring(((result, result_out),), out_sem)
    put_wide(g1, 16, mm_tn(mixed[...], dn[...]))
    d_mixed[...] = mm_nt(dn[...], wide_block(w1, 16)).astype(BF)
    big[...] = d_mixed[...].astype(F32).T
    state = {0: start(0, 0, lent[0], sib_up), 1: start(1, 0, lent[1], sib_down)}

    def inner(h, _):
        channels = pl.ds(pl.multiple_of(h * 16, 16), 16)
        hi, mid, lo = three(-total(big[channels, :] * mixed_t[channels, :]))
        rows_b[pl.ds(h, 1), :] = hi
        rows_b[pl.ds(h + 32, 1), :] = mid
        rows_b[pl.ds(h + 64, 1), :] = lo
        return 0

    lax.fori_loop(0, 32, inner, 0)
    ya[...] = rows_b[...].T.astype(BF)
    dk[...] = jnp.zeros_like(dk)
    dv[...] = jnp.zeros_like(dv)
    ones = jnp.where(spot < 96, 1.0, 0.0).astype(BF)

    def backward_head(h):
        group, mine, extra, channels = head_places(h)
        q_h = q[:, group] * mine
        m_h = d_mixed[:, group] * mine
        p = jnp.exp(mm_nt(keys_of(group), jnp.concatenate([q_h, xa[...] * extra], axis=1)))
        values = jnp.concatenate([v[:, group], ones], axis=1)
        slope = mm_nt(values, jnp.concatenate([m_h, ya[...] * extra], axis=1))
        ds = (p * slope).astype(BF)
        dv[:, group] += mm(p.astype(BF), m_h)
        dk[:, group] += mm(ds, q_h)
        dq_t[channels, :] = mm(k_t[channels, :], ds)

    backward_heads = two_heads(backward_head)
    lax.fori_loop(0, 4, backward_heads, 0)
    for i in both:
        middle(i, 0, state[i])
    lax.fori_loop(4, 8, backward_heads, 0)
    for i in both:
        close(i, 0, state[i])
        state[i] = start(i, 1)
    lax.fori_loop(8, 11, backward_heads, 0)
    for i in both:
        middle(i, 1, state[i])
    lax.fori_loop(11, 13, backward_heads, 0)
    for i in both:
        close(i, 1, state[i])
        state[i] = start(i, 2)
    lax.fori_loop(13, 16, backward_heads, 0)
    for i in both:
        middle(i, 2, state[i])
    q[...] = (0.25 * dq_t[...].T).astype(BF)
    k[...] = dk[...].astype(BF)
    v[...] = dv[...].astype(BF)
    gain(V_QUERY, q[...].astype(F32))
    gain(V_VALUE, v[...].astype(F32))
    put_wide(g1, 4, mm(normed_t[...], q[...]))
    put_wide(g1, 8, mm(normed_t[...], k[...]))
    put_wide(g1, 12, mm(normed_t[...], v[...]))
    for i in both:
        close(i, 2, state[i])
    o2[...] = g_down.reshape((4, 4, 2, 4, 16, 512))[at["x"], at["y"], at["c"], at["z"]].astype(F32)
    rows_up = g_up.reshape((4, 4, 4, 4, 2, 16, 128))[at["z"], :, at["x"], at["y"], at["c"]].astype(F32)
    swaps = swap_rows(rows_up, post, postr, at, swap_s, swap_r, pending)
    acc2[...] = (
        mm_nt(q[...], wide_block(w1, 4)) + mm_nt(k[...], wide_block(w1, 8)) + mm_nt(v[...], wide_block(w1, 12))
    )

    def before_attention(r):
        grad = acc2[r, :]
        hat = hat1[r, :]
        gain(V_GAIN1, grad * hat)
        gain(V_SHIFT1, grad)
        here = second[r, :] + norm_pull(hat, rstd1[r, :], row(V_GAIN1), grad)
        first_grad[r, :] = here
        hat = hat0[r, :]
        gain(V_GAIN0, here * hat)
        gain(V_SHIFT0, here)
        low = norm_pull(hat, rstd0[r, :], row(V_GAIN0), here).astype(BF)
        dn[r, :] = low
        gain(V_ENC, low.astype(F32))

    over_rows(before_attention)
    put_wide(g1, 0, mm_tn(conv[...], dn[...]))
    out_copies += bring(((g1, g1_out), (first_grad, first_grad_out)), out_sem, 1)
    conv_grad[...] = mm_nt(dn[...], wide_block(w1, 0)).astype(BF)
    out_copies += bring(((conv_grad, conv_grad_out),), out_sem, 3)
    gain(V_CONV, conv_grad[...].astype(F32))
    lane_to = lax.broadcasted_iota(jnp.int32, (128, 512), 1)
    lane_from = lax.broadcasted_iota(jnp.int32, (128, 512), 0)
    shuffle = jnp.where(lane_from == lax.div(lane_to, 16) * 4 + lax.rem(lane_to, 4), 1.0, 0.0).astype(BF)
    which = lax.div(lax.rem(lax.broadcasted_iota(jnp.int32, (16, 512), 1), 16), 4)
    level = lax.broadcasted_iota(jnp.int32, (16, 512), 0) - 12
    for x in range(4):
        chosen = jnp.where(which == level, jnp.broadcast_to(gv[12 + x : 13 + x, :], (16, 512)), 0.0)
        hi, mid, lo = three(chosen)
        dealt_rows = (
            mm_nt(hi.astype(BF), shuffle) + mm_nt(mid.astype(BF), shuffle) + mm_nt(lo.astype(BF), shuffle)
        )
        gv_tiles[x, 0:12, :] = gv[0:12, 128 * x : 128 * (x + 1)]
        gv_tiles[x, 12:16, :] = dealt_rows[12:16, :]
    out_copies += bring(((gv_tiles, gv_out),), out_sem, 4)
    swapped_rows(swaps, post, postr, at, o1)
    for copy in pending:
        copy.wait_send()
    for copy in out_copies:
        copy.wait()


def block(length, conv, ordered, go, w1, up_own, down_own, vec, xb):
    shape = jax.ShapeDtypeStruct
    full = (512, 512)
    f, b, col = pltpu.VMEM(full, F32), pltpu.VMEM(full, BF), pltpu.VMEM((512, 1), F32)
    rows, lanes = pltpu.VMEM((128, 512), F32), pltpu.VMEM((512, 128), BF)
    dma = pltpu.SemaphoreType.DMA
    return pl.pallas_call(
        block_kernel,
        out_shape=(
            shape(full, BF),
            shape(full, F32),
            shape(full, BF),
            shape((20, 512, 128), BF),
            shape((4, 16, 128), F32),
            shape((4, 4, 4, 128), F32),
            shape((16, 512), F32),
        ),
        in_specs=[SM] + [ANY] * 8,
        out_specs=[ANY] * 5 + [VM] * 2,
        scratch_shapes=[
            b, b, b, pltpu.VMEM((20, 512, 128), BF), pltpu.VMEM((4, 16, 128), BF), pltpu.VMEM((16, 512), BF),
            pltpu.VMEM((16, 512), F32), pltpu.VMEM((4, 512), F32),
            b, f, b, pltpu.VMEM((20, 512, 128), BF), pltpu.VMEM((16, 512), F32), pltpu.VMEM((4, 16, 128), F32),
            f, f, col, f, f, col, b, b, b, b, b, b, pltpu.VMEM((32, 32, 512), BF),
            f, b, rows, rows, lanes, lanes, lanes, f, col, b, b,
            f, b, b, f, f, f, b, b, f, f, f, pltpu.VMEM((2, 512, 512), F32),
            pltpu.VMEM((4, 4, 4, 4, 2, 16, 128), BF),
            pltpu.VMEM((4, 4, 2, 4, 16, 512), BF),
            pltpu.VMEM((16, 512, 128), BF),
            pltpu.VMEM((2048, 512), BF),
            pltpu.VMEM((4, 4, 4, 4, 16, 128), BF),
            pltpu.VMEM((4, 4, 4, 16, 512), BF),
        ]
        + [pltpu.VMEM(s, BF) for chain in BLOCK_CHAINS for s in landing_shapes(chain)]
        + [
            pltpu.VMEM((4, 4, 4, 128), BF),
            pltpu.VMEM((4, 4, 4, 128), BF),
            dma((2, SLOTS)),
            dma((2, SLOTS)),
            dma((2, 2)),
            dma((2, 22)),
            dma((2, 22)),
            dma((4,)),
            dma((4,)),
            dma((8,)),
            dma((5,)),
        ],
        compiler_params=pltpu.CompilerParams(
            collective_id=2, has_side_effects=True, vmem_limit_bytes=62 * 2**20
        ),
        name="block",
    )(length, conv, ordered, go, w1, up_own, down_own, vec, xb)


def spread_rows(picks, j, b):
    seat = lax.broadcasted_iota(jnp.int32, (512, 256), 0)
    return jnp.where(seat == picks[j : j + 1, 256 * b : 256 * (b + 1)], 1.0, 0.0).astype(BF)


def line_neighbour(at, step):
    linear = lax.rem(((at["x"] * 4 + at["y"]) * 2 + at["c"]) * 4 + at["z"] + step, 128)
    return (lax.div(linear, 4), lax.rem(linear, 4))


def device_after(me, s):
    linear = lax.rem(me + s, 128)
    return (lax.div(linear, 4), lax.rem(linear, 4))


def deal(rows, landing, me, send, recv):
    def one(s, _):
        pltpu.make_async_remote_copy(
            src_ref=rows.at[lax.rem(me + s, 128)],
            dst_ref=landing.at[me],
            send_sem=send,
            recv_sem=recv,
            device_id=device_after(me, s),
            device_id_type=MESH,
        ).start()
        return 0

    lax.fori_loop(1, 128, one, 0)
    landing[me] = rows[me]


def dealt(rows, landing, me, send, recv):
    return pltpu.make_async_remote_copy(
        src_ref=rows.at[pl.ds(0, 127)],
        dst_ref=landing.at[pl.ds(0, 127)],
        send_sem=send,
        recv_sem=recv,
        device_id=device_after(me, 1),
        device_id_type=MESH,
    )


def fold_rows(index, rows, out):
    for n in range(4):
        seat = lax.broadcasted_iota(jnp.int32, (256, 512), 0) + 256 * n
        hot = jnp.where(seat == index, 1.0, 0.0).astype(BF)
        out[32 * n : 32 * (n + 1)] = mm(hot, rows).reshape(32, 8, 512).astype(BF)


def unfold_rows(index, blocks):
    seat = lax.broadcasted_iota(jnp.int32, (1024, 512), 0)
    hot = jnp.where(seat == index, 1.0, 0.0).astype(BF)
    return mm_tn(hot, blocks[...].astype(F32).reshape(1024, 512).astype(BF)).astype(BF)


def column_of(row):
    return jnp.broadcast_to(row, (128, 512)).T[:, 0:1]


def front_kernel(
    conv_in, encode_in, triple_in, output_in, expand_in, small_in, points_in, inverse_in, perm_in, neighbours_in,
    gc, g1, up_out, picked, conv_out, ordered_out, vectors_out, natural_out, take_out, send_out, picks_out,
    encode, triple, output, expand, small, points, inverse, perm, neighbours, conv,
    up_own, conv_low, ordered, vectors, natural, take, send, picks,
    outgoing, incoming, m1p, vt,
    extended, all_picks, acc, w_buf, pick_cols, pre, m1b, prev, vb, gv,
    sends, recvs, locs, presend, prerecv, halo_s, halo_r, p_sem, w_sem, deal_s, deal_r, met, in_sem, out_sem,
):
    at = place()
    width = 512
    me = ((at["x"] * 4 + at["y"]) * 2 + at["c"]) * 4 + at["z"]
    greet_lines(at)
    fetched = bring(
        (
            (encode_in, encode), (triple_in, triple), (output_in, output), (expand_in, expand), (small_in, small),
            (conv_in, conv), (points_in, points), (inverse_in, inverse), (perm_in, perm), (neighbours_in, neighbours),
        ),
        in_sem,
    )
    for copy in fetched[:6]:
        copy.wait()
    for first_block, per, base, refs in (
        (0, 5, 0, ((encode, 4), (triple, 12), (output, 4))), (0, 4, 5, ((expand, 16),))
    ):
        n = 0
        for ref, blocks in refs:
            for j in range(blocks):
                m1p[n // per, base + n % per] = ref[:, 128 * j : 128 * (j + 1)]
                n += 1
    row64 = lax.broadcasted_iota(jnp.int32, (16, 64), 0)
    lane64 = lax.broadcasted_iota(jnp.int32, (16, 64), 1)
    alone = jnp.where(lax.div(lane64, 4) == row64, jnp.broadcast_to(small[...], (16, 64)), 0.0).astype(BF)
    from64 = lax.broadcasted_iota(jnp.int32, (64, 128), 0)
    to128 = lax.broadcasted_iota(jnp.int32, (64, 128), 1)
    lane0 = lax.rem(at["y"] * 2 + at["c"], 8) * 16 + at["z"] * 4
    vt[...] = mm(alone, jnp.where(to128 == lane0 + lax.rem(from64, 4), 1.0, 0.0).astype(BF)).astype(BF)
    meet_lines()
    tell_line(at, "x", met.at[0])
    pending = []

    def own_view(i, h):
        name, op, view, order, halves = FRONT_STREAMS[i]
        if op == 0:
            return conv.at[pl.ds(h[0], h[1] - h[0]), :]
        return m1b.at[pl.ds(h[0], h[1] - h[0])] if op == 1 else vb

    begin, relay, finish, crossed = gather_steps(
        FRONT_STREAMS, own_view, (gc, g1, gv), at, sends, recvs, locs, pending
    )

    def remote(src, dst, send, recv, device):
        copy = remote_copy(src, dst, send, recv, device)
        copy.start()
        pending.append(copy)
        return copy

    pre_copies = []
    for step in (1, 2, 3):
        to = moved(at, "z", step)
        for j, (src, dst) in enumerate(((m1p.at[to["z"]], pre.at[step]), (vt, prev.at[step]))):
            pre_copies.append(remote(src, dst, presend.at[j, step], prerecv.at[j, step], device_at(to)))
    first, more = (0, 1, 2), (3, 4)
    for i in first:
        begin(i, 0)
    for copy in fetched[6:]:
        copy.wait()
    home = lax.div(inverse[...], width)
    row_id = lax.broadcasted_iota(jnp.int32, (width, width), 0)
    lane_id = lax.broadcasted_iota(jnp.int32, (width, width), 1)
    ahead = jnp.where((column_of(home.astype(F32)) == home.astype(F32)) & (row_id < lane_id), 1.0, 0.0)
    send[...] = home * 8 + total(ahead).astype(jnp.int32)
    pl.semaphore_wait(met.at[0], 3)
    tell_line(at, "y", met.at[1])
    fold_rows(send[...], points[...], outgoing)
    pl.semaphore_wait(met.at[1], 3)
    tell_line(at, "c", met.at[2])
    for copy in pre_copies:
        copy.wait_recv()
    pre[0] = m1p[at["z"]]

    def tile(k, _):
        pieces = [pre[lax.rem(at["z"] - s + 4, 4), k].astype(F32) for s in range(4)]
        m1b[k] = jnp.concatenate(pieces, axis=0).astype(BF)
        return 0

    lax.fori_loop(0, 9, tile, 0)
    vb[...] = (
        vt[...].astype(F32) + prev[1].astype(F32) + prev[2].astype(F32) + prev[3].astype(F32)
    ).astype(BF)
    up_own[...] = m1b[5:9]
    for i in more:
        begin(i, 0)
    pl.semaphore_wait(met.at[2], 1)
    deal(outgoing, incoming, me, deal_s, deal_r)
    for i in first + more:
        finish(i, 0)
        begin(i, 1)
    source = lax.div(perm[...], width)
    column = column_of(perm[...].astype(F32))
    source_column = lax.div(column.astype(jnp.int32), width)
    ahead = jnp.where((source_column == source) & (column < perm[...].astype(F32)), 1.0, 0.0)
    take[...] = source * 8 + total(ahead).astype(jnp.int32)
    token = lax.broadcasted_iota(jnp.int32, (1, width), 1)
    shift = me * width - 128 + lax.div(token, 256) * 256

    for u in range(9):
        raw = neighbours[3 * u : 3 * u + 3, :]
        local = jnp.where(raw >= 0, raw - shift, -1)
        picks[u] = local
        pick_cols[u] = jnp.concatenate([local, local, local[0:2]], axis=0).astype(F32)
    out_copies = bring(((up_own, up_out), (take, take_out), (send, send_out), (picks, picks_out)), out_sem)
    for i in first + more:
        relay(i, 1)
    for i in first:
        finish(i, 1)
        begin(i, 2)
    acc[...] = jnp.zeros_like(acc)
    for i in more:
        finish(i, 1)
    dealt(outgoing, incoming, me, deal_s, deal_r).wait_recv()
    mine = unfold_rows(take[...], incoming)
    ordered[...] = mine
    out_copies += bring(((ordered, ordered_out),), out_sem, 4)
    extended[128:640, :] = mine
    halos = []
    for j, (src, dst, step) in enumerate(((128, 640, 127), (512, 0, 1))):
        halos.append(
            remote(
                extended.at[pl.ds(src, 128), :], extended.at[pl.ds(dst, 128), :],
                halo_s.at[j], halo_r.at[j], line_neighbour(at, step),
            )
        )

    def p_copy(u):
        return pltpu.make_async_copy(all_picks.at[pl.ds(u * 3, 3)], picked.at[pl.ds(u * 3, 3)], p_sem.at[u])

    def pick_unit(u, _):
        columns = pick_cols[u].T
        for j in range(3):
            for b in range(2):
                seat = lax.broadcasted_iota(jnp.int32, (256, 512), 1).astype(F32)
                hot = jnp.where(seat == columns[256 * b : 256 * (b + 1), j : j + 1], 1.0, 0.0).astype(BF)
                window = extended[256 * b : 256 * b + 512, :]
                all_picks[u * 3 + j, 256 * b : 256 * (b + 1), :] = mm(hot, window).astype(BF)
        p_copy(u).start()
        return 0

    def w_copy(u):
        slot = lax.rem(u, 2)
        return pltpu.make_async_copy(
            gc.reshape((4, 27, 512, 128)).at[:, pl.ds(u * 3, 3)], w_buf.at[slot], w_sem.at[slot]
        )

    def conv_unit(u, _):
        @pl.when(u < 8)
        def _():
            w_copy(u + 1).start()

        w_copy(u).wait()
        slot = lax.rem(u, 2)
        parts = [
            mm(all_picks[u * 3 + j], jnp.concatenate([w_buf[slot, n, j] for n in range(4)], axis=1))
            for j in range(3)
        ]
        acc[...] += parts[0] + parts[1] + parts[2]
        return 0

    for i in first:
        relay(i, 2)
    for i in (3,):
        begin(i, 2)
    for copy in halos:
        copy.wait_recv()
    lax.fori_loop(0, 5, pick_unit, 0)
    for i in (3,):
        relay(i, 2)
    lax.fori_loop(5, 9, pick_unit, 0)
    for i in first:
        finish(i, 2)
    for i in first:
        crossed(i)
    w_copy(0).start()
    lax.fori_loop(0, 6, conv_unit, 0)
    for i in (3,):
        finish(i, 2)
    lax.fori_loop(6, 9, conv_unit, 0)
    for i in more:
        crossed(i)
    chunks = []
    for x in range(4):
        chunk = jnp.zeros((16, 128), F32)
        for y in range(4):
            for c in range(2):
                chunk = chunk + gv[x, y, c].astype(F32)
        chunks.append(chunk)
    together = jnp.concatenate(chunks, axis=1)
    vectors[...] = together
    lane = lax.broadcasted_iota(jnp.int32, (128, width), 1)
    from_lane = lax.broadcasted_iota(jnp.int32, (128, width), 0)
    shuffle = jnp.where(from_lane == lax.div(lane, 16) * 4 + lax.rem(lane, 4), 1.0, 0.0).astype(BF)
    which = lax.div(lax.rem(lax.broadcasted_iota(jnp.int32, (4, width), 1), 16), 4)
    group = lax.broadcasted_iota(jnp.int32, (4, width), 0)
    for x in range(4):
        spreaded = mm(chunks[x].astype(BF), shuffle)[12:16, :]
        natural[x : x + 1, :] = total(jnp.where(which == group, spreaded, 0.0))
    conv_low[...] = (acc[...] + together[0:1, :]).astype(BF)
    out_copies += bring(((conv_low, conv_out), (vectors, vectors_out), (natural, natural_out)), out_sem, 5)
    for copy in pending:
        copy.wait_send()
    dealt(outgoing, incoming, me, deal_s, deal_r).wait_send()

    def stored(u, _):
        p_copy(u).wait()
        return 0

    lax.fori_loop(0, 9, stored, 0)
    for copy in out_copies:
        copy.wait()


def front(conv, encode, triple, output, expand, small, points, inverse, perm, neighbours):
    shape = jax.ShapeDtypeStruct
    n = len(FRONT_STREAMS)
    dma = pltpu.SemaphoreType.DMA
    i32 = jnp.int32
    kept = (
        ((4, 16, 128), BF),
        ((512, 512), BF),
        ((512, 512), BF),
        ((16, 512), F32),
        ((4, 512), F32),
        ((1, 512), i32),
        ((1, 512), i32),
        ((9, 3, 512), i32),
    )
    return pl.pallas_call(
        front_kernel,
        out_shape=(
            shape((4, 4, 4, 2, 432, 128), BF),
            shape((4, 5, 4, 4, 2, 16, 128), BF),
            shape(*kept[0]),
            shape((27, 512, 512), BF),
        )
        + tuple(shape(*k) for k in kept[1:]),
        in_specs=[ANY] * 10,
        out_specs=[ANY] * 11,
        scratch_shapes=[
            pltpu.VMEM((4, 512), BF),
            pltpu.VMEM((4, 1536), BF),
            pltpu.VMEM((4, 512), BF),
            pltpu.VMEM((4, 2048), BF),
            pltpu.VMEM((1, 64), F32),
            pltpu.VMEM((512, 512), BF),
            pltpu.VMEM((1, 512), i32),
            pltpu.VMEM((1, 512), i32),
            pltpu.VMEM((27, 512), i32),
            pltpu.VMEM((432, 128), BF),
        ]
        + [pltpu.VMEM(*k) for k in kept]
        + [
            pltpu.VMEM((128, 8, 512), BF),
            pltpu.VMEM((128, 8, 512), BF),
            pltpu.VMEM((4, 9, 4, 128), BF),
            pltpu.VMEM((16, 128), BF),
            pltpu.VMEM((768, 512), BF),
            pltpu.VMEM((27, 512, 512), BF),
            pltpu.VMEM((512, 512), F32),
            pltpu.VMEM((2, 4, 3, 512, 128), BF),
            pltpu.VMEM((9, 8, 512), F32),
            pltpu.VMEM((4, 9, 4, 128), BF),
            pltpu.VMEM((9, 16, 128), BF),
            pltpu.VMEM((4, 16, 128), BF),
            pltpu.VMEM((16, 128), BF),
            pltpu.VMEM((4, 4, 2, 16, 128), BF),
            dma((n, SLOTS)),
            dma((n, SLOTS)),
            dma((n, 2)),
            dma((2, 4)),
            dma((2, 4)),
            dma((2,)),
            dma((2,)),
            dma((9,)),
            dma((2,)),
            dma,
            dma,
            pltpu.SemaphoreType.REGULAR((3,)),
            dma((10,)),
            dma((8,)),
        ],
        compiler_params=pltpu.CompilerParams(
            collective_id=0, has_side_effects=True, vmem_limit_bytes=56 * 2**20
        ),
        name="front",
    )(conv, encode, triple, output, expand, small, points, inverse, perm, neighbours)


BACK_CHAINS = (
    ("cz", "zxycRL", {"R": 96, "L": 128}, "R", 0, "zyx", ((0, 48), (48, 96))),
    ("cx", "zxycRL", {"R": 160, "L": 128}, "R", 96, "xzy", ((0, 80), (80, 160))),
    ("cy", "zxycRL", {"R": 176, "L": 128}, "R", 256, "yxz", ((0, 96), (96, 176))),
    ("wide", "zKxycSL", {"K": 5, "S": 16, "L": 128}, "K", 0, "zyx", ((0, 3), (3, 5))),
)


def back_kernel(
    grad_in, first_grad_in, take_in, picks_in, w, picked, g1, gv_in,
    arrived_out, oc, o1, ov,
    returning, arrived, wide, grad, first_grad, take, picks, gv,
    kernel_grad, theirs, spread, p_buf, w_buf, rims, landed, sib, *rest,
):
    count = 12 * len(BACK_CHAINS)
    landing, rest = rest[:count], rest[count:]
    post, postr, vx, vr, p_sem, w_sem, xy_send, xy_recv, sends, recvs, vsend, vrecv, psend, precv, rim_s, rim_r, deal_s, deal_r, met, in_sem = rest
    at = place()
    me = ((at["x"] * 4 + at["y"]) * 2 + at["c"]) * 4 + at["z"]
    greet_lines(at)
    fetched = bring(
        (
            (gv_in, gv), (g1, wide), (grad_in, grad), (picks_in, picks), (take_in, take),
            (first_grad_in, first_grad),
        ),
        in_sem,
    )
    meet_lines()
    tell_line(at, "x", met.at[0])
    other = moved(at, "c", 1)
    pending = []
    tiles = kernel_grad.reshape((4, 4, 4, 2, 432, 128))

    def push(src, dst, send, recv, to):
        copy = remote_copy(src, dst, send, recv, device_at(to))
        copy.start()
        pending.append(copy)
        return copy

    mine = (tiles, "zxycRL", {"c": at["c"]})
    stores = (mine, mine, mine, (wide, "zKxycSL", {"c": at["c"]}))
    lend, start, middle, close, view = scatter_steps(
        BACK_CHAINS, stores, landing, at, sends, recvs, pending
    )
    conv_chains = (0, 1, 2)

    def vector_step(k):
        axis, steps = (("c", (1,)), ("z", (1, 2, 3)), ("y", (1, 2, 3)), ("x", (1, 2, 3)))[k]
        copies = []
        for s in steps:
            to = moved(at, axis, s)
            if axis == "x":
                src, dst = vx.at[3, to["x"]], vr.at[3, s, 0]
            else:
                src, dst = (gv if k == 0 else vx.at[k]), vr.at[k, s]
            copies.append(push(src, dst, vsend.at[k, s], vrecv.at[k, s], to))
        return copies

    def vector_add(k, copies):
        for copy in copies:
            copy.wait_recv()
        if k == 3:
            ov[...] = vx[3, at["x"]] + vr[3, 1, 0] + vr[3, 2, 0] + vr[3, 3, 0]
            return
        sum_now = gv[...] if k == 0 else vx[k]
        for s in (1,) if k == 0 else (1, 2, 3):
            sum_now = sum_now + vr[k, s]
        vx[k + 1] = sum_now

    def p_copy(u):
        slot = lax.rem(u, 2)
        return pltpu.make_async_copy(picked.at[pl.ds(u * 3, 3)], p_buf.at[slot], p_sem.at[slot])

    def w_copy(u):
        slot = lax.rem(u, 2)
        return pltpu.make_async_copy(w.at[:, pl.ds(u * 3, 3)], w_buf.at[slot], w_sem.at[slot])

    def xy_copy(n):
        x, y = lax.div(n, 4), lax.rem(n, 4)
        return remote_copy(
            tiles.at[:, x, y, other["c"]], theirs.at[:, x, y], xy_send.at[n], xy_recv.at[n], device_at(other)
        )

    def join(n):
        x, y = lax.div(n, 4), lax.rem(n, 4)
        xy_copy(n).wait_recv()
        where = tiles.at[:, x, y, at["c"]]
        where[...] = where[...] + theirs[:, x, y]

    def weight_unit(u, _):
        @pl.when(u < 8)
        def _():
            p_copy(u + 1).start()

        p_copy(u).wait()
        for j in range(3):
            product = mm_tn(p_buf[lax.rem(u, 2), j], grad[...])
            span = pl.ds(pl.multiple_of(u * 1536 + j * 512, 512), 512)
            for n in range(4):
                kernel_grad[n, span, :] = product[:, 128 * n : 128 * (n + 1)].astype(BF)
        ready, ready_next = lax.div(u * 16, 9), lax.div((u + 1) * 16, 9)
        for j in range(2):
            @pl.when(ready + j < ready_next)
            def _():
                xy_copy(ready + j).start()

        for j in range(2):
            n = lax.div((u - 2) * 16, 9) + j

            @pl.when((u >= 2) & (n < lax.div((u - 1) * 16, 9)))
            def _():
                join(n)

        return 0

    def row_unit(u, _):
        @pl.when(u < 8)
        def _():
            w_copy(u + 1).start()

        w_copy(u).wait()
        slot = lax.rem(u, 2)
        g = grad[...]
        back = [
            mm_nt(g, jnp.concatenate([w_buf[slot, n, j] for n in range(4)], axis=1)).astype(BF)
            for j in range(3)
        ]
        for b in range(2):
            hot = jnp.concatenate([spread_rows(picks.at[u], j, b) for j in range(3)], axis=1)
            terms = jnp.concatenate([back[j][256 * b : 256 * (b + 1), :] for j in range(3)], axis=0)
            spread[256 * b : 256 * b + 512, :] += mm(hot, terms)
        return 0

    p_copy(0).start()
    spread[...] = jnp.zeros_like(spread)
    fetched[0].wait()
    vectors = vector_step(0)
    state = {}
    fetched[1].wait()
    lent = lend(3, sib)
    w_copy(0).start()
    for copy in fetched[2:]:
        copy.wait()
    lax.fori_loop(0, 3, weight_unit, 0)
    pl.semaphore_wait(met.at[0], 3)
    tell_line(at, "y", met.at[1])
    state[3] = start(3, 0, lent, sib)
    vector_add(0, vectors)
    vectors = vector_step(1)
    lax.fori_loop(3, 6, weight_unit, 0)
    pl.semaphore_wait(met.at[1], 3)
    tell_line(at, "c", met.at[2])
    for i in (3,):
        middle(i, 0, state[i])
    lax.fori_loop(6, 9, weight_unit, 0)
    pl.semaphore_wait(met.at[2], 1)
    vector_add(1, vectors)
    vectors = vector_step(2)
    for i in (3,):
        close(i, 0, state[i])
        state[i] = start(i, 1)
    for n in range(12, 16):
        join(n)
    for i in conv_chains:
        state[i] = start(i, 0)
    for i in (3,):
        middle(i, 1, state[i])
    lax.fori_loop(0, 2, row_unit, 0)
    vector_add(2, vectors)
    vectors = vector_step(3)
    for i in (3,):
        close(i, 1, state[i])
        state[i] = start(i, 2)
    lax.fori_loop(2, 4, row_unit, 0)
    for i in conv_chains:
        middle(i, 0, state[i])
    for i in (3,):
        middle(i, 2, state[i])
    lax.fori_loop(4, 9, row_unit, 0)
    rims[0] = spread[0:128, :].astype(BF)
    rims[1] = spread[640:768, :].astype(BF)
    rim_copies = []
    for j, step in ((0, 127), (1, 1)):
        copy = remote_copy(rims.at[j], landed.at[j], rim_s.at[j], rim_r.at[j], line_neighbour(at, step))
        copy.start()
        pending.append(copy)
        rim_copies.append(copy)
    for i in conv_chains:
        close(i, 0, state[i])
        state[i] = start(i, 1)
    for i in (3,):
        close(i, 2, state[i])
    vector_add(3, vectors)
    swaps = swap_rows(
        wide[at["z"], :, at["x"], at["y"], at["c"]].astype(F32), post, postr, at, psend, precv, pending
    )
    for copy in rim_copies:
        copy.wait_recv()
    spread[512:640, :] += landed[0].astype(F32)
    spread[128:256, :] += landed[1].astype(F32)
    ordered_grad = (first_grad[...] + spread[128:640, :]).astype(BF)
    fold_rows(take[...], ordered_grad, returning)
    deal(returning, arrived, me, deal_s, deal_r)
    for i in conv_chains:
        middle(i, 1, state[i])
    for i in conv_chains:
        close(i, 1, state[i])
        state[i] = start(i, 2)
    swapped_rows(swaps, post, postr, at, o1)
    for i in conv_chains:
        middle(i, 2, state[i])
    for i in conv_chains:
        close(i, 2, state[i])
        name, layout, plain, cut, base, order, halves = BACK_CHAINS[i]
        oc[pl.ds(base, plain["R"]), :] = tiles[at["z"], at["x"], at["y"], at["c"], pl.ds(base, plain["R"]), :].astype(F32)
    dealt(returning, arrived, me, deal_s, deal_r).wait_recv()
    last = pltpu.make_async_copy(arrived, arrived_out, in_sem.at[6])
    last.start()
    for copy in pending:
        copy.wait_send()
    for n in range(16):
        xy_copy(n).wait_send()
    dealt(returning, arrived, me, deal_s, deal_r).wait_send()
    last.wait()


def back_scatter(grad, first_grad, take, picks, w, picked, g1, gv):
    shape = jax.ShapeDtypeStruct
    n = len(BACK_CHAINS)
    dma = pltpu.SemaphoreType.DMA
    return pl.pallas_call(
        back_kernel,
        out_shape=(
            shape((128, 8, 512), BF),
            shape((432, 128), F32),
            shape((4, 5, 4, 128), F32),
            shape((16, 128), F32),
        ),
        in_specs=[ANY] * 8,
        out_specs=[ANY] + [VM] * 3,
        scratch_shapes=[
            pltpu.VMEM((128, 8, 512), BF),
            pltpu.VMEM((128, 8, 512), BF),
            pltpu.VMEM((4, 5, 4, 4, 2, 16, 128), BF),
            pltpu.VMEM((512, 512), BF),
            pltpu.VMEM((512, 512), F32),
            pltpu.VMEM((1, 512), jnp.int32),
            pltpu.VMEM((9, 3, 512), jnp.int32),
            pltpu.VMEM((4, 16, 128), F32),
            pltpu.VMEM((4, 13824, 128), BF),
            pltpu.VMEM((4, 4, 4, 432, 128), BF),
            pltpu.VMEM((768, 512), F32),
            pltpu.VMEM((2, 3, 512, 512), BF),
            pltpu.VMEM((2, 4, 3, 512, 128), BF),
            pltpu.VMEM((2, 128, 512), BF),
            pltpu.VMEM((2, 128, 512), BF),
            pltpu.VMEM((4, 5, 4, 4, 16, 128), BF),
        ]
        + [pltpu.VMEM(s, BF) for chain in BACK_CHAINS for s in landing_shapes(chain)]
        + [
            pltpu.VMEM((4, 5, 4, 128), BF),
            pltpu.VMEM((4, 5, 4, 128), BF),
            pltpu.VMEM((4, 4, 16, 128), F32),
            pltpu.VMEM((4, 4, 4, 16, 128), F32),
            dma((2,)),
            dma((2,)),
            dma((16,)),
            dma((16,)),
            dma((n, 22)),
            dma((n, 22)),
            dma((4, 4)),
            dma((4, 4)),
            dma((4,)),
            dma((4,)),
            dma((2,)),
            dma((2,)),
            dma,
            dma,
            pltpu.SemaphoreType.REGULAR((3,)),
            dma((7,)),
        ],
        compiler_params=pltpu.CompilerParams(
            collective_id=1, has_side_effects=True, vmem_limit_bytes=62 * 2**20
        ),
        name="back_scatter",
    )(grad, first_grad, take, picks, w, picked, g1, gv)


def last_kernel(
    arrived_in, send_in, result_in, oc_in, wide_in, up_in, tall_in, ov_in,
    result, points_grad, oc, tall, encode, triple, output, expand, small,
    arrived, send, wide, up, ov, rows, encode_v, triple_v, output_v, expand_v, small_v, result_v, oc_v, tall_v, in_sem, out_sem,
):
    through = bring(((result_in, result_v), (oc_in, oc_v), (tall_in, tall_v)), in_sem)
    fetched = bring(
        ((wide_in, wide), (up_in, up), (ov_in, ov), (send_in, send), (arrived_in, arrived)), in_sem, 3
    )
    at = place()
    fetched[0].wait()
    n = 0
    for ref, blocks in ((encode_v, 4), (triple_v, 12), (output_v, 4)):
        for j in range(blocks):
            ref[:, 128 * j : 128 * (j + 1)] = wide[n // 5, n % 5]
            n += 1
    out = bring(((encode_v, encode), (triple_v, triple), (output_v, output)), out_sem)
    fetched[1].wait()
    for j in range(16):
        expand_v[:, 128 * j : 128 * (j + 1)] = up[j // 4, j % 4]
    out += bring(((expand_v, expand),), out_sem, 3)
    fetched[2].wait()
    lane0 = lax.rem(at["y"] * 2 + at["c"], 8) * 16 + at["z"] * 4
    lane = lax.broadcasted_iota(jnp.int32, (128, 128), 0)
    to = lax.broadcasted_iota(jnp.int32, (128, 128), 1)
    pick = jnp.where((lane == lane0 + to) & (to < 4), 1.0, 0.0).astype(BF)
    hi, mid, lo = three(ov[...])
    small_v[...] = mm(hi.astype(BF), pick) + mm(mid.astype(BF), pick) + mm(lo.astype(BF), pick)
    out += bring(((small_v, small),), out_sem, 4)
    for copy in through:
        copy.wait()
    out += bring(((result_v, result), (oc_v, oc), (tall_v, tall)), out_sem, 6)
    fetched[3].wait()
    fetched[4].wait()
    rows[...] = unfold_rows(send[...], arrived)
    out += bring(((rows, points_grad),), out_sem, 5)
    for copy in out:
        copy.wait()


def last(arrived, send, result, oc, wide, up, tall, ov):
    shape = jax.ShapeDtypeStruct
    widths = (512, 1536, 512, 2048)
    return pl.pallas_call(
        last_kernel,
        out_shape=(
            shape((512, 512), BF),
            shape((512, 512), BF),
            shape((432, 128), F32),
            shape((16, 512), F32),
        )
        + tuple(shape((4, w), F32) for w in widths)
        + (shape((16, 128), F32),),
        in_specs=[ANY] * 8,
        out_specs=[ANY] * 9,
        scratch_shapes=[
            pltpu.VMEM((128, 8, 512), BF),
            pltpu.VMEM((1, 512), jnp.int32),
            pltpu.VMEM((4, 5, 4, 128), F32),
            pltpu.VMEM((4, 4, 4, 128), F32),
            pltpu.VMEM((16, 128), F32),
            pltpu.VMEM((512, 512), BF),
        ]
        + [pltpu.VMEM((4, w), F32) for w in widths]
        + [
            pltpu.VMEM((16, 128), F32),
            pltpu.VMEM((512, 512), BF),
            pltpu.VMEM((432, 128), F32),
            pltpu.VMEM((16, 512), F32),
            pltpu.SemaphoreType.DMA((8,)),
            pltpu.SemaphoreType.DMA((9,)),
        ],
        compiler_params=pltpu.CompilerParams(vmem_limit_bytes=60 * 2**20),
        name="last",
    )(arrived, send, result, oc, wide, up, tall, ov)


def per_device(
    points,
    perm,
    inverse,
    lengths,
    neighbours,
    conv_weight,
    conv_bias,
    encode_weight,
    encode_bias,
    encode_gain,
    encode_shift,
    before_gain,
    before_shift,
    triple_weight,
    query_bias,
    value_bias,
    output_weight,
    output_bias,
    second_gain,
    second_shift,
    expand_weight,
    expand_bias,
    reduce_weight,
    reduce_bias,
    grad_out,
):
    small = jnp.concatenate(
        [
            conv_bias,
            encode_bias,
            encode_gain,
            encode_shift,
            before_gain,
            before_shift,
            query_bias,
            value_bias,
            output_bias,
            second_gain,
            second_shift,
            reduce_bias,
            expand_bias,
        ]
    )
    kernel, wide, up_own, picked, conv, ordered, vectors, wide_bias, take, send, picks = front(
        conv_weight,
        encode_weight,
        triple_weight,
        output_weight,
        expand_weight,
        small.astype(F32).reshape(1, 64),
        points,
        inverse.reshape(1, 512),
        perm.reshape(1, 512),
        neighbours,
    )
    result, grad_first, grad_conv, grad_wide, vector_grads, up_out, tall_out = block(
        lengths,
        conv,
        ordered,
        grad_out,
        wide.reshape(20, 512, 128),
        up_own,
        reduce_weight,
        vectors,
        wide_bias,
    )
    arrived, kernel_out, wide_out, vector_out = back_scatter(
        grad_conv,
        grad_first,
        take,
        picks,
        kernel.reshape(4, 27, 512, 128),
        picked,
        grad_wide.reshape(4, 5, 4, 4, 2, 16, 128),
        vector_grads,
    )
    result, points_grad, kernel_out, tall_out, encode_out, triple_out, output_out, up_out, vector_out = last(
        arrived, send, result, kernel_out, wide_out, up_out, tall_out, vector_out
    )
    vector_out = vector_out[:, :4]
    reduced = (
        vector_out[V_CONV],
        encode_out,
        vector_out[V_ENC],
        vector_out[V_GAIN0],
        vector_out[V_SHIFT0],
        vector_out[V_GAIN1],
        vector_out[V_SHIFT1],
        triple_out,
        vector_out[V_QUERY],
        vector_out[V_VALUE],
        output_out,
        vector_out[V_OUT],
        vector_out[V_GAIN2],
        vector_out[V_SHIFT2],
        up_out,
        vector_out[12:].reshape(16),
        tall_out,
        vector_out[V_RED],
    )
    return (result, points_grad, kernel_out) + reduced


def solution(mesh):
    in_specs = (
        P(("pts", "rep"), None),
        P(("pts", "rep")),
        P(("pts", "rep")),
        P(("pts", "rep")),
        P(None, ("pts", "rep")),
        P("pts", "rep"),
        P(("pts", "rep")),
        P(("pts", "rep"), None),
        P(("pts", "rep")),
        P(("pts", "rep")),
        P(("pts", "rep")),
        P(("pts", "rep")),
        P(("pts", "rep")),
        P(("pts", "rep"), None),
        P(("pts", "rep")),
        P(("pts", "rep")),
        P(("pts", "rep"), None),
        P(("pts", "rep")),
        P(("pts", "rep")),
        P(("pts", "rep")),
        P(("pts", "rep"), None),
        P(("pts", "rep")),
        P(("pts", "rep"), None),
        P(("pts", "rep")),
        P(("pts", "rep"), None),
    )
    out_specs = (
        P(("pts", "rep"), None),
        P(("pts", "rep"), None),
        P("pts", "rep"),
        P(("pts", "rep")),
        P(("pts", "rep"), None),
        P(("pts", "rep")),
        P(("pts", "rep")),
        P(("pts", "rep")),
        P(("pts", "rep")),
        P(("pts", "rep")),
        P(("pts", "rep"), None),
        P(("pts", "rep")),
        P(("pts", "rep")),
        P(("pts", "rep"), None),
        P(("pts", "rep")),
        P(("pts", "rep")),
        P(("pts", "rep")),
        P(("pts", "rep"), None),
        P(("pts", "rep")),
        P(("pts", "rep"), None),
        P(("pts", "rep")),
    )
    return jax.shard_map(
        per_device, mesh=mesh, in_specs=in_specs, out_specs=out_specs, check_vma=False
    )
```
